32 devices in a mesh: wrap: 8 (over y, x, core), normal: 4 (over z).
Axes of the slice: x: 2, y: 2, z: 4, core: 2. Of those that a mesh axis runs over, the one named last changes fastest.
Arguments:
- residual: float32 [5, 2, 256, 1024], P(None, None, 'normal', 'wrap'), may hold values from -144 to 144
- courant_xi: float32 [5, 2, 256, 1024], P(None, None, 'normal', 'wrap'), may hold values from -300 to 300
- courant_eta: float32 [5, 2, 256, 1024], P(None, None, 'normal', 'wrap'), may hold values from -300 to 300
- dissip_xi: float32 [2, 256, 1024], P(None, 'normal', 'wrap'), may hold values from 0.02 to 2
- dissip_eta: float32 [2, 256, 1024], P(None, 'normal', 'wrap'), may hold values from 0.02 to 2
- coupling: bfloat16 [5, 5, 2, 256, 1024], P(None, None, None, 'normal', 'wrap'), may hold values from -2.5 to 2.5
Outputs:
- update: float32 [5, 2, 256, 1024], P(None, None, 'normal', 'wrap')
The draws below stay inside these ranges and needn't reach their ends.
All inputs are finite; a program needn't handle non-finite values.
Results may differ from the reference program's by a relative error of at most 0.0003.
Values sent between devices are 32-bit elements; how exact they have to be, the bound alone decides.
No kernel may reach another device: no remote copies, remote signals or barrier semaphores. Data moves between devices by JAX's collectives and lax.ppermute only.
A program may use at most 128 MiB of HBM per device.

```python
import math
import jax
import jax.numpy as jnp
from jax import lax

FIELDS = 5
SPAN = 2
NW = 1024
NN = 256


def speeds(key):
    line_shape = (FIELDS, SPAN, NN, NW)
    first_key, second_key, third_key = jax.random.split(key, 3)
    lowest = math.log(12.0)
    base = jnp.exp(jax.random.uniform(first_key, (FIELDS, SPAN, 1, 1), jnp.float32, lowest, math.log(300.0)))
    rough = jnp.exp(jax.random.uniform(second_key, line_shape, jnp.float32, math.log(0.5), 0.0))
    sign_part = jnp.where(jax.random.bernoulli(third_key, 0.5, (FIELDS, SPAN, 1, 1)), 1.0, -1.0)
    return jnp.clip(sign_part * base * rough, -300.0, 300.0).astype(jnp.float32)


def draw_courant_xi(key, part):
    return speeds(jax.random.fold_in(key, 11))


def draw_courant_eta(key, part):
    return speeds(jax.random.fold_in(key, 23))


def levels(rng, shape, cuts, low, largest):
    factor_of, own = 1.0, jax.random.fold_in(rng, 6)
    for dim, parts in cuts:
        steps = jnp.exp(jax.random.uniform(jax.random.fold_in(own, dim), (parts,), jnp.float32, low / len(cuts), largest / len(cuts)))
        factor_of = factor_of * jnp.repeat(steps, shape[dim] // parts).reshape([-1 if axis == dim else 1 for axis in range(len(shape))])
    return factor_of


def gaussian(key, dims, width, reach, cuts=(), kind=jnp.bfloat16):
    entries = jax.random.normal(key, dims, jnp.float32) * width
    if len(cuts) > 0:
        entries = levels(key, dims, cuts, -0.22, 0.18) * entries
    return jnp.clip(entries, min=-reach, max=reach).astype(kind)


def setup_inputs(seed: int = 0) -> dict:
    streams_of = jax.random.split(jax.random.key(seed), 7)
    return {
        "residual": gaussian(streams_of[0], (FIELDS, SPAN, NN, NW), 24.0, 144.0, ((2, 4), (3, 8)), jnp.float32),
        "courant_xi": draw_courant_xi(jax.random.fold_in(streams_of[6], 71), 0),
        "courant_eta": draw_courant_eta(jax.random.fold_in(streams_of[6], 71), 0),
        "dissip_xi": jnp.clip(jnp.exp(math.log(2.0) - 4.6051702 * jax.random.uniform(streams_of[3], (SPAN, NN, NW), jnp.float32) ** levels(streams_of[3], (SPAN, NN, NW), ((1, 4), (2, 8)), -0.2, 0.2)), 0.02, 2.0),
        "dissip_eta": jnp.clip(jnp.exp(math.log(2.0) - 4.6051702 * jax.random.uniform(streams_of[4], (SPAN, NN, NW), jnp.float32) ** levels(streams_of[4], (SPAN, NN, NW), ((1, 4), (2, 8)), -0.2, 0.2)), 0.02, 2.0),
        "coupling": gaussian(streams_of[5], (FIELDS, FIELDS, SPAN, NN, NW), FIELDS ** -0.5, 2.5, ((3, 4), (4, 8))),
    }


def block_product(left_block, right_block):
    return jnp.sum(left_block[:, :, None] * right_block[None], axis=1)


def identity(block_width, batch_shape):
    batch_shape = tuple(batch_shape)
    square = jnp.eye(block_width, dtype=jnp.float32).reshape((block_width, block_width) + (1,) * len(batch_shape))
    return jnp.broadcast_to(square, (block_width, block_width) + batch_shape)


def small_solve(matrix, values):
    block_width = matrix.shape[0]
    matrix_rows = [matrix[i] for i in range(block_width)]
    right_sides = [values[i] for i in range(block_width)]
    for column in range(block_width):
        inverse = 1.0 / matrix_rows[column][column]
        matrix_rows[column] = matrix_rows[column] * inverse[None]
        right_sides[column] = right_sides[column] * inverse[None]
        for target in range(block_width):
            if target != column:
                factor = matrix_rows[target][column]
                matrix_rows[target] = matrix_rows[target] - factor[None] * matrix_rows[column]
                right_sides[target] = right_sides[target] - factor[None] * right_sides[column]
    return jnp.stack(right_sides)


def thomas(lower, diag, upper, values):
    block_width = diag.shape[0]
    columns = values.shape[1]
    batch_shape = diag.shape[3:]

    def forward_sweep(scan_carry, row_entries):
        eliminate_previous, substitute_previous = scan_carry
        lower_neighbour, center_block, above, source = row_entries
        pivot_matrix = center_block - block_product(lower_neighbour, eliminate_previous)
        joined = small_solve(pivot_matrix, jnp.concatenate([above, source - block_product(lower_neighbour, substitute_previous)], axis=1))
        outputs = (joined[:, :block_width], joined[:, block_width:])
        return outputs, outputs

    start_state = (jnp.zeros((block_width, block_width) + batch_shape, jnp.float32),
             jnp.zeros((block_width, columns) + batch_shape, jnp.float32))
    input_rows = tuple(jnp.moveaxis(operand, 2, 0) for operand in (lower, diag, upper, values))
    ignored_output, (eliminated_rows, substituted_rows) = lax.scan(forward_sweep, start_state, input_rows)

    def backward(following_value, row_entries):
        eliminate_row, substitute_row = row_entries
        current_row = substitute_row - block_product(eliminate_row, following_value)
        return current_row, current_row

    unused_last, solution = lax.scan(backward, jnp.zeros((block_width, columns) + batch_shape, jnp.float32),
                                     (eliminated_rows, substituted_rows), reverse=True)
    return jnp.moveaxis(solution, 0, 2)


def periodic_solve(lower, diag, upper, values):
    block_width = diag.shape[0]
    row_count = diag.shape[2]
    batch_shape = diag.shape[3:]
    columns = values.shape[1]
    filler = jnp.zeros((block_width, block_width, row_count - 1) + batch_shape, jnp.float32)
    left_cols = jnp.concatenate([-lower[:, :, :1], filler], axis=2)
    right_cols = jnp.concatenate([filler, -upper[:, :, -1:]], axis=2)
    solved = thomas(lower, diag, upper, jnp.concatenate([values, left_cols, right_cols], axis=1))
    base_part = solved[:, :columns]
    last_coef = solved[:, columns:columns + block_width]
    first_coef = solved[:, columns + block_width:]
    corner = jnp.concatenate([
        jnp.concatenate([first_coef[:, :, 0], last_coef[:, :, 0]], axis=1),
        jnp.concatenate([first_coef[:, :, -1], last_coef[:, :, -1]], axis=1)], axis=0)
    corner_values = small_solve(identity(2 * block_width, batch_shape) - corner,
                                jnp.concatenate([base_part[:, :, 0], base_part[:, :, -1]], axis=0))
    return (base_part + block_product(last_coef, corner_values[block_width:][:, :, None])
            + block_product(first_coef, corner_values[:block_width][:, :, None]))


def even_rows(array):
    return array[0::2]


def odd_rows(array):
    return array[1::2]


def pair_system(before, speed, after, damp_before, damping, damp_after, source):
    minus_two = damp_before
    plus_two = damp_after
    minus_one = -2.0 * (damp_before + damping) - 0.25 * (before + speed)
    plus_one = -2.0 * (damping + damp_after) + 0.25 * (speed + after)
    center_block = 1.0 + damp_before + 4.0 * damping + damp_after
    empty = jnp.zeros_like(even_rows(damping))
    lower = jnp.stack([jnp.stack([even_rows(minus_two), even_rows(minus_one)]),
                       jnp.stack([empty, odd_rows(minus_two)])])
    diag = jnp.stack([jnp.stack([even_rows(center_block), even_rows(plus_one)]),
                      jnp.stack([odd_rows(minus_one), odd_rows(center_block)])])
    upper = jnp.stack([jnp.stack([even_rows(plus_two), empty]),
                       jnp.stack([odd_rows(plus_one), odd_rows(plus_two)])])
    values = jnp.stack([even_rows(source), odd_rows(source)])[:, None]
    return lower, diag, upper, values


def unpair(paired):
    cells = paired[:, 0]
    return jnp.moveaxis(cells, 0, 1).reshape((cells.shape[1] * 2,) + cells.shape[2:])


def reference(residual, courant_xi, courant_eta, dissip_xi, dissip_eta, coupling):
    full_shape = residual.shape
    groups = full_shape[0] * full_shape[1]

    def grouped(array):
        return jnp.broadcast_to(array.astype(jnp.float32), full_shape).reshape((groups,) + full_shape[2:])

    def wrap_solve(operands):
        lines = [jnp.transpose(operand) for operand in operands]
        speed = lines[1]
        damping = lines[2]
        lower, diag, upper, values = pair_system(jnp.roll(speed, 1, axis=0), speed, jnp.roll(speed, -1, axis=0),
                                                 jnp.roll(damping, 1, axis=0), damping,
                                                 jnp.roll(damping, -1, axis=0), lines[0])
        return jnp.transpose(unpair(periodic_solve(lower, diag, upper, values)))

    xi_update = lax.map(wrap_solve, (grouped(residual), grouped(courant_xi), grouped(dissip_xi))).reshape(full_shape)
    mixed = coupling[:, 0].astype(jnp.float32) * xi_update[0]
    for source_field in range(1, full_shape[0]):
        mixed = mixed + coupling[:, source_field].astype(jnp.float32) * xi_update[source_field]

    def wall_solve(operands):
        source, speed, damping = operands
        edge = jnp.zeros((1,) + speed.shape[1:], jnp.float32)
        before = jnp.concatenate([edge, speed[:-1]], axis=0)
        after = jnp.concatenate([speed[1:], edge], axis=0)
        damp_before = jnp.concatenate([edge, damping[:-1]], axis=0)
        damp_after = jnp.concatenate([damping[1:], edge], axis=0)
        lower, diag, upper, values = pair_system(before, speed, after, damp_before, damping, damp_after, source)
        return unpair(thomas(lower, diag, upper, values))

    update = lax.map(wall_solve, (grouped(mixed), grouped(courant_eta), grouped(dissip_eta))).reshape(full_shape)
    return update
```

```python
import functools

import jax
import jax.numpy as jnp
from jax import lax
from jax.experimental import pallas as pl
from jax.experimental.pallas import tpu as pltpu
from jax.sharding import PartitionSpec as P

VALUES = 20
FACTORS = 10
CHUNKS = 8


def inverse(a, b, c, d):
    scale = 1.0 / (a * d - b * c)
    return (d * scale, -b * scale, -c * scale, a * scale)


def times(x, y):
    return (
        x[0] * y[0] + x[1] * y[2],
        x[0] * y[1] + x[1] * y[3],
        x[2] * y[0] + x[3] * y[2],
        x[2] * y[1] + x[3] * y[3],
    )


def apply(x, v):
    return (x[0] * v[0] + x[1] * v[1], x[2] * v[0] + x[3] * v[1])


def minus(x, y):
    return tuple(a - b for a, b in zip(x, y))


def plus(x, y):
    return tuple(a + b for a, b in zip(x, y))


def negative(x):
    return tuple(-a for a in x)


def split(element):
    return (
        element[0:4],
        element[4:8],
        element[8:12],
        element[12:16],
        element[16:18],
        element[18:20],
    )


def merge(first, second):
    ll, lm, ml, mm, fl, fm = split(first)
    nn, mr, rm, rr, gm, fr = split(second)
    pivot = inverse(*plus(mm, nn))
    wl = times(pivot, ml)
    wr = times(pivot, mr)
    w = apply(pivot, plus(fm, gm))
    merged = (
        minus(ll, times(lm, wl))
        + negative(times(lm, wr))
        + negative(times(rm, wl))
        + minus(rr, times(rm, wr))
        + minus(fl, apply(lm, w))
        + minus(fr, apply(rm, w))
    )
    return merged, wl + wr + w


def inner(factors, left, right):
    wl, wr, w = factors[0:4], factors[4:8], factors[8:10]
    return minus(minus(w, apply(wl, left)), apply(wr, right))


def chunk_element(speed, damp, source, cells, save):
    def link(i):
        p = 2.0 * (damp(i) + damp(i + 1))
        q = 0.25 * (speed(i) + speed(i + 1))
        return q - p, -q - p

    def centre(i):
        return 1.0 + damp(i - 1) + 4.0 * damp(i) + damp(i + 1)

    b0, b1 = damp(0), damp(1)
    quarter = 0.25 * speed(0)
    up, low = link(0)
    zero = jnp.zeros_like(b0)
    ll = (b0, quarter - 2.0 * b0, -quarter - 2.0 * b0, 1.0 + 4.0 * b0 + b1)
    lk = (b0, zero, up, b1)
    kl = (b0, low, zero, b1)
    up, low = link(1)
    kk = (centre(1), up, low, centre(2))
    fl = (zero, source(0))
    fk = (source(1), source(2))
    pairs = (cells - 2) // 2
    for k in range(1, pairs + 1):
        i = 2 * k
        pivot = inverse(*kk)
        wl = times(pivot, kl)
        up, low = link(i)
        here, there = damp(i), damp(i + 1)
        wr = (
            pivot[0] * here + pivot[1] * up,
            pivot[1] * there,
            pivot[2] * here + pivot[3] * up,
            pivot[3] * there,
        )
        w = apply(pivot, fk)
        save(k - 1, wl + wr + w)

        def below(x):
            return (
                here * x[0] + low * x[2],
                here * x[1] + low * x[3],
                there * x[2],
                there * x[3],
            )

        ll = minus(ll, times(lk, wl))
        fl = minus(fl, apply(lk, w))
        lk = negative(times(lk, wr))
        kl = negative(below(wl))
        if k < pairs:
            up, low_next = link(i + 1)
            kk = (centre(i + 1), up, low_next, centre(i + 2))
            fk = (source(i + 1), source(i + 2))
        else:
            quarter = 0.25 * speed(i + 1)
            kk = (
                1.0 + here + 4.0 * there,
                quarter - 2.0 * there,
                -quarter - 2.0 * there,
                there,
            )
            fk = (source(i + 1), zero)
        kk = minus(kk, below(wr))
        fk = minus(fk, (here * w[0] + low * w[1], there * w[1]))
    return ll + lk + kl + kk + fl + fk


def blocks(rows, size):
    return [(at, min(size, rows - at)) for at in range(0, rows, size)]


def merge_level(source_ref, target_ref, factor_ref, rows):
    for at, size in blocks(rows, 8):
        first = tuple(source_ref[v, pl.ds(2 * at, size, stride=2), :] for v in range(VALUES))
        second = tuple(source_ref[v, pl.ds(2 * at + 1, size, stride=2), :] for v in range(VALUES))
        merged, factors = merge(first, second)
        for v in range(VALUES):
            target_ref[v, pl.ds(at, size), :] = merged[v]
        for v in range(FACTORS):
            factor_ref[v, pl.ds(at, size), :] = factors[v]


def split_level(source_ref, target_ref, factor_ref, rows):
    for at, size in blocks(rows, 8):
        left = tuple(source_ref[v, pl.ds(at, size), :] for v in (0, 1))
        right = tuple(source_ref[v, pl.ds(at, size), :] for v in (2, 3))
        factors = tuple(factor_ref[v, pl.ds(at, size), :] for v in range(FACTORS))
        middle = inner(factors, left, right)
        for v in range(2):
            target_ref[v, pl.ds(2 * at, size, stride=2), :] = left[v]
            target_ref[v, pl.ds(2 * at + 1, size, stride=2), :] = middle[v]
            target_ref[2 + v, pl.ds(2 * at, size, stride=2), :] = middle[v]
            target_ref[2 + v, pl.ds(2 * at + 1, size, stride=2), :] = right[v]


def tree(items):
    while len(items) > 1:
        paired = [merge(items[i], items[i + 1])[0] for i in range(0, len(items) - 1, 2)]
        items = paired + items[len(items) - len(items) % 2 :]
    return items[0]


def ring_ends(gathered_ref, place, count, rows):
    ends = []
    for at, size in blocks(rows, 8):
        elements = []
        for k in range(count):
            owner = lax.rem(place + k, count)
            elements.append(
                tuple(gathered_ref[owner, pl.ds(v * rows + at, size), :] for v in range(VALUES))
            )
        own = split(elements[0])
        rest = split(tree(elements[1:]))
        a = plus(own[0], rest[3])
        b = plus(own[1], rest[2])
        c = plus(own[2], rest[1])
        pivot = inverse(*plus(own[3], rest[0]))
        f = plus(own[4], rest[5])
        g = plus(own[5], rest[4])
        bd = times(b, pivot)
        left = apply(inverse(*minus(a, times(bd, c))), minus(f, apply(bd, g)))
        right = apply(pivot, minus(g, apply(c, left)))
        ends.append((at, size, left, right))
    return ends


def levels_of(lines):
    sizes = []
    rows = lines * CHUNKS
    while rows > lines:
        rows //= 2
        sizes.append(rows)
    return sizes


def merge_all(first_ref, element_refs, factor_refs, sizes):
    source = first_ref
    for rows, target, factor in zip(sizes, element_refs, factor_refs):
        merge_level(source, target, factor, rows)
        source = target
    return source


def split_all(top_ref, end_refs, factor_refs, sizes):
    source = top_ref
    for rows, target, factor in zip(reversed(sizes), end_refs, reversed(factor_refs)):
        split_level(source, target, factor, rows)
        source = target
    return source


def back_substitute(ends_ref, factor_ref, cells, at, size, put):
    left = tuple(ends_ref[v, pl.ds(at, size), :] for v in (0, 1))
    right = tuple(ends_ref[v, pl.ds(at, size), :] for v in (2, 3))
    put(0, left[1])
    put(cells - 1, right[0])
    following = right
    for k in range((cells - 2) // 2 - 1, -1, -1):
        factors = tuple(factor_ref[k * FACTORS + v, pl.ds(at, size), :] for v in range(FACTORS))
        following = inner(factors, left, following)
        put(2 * k + 1, following[0])
        put(2 * k + 2, following[1])


def wrap_down(
    fields, cells, residual, courant, dissip, packed, chunk_factors, f0, f1, f2,
    source_t, speed_t, damp_t, e0, e1, e2, e3,
):
    lanes = dissip.shape[0]
    length = cells * CHUNKS
    damp_t[...] = dissip[...].T
    for field in range(fields):
        source_t[pl.ds(field * length, length), :] = residual[pl.ds(field * lanes, lanes), :].T
        speed_t[pl.ds(field * length, length), :] = courant[pl.ds(field * lanes, lanes), :].T
    for at, size in blocks(fields * CHUNKS, 16):
        repeat = size // CHUNKS

        def speed(i):
            return speed_t[pl.ds(at * cells + i, size, stride=cells), :]

        def source(i):
            return source_t[pl.ds(at * cells + i, size, stride=cells), :]

        def damp(i):
            rows = damp_t[pl.ds(i, CHUNKS, stride=cells), :]
            return jnp.concatenate([rows] * repeat, axis=0) if repeat > 1 else rows

        def save(k, factors):
            for v in range(FACTORS):
                chunk_factors[k * FACTORS + v, pl.ds(at, size), :] = factors[v]

        element = chunk_element(speed, damp, source, cells, save)
        for v in range(VALUES):
            e0[v, pl.ds(at, size), :] = element[v]
    sizes = levels_of(fields)
    merge_all(e0, (e1, e2, e3), (f0, f1, f2), sizes)
    for v in range(VALUES):
        packed[pl.ds(v * fields, fields), :] = e3[v]


def middle(
    fields, span, wrap_cells, wall_cells, wrap_count,
    place, gathered, chunk_factors, f0, f1, f2, coupling, courant, dissip,
    packed, wall_factors, g0, g1, g2,
    x3, x2, x1, x0, solved_t, solved, mixed, e0, e1, e2, e3,
):
    for at, size, left, right in ring_ends(gathered, place[0], wrap_count, fields):
        for v in range(2):
            x3[v, pl.ds(at, size), :] = left[v]
            x3[2 + v, pl.ds(at, size), :] = right[v]
    ends = split_all(x3, (x2, x1, x0), (f0, f1, f2), levels_of(fields))
    length = wrap_cells * CHUNKS
    for at, size in blocks(fields * CHUNKS, 16):

        def put(i, value):
            solved_t[pl.ds(at * wrap_cells + i, size, stride=wrap_cells), :] = value

        back_substitute(ends, chunk_factors, wrap_cells, at, size, put)
    lanes = solved.shape[0] // fields
    for field in range(fields):
        solved[pl.ds(field * lanes, lanes), :] = solved_t[pl.ds(field * length, length), :].T

    for at, size in blocks(lanes, 16):
        update = [solved[pl.ds(j * lanes + at, size), :] for j in range(fields)]
        for k in range(fields):
            total = coupling[k, 0, pl.ds(at, size), :].astype(jnp.float32) * update[0]
            for j in range(1, fields):
                total = total + coupling[k, j, pl.ds(at, size), :].astype(jnp.float32) * update[j]
            mixed[pl.ds(k * lanes + at, size), :] = total

    lines = fields * span
    for field in range(fields):
        rows = span * CHUNKS
        at = field * rows

        def speed(i):
            return courant[pl.ds(at * wall_cells + i, rows, stride=wall_cells), :]

        def source(i):
            return mixed[pl.ds(at * wall_cells + i, rows, stride=wall_cells), :]

        def damp(i):
            return dissip[pl.ds(i, rows, stride=wall_cells), :]

        def save(k, factors):
            for v in range(FACTORS):
                wall_factors[k * FACTORS + v, pl.ds(at, rows), :] = factors[v]

        element = chunk_element(speed, damp, source, wall_cells, save)
        for v in range(VALUES):
            e0[v, pl.ds(at, rows), :] = element[v]
    merge_all(e0, (e1, e2, e3), (g0, g1, g2), levels_of(lines))
    not_first = jnp.where(place[1] > 0, 1.0, 0.0)
    not_last = jnp.where(place[1] < place[2] - 1, 1.0, 0.0)
    outside_left = (0, 1, 2, 4, 5, 8, 10, 16)
    outside_right = (5, 7, 10, 11, 13, 14, 15, 19)
    for v in range(VALUES):
        value = e3[v]
        if v in outside_left:
            value = value * not_first
        if v in outside_right:
            value = value * not_last
        packed[pl.ds(v * lines, lines), :] = value


def wall_up(
    lines, cells, wall_count,
    place, gathered, chunk_factors, g0, g1, g2,
    update,
    x3, x2, x1, x0,
):
    not_first = jnp.where(place[1] > 0, 1.0, 0.0)
    not_last = jnp.where(place[1] < place[2] - 1, 1.0, 0.0)
    for at, size, left, right in ring_ends(gathered, place[1], wall_count, lines):
        x3[0, pl.ds(at, size), :] = left[0] * not_first
        x3[1, pl.ds(at, size), :] = left[1]
        x3[2, pl.ds(at, size), :] = right[0]
        x3[3, pl.ds(at, size), :] = right[1] * not_last
    ends = split_all(x3, (x2, x1, x0), (g0, g1, g2), levels_of(lines))
    for at, size in blocks(lines * CHUNKS, 16):

        def put(i, value):
            update[pl.ds(at * cells + i, size, stride=cells), :] = value

        back_substitute(ends, chunk_factors, cells, at, size, put)


def f32(*shape):
    return jax.ShapeDtypeStruct(shape, jnp.float32)


def vmem(*shape):
    return pltpu.VMEM(shape, jnp.float32)


IN_VMEM = pl.BlockSpec(memory_space=pltpu.VMEM)
IN_SMEM = pl.BlockSpec(memory_space=pltpu.SMEM)
PARAMS = pltpu.CompilerParams(vmem_limit_bytes=32 * 2**20)


def factor_shapes(rows, cells):
    sizes = levels_of(rows)
    return [f32(FACTORS * ((cells - 2) // 2), rows * CHUNKS, 128)] + [
        f32(FACTORS, size, 128) for size in sizes
    ]


def element_scratch(rows):
    return [vmem(VALUES, size, 128) for size in [rows * CHUNKS] + levels_of(rows)]


def end_scratch(rows):
    return [vmem(4, size, 128) for size in reversed([rows * CHUNKS] + levels_of(rows))]


def local(residual, courant_xi, courant_eta, dissip_xi, dissip_eta, coupling):
    fields, span, high, wide = residual.shape
    lanes = span * high
    wrap_cells, wall_cells = wide // CHUNKS, high // CHUNKS
    wrap_count, wall_count = lax.axis_size("wrap"), lax.axis_size("normal")
    lines = fields * span
    place = jnp.stack(
        [lax.axis_index("wrap"), lax.axis_index("normal"), jnp.int32(wall_count)]
    ).astype(jnp.int32)

    def rows_of(array):
        return array.reshape(-1, wide)

    packed, *wrap_factors = pl.pallas_call(
        functools.partial(wrap_down, fields, wrap_cells),
        out_shape=[f32(VALUES * fields, lanes)] + factor_shapes(fields, wrap_cells),
        in_specs=[IN_VMEM] * 3,
        out_specs=[IN_VMEM] * 5,
        scratch_shapes=[
            vmem(fields * wide, lanes),
            vmem(fields * wide, lanes),
            vmem(wide, lanes),
        ]
        + element_scratch(fields),
        compiler_params=PARAMS,
        name="wrap_down",
    )(rows_of(residual), rows_of(courant_xi), rows_of(dissip_xi))
    gathered = lax.all_gather(packed, "wrap", axis=0, tiled=False)
    packed, *wall_factors = pl.pallas_call(
        functools.partial(middle, fields, span, wrap_cells, wall_cells, wrap_count),
        out_shape=[f32(VALUES * lines, wide)] + factor_shapes(lines, wall_cells),
        in_specs=[IN_SMEM] + [IN_VMEM] * 8,
        out_specs=[IN_VMEM] * 5,
        scratch_shapes=end_scratch(fields)
        + [vmem(fields * wide, lanes), vmem(fields * lanes, wide), vmem(fields * lanes, wide)]
        + element_scratch(lines),
        compiler_params=PARAMS,
        name="middle",
    )(
        place,
        gathered,
        *wrap_factors,
        coupling.reshape(fields, fields, lanes, wide),
        rows_of(courant_eta),
        rows_of(dissip_eta),
    )
    gathered = lax.all_gather(packed, "normal", axis=0, tiled=False)
    update = pl.pallas_call(
        functools.partial(wall_up, lines, wall_cells, wall_count),
        out_shape=f32(fields * lanes, wide),
        in_specs=[IN_SMEM] + [IN_VMEM] * 5,
        out_specs=IN_VMEM,
        scratch_shapes=end_scratch(lines),
        compiler_params=PARAMS,
        name="wall_up",
    )(place, gathered, *wall_factors)
    return update.reshape(residual.shape)


def solution(mesh):
    placed = (
        P(None, None, "normal", "wrap"),
        P(None, None, "normal", "wrap"),
        P(None, None, "normal", "wrap"),
        P(None, "normal", "wrap"),
        P(None, "normal", "wrap"),
        P(None, None, None, "normal", "wrap"),
    )
    return jax.shard_map(
        local,
        mesh=mesh,
        in_specs=placed,
        out_specs=P(None, None, "normal", "wrap"),
        check_vma=False,
    )
```

```python
import functools

import jax
import jax.numpy as jnp
from jax import lax
from jax.experimental import pallas as pl
from jax.experimental.pallas import tpu as pltpu
from jax.sharding import PartitionSpec as P

MATRIX = 16
SOURCE = 4
VALUES = MATRIX + SOURCE
UP = 8
CHUNK_DOWN = 9
MERGE_DOWN = 12
CHUNKS = 8


def inverse(a, b, c, d):
    scale = 1.0 / (a * d - b * c)
    return (d * scale, -b * scale, -c * scale, a * scale)


def times(x, y):
    return (
        x[0] * y[0] + x[1] * y[2],
        x[0] * y[1] + x[1] * y[3],
        x[2] * y[0] + x[3] * y[2],
        x[2] * y[1] + x[3] * y[3],
    )


def apply(x, v):
    return (x[0] * v[0] + x[1] * v[1], x[2] * v[0] + x[3] * v[1])


def minus(x, y):
    return tuple(a - b for a, b in zip(x, y))


def plus(x, y):
    return tuple(a + b for a, b in zip(x, y))


def negative(x):
    return tuple(-a for a in x)


def quads(element):
    return (element[0:4], element[4:8], element[8:12], element[12:16])


def merge_matrix(first, second):
    ll, lm, ml, mm = quads(first)
    nn, mr, rm, rr = quads(second)
    pivot = inverse(*plus(mm, nn))
    wl = times(pivot, ml)
    wr = times(pivot, mr)
    merged = (
        minus(ll, times(lm, wl))
        + negative(times(lm, wr))
        + negative(times(rm, wl))
        + minus(rr, times(rm, wr))
    )
    return merged, wl + wr, pivot + lm + rm


def merge_source(down, first, second):
    pivot, lm, rm = down[0:4], down[4:8], down[8:12]
    w = apply(pivot, plus(first[2:4], second[0:2]))
    return minus(first[0:2], apply(lm, w)) + minus(second[2:4], apply(rm, w)), w


def merge(first, second):
    matrix, up, down = merge_matrix(first[:MATRIX], second[:MATRIX])
    source, w = merge_source(down, first[MATRIX:], second[MATRIX:])
    return matrix + source, up, w


def inner(up, w, left, right):
    return minus(minus(w, apply(up[0:4], left)), apply(up[4:8], right))


def chunk_matrix(speed, damp, cells):
    def link(i):
        p = 2.0 * (damp(i) + damp(i + 1))
        q = 0.25 * (speed(i) + speed(i + 1))
        return q - p, -q - p

    def centre(i):
        return 1.0 + damp(i - 1) + 4.0 * damp(i) + damp(i + 1)

    b0, b1 = damp(0), damp(1)
    quarter = 0.25 * speed(0)
    up, low = link(0)
    zero = jnp.zeros_like(b0)
    ll = (b0, quarter - 2.0 * b0, -quarter - 2.0 * b0, 1.0 + 4.0 * b0 + b1)
    lk = (b0, zero, up, b1)
    kl = (b0, low, zero, b1)
    up, low = link(1)
    kk = (centre(1), up, low, centre(2))
    pairs = (cells - 2) // 2
    for k in range(1, pairs + 1):
        i = 2 * k
        pivot = inverse(*kk)
        wl = times(pivot, kl)
        up, low = link(i)
        here, there = damp(i), damp(i + 1)
        wr = (
            pivot[0] * here + pivot[1] * up,
            pivot[1] * there,
            pivot[2] * here + pivot[3] * up,
            pivot[3] * there,
        )
        yield wl + wr, pivot + lk + (low,), (here, there)

        def below(x):
            return (
                here * x[0] + low * x[2],
                here * x[1] + low * x[3],
                there * x[2],
                there * x[3],
            )

        ll = minus(ll, times(lk, wl))
        lk = negative(times(lk, wr))
        kl = negative(below(wl))
        if k < pairs:
            up, low_next = link(i + 1)
            kk = (centre(i + 1), up, low_next, centre(i + 2))
        else:
            quarter = 0.25 * speed(i + 1)
            kk = (
                1.0 + here + 4.0 * there,
                quarter - 2.0 * there,
                -quarter - 2.0 * there,
                there,
            )
        kk = minus(kk, below(wr))
    yield ll + lk + kl + kk


def pair_source(down, damps, left, pair, following):
    pivot, lk, low = down[0:4], down[4:8], down[8]
    w = apply(pivot, pair)
    left = minus(left, apply(lk, w))
    following = minus(following, (damps[0] * w[0] + low * w[1], damps[1] * w[1]))
    return left, following, w


def pair_of(source, k, cells):
    if k == (cells - 2) // 2:
        last = source(cells - 1)
        return (last, jnp.zeros_like(last))
    return (source(2 * k + 1), source(2 * k + 2))


def first_pair(source):
    first = source(0)
    return (jnp.zeros_like(first), first)


def blocks(rows, size):
    return [(at, min(size, rows - at)) for at in range(0, rows, size)]


def get(ref, count, at, size, base=0):
    return tuple(ref[base + v, pl.ds(at, size), :] for v in range(count))


def put(ref, values, at, size, base=0):
    for v, value in enumerate(values):
        ref[base + v, pl.ds(at, size), :] = value


def get_both(ref, count, at, size):
    return tuple(
        tuple(ref[v, pl.ds(2 * at + half, size, stride=2), :] for v in range(count))
        for half in (0, 1)
    )


def levels_of(lines):
    sizes = []
    rows = lines * CHUNKS
    while rows > lines:
        rows //= 2
        sizes.append(rows)
    return sizes


def split_all(top_ref, end_refs, up_refs, w_refs, sizes):
    source = top_ref
    for rows, target, ups, ws in zip(
        reversed(sizes), end_refs, reversed(up_refs), reversed(w_refs)
    ):
        for at, size in blocks(rows, 8):
            ends = get(source, 4, at, size)
            left, right = ends[0:2], ends[2:4]
            middle = inner(get(ups, UP, at, size), get(ws, 2, at, size), left, right)
            for v in range(2):
                target[v, pl.ds(2 * at, size, stride=2), :] = left[v]
                target[v, pl.ds(2 * at + 1, size, stride=2), :] = middle[v]
                target[2 + v, pl.ds(2 * at, size, stride=2), :] = middle[v]
                target[2 + v, pl.ds(2 * at + 1, size, stride=2), :] = right[v]
        source = target
    return source


def back_substitute(ends_ref, up_ref, w_ref, cells, at, size, store):
    ends = get(ends_ref, 4, at, size)
    left, following = ends[0:2], ends[2:4]
    store(0, left[1])
    store(cells - 1, following[0])
    for k in range((cells - 2) // 2 - 1, -1, -1):
        following = inner(
            get(up_ref, UP, at, size, k * UP), get(w_ref, 2, at, size, k * 2), left, following
        )
        store(2 * k + 1, following[0])
        store(2 * k + 2, following[1])


def tree(items):
    while len(items) > 1:
        paired = [merge(items[i], items[i + 1])[0] for i in range(0, len(items) - 1, 2)]
        items = paired + items[len(items) - len(items) % 2 :]
    return items[0]


def ring_ends(value_of, count, at, size):
    elements = [tuple(value_of(k, v, at, size) for v in range(VALUES)) for k in range(count)]
    own, rest = elements[0], tree(elements[1:])
    ll, lr, rl, rr = quads(own)
    nn, nm, mn, mm = quads(rest)
    b = plus(lr, mn)
    c = plus(rl, nm)
    pivot = inverse(*plus(rr, nn))
    f = plus(own[16:18], rest[18:20])
    g = plus(own[18:20], rest[16:18])
    bd = times(b, pivot)
    left = apply(inverse(*minus(plus(ll, mm), times(bd, c))), minus(f, apply(bd, g)))
    right = apply(pivot, minus(g, apply(c, left)))
    return left, right


def open_ends(axis):
    place = lax.axis_index(axis)
    last = lax.axis_size(axis) - 1
    return jnp.where(place > 0, 1.0, 0.0), jnp.where(place < last, 1.0, 0.0)


def copies(pairs, sems):
    started = []
    for i, (source, target) in enumerate(pairs):
        copy = pltpu.make_async_copy(source, target, sems.at[i])
        copy.start()
        started.append(copy)
    return started


def wrap_down(fields, cells, *refs):
    residual, courant, dissip = refs[0:3]
    packed, chunk_up, chunk_w = refs[3:6]
    ups, ws = refs[6:9], refs[9:12]
    source_in, speed_in, damp_in, source_t, speed_t, damp_t = refs[12:18]
    elements, sems = refs[18:22], refs[22]
    lanes = damp_in.shape[0]
    length = cells * CHUNKS
    moves = [(dissip, damp_in)]
    for field in range(fields):
        rows = pl.ds(field * lanes, lanes)
        moves.append((courant.at[rows], speed_in.at[rows]))
        moves.append((residual.at[rows], source_in.at[rows]))
    started = copies(moves, sems)
    started[0].wait()
    damp_t[...] = damp_in[...].T

    def turn(field):
        started[1 + 2 * field].wait()
        speed_t[pl.ds(field * length, length), :] = speed_in[pl.ds(field * lanes, lanes), :].T
        started[2 + 2 * field].wait()
        source_t[pl.ds(field * length, length), :] = source_in[pl.ds(field * lanes, lanes), :].T

    for at, size in blocks(fields * CHUNKS, 16):
        repeat = size // CHUNKS
        for field in range(at // CHUNKS, at // CHUNKS + repeat):
            turn(field)

        def speed(i):
            return speed_t[pl.ds(at * cells + i, size, stride=cells), :]

        def source(i):
            return source_t[pl.ds(at * cells + i, size, stride=cells), :]

        def damp(i):
            rows = damp_t[pl.ds(i, CHUNKS, stride=cells), :]
            return jnp.concatenate([rows] * repeat, axis=0) if repeat > 1 else rows

        left, pair = first_pair(source), pair_of(source, 0, cells)
        for k, step in enumerate(chunk_matrix(speed, damp, cells)):
            if k == (cells - 2) // 2:
                put(elements[0], step + left + pair, at, size)
                break
            up, down, damps = step
            left, pair, w = pair_source(down, damps, left, pair, pair_of(source, k + 1, cells))
            put(chunk_up, up, at, size, k * UP)
            put(chunk_w, w, at, size, k * 2)
    for level, rows in enumerate(levels_of(fields)):
        for at, size in blocks(rows, 8):
            merged, up, w = merge(*get_both(elements[level], VALUES, at, size))
            put(elements[level + 1], merged, at, size)
            put(ups[level], up, at, size)
            put(ws[level], w, at, size)
    for v in range(VALUES):
        packed[pl.ds(v * fields, fields), :] = elements[-1][v]


def wall_matrix(fields, span, cells, *refs):
    courant, dissip = refs[0:2]
    packed, damp_out, chunk_up, chunk_down = refs[2:6]
    ups, downs = refs[6:9], refs[9:12]
    speed_in, damp_in = refs[12:14]
    elements, sems = refs[14:18], refs[18]
    lanes = damp_in.shape[0]
    moves = [(dissip, damp_in)]
    for field in range(fields):
        rows = pl.ds(field * lanes, lanes)
        moves.append((courant.at[rows], speed_in.at[rows]))
    started = copies(moves, sems)
    started[0].wait()
    size = span * CHUNKS
    for field in range(fields):
        started[1 + field].wait()
        at = field * size

        def speed(i):
            return speed_in[pl.ds(at * cells + i, size, stride=cells), :]

        def damp(i):
            return damp_in[pl.ds(i, size, stride=cells), :]

        for k, step in enumerate(chunk_matrix(speed, damp, cells)):
            if k == (cells - 2) // 2:
                put(elements[0], step, at, size)
                break
            up, down, damps = step
            put(chunk_up, up, at, size, k * UP)
            put(chunk_down, down, at, size, k * CHUNK_DOWN)
            if field == 0:
                put(damp_out, damps, 0, size, k * 2)
    lines = fields * span
    for level, rows in enumerate(levels_of(lines)):
        for at, size in blocks(rows, 8):
            merged, up, down = merge_matrix(*get_both(elements[level], MATRIX, at, size))
            put(elements[level + 1], merged, at, size)
            put(ups[level], up, at, size)
            put(downs[level], down, at, size)
    not_first, not_last = open_ends("normal")
    for v in range(MATRIX):
        value = elements[-1][v]
        if v in (0, 1, 2, 4, 5, 8, 10):
            value = value * not_first
        if v in (5, 7, 10, 11, 13, 14, 15):
            value = value * not_last
        packed[pl.ds(v * lines, lines), :] = value


def middle(fields, span, wrap_cells, wall_cells, wrap_count, *refs):
    elements = refs[:wrap_count]
    refs = refs[wrap_count:]
    chunk_up, chunk_w, ups, ws = refs[0], refs[1], refs[2:5], refs[5:8]
    coupling, damps_in, chunk_down, downs = refs[8], refs[9], refs[10], refs[11:14]
    packed, wall_w, wall_ws = refs[14], refs[15], refs[16:19]
    ends, solved_t, solved, mixed = refs[19:23], refs[23], refs[24], refs[25]
    sources = refs[26:30]

    def value_of(k, v, at, size):
        return elements[k][pl.ds(v * fields + at, size), :]

    for at, size in blocks(fields, 8):
        left, right = ring_ends(value_of, wrap_count, at, size)
        put(ends[0], left + right, at, size)
    last = split_all(ends[0], ends[1:], ups, ws, levels_of(fields))
    length = wrap_cells * CHUNKS
    for at, size in blocks(fields * CHUNKS, 16):

        def store(i, value):
            solved_t[pl.ds(at * wrap_cells + i, size, stride=wrap_cells), :] = value

        back_substitute(last, chunk_up, chunk_w, wrap_cells, at, size, store)
    lanes = solved.shape[0] // fields
    for field in range(fields):
        solved[pl.ds(field * lanes, lanes), :] = solved_t[pl.ds(field * length, length), :].T

    for at, size in blocks(lanes, 16):
        update = [solved[pl.ds(j * lanes + at, size), :] for j in range(fields)]
        for k in range(fields):
            total = coupling[k, 0, pl.ds(at, size), :].astype(jnp.float32) * update[0]
            for j in range(1, fields):
                total = total + coupling[k, j, pl.ds(at, size), :].astype(jnp.float32) * update[j]
            mixed[pl.ds(k * lanes + at, size), :] = total

    pairs = (wall_cells - 2) // 2
    size = span * CHUNKS
    for field in range(fields):
        at = field * size

        def source(i):
            return mixed[pl.ds(at * wall_cells + i, size, stride=wall_cells), :]

        left, pair = first_pair(source), pair_of(source, 0, wall_cells)
        for k in range(pairs):
            left, pair, w = pair_source(
                get(chunk_down, CHUNK_DOWN, at, size, k * CHUNK_DOWN),
                get(damps_in, 2, 0, size, k * 2),
                left,
                pair,
                pair_of(source, k + 1, wall_cells),
            )
            put(wall_w, w, at, size, k * 2)
        put(sources[0], left + pair, at, size)
    lines = fields * span
    for level, rows in enumerate(levels_of(lines)):
        for at, size in blocks(rows, 8):
            down = get(downs[level], MERGE_DOWN, at, size)
            merged, w = merge_source(down, *get_both(sources[level], SOURCE, at, size))
            put(sources[level + 1], merged, at, size)
            put(wall_ws[level], w, at, size)
    not_first, not_last = open_ends("normal")
    for v, keep in enumerate((not_first, None, None, not_last)):
        value = sources[-1][v]
        packed[pl.ds(v * lines, lines), :] = value if keep is None else value * keep


def wall_up(fields, span, cells, wall_count, *refs):
    matrices, sources = refs[:wall_count], refs[wall_count : 2 * wall_count]
    refs = refs[2 * wall_count :]
    chunk_up, chunk_w, ups, ws = refs[0], refs[1], refs[2:5], refs[5:8]
    update = refs[8]
    ends, result, sems = refs[9:13], refs[13], refs[14]
    lines = fields * span

    def value_of(k, v, at, size):
        if v < MATRIX:
            return matrices[k][pl.ds(v * lines + at, size), :]
        return sources[k][pl.ds((v - MATRIX) * lines + at, size), :]

    not_first, not_last = open_ends("normal")
    for at, size in blocks(lines, 8):
        left, right = ring_ends(value_of, wall_count, at, size)
        put(
            ends[0],
            (left[0] * not_first, left[1], right[0], right[1] * not_last),
            at,
            size,
        )
    last = split_all(ends[0], ends[1:], ups, ws, levels_of(lines))
    size = span * CHUNKS
    length = size * cells
    started = []
    for field in range(fields):
        at = field * size

        def store(i, value):
            result[pl.ds(at * cells + i, size, stride=cells), :] = value

        back_substitute(last, chunk_up, chunk_w, cells, at, size, store)
        rows = pl.ds(field * length, length)
        copy = pltpu.make_async_copy(result.at[rows], update.at[rows], sems.at[field])
        copy.start()
        started.append(copy)
    for copy in started:
        copy.wait()


def f32(*shape):
    return jax.ShapeDtypeStruct(shape, jnp.float32)


def vmem(*shape):
    return pltpu.VMEM(shape, jnp.float32)


IN_VMEM = pl.BlockSpec(memory_space=pltpu.VMEM)
IN_HBM = pl.BlockSpec(memory_space=pltpu.HBM)
PARAMS = pltpu.CompilerParams(vmem_limit_bytes=24 * 2**20)


def kernel(name, body, ins, outs, scratch, flops):
    in_bytes = sum(a.size * a.dtype.itemsize for a, _ in ins)
    out_bytes = sum(a.size * 4 for a, _ in outs)
    return pl.pallas_call(
        body,
        out_shape=[a for a, _ in outs],
        in_specs=[spec for _, spec in ins],
        out_specs=[spec for _, spec in outs],
        scratch_shapes=scratch,
        compiler_params=PARAMS,
        cost_estimate=pl.CostEstimate(
            flops=flops, bytes_accessed=in_bytes + out_bytes, transcendentals=0
        ),
        name=name,
    )(*[a for a, _ in ins])


def inside(arrays):
    return [(a, IN_VMEM) for a in arrays]


def outside(arrays):
    return [(pltpu.with_memory_space_constraint(a, pltpu.HBM), IN_HBM) for a in arrays]


def others(array, axis):
    count = lax.axis_size(axis)
    return [array] + [
        lax.ppermute(array, axis, [((i + k) % count, i) for i in range(count)])
        for k in range(1, count)
    ]


def local(residual, courant_xi, courant_eta, dissip_xi, dissip_eta, coupling):
    fields, span, high, wide = residual.shape
    lanes = span * high
    wrap_cells, wall_cells = wide // CHUNKS, high // CHUNKS
    wrap_pairs, wall_pairs = (wrap_cells - 2) // 2, (wall_cells - 2) // 2
    wrap_count, wall_count = lax.axis_size("wrap"), lax.axis_size("normal")
    lines = fields * span
    wrap_levels, wall_levels = levels_of(fields), levels_of(lines)
    wrap_rows, wall_rows = fields * CHUNKS, lines * CHUNKS

    def rows_of(array):
        return array.reshape(-1, wide)

    packed, *wrap_factors = kernel(
        "wrap_down",
        functools.partial(wrap_down, fields, wrap_cells),
        outside([rows_of(residual), rows_of(courant_xi), rows_of(dissip_xi)]),
        inside(
            [
                f32(VALUES * fields, lanes),
                f32(wrap_pairs * UP, wrap_rows, lanes),
                f32(wrap_pairs * 2, wrap_rows, lanes),
            ]
            + [f32(UP, n, lanes) for n in wrap_levels]
            + [f32(2, n, lanes) for n in wrap_levels]
        ),
        [vmem(fields * lanes, wide)] * 2
        + [vmem(lanes, wide)]
        + [vmem(fields * wide, lanes)] * 2
        + [vmem(wide, lanes)]
        + [vmem(VALUES, n, lanes) for n in [wrap_rows] + wrap_levels]
        + [pltpu.SemaphoreType.DMA((2 * fields + 1,))],
        100 * residual.size,
    )
    wrap_elements = others(packed, "wrap")
    packed, damps, chunk_up, chunk_down, *wall_factors = kernel(
        "wall_matrix",
        functools.partial(wall_matrix, fields, span, wall_cells),
        outside([rows_of(courant_eta), rows_of(dissip_eta)]),
        inside(
            [
                f32(MATRIX * lines, wide),
                f32(wall_pairs * 2, span * CHUNKS, wide),
                f32(wall_pairs * UP, wall_rows, wide),
                f32(wall_pairs * CHUNK_DOWN, wall_rows, wide),
            ]
            + [f32(UP, n, wide) for n in wall_levels]
            + [f32(MERGE_DOWN, n, wide) for n in wall_levels]
        ),
        [vmem(fields * lanes, wide), vmem(lanes, wide)]
        + [vmem(MATRIX, n, wide) for n in [wall_rows] + wall_levels]
        + [pltpu.SemaphoreType.DMA((fields + 1,))],
        100 * residual.size,
    )
    wall_matrices = others(packed, "normal")
    packed, *wall_ws = kernel(
        "middle",
        functools.partial(middle, fields, span, wrap_cells, wall_cells, wrap_count),
        inside(
            wrap_elements
            + wrap_factors
            + [coupling.reshape(fields, fields, lanes, wide), damps, chunk_down]
            + wall_factors[3:]
        ),
        inside(
            [f32(SOURCE * lines, wide), f32(wall_pairs * 2, wall_rows, wide)]
            + [f32(2, n, wide) for n in wall_levels]
        ),
        [vmem(4, n, lanes) for n in reversed([wrap_rows] + wrap_levels)]
        + [vmem(fields * wide, lanes), vmem(fields * lanes, wide), vmem(fields * lanes, wide)]
        + [vmem(SOURCE, n, wide) for n in [wall_rows] + wall_levels],
        100 * residual.size,
    )
    wall_sources = others(packed, "normal")
    (update,) = kernel(
        "wall_up",
        functools.partial(wall_up, fields, span, wall_cells, wall_count),
        inside(
            wall_matrices
            + wall_sources
            + [chunk_up, wall_ws[0]]
            + wall_factors[:3]
            + wall_ws[1:]
        ),
        [(f32(fields * lanes, wide), IN_HBM)],
        [vmem(4, n, wide) for n in reversed([wall_rows] + wall_levels)]
        + [vmem(fields * lanes, wide), pltpu.SemaphoreType.DMA((fields,))],
        30 * residual.size,
    )
    return update.reshape(residual.shape)


def solution(mesh):
    placed = (
        P(None, None, "normal", "wrap"),
        P(None, None, "normal", "wrap"),
        P(None, None, "normal", "wrap"),
        P(None, "normal", "wrap"),
        P(None, "normal", "wrap"),
        P(None, None, None, "normal", "wrap"),
    )
    return jax.shard_map(
        local,
        mesh=mesh,
        in_specs=placed,
        out_specs=P(None, None, "normal", "wrap"),
        check_vma=False,
    )
```

```python
import functools

import jax
import jax.numpy as jnp
from jax import lax
from jax.experimental import pallas as pl
from jax.experimental.pallas import tpu as pltpu
from jax.sharding import PartitionSpec as P

MATRIX = 16
SOURCE = 4
VALUES = MATRIX + SOURCE
UP = 8
CHUNK_DOWN = 9
MERGE_DOWN = 12
CHUNKS = 8


def inverse(a, b, c, d):
    scale = 1.0 / (a * d - b * c)
    return (d * scale, -b * scale, -c * scale, a * scale)


def times(x, y):
    return (
        x[0] * y[0] + x[1] * y[2],
        x[0] * y[1] + x[1] * y[3],
        x[2] * y[0] + x[3] * y[2],
        x[2] * y[1] + x[3] * y[3],
    )


def apply(x, v):
    return (x[0] * v[0] + x[1] * v[1], x[2] * v[0] + x[3] * v[1])


def minus(x, y):
    return tuple(a - b for a, b in zip(x, y))


def plus(x, y):
    return tuple(a + b for a, b in zip(x, y))


def negative(x):
    return tuple(-a for a in x)


def quads(element):
    return (element[0:4], element[4:8], element[8:12], element[12:16])


def merge_matrix(first, second):
    ll, lm, ml, mm = quads(first)
    nn, mr, rm, rr = quads(second)
    pivot = inverse(*plus(mm, nn))
    wl = times(pivot, ml)
    wr = times(pivot, mr)
    merged = (
        minus(ll, times(lm, wl))
        + negative(times(lm, wr))
        + negative(times(rm, wl))
        + minus(rr, times(rm, wr))
    )
    return merged, wl + wr, pivot + lm + rm


def merge_source(down, first, second):
    pivot, lm, rm = down[0:4], down[4:8], down[8:12]
    w = apply(pivot, plus(first[2:4], second[0:2]))
    return minus(first[0:2], apply(lm, w)) + minus(second[2:4], apply(rm, w)), w


def merge(first, second):
    matrix, up, down = merge_matrix(first[:MATRIX], second[:MATRIX])
    source, w = merge_source(down, first[MATRIX:], second[MATRIX:])
    return matrix + source, up, w


def inner(up, w, left, right):
    return minus(minus(w, apply(up[0:4], left)), apply(up[4:8], right))


def chunk_matrix(speed, damp, cells):
    def link(i):
        p = 2.0 * (damp(i) + damp(i + 1))
        q = 0.25 * (speed(i) + speed(i + 1))
        return q - p, -q - p

    def centre(i):
        return 1.0 + damp(i - 1) + 4.0 * damp(i) + damp(i + 1)

    b0, b1 = damp(0), damp(1)
    quarter = 0.25 * speed(0)
    up, low = link(0)
    zero = jnp.zeros_like(b0)
    ll = (b0, quarter - 2.0 * b0, -quarter - 2.0 * b0, 1.0 + 4.0 * b0 + b1)
    lk = (b0, zero, up, b1)
    kl = (b0, low, zero, b1)
    up, low = link(1)
    kk = (centre(1), up, low, centre(2))
    pairs = (cells - 2) // 2
    for k in range(1, pairs + 1):
        i = 2 * k
        pivot = inverse(*kk)
        wl = times(pivot, kl)
        up, low = link(i)
        here, there = damp(i), damp(i + 1)
        wr = (
            pivot[0] * here + pivot[1] * up,
            pivot[1] * there,
            pivot[2] * here + pivot[3] * up,
            pivot[3] * there,
        )
        yield wl + wr, pivot + lk + (low,), (here, there)

        def below(x):
            return (
                here * x[0] + low * x[2],
                here * x[1] + low * x[3],
                there * x[2],
                there * x[3],
            )

        ll = minus(ll, times(lk, wl))
        lk = negative(times(lk, wr))
        kl = negative(below(wl))
        if k < pairs:
            up, low_next = link(i + 1)
            kk = (centre(i + 1), up, low_next, centre(i + 2))
        else:
            quarter = 0.25 * speed(i + 1)
            kk = (
                1.0 + here + 4.0 * there,
                quarter - 2.0 * there,
                -quarter - 2.0 * there,
                there,
            )
        kk = minus(kk, below(wr))
    yield ll + lk + kl + kk


def pair_source(down, damps, left, pair, following):
    pivot, lk, low = down[0:4], down[4:8], down[8]
    w = apply(pivot, pair)
    left = minus(left, apply(lk, w))
    following = minus(following, (damps[0] * w[0] + low * w[1], damps[1] * w[1]))
    return left, following, w


def pair_of(source, k, cells):
    if k == (cells - 2) // 2:
        last = source(cells - 1)
        return (last, jnp.zeros_like(last))
    return (source(2 * k + 1), source(2 * k + 2))


def first_pair(source):
    first = source(0)
    return (jnp.zeros_like(first), first)


def blocks(rows, size):
    return [(at, min(size, rows - at)) for at in range(0, rows, size)]


def get(ref, count, at, size, base=0):
    return tuple(ref[base + v, pl.ds(at, size), :] for v in range(count))


def put(ref, values, at, size, base=0):
    for v, value in enumerate(values):
        ref[base + v, pl.ds(at, size), :] = value


def get_both(ref, count, at, size):
    return tuple(
        tuple(ref[v, pl.ds(2 * at + half, size, stride=2), :] for v in range(count))
        for half in (0, 1)
    )


def levels_of(lines):
    sizes = []
    rows = lines * CHUNKS
    while rows > lines:
        rows //= 2
        sizes.append(rows)
    return sizes


def split_all(top_ref, end_refs, up_refs, w_refs, sizes):
    source = top_ref
    for rows, target, ups, ws in zip(
        reversed(sizes), end_refs, reversed(up_refs), reversed(w_refs)
    ):
        for at, size in blocks(rows, 8):
            ends = get(source, 4, at, size)
            left, right = ends[0:2], ends[2:4]
            middle = inner(get(ups, UP, at, size), get(ws, 2, at, size), left, right)
            for v in range(2):
                target[v, pl.ds(2 * at, size, stride=2), :] = left[v]
                target[v, pl.ds(2 * at + 1, size, stride=2), :] = middle[v]
                target[2 + v, pl.ds(2 * at, size, stride=2), :] = middle[v]
                target[2 + v, pl.ds(2 * at + 1, size, stride=2), :] = right[v]
        source = target
    return source


def back_substitute(ends_ref, up_ref, w_ref, cells, at, size, store):
    ends = get(ends_ref, 4, at, size)
    left, following = ends[0:2], ends[2:4]
    store(0, left[1])
    store(cells - 1, following[0])
    for k in range((cells - 2) // 2 - 1, -1, -1):
        following = inner(
            get(up_ref, UP, at, size, k * UP), get(w_ref, 2, at, size, k * 2), left, following
        )
        store(2 * k + 1, following[0])
        store(2 * k + 2, following[1])


def tree(items):
    while len(items) > 1:
        paired = [merge(items[i], items[i + 1])[0] for i in range(0, len(items) - 1, 2)]
        items = paired + items[len(items) - len(items) % 2 :]
    return items[0]


def ring_ends(value_of, count, at, size):
    elements = [tuple(value_of(k, v, at, size) for v in range(VALUES)) for k in range(count)]
    own, rest = elements[0], tree(elements[1:])
    ll, lr, rl, rr = quads(own)
    nn, nm, mn, mm = quads(rest)
    b = plus(lr, mn)
    c = plus(rl, nm)
    pivot = inverse(*plus(rr, nn))
    f = plus(own[16:18], rest[18:20])
    g = plus(own[18:20], rest[16:18])
    bd = times(b, pivot)
    left = apply(inverse(*minus(plus(ll, mm), times(bd, c))), minus(f, apply(bd, g)))
    right = apply(pivot, minus(g, apply(c, left)))
    return left, right


def open_ends(axis):
    place = lax.axis_index(axis)
    last = lax.axis_size(axis) - 1
    return jnp.where(place > 0, 1.0, 0.0), jnp.where(place < last, 1.0, 0.0)


def copies(pairs, sems):
    started = []
    for i, (source, target) in enumerate(pairs):
        copy = pltpu.make_async_copy(source, target, sems.at[i])
        copy.start()
        started.append(copy)
    return started


def wrap_down(fields, cells, refs, started):
    source_in, speed_in, damp_in = refs[0:3]
    packed, chunk_up, chunk_w, ups, ws = refs[3], refs[4], refs[5], refs[6:9], refs[9:12]
    source_t, speed_t, damp_t, packed_t = refs[12:16]
    elements = refs[16:20]
    lanes = damp_in.shape[0]
    length = cells * CHUNKS
    started[0].wait()
    damp_t[...] = damp_in[...].T

    def turn(field):
        started[1 + 2 * field].wait()
        speed_t[pl.ds(field * length, length), :] = speed_in[pl.ds(field * lanes, lanes), :].T
        started[2 + 2 * field].wait()
        source_t[pl.ds(field * length, length), :] = source_in[pl.ds(field * lanes, lanes), :].T

    for at, size in blocks(fields * CHUNKS, 16):
        repeat = size // CHUNKS
        for field in range(at // CHUNKS, at // CHUNKS + repeat):
            turn(field)

        def speed(i):
            return speed_t[pl.ds(at * cells + i, size, stride=cells), :]

        def source(i):
            return source_t[pl.ds(at * cells + i, size, stride=cells), :]

        def damp(i):
            rows = damp_t[pl.ds(i, CHUNKS, stride=cells), :]
            return jnp.concatenate([rows] * repeat, axis=0) if repeat > 1 else rows

        left, pair = first_pair(source), pair_of(source, 0, cells)
        for k, step in enumerate(chunk_matrix(speed, damp, cells)):
            if k == (cells - 2) // 2:
                put(elements[0], step + left + pair, at, size)
                break
            up, down, damps = step
            left, pair, w = pair_source(down, damps, left, pair, pair_of(source, k + 1, cells))
            put(chunk_up, up, at, size, k * UP)
            put(chunk_w, w, at, size, k * 2)
    for level, rows in enumerate(levels_of(fields)):
        for at, size in blocks(rows, 8):
            merged, up, w = merge(*get_both(elements[level], VALUES, at, size))
            put(elements[level + 1], merged, at, size)
            put(ups[level], up, at, size)
            put(ws[level], w, at, size)
    pack(packed, packed_t, [elements[-1][v] for v in range(VALUES)])


def pack(packed, packed_t, values):
    fields = values[0].shape[0]
    used = len(values) * fields
    start = used // 8 * 8
    packed_t[pl.ds(start, packed_t.shape[0] - start), :] = jnp.zeros(
        (packed_t.shape[0] - start, packed_t.shape[1]), jnp.float32
    )
    for v, value in enumerate(values):
        packed_t[pl.ds(v * fields, fields), :] = value
    packed[...] = packed_t[...].T


def wall_matrix(fields, span, cells, refs, started):
    speed_in, damp_in = refs[0:2]
    packed, damp_out, chunk_up, chunk_down = refs[2:6]
    ups, downs = refs[6:9], refs[9:12]
    elements = refs[12:16]
    started[0].wait()
    size = span * CHUNKS
    for field in range(fields):
        started[1 + field].wait()
        at = field * size

        def speed(i):
            return speed_in[pl.ds(at * cells + i, size, stride=cells), :]

        def damp(i):
            return damp_in[pl.ds(i, size, stride=cells), :]

        for k, step in enumerate(chunk_matrix(speed, damp, cells)):
            if k == (cells - 2) // 2:
                put(elements[0], step, at, size)
                break
            up, down, damps = step
            put(chunk_up, up, at, size, k * UP)
            put(chunk_down, down, at, size, k * CHUNK_DOWN)
            if field == 0:
                put(damp_out, damps, 0, size, k * 2)
    lines = fields * span
    for level, rows in enumerate(levels_of(lines)):
        for at, size in blocks(rows, 8):
            merged, up, down = merge_matrix(*get_both(elements[level], MATRIX, at, size))
            put(elements[level + 1], merged, at, size)
            put(ups[level], up, at, size)
            put(downs[level], down, at, size)
    not_first, not_last = open_ends("normal")
    for v in range(MATRIX):
        value = elements[-1][v]
        if v in (0, 1, 2, 4, 5, 8, 10):
            value = value * not_first
        if v in (5, 7, 10, 11, 13, 14, 15):
            value = value * not_last
        packed[pl.ds(v * lines, lines), :] = value


def down(fields, span, wrap_cells, wall_cells, *refs):
    residual, wrap_speed, wall_speed, wrap_damp, wall_damp = refs[0:5]
    wall_outs, wrap_outs, refs = refs[5:15], refs[15:24], refs[24:]
    wall_ins, wrap_ins, refs = refs[0:2], refs[2:5], refs[5:]
    wall_scratch, wrap_scratch, sems = refs[0:4], refs[4:12], refs[12]
    lanes = wall_ins[1].shape[0]
    blocks_of = [pl.ds(field * lanes, lanes) for field in range(fields)]
    moves = [(wall_damp, wall_ins[1])]
    moves += [(wall_speed.at[rows], wall_ins[0].at[rows]) for rows in blocks_of]
    moves += [(wrap_damp, wrap_ins[2])]
    for rows in blocks_of:
        moves.append((wrap_speed.at[rows], wrap_ins[1].at[rows]))
        moves.append((residual.at[rows], wrap_ins[0].at[rows]))
    started = copies(moves, sems)
    wall_matrix(
        fields, span, wall_cells, wall_ins + wall_outs + wall_scratch, started[: fields + 1]
    )
    wrap_down(fields, wrap_cells, wrap_ins + wrap_outs + wrap_scratch, started[fields + 1 :])


def ring(fields, count, received, packed, values_t, packed_t):
    values_t[...] = received[...].T
    lanes = values_t.shape[1]
    share = lanes // count

    def ahead(value, places):
        return pltpu.roll(value, lanes - places * share, 1)

    size = blocks(fields, 8)[0][1]
    element = tuple(values_t[pl.ds(v * fields, size), :] for v in range(VALUES))
    places = 1
    while places < count:
        element = merge(element, tuple(ahead(value, places) for value in element))[0]
        places *= 2
    ll, lr, rl, rr = quads(element)
    left = apply(
        inverse(*plus(plus(ll, rr), plus(lr, rl))), plus(element[16:18], element[18:20])
    )
    right = tuple(ahead(value, 1) for value in left)
    pack(packed, packed_t, left + right)


def middle(fields, span, wrap_cells, wall_cells, *refs):
    received, refs = refs[0], refs[1:]
    chunk_up, chunk_w, ups, ws = refs[0], refs[1], refs[2:5], refs[5:8]
    coupling, damps_in, chunk_down, downs = refs[8], refs[9], refs[10], refs[11:14]
    packed, wall_w, wall_ws = refs[14], refs[15], refs[16:19]
    ends, solved_t, solved, mixed = refs[19:23], refs[23], refs[24], refs[25]
    sources, ends_t = refs[26:30], refs[30]

    ends_t[...] = received[...].T
    for v in range(4):
        ends[0][v] = ends_t[pl.ds(v * fields, fields), :]
    last = split_all(ends[0], ends[1:], ups, ws, levels_of(fields))
    length = wrap_cells * CHUNKS
    for at, size in blocks(fields * CHUNKS, 16):

        def store(i, value):
            solved_t[pl.ds(at * wrap_cells + i, size, stride=wrap_cells), :] = value

        back_substitute(last, chunk_up, chunk_w, wrap_cells, at, size, store)
    lanes = solved.shape[0] // fields
    for field in range(fields):
        solved[pl.ds(field * lanes, lanes), :] = solved_t[pl.ds(field * length, length), :].T

    for at, size in blocks(lanes, 16):
        update = [solved[pl.ds(j * lanes + at, size), :] for j in range(fields)]
        for k in range(fields):
            total = coupling[k, 0, pl.ds(at, size), :].astype(jnp.float32) * update[0]
            for j in range(1, fields):
                total = total + coupling[k, j, pl.ds(at, size), :].astype(jnp.float32) * update[j]
            mixed[pl.ds(k * lanes + at, size), :] = total

    pairs = (wall_cells - 2) // 2
    size = span * CHUNKS
    for field in range(fields):
        at = field * size

        def source(i):
            return mixed[pl.ds(at * wall_cells + i, size, stride=wall_cells), :]

        left, pair = first_pair(source), pair_of(source, 0, wall_cells)
        for k in range(pairs):
            left, pair, w = pair_source(
                get(chunk_down, CHUNK_DOWN, at, size, k * CHUNK_DOWN),
                get(damps_in, 2, 0, size, k * 2),
                left,
                pair,
                pair_of(source, k + 1, wall_cells),
            )
            put(wall_w, w, at, size, k * 2)
        put(sources[0], left + pair, at, size)
    lines = fields * span
    for level, rows in enumerate(levels_of(lines)):
        for at, size in blocks(rows, 8):
            down = get(downs[level], MERGE_DOWN, at, size)
            merged, w = merge_source(down, *get_both(sources[level], SOURCE, at, size))
            put(sources[level + 1], merged, at, size)
            put(wall_ws[level], w, at, size)
    not_first, not_last = open_ends("normal")
    for v, keep in enumerate((not_first, None, None, not_last)):
        value = sources[-1][v]
        packed[pl.ds(v * lines, lines), :] = value if keep is None else value * keep


def wall_up(fields, span, cells, wall_count, *refs):
    matrices, sources, refs = refs[:wall_count], refs[wall_count], refs[wall_count + 1 :]
    chunk_up, chunk_w, ups, ws = refs[0], refs[1], refs[2:5], refs[5:8]
    update = refs[8]
    ends, result, sems = refs[9:13], refs[13], refs[14]
    lines = fields * span
    place = lax.axis_index("normal")

    def value_of(k, v, at, size):
        if v < MATRIX:
            return matrices[k][pl.ds(v * lines + at, size), :]
        owner = lax.rem(place + k, wall_count)
        return sources[owner, pl.ds((v - MATRIX) * lines + at, size), :]

    not_first, not_last = open_ends("normal")
    for at, size in blocks(lines, 8):
        left, right = ring_ends(value_of, wall_count, at, size)
        put(
            ends[0],
            (left[0] * not_first, left[1], right[0], right[1] * not_last),
            at,
            size,
        )
    last = split_all(ends[0], ends[1:], ups, ws, levels_of(lines))
    size = span * CHUNKS
    length = size * cells
    started = []
    for field in range(fields):
        at = field * size

        def store(i, value):
            result[pl.ds(at * cells + i, size, stride=cells), :] = value

        back_substitute(last, chunk_up, chunk_w, cells, at, size, store)
        rows = pl.ds(field * length, length)
        copy = pltpu.make_async_copy(result.at[rows], update.at[rows], sems.at[field])
        copy.start()
        started.append(copy)
    for copy in started:
        copy.wait()


def f32(*shape):
    return jax.ShapeDtypeStruct(shape, jnp.float32)


def vmem(*shape):
    return pltpu.VMEM(shape, jnp.float32)


IN_VMEM = pl.BlockSpec(memory_space=pltpu.VMEM)
IN_HBM = pl.BlockSpec(memory_space=pltpu.HBM)
PARAMS = pltpu.CompilerParams(vmem_limit_bytes=24 * 2**20)


def kernel(name, body, ins, outs, scratch, flops):
    in_bytes = sum(a.size * a.dtype.itemsize for a, _ in ins)
    out_bytes = sum(a.size * 4 for a, _ in outs)
    outputs = pl.pallas_call(
        body,
        out_shape=[a for a, _ in outs],
        in_specs=[spec for _, spec in ins],
        out_specs=[spec for _, spec in outs],
        scratch_shapes=scratch,
        compiler_params=PARAMS,
        cost_estimate=pl.CostEstimate(
            flops=flops, bytes_accessed=in_bytes + out_bytes, transcendentals=0
        ),
        name=name,
    )(*[a for a, _ in ins])
    return list(outputs)


def inside(arrays):
    return [(a, IN_VMEM) for a in arrays]


def outside(arrays):
    return [(pltpu.with_memory_space_constraint(a, pltpu.HBM), IN_HBM) for a in arrays]


def others(array, axis):
    count = lax.axis_size(axis)
    return [array] + [
        lax.ppermute(array, axis, [((i + k) % count, i) for i in range(count)])
        for k in range(1, count)
    ]


def local(residual, courant_xi, courant_eta, dissip_xi, dissip_eta, coupling):
    fields, span, high, wide = residual.shape
    lanes = span * high
    wrap_cells, wall_cells = wide // CHUNKS, high // CHUNKS
    wrap_pairs, wall_pairs = (wrap_cells - 2) // 2, (wall_cells - 2) // 2
    wrap_count, wall_count = lax.axis_size("wrap"), lax.axis_size("normal")
    lines = fields * span
    wrap_levels, wall_levels = levels_of(fields), levels_of(lines)
    wrap_rows, wall_rows = fields * CHUNKS, lines * CHUNKS

    def rows_of(array):
        return array.reshape(-1, wide)

    results = kernel(
        "down",
        functools.partial(down, fields, span, wrap_cells, wall_cells),
        outside(
            [rows_of(a) for a in (residual, courant_xi, courant_eta, dissip_xi, dissip_eta)]
        ),
        inside(
            [
                f32(MATRIX * lines, wide),
                f32(wall_pairs * 2, span * CHUNKS, wide),
                f32(wall_pairs * UP, wall_rows, wide),
                f32(wall_pairs * CHUNK_DOWN, wall_rows, wide),
            ]
            + [f32(UP, n, wide) for n in wall_levels]
            + [f32(MERGE_DOWN, n, wide) for n in wall_levels]
            + [
                f32(lanes, wide),
                f32(wrap_pairs * UP, wrap_rows, lanes),
                f32(wrap_pairs * 2, wrap_rows, lanes),
            ]
            + [f32(UP, n, lanes) for n in wrap_levels]
            + [f32(2, n, lanes) for n in wrap_levels]
        ),
        [vmem(fields * lanes, wide), vmem(lanes, wide)]
        + [vmem(fields * lanes, wide)] * 2
        + [vmem(lanes, wide)]
        + [vmem(MATRIX, n, wide) for n in [wall_rows] + wall_levels]
        + [vmem(fields * wide, lanes)] * 2
        + [vmem(wide, lanes)]
        + [vmem(wide, lanes)]
        + [vmem(VALUES, n, lanes) for n in [wrap_rows] + wrap_levels]
        + [pltpu.SemaphoreType.DMA((3 * fields + 2,))],
        200 * residual.size,
    )
    packed, damps, chunk_up, chunk_down = results[0:4]
    wall_ups, wall_downs = results[4:7], results[7:10]
    wrap_packed, wrap_factors = results[10], results[11:]
    wall_matrices = others(packed, "normal")
    (packed,) = kernel(
        "ring",
        functools.partial(ring, fields, wrap_count),
        inside([lax.all_to_all(wrap_packed, "wrap", 0, 0, tiled=True)]),
        inside([f32(lanes, wide)]),
        [vmem(wide, lanes)] * 2,
        residual.size,
    )
    packed, *wall_ws = kernel(
        "middle",
        functools.partial(middle, fields, span, wrap_cells, wall_cells),
        inside(
            [lax.all_to_all(packed, "wrap", 0, 0, tiled=True)]
            + wrap_factors
            + [coupling.reshape(fields, fields, lanes, wide), damps, chunk_down]
            + wall_downs
        ),
        inside(
            [f32(SOURCE * lines, wide), f32(wall_pairs * 2, wall_rows, wide)]
            + [f32(2, n, wide) for n in wall_levels]
        ),
        [vmem(4, n, lanes) for n in reversed([wrap_rows] + wrap_levels)]
        + [vmem(fields * wide, lanes), vmem(fields * lanes, wide), vmem(fields * lanes, wide)]
        + [vmem(SOURCE, n, wide) for n in [wall_rows] + wall_levels]
        + [vmem(wide, lanes)],
        100 * residual.size,
    )
    (update,) = kernel(
        "wall_up",
        functools.partial(wall_up, fields, span, wall_cells, wall_count),
        inside(
            wall_matrices
            + [lax.all_gather(packed, "normal", axis=0, tiled=False), chunk_up, wall_ws[0]]
            + wall_ups
            + wall_ws[1:]
        ),
        [(f32(fields * lanes, wide), IN_HBM)],
        [vmem(4, n, wide) for n in reversed([wall_rows] + wall_levels)]
        + [vmem(fields * lanes, wide), pltpu.SemaphoreType.DMA((fields,))],
        30 * residual.size,
    )
    return update.reshape(residual.shape)


def solution(mesh):
    placed = (
        P(None, None, "normal", "wrap"),
        P(None, None, "normal", "wrap"),
        P(None, None, "normal", "wrap"),
        P(None, "normal", "wrap"),
        P(None, "normal", "wrap"),
        P(None, None, None, "normal", "wrap"),
    )
    return jax.shard_map(
        local,
        mesh=mesh,
        in_specs=placed,
        out_specs=P(None, None, "normal", "wrap"),
        check_vma=False,
    )
```

```python
import functools

import jax
import jax.numpy as jnp
from jax import lax
from jax.experimental import pallas as pl
from jax.experimental.pallas import tpu as pltpu
from jax.sharding import PartitionSpec as P

MATRIX = 16
SOURCE = 4
VALUES = MATRIX + SOURCE
UP = 8
CHUNK_DOWN = 9
MERGE_DOWN = 12
CHUNKS = 8


def inverse(a, b, c, d):
    scale = 1.0 / (a * d - b * c)
    return (d * scale, -b * scale, -c * scale, a * scale)


def times(x, y):
    return (
        x[0] * y[0] + x[1] * y[2],
        x[0] * y[1] + x[1] * y[3],
        x[2] * y[0] + x[3] * y[2],
        x[2] * y[1] + x[3] * y[3],
    )


def apply(x, v):
    return (x[0] * v[0] + x[1] * v[1], x[2] * v[0] + x[3] * v[1])


def minus(x, y):
    return tuple(a - b for a, b in zip(x, y))


def plus(x, y):
    return tuple(a + b for a, b in zip(x, y))


def negative(x):
    return tuple(-a for a in x)


def quads(element):
    return (element[0:4], element[4:8], element[8:12], element[12:16])


def merge_matrix(first, second):
    ll, lm, ml, mm = quads(first)
    nn, mr, rm, rr = quads(second)
    pivot = inverse(*plus(mm, nn))
    wl = times(pivot, ml)
    wr = times(pivot, mr)
    merged = (
        minus(ll, times(lm, wl))
        + negative(times(lm, wr))
        + negative(times(rm, wl))
        + minus(rr, times(rm, wr))
    )
    return merged, wl + wr, pivot + lm + rm


def merge_source(down, first, second):
    pivot, lm, rm = down[0:4], down[4:8], down[8:12]
    w = apply(pivot, plus(first[2:4], second[0:2]))
    return minus(first[0:2], apply(lm, w)) + minus(second[2:4], apply(rm, w)), w


def merge(first, second):
    matrix, up, down = merge_matrix(first[:MATRIX], second[:MATRIX])
    source, w = merge_source(down, first[MATRIX:], second[MATRIX:])
    return matrix + source, up, w


def inner(up, w, left, right):
    return minus(minus(w, apply(up[0:4], left)), apply(up[4:8], right))


def chunk_matrix(speed, damp, cells):
    def link(i):
        p = 2.0 * (damp(i) + damp(i + 1))
        q = 0.25 * (speed(i) + speed(i + 1))
        return q - p, -q - p

    def centre(i):
        return 1.0 + damp(i - 1) + 4.0 * damp(i) + damp(i + 1)

    b0, b1 = damp(0), damp(1)
    quarter = 0.25 * speed(0)
    up, low = link(0)
    zero = jnp.zeros_like(b0)
    ll = (b0, quarter - 2.0 * b0, -quarter - 2.0 * b0, 1.0 + 4.0 * b0 + b1)
    lk = (b0, zero, up, b1)
    kl = (b0, low, zero, b1)
    up, low = link(1)
    kk = (centre(1), up, low, centre(2))
    pairs = (cells - 2) // 2
    for k in range(1, pairs + 1):
        i = 2 * k
        pivot = inverse(*kk)
        wl = times(pivot, kl)
        up, low = link(i)
        here, there = damp(i), damp(i + 1)
        wr = (
            pivot[0] * here + pivot[1] * up,
            pivot[1] * there,
            pivot[2] * here + pivot[3] * up,
            pivot[3] * there,
        )
        yield wl + wr, pivot + lk + (low,), (here, there)

        def below(x):
            return (
                here * x[0] + low * x[2],
                here * x[1] + low * x[3],
                there * x[2],
                there * x[3],
            )

        ll = minus(ll, times(lk, wl))
        lk = negative(times(lk, wr))
        kl = negative(below(wl))
        if k < pairs:
            up, low_next = link(i + 1)
            kk = (centre(i + 1), up, low_next, centre(i + 2))
        else:
            quarter = 0.25 * speed(i + 1)
            kk = (
                1.0 + here + 4.0 * there,
                quarter - 2.0 * there,
                -quarter - 2.0 * there,
                there,
            )
        kk = minus(kk, below(wr))
    yield ll + lk + kl + kk


def pair_source(down, damps, left, pair, following):
    pivot, lk, low = down[0:4], down[4:8], down[8]
    w = apply(pivot, pair)
    left = minus(left, apply(lk, w))
    following = minus(following, (damps[0] * w[0] + low * w[1], damps[1] * w[1]))
    return left, following, w


def pair_of(source, k, cells):
    if k == (cells - 2) // 2:
        last = source(cells - 1)
        return (last, jnp.zeros_like(last))
    return (source(2 * k + 1), source(2 * k + 2))


def first_pair(source):
    first = source(0)
    return (jnp.zeros_like(first), first)


def blocks(rows, size):
    return [(at, min(size, rows - at)) for at in range(0, rows, size)]


def get(ref, count, at, size, base=0):
    return tuple(ref[base + v, pl.ds(at, size), :] for v in range(count))


def put(ref, values, at, size, base=0):
    for v, value in enumerate(values):
        ref[base + v, pl.ds(at, size), :] = value


def get_both(ref, count, at, size):
    return tuple(
        tuple(ref[v, pl.ds(2 * at + half, size, stride=2), :] for v in range(count))
        for half in (0, 1)
    )


def levels_of(lines):
    sizes = []
    rows = lines * CHUNKS
    while rows > lines:
        rows //= 2
        sizes.append(rows)
    return sizes


def split_all(top_ref, end_refs, up_refs, w_refs, sizes):
    source = top_ref
    for rows, target, ups, ws in zip(
        reversed(sizes), end_refs, reversed(up_refs), reversed(w_refs)
    ):
        for at, size in blocks(rows, 8):
            ends = get(source, 4, at, size)
            left, right = ends[0:2], ends[2:4]
            middle = inner(get(ups, UP, at, size), get(ws, 2, at, size), left, right)
            for v in range(2):
                target[v, pl.ds(2 * at, size, stride=2), :] = left[v]
                target[v, pl.ds(2 * at + 1, size, stride=2), :] = middle[v]
                target[2 + v, pl.ds(2 * at, size, stride=2), :] = middle[v]
                target[2 + v, pl.ds(2 * at + 1, size, stride=2), :] = right[v]
        source = target
    return source


def back_substitute(ends_ref, up_ref, w_ref, cells, at, size, store):
    ends = get(ends_ref, 4, at, size)
    left, following = ends[0:2], ends[2:4]
    store(0, left[1])
    store(cells - 1, following[0])
    for k in range((cells - 2) // 2 - 1, -1, -1):
        following = inner(
            get(up_ref, UP, at, size, k * UP), get(w_ref, 2, at, size, k * 2), left, following
        )
        store(2 * k + 1, following[0])
        store(2 * k + 2, following[1])


def close_ring(own, rest):
    ll, lr, rl, rr = quads(own)
    nn, nm, mn, mm = quads(rest)
    b = plus(lr, mn)
    c = plus(rl, nm)
    pivot = inverse(*plus(rr, nn))
    f = plus(own[16:18], rest[18:20])
    g = plus(own[18:20], rest[16:18])
    bd = times(b, pivot)
    left = apply(inverse(*minus(plus(ll, mm), times(bd, c))), minus(f, apply(bd, g)))
    right = apply(pivot, minus(g, apply(c, left)))
    return left, right


def open_ends(axis):
    place = lax.axis_index(axis)
    last = lax.axis_size(axis) - 1
    return jnp.where(place > 0, 1.0, 0.0), jnp.where(place < last, 1.0, 0.0)


def is_second(axis, bit):
    return lax.rem(lax.axis_index(axis) // (1 << bit), 2) == 1


def choose(second, one, other):
    return tuple(jnp.where(second, a, b) for a, b in zip(one, other))


def flat(ref, count, rows, at, size):
    return tuple(ref[pl.ds(v * rows + at, size), :] for v in range(count))


def put_flat(ref, values, rows, at, size):
    for v, value in enumerate(values):
        ref[pl.ds(v * rows + at, size), :] = value


def round_down(ups, ws, axis, bits, at, size, left, right):
    for bit in reversed(range(bits)):
        middle = inner(get(ups[bit], UP, at, size), get(ws[bit], 2, at, size), left, right)
        second = is_second(axis, bit)
        left, right = choose(second, middle, left), choose(second, right, middle)
    return left, right


def copies(pairs, sems):
    started = []
    for i, (source, target) in enumerate(pairs):
        copy = pltpu.make_async_copy(source, target, sems.at[i])
        copy.start()
        started.append(copy)
    return started


def wrap_down(fields, cells, *refs):
    residual, courant, dissip, wall_courant, wall_dissip = refs[0:5]
    packed, chunk_up, chunk_w = refs[5:8]
    ups, ws = refs[8:11], refs[11:14]
    wall_speed, wall_damp = refs[14:16]
    source_in, speed_in, damp_in, source_t, speed_t, damp_t = refs[16:22]
    elements, sems = refs[22:26], refs[26]
    lanes = damp_in.shape[0]
    length = cells * CHUNKS
    moves = [(dissip, damp_in)]
    for field in range(fields):
        rows = pl.ds(field * lanes, lanes)
        moves.append((courant.at[rows], speed_in.at[rows]))
        moves.append((residual.at[rows], source_in.at[rows]))
    moves += [(wall_dissip, wall_damp), (wall_courant, wall_speed)]
    started = copies(moves, sems)
    started[0].wait()
    damp_t[...] = damp_in[...].T

    def turn(field):
        started[1 + 2 * field].wait()
        speed_t[pl.ds(field * length, length), :] = speed_in[pl.ds(field * lanes, lanes), :].T
        started[2 + 2 * field].wait()
        source_t[pl.ds(field * length, length), :] = source_in[pl.ds(field * lanes, lanes), :].T

    for at, size in blocks(fields * CHUNKS, 16):
        repeat = size // CHUNKS
        for field in range(at // CHUNKS, at // CHUNKS + repeat):
            turn(field)

        def speed(i):
            return speed_t[pl.ds(at * cells + i, size, stride=cells), :]

        def source(i):
            return source_t[pl.ds(at * cells + i, size, stride=cells), :]

        def damp(i):
            rows = damp_t[pl.ds(i, CHUNKS, stride=cells), :]
            return jnp.concatenate([rows] * repeat, axis=0) if repeat > 1 else rows

        left, pair = first_pair(source), pair_of(source, 0, cells)
        for k, step in enumerate(chunk_matrix(speed, damp, cells)):
            if k == (cells - 2) // 2:
                put(elements[0], step + left + pair, at, size)
                break
            up, down, damps = step
            left, pair, w = pair_source(down, damps, left, pair, pair_of(source, k + 1, cells))
            put(chunk_up, up, at, size, k * UP)
            put(chunk_w, w, at, size, k * 2)
    for level, rows in enumerate(levels_of(fields)):
        for at, size in blocks(rows, 8):
            merged, up, w = merge(*get_both(elements[level], VALUES, at, size))
            put(elements[level + 1], merged, at, size)
            put(ups[level], up, at, size)
            put(ws[level], w, at, size)
    for v in range(VALUES):
        packed[pl.ds(v * fields, fields), :] = elements[-1][v]
    started[-2].wait()
    started[-1].wait()


def wrap_round(fields, bit, own, other, packed, up_out, w_out):
    second = is_second("wrap", bit)
    for at, size in blocks(fields, 8):
        mine = flat(own, VALUES, fields, at, size)
        theirs = flat(other, VALUES, fields, at, size)
        merged, up, w = merge(choose(second, theirs, mine), choose(second, mine, theirs))
        put_flat(packed, merged, fields, at, size)
        put(up_out, up, at, size)
        put(w_out, w, at, size)


def wall_matrix(fields, span, cells, *refs):
    speed_in, damp_in = refs[0:2]
    packed, damp_out, chunk_up, chunk_down = refs[2:6]
    ups, downs = refs[6:9], refs[9:12]
    elements = refs[12:16]
    size = span * CHUNKS
    for field in range(fields):
        at = field * size

        def speed(i):
            return speed_in[pl.ds(at * cells + i, size, stride=cells), :]

        def damp(i):
            return damp_in[pl.ds(i, size, stride=cells), :]

        for k, step in enumerate(chunk_matrix(speed, damp, cells)):
            if k == (cells - 2) // 2:
                put(elements[0], step, at, size)
                break
            up, down, damps = step
            put(chunk_up, up, at, size, k * UP)
            put(chunk_down, down, at, size, k * CHUNK_DOWN)
            if field == 0:
                put(damp_out, damps, 0, size, k * 2)
    lines = fields * span
    for level, rows in enumerate(levels_of(lines)):
        for at, size in blocks(rows, 8):
            merged, up, down = merge_matrix(*get_both(elements[level], MATRIX, at, size))
            put(elements[level + 1], merged, at, size)
            put(ups[level], up, at, size)
            put(downs[level], down, at, size)
    not_first, not_last = open_ends("normal")
    for v in range(MATRIX):
        value = elements[-1][v]
        if v in (0, 1, 2, 4, 5, 8, 10):
            value = value * not_first
        if v in (5, 7, 10, 11, 13, 14, 15):
            value = value * not_last
        packed[pl.ds(v * lines, lines), :] = value


def wall_round(lines, bit, final, own, other, packed, up_out, down_out, *outer_out):
    second = is_second("normal", bit)
    upper = is_second("normal", bit + 1)
    for at, size in blocks(lines, 8):
        mine = flat(own, MATRIX, lines, at, size)
        theirs = flat(other, MATRIX, lines, at, size)
        merged, up, down = merge_matrix(
            choose(second, theirs, mine), choose(second, mine, theirs)
        )
        put(up_out, up, at, size)
        put(down_out, down, at, size)
        if not final:
            put_flat(packed, merged, lines, at, size)
            continue
        ll, lr, rl, rr = quads(merged)
        outer, into = choose(upper, rr, ll), choose(upper, rl, lr)
        out, middle = choose(upper, lr, rl), choose(upper, ll, rr)
        is_upper = jnp.where(upper, 1.0, 0.0)
        pivot = inverse(
            outer[0] + (1.0 - is_upper), outer[1], outer[2], outer[3] + is_upper
        )
        put_flat(packed, minus(middle, times(out, times(pivot, into))), lines, at, size)
        put(outer_out[0], pivot + into + out, at, size)


def wall_source_round(lines, bit, final, own, other, down_in, *refs):
    second = is_second("normal", bit)
    upper = is_second("normal", bit + 1)
    if final:
        outer_in, packed, w_out, outer_out = refs
    else:
        packed, w_out = refs
    for at, size in blocks(lines, 8):
        mine = flat(own, SOURCE, lines, at, size)
        theirs = flat(other, SOURCE, lines, at, size)
        merged, w = merge_source(
            get(down_in, MERGE_DOWN, at, size),
            choose(second, theirs, mine),
            choose(second, mine, theirs),
        )
        put(w_out, w, at, size)
        if not final:
            put_flat(packed, merged, lines, at, size)
            continue
        outer = choose(upper, merged[2:4], merged[0:2])
        middle = choose(upper, merged[0:2], merged[2:4])
        factors = get(outer_in, 12, at, size)
        outer = apply(factors[0:4], outer)
        put_flat(packed, minus(middle, apply(factors[8:12], outer)), lines, at, size)
        put(outer_out, outer, at, size)


def middle(fields, span, wrap_cells, wall_cells, bits, *refs):
    own, other, refs = refs[0], refs[1], refs[2:]
    round_ups, round_ws, refs = refs[:bits], refs[bits : 2 * bits], refs[2 * bits :]
    chunk_up, chunk_w, ups, ws = refs[0], refs[1], refs[2:5], refs[5:8]
    coupling, damps_in, chunk_down, downs = refs[8], refs[9], refs[10], refs[11:14]
    packed, wall_w, wall_ws = refs[14], refs[15], refs[16:19]
    ends, solved_t, solved, mixed = refs[19:23], refs[23], refs[24], refs[25]
    sources = refs[26:30]

    for at, size in blocks(fields, 8):
        left, right = close_ring(
            flat(own, VALUES, fields, at, size), flat(other, VALUES, fields, at, size)
        )
        left, right = round_down(round_ups, round_ws, "wrap", bits, at, size, left, right)
        put(ends[0], left + right, at, size)
    last = split_all(ends[0], ends[1:], ups, ws, levels_of(fields))
    length = wrap_cells * CHUNKS
    for at, size in blocks(fields * CHUNKS, 16):

        def store(i, value):
            solved_t[pl.ds(at * wrap_cells + i, size, stride=wrap_cells), :] = value

        back_substitute(last, chunk_up, chunk_w, wrap_cells, at, size, store)
    lanes = solved.shape[0] // fields
    for field in range(fields):
        solved[pl.ds(field * lanes, lanes), :] = solved_t[pl.ds(field * length, length), :].T

    for at, size in blocks(lanes, 16):
        update = [solved[pl.ds(j * lanes + at, size), :] for j in range(fields)]
        for k in range(fields):
            total = coupling[k, 0, pl.ds(at, size), :].astype(jnp.float32) * update[0]
            for j in range(1, fields):
                total = total + coupling[k, j, pl.ds(at, size), :].astype(jnp.float32) * update[j]
            mixed[pl.ds(k * lanes + at, size), :] = total

    pairs = (wall_cells - 2) // 2
    size = span * CHUNKS
    for field in range(fields):
        at = field * size

        def source(i):
            return mixed[pl.ds(at * wall_cells + i, size, stride=wall_cells), :]

        left, pair = first_pair(source), pair_of(source, 0, wall_cells)
        for k in range(pairs):
            left, pair, w = pair_source(
                get(chunk_down, CHUNK_DOWN, at, size, k * CHUNK_DOWN),
                get(damps_in, 2, 0, size, k * 2),
                left,
                pair,
                pair_of(source, k + 1, wall_cells),
            )
            put(wall_w, w, at, size, k * 2)
        put(sources[0], left + pair, at, size)
    lines = fields * span
    for level, rows in enumerate(levels_of(lines)):
        for at, size in blocks(rows, 8):
            down = get(downs[level], MERGE_DOWN, at, size)
            merged, w = merge_source(down, *get_both(sources[level], SOURCE, at, size))
            put(sources[level + 1], merged, at, size)
            put(wall_ws[level], w, at, size)
    not_first, not_last = open_ends("normal")
    for v, keep in enumerate((not_first, None, None, not_last)):
        value = sources[-1][v]
        packed[pl.ds(v * lines, lines), :] = value if keep is None else value * keep


def wall_up(fields, span, cells, bits, *refs):
    own, other, own_source, other_source, outer_in, outer_w = refs[0:6]
    refs = refs[6:]
    round_ups, round_ws, refs = refs[:bits], refs[bits : 2 * bits], refs[2 * bits :]
    chunk_up, chunk_w, ups, ws = refs[0], refs[1], refs[2:5], refs[5:8]
    update = refs[8]
    ends, result, sems = refs[9:13], refs[13], refs[14]
    lines = fields * span
    upper = is_second("normal", bits)
    for at, size in blocks(lines, 8):
        matrix = plus(flat(own, 4, lines, at, size), flat(other, 4, lines, at, size))
        source = plus(flat(own_source, 2, lines, at, size), flat(other_source, 2, lines, at, size))
        centre = apply(inverse(*matrix), source)
        factors = get(outer_in, 12, at, size)
        outer = minus(
            get(outer_w, 2, at, size), apply(factors[0:4], apply(factors[4:8], centre))
        )
        left, right = choose(upper, centre, outer), choose(upper, outer, centre)
        left, right = round_down(round_ups, round_ws, "normal", bits, at, size, left, right)
        put(ends[0], left + right, at, size)
    last = split_all(ends[0], ends[1:], ups, ws, levels_of(lines))
    size = span * CHUNKS
    length = size * cells
    started = []
    for field in range(fields):
        at = field * size

        def store(i, value):
            result[pl.ds(at * cells + i, size, stride=cells), :] = value

        back_substitute(last, chunk_up, chunk_w, cells, at, size, store)
        rows = pl.ds(field * length, length)
        copy = pltpu.make_async_copy(result.at[rows], update.at[rows], sems.at[field])
        copy.start()
        started.append(copy)
    for copy in started:
        copy.wait()


def f32(*shape):
    return jax.ShapeDtypeStruct(shape, jnp.float32)


def vmem(*shape):
    return pltpu.VMEM(shape, jnp.float32)


IN_VMEM = pl.BlockSpec(memory_space=pltpu.VMEM)
IN_HBM = pl.BlockSpec(memory_space=pltpu.HBM)
PARAMS = pltpu.CompilerParams(vmem_limit_bytes=24 * 2**20)


def kernel(name, body, ins, outs, scratch, flops):
    in_bytes = sum(a.size * a.dtype.itemsize for a, _ in ins)
    out_bytes = sum(a.size * 4 for a, _ in outs)
    outputs = pl.pallas_call(
        body,
        out_shape=[a for a, _ in outs],
        in_specs=[spec for _, spec in ins],
        out_specs=[spec for _, spec in outs],
        scratch_shapes=scratch,
        compiler_params=PARAMS,
        cost_estimate=pl.CostEstimate(
            flops=flops, bytes_accessed=in_bytes + out_bytes, transcendentals=0
        ),
        name=name,
    )(*[a for a, _ in ins])
    return list(outputs)


def inside(arrays):
    return [(a, IN_VMEM) for a in arrays]


def outside(arrays):
    return [(pltpu.with_memory_space_constraint(a, pltpu.HBM), IN_HBM) for a in arrays]


def exchange(array, axis, bit):
    count = lax.axis_size(axis)
    return lax.ppermute(array, axis, [(i ^ (1 << bit), i) for i in range(count)])


def local(residual, courant_xi, courant_eta, dissip_xi, dissip_eta, coupling):
    fields, span, high, wide = residual.shape
    lanes = span * high
    wrap_cells, wall_cells = wide // CHUNKS, high // CHUNKS
    wrap_pairs, wall_pairs = (wrap_cells - 2) // 2, (wall_cells - 2) // 2
    wrap_count, wall_count = lax.axis_size("wrap"), lax.axis_size("normal")
    lines = fields * span
    wrap_levels, wall_levels = levels_of(fields), levels_of(lines)
    wrap_rows, wall_rows = fields * CHUNKS, lines * CHUNKS

    def rows_of(array):
        return array.reshape(-1, wide)

    wrap_bits = wrap_count.bit_length() - 2
    wall_bits = wall_count.bit_length() - 2
    results = kernel(
        "wrap_down",
        functools.partial(wrap_down, fields, wrap_cells),
        outside(
            [rows_of(a) for a in (residual, courant_xi, dissip_xi, courant_eta, dissip_eta)]
        ),
        inside(
            [
                f32(VALUES * fields, lanes),
                f32(wrap_pairs * UP, wrap_rows, lanes),
                f32(wrap_pairs * 2, wrap_rows, lanes),
            ]
            + [f32(UP, n, lanes) for n in wrap_levels]
            + [f32(2, n, lanes) for n in wrap_levels]
            + [f32(fields * lanes, wide), f32(lanes, wide)]
        ),
        [vmem(fields * lanes, wide)] * 2
        + [vmem(lanes, wide)]
        + [vmem(fields * wide, lanes)] * 2
        + [vmem(wide, lanes)]
        + [vmem(VALUES, n, lanes) for n in [wrap_rows] + wrap_levels]
        + [pltpu.SemaphoreType.DMA((2 * fields + 3,))],
        100 * residual.size,
    )
    element, wrap_factors, wall_inputs = results[0], results[1:9], results[9:11]
    wrap_ups, wrap_ws = [], []
    for bit in range(wrap_bits):
        element, up, w = kernel(
            f"wrap_round_{bit}",
            functools.partial(wrap_round, fields, bit),
            inside([element, exchange(element, "wrap", bit)]),
            inside([f32(VALUES * fields, lanes), f32(UP, fields, lanes), f32(2, fields, lanes)]),
            [],
            200 * fields * lanes,
        )
        wrap_ups.append(up)
        wrap_ws.append(w)
    wrap_other = exchange(element, "wrap", wrap_bits)
    results = kernel(
        "wall_matrix",
        functools.partial(wall_matrix, fields, span, wall_cells),
        inside(wall_inputs),
        inside(
            [
                f32(MATRIX * lines, wide),
                f32(wall_pairs * 2, span * CHUNKS, wide),
                f32(wall_pairs * UP, wall_rows, wide),
                f32(wall_pairs * CHUNK_DOWN, wall_rows, wide),
            ]
            + [f32(UP, n, wide) for n in wall_levels]
            + [f32(MERGE_DOWN, n, wide) for n in wall_levels]
        ),
        [vmem(MATRIX, n, wide) for n in [wall_rows] + wall_levels],
        100 * residual.size,
    )
    matrix, damps, chunk_up, chunk_down = results[0:4]
    wall_ups, wall_downs = results[4:7], results[7:10]
    round_ups, round_downs = [], []
    for bit in range(wall_bits):
        final = bit == wall_bits - 1
        matrix, up, down, *outer = kernel(
            f"wall_round_{bit}",
            functools.partial(wall_round, lines, bit, final),
            inside([matrix, exchange(matrix, "normal", bit)]),
            inside(
                [
                    f32((4 if final else MATRIX) * lines, wide),
                    f32(UP, lines, wide),
                    f32(MERGE_DOWN, lines, wide),
                ]
                + ([f32(12, lines, wide)] if final else [])
            ),
            [],
            200 * lines * wide,
        )
        round_ups.append(up)
        round_downs.append(down)
    matrix_other = exchange(matrix, "normal", wall_bits)
    source, *wall_ws = kernel(
        "middle",
        functools.partial(middle, fields, span, wrap_cells, wall_cells, wrap_bits),
        inside(
            [element, wrap_other]
            + wrap_ups
            + wrap_ws
            + wrap_factors
            + [coupling.reshape(fields, fields, lanes, wide), damps, chunk_down]
            + wall_downs
        ),
        inside(
            [f32(SOURCE * lines, wide), f32(wall_pairs * 2, wall_rows, wide)]
            + [f32(2, n, wide) for n in wall_levels]
        ),
        [vmem(4, n, lanes) for n in reversed([wrap_rows] + wrap_levels)]
        + [vmem(fields * wide, lanes), vmem(fields * lanes, wide), vmem(fields * lanes, wide)]
        + [vmem(SOURCE, n, wide) for n in [wall_rows] + wall_levels],
        100 * residual.size,
    )
    round_ws = []
    for bit in range(wall_bits):
        final = bit == wall_bits - 1
        source, w, *outer_w = kernel(
            f"wall_source_round_{bit}",
            functools.partial(wall_source_round, lines, bit, final),
            inside(
                [source, exchange(source, "normal", bit), round_downs[bit]]
                + (outer if final else [])
            ),
            inside(
                [f32((2 if final else SOURCE) * lines, wide), f32(2, lines, wide)]
                + ([f32(2, lines, wide)] if final else [])
            ),
            [],
            50 * lines * wide,
        )
        round_ws.append(w)
    (update,) = kernel(
        "wall_up",
        functools.partial(wall_up, fields, span, wall_cells, wall_bits),
        inside(
            [matrix, matrix_other, source, exchange(source, "normal", wall_bits)]
            + outer
            + outer_w
            + round_ups
            + round_ws
            + [chunk_up, wall_ws[0]]
            + wall_ups
            + wall_ws[1:]
        ),
        [(f32(fields * lanes, wide), IN_HBM)],
        [vmem(4, n, wide) for n in reversed([wall_rows] + wall_levels)]
        + [vmem(fields * lanes, wide), pltpu.SemaphoreType.DMA((fields,))],
        30 * residual.size,
    )
    return update.reshape(residual.shape)


def solution(mesh):
    placed = (
        P(None, None, "normal", "wrap"),
        P(None, None, "normal", "wrap"),
        P(None, None, "normal", "wrap"),
        P(None, "normal", "wrap"),
        P(None, "normal", "wrap"),
        P(None, None, None, "normal", "wrap"),
    )
    return jax.shard_map(
        local,
        mesh=mesh,
        in_specs=placed,
        out_specs=P(None, None, "normal", "wrap"),
        check_vma=False,
    )
```

```python
import functools

import jax
import jax.numpy as jnp
from jax import lax
from jax.experimental import pallas as pl
from jax.experimental.pallas import tpu as pltpu
from jax.sharding import PartitionSpec as P

MATRIX = 16
SOURCE = 4
VALUES = MATRIX + SOURCE
UP = 8
CHUNK_DOWN = 9
MERGE_DOWN = 12
CHUNKS = 8


def inverse(a, b, c, d):
    scale = 1.0 / (a * d - b * c)
    return (d * scale, -b * scale, -c * scale, a * scale)


def times(x, y):
    return (
        x[0] * y[0] + x[1] * y[2],
        x[0] * y[1] + x[1] * y[3],
        x[2] * y[0] + x[3] * y[2],
        x[2] * y[1] + x[3] * y[3],
    )


def apply(x, v):
    return (x[0] * v[0] + x[1] * v[1], x[2] * v[0] + x[3] * v[1])


def minus(x, y):
    return tuple(a - b for a, b in zip(x, y))


def plus(x, y):
    return tuple(a + b for a, b in zip(x, y))


def negative(x):
    return tuple(-a for a in x)


def quads(element):
    return (element[0:4], element[4:8], element[8:12], element[12:16])


def merge_matrix(first, second):
    ll, lm, ml, mm = quads(first)
    nn, mr, rm, rr = quads(second)
    pivot = inverse(*plus(mm, nn))
    wl = times(pivot, ml)
    wr = times(pivot, mr)
    merged = (
        minus(ll, times(lm, wl))
        + negative(times(lm, wr))
        + negative(times(rm, wl))
        + minus(rr, times(rm, wr))
    )
    return merged, wl + wr, pivot + lm + rm


def merge_source(down, first, second):
    pivot, lm, rm = down[0:4], down[4:8], down[8:12]
    w = apply(pivot, plus(first[2:4], second[0:2]))
    return minus(first[0:2], apply(lm, w)) + minus(second[2:4], apply(rm, w)), w


def merge(first, second):
    matrix, up, down = merge_matrix(first[:MATRIX], second[:MATRIX])
    source, w = merge_source(down, first[MATRIX:], second[MATRIX:])
    return matrix + source, up, w


def inner(up, w, left, right):
    return minus(minus(w, apply(up[0:4], left)), apply(up[4:8], right))


def chunk_matrix(speed, damp, cells):
    def link(i):
        p = 2.0 * (damp(i) + damp(i + 1))
        q = 0.25 * (speed(i) + speed(i + 1))
        return q - p, -q - p

    def centre(i):
        return 1.0 + damp(i - 1) + 4.0 * damp(i) + damp(i + 1)

    b0, b1 = damp(0), damp(1)
    quarter = 0.25 * speed(0)
    up, low = link(0)
    zero = jnp.zeros_like(b0)
    ll = (b0, quarter - 2.0 * b0, -quarter - 2.0 * b0, 1.0 + 4.0 * b0 + b1)
    lk = (b0, zero, up, b1)
    kl = (b0, low, zero, b1)
    up, low = link(1)
    kk = (centre(1), up, low, centre(2))
    pairs = (cells - 2) // 2
    for k in range(1, pairs + 1):
        i = 2 * k
        pivot = inverse(*kk)
        wl = times(pivot, kl)
        up, low = link(i)
        here, there = damp(i), damp(i + 1)
        wr = (
            pivot[0] * here + pivot[1] * up,
            pivot[1] * there,
            pivot[2] * here + pivot[3] * up,
            pivot[3] * there,
        )
        yield wl + wr, pivot + lk + (low,), (here, there)

        def below(x):
            return (
                here * x[0] + low * x[2],
                here * x[1] + low * x[3],
                there * x[2],
                there * x[3],
            )

        ll = minus(ll, times(lk, wl))
        lk = negative(times(lk, wr))
        kl = negative(below(wl))
        if k < pairs:
            up, low_next = link(i + 1)
            kk = (centre(i + 1), up, low_next, centre(i + 2))
        else:
            quarter = 0.25 * speed(i + 1)
            kk = (
                1.0 + here + 4.0 * there,
                quarter - 2.0 * there,
                -quarter - 2.0 * there,
                there,
            )
        kk = minus(kk, below(wr))
    yield ll + lk + kl + kk


def pair_source(down, damps, left, pair, following):
    pivot, lk, low = down[0:4], down[4:8], down[8]
    w = apply(pivot, pair)
    left = minus(left, apply(lk, w))
    following = minus(following, (damps[0] * w[0] + low * w[1], damps[1] * w[1]))
    return left, following, w


def pair_of(source, k, cells):
    if k == (cells - 2) // 2:
        last = source(cells - 1)
        return (last, jnp.zeros_like(last))
    return (source(2 * k + 1), source(2 * k + 2))


def first_pair(source):
    first = source(0)
    return (jnp.zeros_like(first), first)


def blocks(rows, size):
    return [(at, min(size, rows - at)) for at in range(0, rows, size)]


def get(ref, count, at, size, base=0):
    return tuple(ref[base + v, pl.ds(at, size), :] for v in range(count))


def put(ref, values, at, size, base=0):
    for v, value in enumerate(values):
        ref[base + v, pl.ds(at, size), :] = value


def get_both(ref, count, at, size):
    return tuple(
        tuple(ref[v, pl.ds(2 * at + half, size, stride=2), :] for v in range(count))
        for half in (0, 1)
    )


def levels_of(lines):
    sizes = []
    rows = lines * CHUNKS
    while rows > lines:
        rows //= 2
        sizes.append(rows)
    return sizes


def split_all(top_ref, end_refs, up_refs, w_refs, sizes):
    source = top_ref
    for rows, target, ups, ws in zip(
        reversed(sizes), end_refs, reversed(up_refs), reversed(w_refs)
    ):
        for at, size in blocks(rows, 8):
            ends = get(source, 4, at, size)
            left, right = ends[0:2], ends[2:4]
            middle = inner(get(ups, UP, at, size), get(ws, 2, at, size), left, right)
            for v in range(2):
                target[v, pl.ds(2 * at, size, stride=2), :] = left[v]
                target[v, pl.ds(2 * at + 1, size, stride=2), :] = middle[v]
                target[2 + v, pl.ds(2 * at, size, stride=2), :] = middle[v]
                target[2 + v, pl.ds(2 * at + 1, size, stride=2), :] = right[v]
        source = target
    return source


def back_substitute(ends_ref, up_ref, w_ref, cells, at, size, store):
    ends = get(ends_ref, 4, at, size)
    left, following = ends[0:2], ends[2:4]
    store(0, left[1])
    store(cells - 1, following[0])
    for k in range((cells - 2) // 2 - 1, -1, -1):
        following = inner(
            get(up_ref, UP, at, size, k * UP), get(w_ref, 2, at, size, k * 2), left, following
        )
        store(2 * k + 1, following[0])
        store(2 * k + 2, following[1])


def close_ring(own, rest):
    ll, lr, rl, rr = quads(own)
    nn, nm, mn, mm = quads(rest)
    b = plus(lr, mn)
    c = plus(rl, nm)
    pivot = inverse(*plus(rr, nn))
    f = plus(own[16:18], rest[18:20])
    g = plus(own[18:20], rest[16:18])
    bd = times(b, pivot)
    left = apply(inverse(*minus(plus(ll, mm), times(bd, c))), minus(f, apply(bd, g)))
    right = apply(pivot, minus(g, apply(c, left)))
    return left, right


def open_ends(axis):
    place = lax.axis_index(axis)
    last = lax.axis_size(axis) - 1
    return jnp.where(place > 0, 1.0, 0.0), jnp.where(place < last, 1.0, 0.0)


def is_second(axis, bit):
    return lax.rem(lax.axis_index(axis) // (1 << bit), 2) == 1


def choose(second, one, other):
    return tuple(jnp.where(second, a, b) for a, b in zip(one, other))


def flat(ref, count, rows, at, size):
    return tuple(ref[pl.ds(v * rows + at, size), :] for v in range(count))


def put_flat(ref, values, rows, at, size):
    for v, value in enumerate(values):
        ref[pl.ds(v * rows + at, size), :] = value


def round_down(ups, ws, axis, bits, at, size, left, right):
    for bit in reversed(range(bits)):
        middle = inner(get(ups[bit], UP, at, size), get(ws[bit], 2, at, size), left, right)
        second = is_second(axis, bit)
        left, right = choose(second, middle, left), choose(second, right, middle)
    return left, right


def copies(pairs, sems):
    started = []
    for i, (source, target) in enumerate(pairs):
        copy = pltpu.make_async_copy(source, target, sems.at[i])
        copy.start()
        started.append(copy)
    return started


def wrap_down(fields, cells, *refs):
    residual, courant, dissip, wall_courant, wall_dissip = refs[0:5]
    packed, chunk_up, chunk_w = refs[5:8]
    ups, ws = refs[8:11], refs[11:14]
    wall_speed, wall_damp = refs[14:16]
    source_in, speed_in, damp_in, source_t, speed_t, damp_t = refs[16:22]
    elements, sems = refs[22:26], refs[26]
    lanes = damp_in.shape[0]
    length = cells * CHUNKS
    moves = [(dissip, damp_in)]
    for field in range(fields):
        rows = pl.ds(field * lanes, lanes)
        moves.append((courant.at[rows], speed_in.at[rows]))
        moves.append((residual.at[rows], source_in.at[rows]))
    moves += [(wall_dissip, wall_damp), (wall_courant, wall_speed)]
    started = copies(moves, sems)
    started[0].wait()
    damp_t[...] = damp_in[...].T

    def turn(field):
        started[1 + 2 * field].wait()
        speed_t[pl.ds(field * length, length), :] = speed_in[pl.ds(field * lanes, lanes), :].T
        started[2 + 2 * field].wait()
        source_t[pl.ds(field * length, length), :] = source_in[pl.ds(field * lanes, lanes), :].T

    for at, size in blocks(fields * CHUNKS, 16):
        repeat = size // CHUNKS
        for field in range(at // CHUNKS, at // CHUNKS + repeat):
            turn(field)

        def speed(i):
            return speed_t[pl.ds(at * cells + i, size, stride=cells), :]

        def source(i):
            return source_t[pl.ds(at * cells + i, size, stride=cells), :]

        def damp(i):
            rows = damp_t[pl.ds(i, CHUNKS, stride=cells), :]
            return jnp.concatenate([rows] * repeat, axis=0) if repeat > 1 else rows

        left, pair = first_pair(source), pair_of(source, 0, cells)
        for k, step in enumerate(chunk_matrix(speed, damp, cells)):
            if k == (cells - 2) // 2:
                put(elements[0], step + left + pair, at, size)
                break
            up, down, damps = step
            left, pair, w = pair_source(down, damps, left, pair, pair_of(source, k + 1, cells))
            put(chunk_up, up, at, size, k * UP)
            put(chunk_w, w, at, size, k * 2)
    for level, rows in enumerate(levels_of(fields)):
        for at, size in blocks(rows, 8):
            merged, up, w = merge(*get_both(elements[level], VALUES, at, size))
            put(elements[level + 1], merged, at, size)
            put(ups[level], up, at, size)
            put(ws[level], w, at, size)
    for v in range(VALUES):
        packed[pl.ds(v * fields, fields), :] = elements[-1][v]
    started[-2].wait()
    started[-1].wait()


def wrap_round(fields, bit, own, other, after, packed, up_out, w_out):
    second = is_second("wrap", bit)
    for at, size in blocks(fields, 8):
        mine = flat(own, VALUES, fields, at, size)
        theirs = flat(other, VALUES, fields, at, size)
        merged, up, w = merge(choose(second, theirs, mine), choose(second, mine, theirs))
        put_flat(packed, merged, fields, at, size)
        put(up_out, up, at, size)
        put(w_out, w, at, size)


def wall_matrix(fields, span, cells, *refs):
    speed_in, damp_in, coupling = refs[0:3]
    packed, damp_out, chunk_up, chunk_down = refs[3:7]
    ups, downs, coupling_out = refs[7:10], refs[10:13], refs[13]
    elements, sems = refs[14:18], refs[18]
    size = span * CHUNKS
    started = copies(
        [(coupling.at[k], coupling_out.at[k]) for k in range(fields)], sems
    )
    for field in range(fields):
        at = field * size

        def speed(i):
            return speed_in[pl.ds(at * cells + i, size, stride=cells), :]

        def damp(i):
            return damp_in[pl.ds(i, size, stride=cells), :]

        for k, step in enumerate(chunk_matrix(speed, damp, cells)):
            if k == (cells - 2) // 2:
                put(elements[0], step, at, size)
                break
            up, down, damps = step
            put(chunk_up, up, at, size, k * UP)
            put(chunk_down, down, at, size, k * CHUNK_DOWN)
            if field == 0:
                put(damp_out, damps, 0, size, k * 2)
    lines = fields * span
    for level, rows in enumerate(levels_of(lines)):
        for at, size in blocks(rows, 8):
            merged, up, down = merge_matrix(*get_both(elements[level], MATRIX, at, size))
            put(elements[level + 1], merged, at, size)
            put(ups[level], up, at, size)
            put(downs[level], down, at, size)
    not_first, not_last = open_ends("normal")
    for v in range(MATRIX):
        value = elements[-1][v]
        if v in (0, 1, 2, 4, 5, 8, 10):
            value = value * not_first
        if v in (5, 7, 10, 11, 13, 14, 15):
            value = value * not_last
        packed[pl.ds(v * lines, lines), :] = value
    for copy in started:
        copy.wait()


def wall_round(lines, bit, final, own, other, packed, up_out, down_out, *outer_out):
    second = is_second("normal", bit)
    upper = is_second("normal", bit + 1)
    for at, size in blocks(lines, 8):
        mine = flat(own, MATRIX, lines, at, size)
        theirs = flat(other, MATRIX, lines, at, size)
        merged, up, down = merge_matrix(
            choose(second, theirs, mine), choose(second, mine, theirs)
        )
        put(up_out, up, at, size)
        put(down_out, down, at, size)
        if not final:
            put_flat(packed, merged, lines, at, size)
            continue
        ll, lr, rl, rr = quads(merged)
        outer, into = choose(upper, rr, ll), choose(upper, rl, lr)
        out, middle = choose(upper, lr, rl), choose(upper, ll, rr)
        is_upper = jnp.where(upper, 1.0, 0.0)
        pivot = inverse(
            outer[0] + (1.0 - is_upper), outer[1], outer[2], outer[3] + is_upper
        )
        put_flat(packed, minus(middle, times(out, times(pivot, into))), lines, at, size)
        put(outer_out[0], pivot + into + out, at, size)


def wall_source_round(lines, bit, own, other, down_in, packed, w_out):
    second = is_second("normal", bit)
    for at, size in blocks(lines, 8):
        mine = flat(own, SOURCE, lines, at, size)
        theirs = flat(other, SOURCE, lines, at, size)
        merged, w = merge_source(
            get(down_in, MERGE_DOWN, at, size),
            choose(second, theirs, mine),
            choose(second, mine, theirs),
        )
        put_flat(packed, merged, lines, at, size)
        put(w_out, w, at, size)


def reduce_source(down, factors, second, upper, mine, theirs):
    merged, w = merge_source(
        down, choose(second, theirs, mine), choose(second, mine, theirs)
    )
    outer = apply(factors[0:4], choose(upper, merged[2:4], merged[0:2]))
    centre = choose(upper, merged[0:2], merged[2:4])
    return minus(centre, apply(factors[8:12], outer)), outer, w


def wall_share(lines, bit, own, down_in, outer_in, share):
    second, upper = is_second("normal", bit), is_second("normal", bit + 1)
    for at, size in blocks(lines, 8):
        mine = flat(own, SOURCE, lines, at, size)
        none = tuple(jnp.zeros_like(value) for value in mine)
        down, factors = get(down_in, MERGE_DOWN, at, size), get(outer_in, 12, at, size)
        part, _, _ = reduce_source(down, factors, second, upper, mine, none)
        put_flat(share, part, lines, at, size)


def middle(fields, span, wrap_cells, wall_cells, bits, *refs):
    own, others, refs = refs[0], refs[1:4], refs[4:]
    round_ups, round_ws, refs = refs[:bits], refs[bits : 2 * bits], refs[2 * bits :]
    chunk_up, chunk_w, ups, ws = refs[0], refs[1], refs[2:5], refs[5:8]
    coupling, damps_in, chunk_down, downs = refs[8], refs[9], refs[10], refs[11:14]
    packed, wall_w, wall_ws = refs[14], refs[15], refs[16:19]
    ends, solved_t, solved, mixed = refs[19:23], refs[23], refs[24], refs[25]
    sources = refs[26:30]

    for at, size in blocks(fields, 8):
        odd = is_second("wrap", bits)
        near, opposite, far = (flat(other, VALUES, fields, at, size) for other in others)
        following, before = choose(odd, far, near), choose(odd, near, far)
        rest = merge(merge(following, opposite)[0], before)[0]
        left, right = close_ring(flat(own, VALUES, fields, at, size), rest)
        left, right = round_down(round_ups, round_ws, "wrap", bits, at, size, left, right)
        put(ends[0], left + right, at, size)
    last = split_all(ends[0], ends[1:], ups, ws, levels_of(fields))
    length = wrap_cells * CHUNKS
    for at, size in blocks(fields * CHUNKS, 16):

        def store(i, value):
            solved_t[pl.ds(at * wrap_cells + i, size, stride=wrap_cells), :] = value

        back_substitute(last, chunk_up, chunk_w, wrap_cells, at, size, store)
    lanes = solved.shape[0] // fields
    for field in range(fields):
        solved[pl.ds(field * lanes, lanes), :] = solved_t[pl.ds(field * length, length), :].T

    for at, size in blocks(lanes, 16):
        update = [solved[pl.ds(j * lanes + at, size), :] for j in range(fields)]
        for k in range(fields):
            total = coupling[k, 0, pl.ds(at, size), :].astype(jnp.float32) * update[0]
            for j in range(1, fields):
                total = total + coupling[k, j, pl.ds(at, size), :].astype(jnp.float32) * update[j]
            mixed[pl.ds(k * lanes + at, size), :] = total

    pairs = (wall_cells - 2) // 2
    size = span * CHUNKS
    for field in range(fields):
        at = field * size

        def source(i):
            return mixed[pl.ds(at * wall_cells + i, size, stride=wall_cells), :]

        left, pair = first_pair(source), pair_of(source, 0, wall_cells)
        for k in range(pairs):
            left, pair, w = pair_source(
                get(chunk_down, CHUNK_DOWN, at, size, k * CHUNK_DOWN),
                get(damps_in, 2, 0, size, k * 2),
                left,
                pair,
                pair_of(source, k + 1, wall_cells),
            )
            put(wall_w, w, at, size, k * 2)
        put(sources[0], left + pair, at, size)
    lines = fields * span
    for level, rows in enumerate(levels_of(lines)):
        for at, size in blocks(rows, 8):
            down = get(downs[level], MERGE_DOWN, at, size)
            merged, w = merge_source(down, *get_both(sources[level], SOURCE, at, size))
            put(sources[level + 1], merged, at, size)
            put(wall_ws[level], w, at, size)
    not_first, not_last = open_ends("normal")
    for v, keep in enumerate((not_first, None, None, not_last)):
        value = sources[-1][v]
        packed[pl.ds(v * lines, lines), :] = value if keep is None else value * keep


def wall_up(fields, span, cells, bits, *refs):
    own_matrix, other_matrix, down_in, outer_in, own, other, share_one, share_two = refs[0:8]
    refs = refs[8:]
    round_ups, round_ws, refs = refs[: bits + 1], refs[bits + 1 : 2 * bits + 1], refs[2 * bits + 1 :]
    chunk_up, chunk_w, ups, ws = refs[0], refs[1], refs[2:5], refs[5:8]
    update = refs[8]
    ends, result, sems = refs[9:13], refs[13], refs[14]
    lines = fields * span
    second, upper = is_second("normal", bits), is_second("normal", bits + 1)
    for at, size in blocks(lines, 8):
        down, factors = get(down_in, MERGE_DOWN, at, size), get(outer_in, 12, at, size)
        part, outer, w = reduce_source(
            down,
            factors,
            second,
            upper,
            flat(own, SOURCE, lines, at, size),
            flat(other, SOURCE, lines, at, size),
        )
        shares = plus(flat(share_one, 2, lines, at, size), flat(share_two, 2, lines, at, size))
        matrix = plus(
            flat(own_matrix, 4, lines, at, size), flat(other_matrix, 4, lines, at, size)
        )
        centre = apply(inverse(*matrix), plus(part, shares))
        outer = minus(outer, apply(factors[0:4], apply(factors[4:8], centre)))
        left, right = choose(upper, centre, outer), choose(upper, outer, centre)
        between = inner(get(round_ups[bits], UP, at, size), w, left, right)
        left, right = choose(second, between, left), choose(second, right, between)
        left, right = round_down(round_ups, round_ws, "normal", bits, at, size, left, right)
        put(ends[0], left + right, at, size)
    last = split_all(ends[0], ends[1:], ups, ws, levels_of(lines))
    size = span * CHUNKS
    length = size * cells
    started = []
    for field in range(fields):
        at = field * size

        def store(i, value):
            result[pl.ds(at * cells + i, size, stride=cells), :] = value

        back_substitute(last, chunk_up, chunk_w, cells, at, size, store)
        rows = pl.ds(field * length, length)
        copy = pltpu.make_async_copy(result.at[rows], update.at[rows], sems.at[field])
        copy.start()
        started.append(copy)
    for copy in started:
        copy.wait()


def f32(*shape):
    return jax.ShapeDtypeStruct(shape, jnp.float32)


def vmem(*shape):
    return pltpu.VMEM(shape, jnp.float32)


IN_VMEM = pl.BlockSpec(memory_space=pltpu.VMEM)
IN_HBM = pl.BlockSpec(memory_space=pltpu.HBM)
PARAMS = pltpu.CompilerParams(vmem_limit_bytes=24 * 2**20)


def kernel(name, body, ins, outs, scratch, flops):
    in_bytes = sum(a.size * a.dtype.itemsize for a, _ in ins)
    out_bytes = sum(a.size * 4 for a, _ in outs)
    outputs = pl.pallas_call(
        body,
        out_shape=[a for a, _ in outs],
        in_specs=[spec for _, spec in ins],
        out_specs=[spec for _, spec in outs],
        scratch_shapes=scratch,
        compiler_params=PARAMS,
        cost_estimate=pl.CostEstimate(
            flops=flops, bytes_accessed=in_bytes + out_bytes, transcendentals=0
        ),
        name=name,
    )(*[a for a, _ in ins])
    return list(outputs)


def inside(arrays):
    return [(a, IN_VMEM) for a in arrays]


def outside(arrays):
    return [(pltpu.with_memory_space_constraint(a, pltpu.HBM), IN_HBM) for a in arrays]


def exchange(array, axis, mask):
    count = lax.axis_size(axis)
    return lax.ppermute(array, axis, [(i ^ mask, i) for i in range(count)])


def local(residual, courant_xi, courant_eta, dissip_xi, dissip_eta, coupling):
    fields, span, high, wide = residual.shape
    lanes = span * high
    wrap_cells, wall_cells = wide // CHUNKS, high // CHUNKS
    wrap_pairs, wall_pairs = (wrap_cells - 2) // 2, (wall_cells - 2) // 2
    wrap_count, wall_count = lax.axis_size("wrap"), lax.axis_size("normal")
    lines = fields * span
    wrap_levels, wall_levels = levels_of(fields), levels_of(lines)
    wrap_rows, wall_rows = fields * CHUNKS, lines * CHUNKS

    def rows_of(array):
        return array.reshape(-1, wide)

    wrap_bits = wrap_count.bit_length() - 3
    wall_bits = wall_count.bit_length() - 3
    results = kernel(
        "wrap_down",
        functools.partial(wrap_down, fields, wrap_cells),
        outside(
            [rows_of(a) for a in (residual, courant_xi, dissip_xi, courant_eta, dissip_eta)]
        ),
        inside(
            [
                f32(VALUES * fields, lanes),
                f32(wrap_pairs * UP, wrap_rows, lanes),
                f32(wrap_pairs * 2, wrap_rows, lanes),
            ]
            + [f32(UP, n, lanes) for n in wrap_levels]
            + [f32(2, n, lanes) for n in wrap_levels]
            + [f32(fields * lanes, wide), f32(lanes, wide)]
        ),
        [vmem(fields * lanes, wide)] * 2
        + [vmem(lanes, wide)]
        + [vmem(fields * wide, lanes)] * 2
        + [vmem(wide, lanes)]
        + [vmem(VALUES, n, lanes) for n in [wrap_rows] + wrap_levels]
        + [pltpu.SemaphoreType.DMA((2 * fields + 3,))],
        100 * residual.size,
    )
    element, wrap_factors, wall_inputs = results[0], results[1:9], results[9:11]
    results = kernel(
        "wall_matrix",
        functools.partial(wall_matrix, fields, span, wall_cells),
        inside(wall_inputs) + outside([coupling.reshape(fields, fields, lanes, wide)]),
        inside(
            [
                f32(MATRIX * lines, wide),
                f32(wall_pairs * 2, span * CHUNKS, wide),
                f32(wall_pairs * UP, wall_rows, wide),
                f32(wall_pairs * CHUNK_DOWN, wall_rows, wide),
            ]
            + [f32(UP, n, wide) for n in wall_levels]
            + [f32(MERGE_DOWN, n, wide) for n in wall_levels]
            + [jax.ShapeDtypeStruct((fields, fields, lanes, wide), coupling.dtype)]
        ),
        [vmem(MATRIX, n, wide) for n in [wall_rows] + wall_levels]
        + [pltpu.SemaphoreType.DMA((fields,))],
        100 * residual.size,
    )
    matrix, damps, chunk_up, chunk_down = results[0:4]
    wall_ups, wall_downs, coupling_in = results[4:7], results[7:10], results[10]
    wrap_ups, wrap_ws = [], []
    for bit in range(wrap_bits):
        element, up, w = kernel(
            f"wrap_round_{bit}",
            functools.partial(wrap_round, fields, bit),
            inside([element, exchange(element, "wrap", 1 << bit), damps]),
            inside([f32(VALUES * fields, lanes), f32(UP, fields, lanes), f32(2, fields, lanes)]),
            [],
            200 * fields * lanes,
        )
        wrap_ups.append(up)
        wrap_ws.append(w)
    wrap_others = [exchange(element, "wrap", mask << wrap_bits) for mask in (1, 2, 3)]
    round_ups, round_downs = [], []
    for bit in range(wall_bits + 1):
        final = bit == wall_bits
        matrix, up, down, *outer = kernel(
            f"wall_round_{bit}",
            functools.partial(wall_round, lines, bit, final),
            inside([matrix, exchange(matrix, "normal", 1 << bit)]),
            inside(
                [
                    f32((4 if final else MATRIX) * lines, wide),
                    f32(UP, lines, wide),
                    f32(MERGE_DOWN, lines, wide),
                ]
                + ([f32(12, lines, wide)] if final else [])
            ),
            [],
            200 * lines * wide,
        )
        round_ups.append(up)
        round_downs.append(down)
    matrix_other = exchange(matrix, "normal", 2 << wall_bits)
    source, *wall_ws = kernel(
        "middle",
        functools.partial(middle, fields, span, wrap_cells, wall_cells, wrap_bits),
        inside(
            [element]
            + wrap_others
            + wrap_ups
            + wrap_ws
            + wrap_factors
            + [coupling_in, damps, chunk_down]
            + wall_downs
        ),
        inside(
            [f32(SOURCE * lines, wide), f32(wall_pairs * 2, wall_rows, wide)]
            + [f32(2, n, wide) for n in wall_levels]
        ),
        [vmem(4, n, lanes) for n in reversed([wrap_rows] + wrap_levels)]
        + [vmem(fields * wide, lanes), vmem(fields * lanes, wide), vmem(fields * lanes, wide)]
        + [vmem(SOURCE, n, wide) for n in [wall_rows] + wall_levels],
        100 * residual.size,
    )
    round_ws = []
    for bit in range(wall_bits):
        source, w = kernel(
            f"wall_source_round_{bit}",
            functools.partial(wall_source_round, lines, bit),
            inside([source, exchange(source, "normal", 1 << bit), round_downs[bit]]),
            inside([f32(SOURCE * lines, wide), f32(2, lines, wide)]),
            [],
            50 * lines * wide,
        )
        round_ws.append(w)
    (share,) = kernel(
        "wall_share",
        functools.partial(wall_share, lines, wall_bits),
        inside([source, round_downs[wall_bits]] + outer),
        inside([f32(2 * lines, wide)]),
        [],
        50 * lines * wide,
    )
    (update,) = kernel(
        "wall_up",
        functools.partial(wall_up, fields, span, wall_cells, wall_bits),
        inside(
            [matrix, matrix_other, round_downs[wall_bits]]
            + outer
            + [source, exchange(source, "normal", 1 << wall_bits)]
            + [exchange(share, "normal", mask << wall_bits) for mask in (2, 3)]
            + round_ups
            + round_ws
            + [chunk_up, wall_ws[0]]
            + wall_ups
            + wall_ws[1:]
        ),
        [(f32(fields * lanes, wide), IN_HBM)],
        [vmem(4, n, wide) for n in reversed([wall_rows] + wall_levels)]
        + [vmem(fields * lanes, wide), pltpu.SemaphoreType.DMA((fields,))],
        30 * residual.size,
    )
    return update.reshape(residual.shape)


def solution(mesh):
    placed = (
        P(None, None, "normal", "wrap"),
        P(None, None, "normal", "wrap"),
        P(None, None, "normal", "wrap"),
        P(None, "normal", "wrap"),
        P(None, "normal", "wrap"),
        P(None, None, None, "normal", "wrap"),
    )
    return jax.shard_map(
        local,
        mesh=mesh,
        in_specs=placed,
        out_specs=P(None, None, "normal", "wrap"),
        check_vma=False,
    )
```

```python
import functools

import jax
import jax.numpy as jnp
from jax import lax
from jax.experimental import pallas as pl
from jax.experimental.pallas import tpu as pltpu
from jax.sharding import PartitionSpec as P

MATRIX = 16
SOURCE = 4
VALUES = MATRIX + SOURCE
UP = 8
CHUNK_DOWN = 9
MERGE_DOWN = 12
CHUNKS = 8


def inverse(a, b, c, d):
    scale = 1.0 / (a * d - b * c)
    return (d * scale, -b * scale, -c * scale, a * scale)


def times(x, y):
    return (
        x[0] * y[0] + x[1] * y[2],
        x[0] * y[1] + x[1] * y[3],
        x[2] * y[0] + x[3] * y[2],
        x[2] * y[1] + x[3] * y[3],
    )


def apply(x, v):
    return (x[0] * v[0] + x[1] * v[1], x[2] * v[0] + x[3] * v[1])


def minus(x, y):
    return tuple(a - b for a, b in zip(x, y))


def plus(x, y):
    return tuple(a + b for a, b in zip(x, y))


def negative(x):
    return tuple(-a for a in x)


def quads(element):
    return (element[0:4], element[4:8], element[8:12], element[12:16])


def merge_matrix(first, second):
    ll, lm, ml, mm = quads(first)
    nn, mr, rm, rr = quads(second)
    pivot = inverse(*plus(mm, nn))
    wl = times(pivot, ml)
    wr = times(pivot, mr)
    merged = (
        minus(ll, times(lm, wl))
        + negative(times(lm, wr))
        + negative(times(rm, wl))
        + minus(rr, times(rm, wr))
    )
    return merged, wl + wr, pivot + lm + rm


def merge_source(down, first, second):
    pivot, lm, rm = down[0:4], down[4:8], down[8:12]
    w = apply(pivot, plus(first[2:4], second[0:2]))
    return minus(first[0:2], apply(lm, w)) + minus(second[2:4], apply(rm, w)), w


def merge(first, second):
    matrix, up, down = merge_matrix(first[:MATRIX], second[:MATRIX])
    source, w = merge_source(down, first[MATRIX:], second[MATRIX:])
    return matrix + source, up, w


def inner(up, w, left, right):
    return minus(minus(w, apply(up[0:4], left)), apply(up[4:8], right))


def chunk_matrix(speed, damp, cells):
    def link(i):
        p = 2.0 * (damp(i) + damp(i + 1))
        q = 0.25 * (speed(i) + speed(i + 1))
        return q - p, -q - p

    def centre(i):
        return 1.0 + damp(i - 1) + 4.0 * damp(i) + damp(i + 1)

    b0, b1 = damp(0), damp(1)
    quarter = 0.25 * speed(0)
    up, low = link(0)
    zero = jnp.zeros_like(b0)
    ll = (b0, quarter - 2.0 * b0, -quarter - 2.0 * b0, 1.0 + 4.0 * b0 + b1)
    lk = (b0, zero, up, b1)
    kl = (b0, low, zero, b1)
    up, low = link(1)
    kk = (centre(1), up, low, centre(2))
    pairs = (cells - 2) // 2
    for k in range(1, pairs + 1):
        i = 2 * k
        pivot = inverse(*kk)
        wl = times(pivot, kl)
        up, low = link(i)
        here, there = damp(i), damp(i + 1)
        wr = (
            pivot[0] * here + pivot[1] * up,
            pivot[1] * there,
            pivot[2] * here + pivot[3] * up,
            pivot[3] * there,
        )
        yield wl + wr, pivot + lk + (low,), (here, there)

        def below(x):
            return (
                here * x[0] + low * x[2],
                here * x[1] + low * x[3],
                there * x[2],
                there * x[3],
            )

        ll = minus(ll, times(lk, wl))
        lk = negative(times(lk, wr))
        kl = negative(below(wl))
        if k < pairs:
            up, low_next = link(i + 1)
            kk = (centre(i + 1), up, low_next, centre(i + 2))
        else:
            quarter = 0.25 * speed(i + 1)
            kk = (
                1.0 + here + 4.0 * there,
                quarter - 2.0 * there,
                -quarter - 2.0 * there,
                there,
            )
        kk = minus(kk, below(wr))
    yield ll + lk + kl + kk


def pair_source(down, damps, left, pair, following):
    pivot, lk, low = down[0:4], down[4:8], down[8]
    w = apply(pivot, pair)
    left = minus(left, apply(lk, w))
    following = minus(following, (damps[0] * w[0] + low * w[1], damps[1] * w[1]))
    return left, following, w


def pair_of(source, k, cells):
    if k == (cells - 2) // 2:
        last = source(cells - 1)
        return (last, jnp.zeros_like(last))
    return (source(2 * k + 1), source(2 * k + 2))


def first_pair(source):
    first = source(0)
    return (jnp.zeros_like(first), first)


def blocks(rows, size):
    return [(at, min(size, rows - at)) for at in range(0, rows, size)]


def get(ref, count, at, size, base=0):
    return tuple(ref[base + v, pl.ds(at, size), :] for v in range(count))


def put(ref, values, at, size, base=0):
    for v, value in enumerate(values):
        ref[base + v, pl.ds(at, size), :] = value


def get_both(ref, count, at, size):
    return tuple(
        tuple(ref[v, pl.ds(2 * at + half, size, stride=2), :] for v in range(count))
        for half in (0, 1)
    )


def levels_of(lines):
    sizes = []
    rows = lines * CHUNKS
    while rows > lines:
        rows //= 2
        sizes.append(rows)
    return sizes


def split_all(top_ref, end_refs, up_refs, w_refs, sizes):
    source = top_ref
    for rows, target, ups, ws in zip(
        reversed(sizes), end_refs, reversed(up_refs), reversed(w_refs)
    ):
        for at, size in blocks(rows, 8):
            ends = get(source, 4, at, size)
            left, right = ends[0:2], ends[2:4]
            middle = inner(get(ups, UP, at, size), get(ws, 2, at, size), left, right)
            for v in range(2):
                target[v, pl.ds(2 * at, size, stride=2), :] = left[v]
                target[v, pl.ds(2 * at + 1, size, stride=2), :] = middle[v]
                target[2 + v, pl.ds(2 * at, size, stride=2), :] = middle[v]
                target[2 + v, pl.ds(2 * at + 1, size, stride=2), :] = right[v]
        source = target
    return source


def back_substitute(ends_ref, up_ref, w_ref, cells, at, size, store):
    ends = get(ends_ref, 4, at, size)
    left, following = ends[0:2], ends[2:4]
    store(0, left[1])
    store(cells - 1, following[0])
    for k in range((cells - 2) // 2 - 1, -1, -1):
        following = inner(
            get(up_ref, UP, at, size, k * UP), get(w_ref, 2, at, size, k * 2), left, following
        )
        store(2 * k + 1, following[0])
        store(2 * k + 2, following[1])


def close_ring(own, rest):
    ll, lr, rl, rr = quads(own)
    nn, nm, mn, mm = quads(rest)
    b = plus(lr, mn)
    c = plus(rl, nm)
    pivot = inverse(*plus(rr, nn))
    f = plus(own[16:18], rest[18:20])
    g = plus(own[18:20], rest[16:18])
    bd = times(b, pivot)
    left = apply(inverse(*minus(plus(ll, mm), times(bd, c))), minus(f, apply(bd, g)))
    right = apply(pivot, minus(g, apply(c, left)))
    return left, right


def open_ends(axis):
    place = lax.axis_index(axis)
    last = lax.axis_size(axis) - 1
    return jnp.where(place > 0, 1.0, 0.0), jnp.where(place < last, 1.0, 0.0)


def is_second(axis, bit):
    return lax.rem(lax.axis_index(axis) // (1 << bit), 2) == 1


def choose(second, one, other):
    return tuple(jnp.where(second, a, b) for a, b in zip(one, other))


def flat(ref, count, rows, at, size):
    return tuple(ref[pl.ds(v * rows + at, size), :] for v in range(count))


def put_flat(ref, values, rows, at, size):
    for v, value in enumerate(values):
        ref[pl.ds(v * rows + at, size), :] = value


def round_down(ups, ws, axis, bits, at, size, left, right):
    for bit in reversed(range(bits)):
        middle = inner(get(ups[bit], UP, at, size), get(ws[bit], 2, at, size), left, right)
        second = is_second(axis, bit)
        left, right = choose(second, middle, left), choose(second, right, middle)
    return left, right


def copies(pairs, sems, first=0):
    started = []
    for i, (source, target) in enumerate(pairs):
        copy = pltpu.make_async_copy(source, target, sems.at[first + i])
        copy.start()
        started.append(copy)
    return started


def wrap_down(fields, cells, *refs):
    residual, courant, dissip, wall_courant, wall_dissip = refs[0:5]
    packed, chunk_up, chunk_w = refs[5:8]
    ups, ws = refs[8:11], refs[11:14]
    wall_speed, wall_damp = refs[14:16]
    source_in, speed_in, damp_in, source_t, speed_t, damp_t = refs[16:22]
    elements, sems = refs[22:26], refs[26]
    lanes = damp_in.shape[0]
    length = cells * CHUNKS
    moves = [(dissip, damp_in)]
    for field in range(fields):
        rows = pl.ds(field * lanes, lanes)
        moves.append((courant.at[rows], speed_in.at[rows]))
        moves.append((residual.at[rows], source_in.at[rows]))
    started = copies(moves, sems)
    started[0].wait()
    damp_t[...] = damp_in[...].T

    def turn(field):
        started[1 + 2 * field].wait()
        speed_t[pl.ds(field * length, length), :] = speed_in[pl.ds(field * lanes, lanes), :].T
        started[2 + 2 * field].wait()
        source_t[pl.ds(field * length, length), :] = source_in[pl.ds(field * lanes, lanes), :].T

    for at, size in blocks(fields * CHUNKS, 16):
        repeat = size // CHUNKS
        for field in range(at // CHUNKS, at // CHUNKS + repeat):
            turn(field)
        if at == 0:
            moves = [(wall_dissip, wall_damp), (wall_courant, wall_speed)]
            started += copies(moves, sems, len(started))

        def speed(i):
            return speed_t[pl.ds(at * cells + i, size, stride=cells), :]

        def source(i):
            return source_t[pl.ds(at * cells + i, size, stride=cells), :]

        def damp(i):
            rows = damp_t[pl.ds(i, CHUNKS, stride=cells), :]
            return jnp.concatenate([rows] * repeat, axis=0) if repeat > 1 else rows

        left, pair = first_pair(source), pair_of(source, 0, cells)
        for k, step in enumerate(chunk_matrix(speed, damp, cells)):
            if k == (cells - 2) // 2:
                put(elements[0], step + left + pair, at, size)
                break
            up, down, damps = step
            left, pair, w = pair_source(down, damps, left, pair, pair_of(source, k + 1, cells))
            put(chunk_up, up, at, size, k * UP)
            put(chunk_w, w, at, size, k * 2)
    for level, rows in enumerate(levels_of(fields)):
        for at, size in blocks(rows, 8):
            merged, up, w = merge(*get_both(elements[level], VALUES, at, size))
            put(elements[level + 1], merged, at, size)
            put(ups[level], up, at, size)
            put(ws[level], w, at, size)
    for v in range(VALUES):
        packed[pl.ds(v * fields, fields), :] = elements[-1][v]
    started[-2].wait()
    started[-1].wait()


def wrap_round(fields, bit, own, other, after, packed, up_out, w_out):
    second = is_second("wrap", bit)
    for at, size in blocks(fields, 8):
        mine = flat(own, VALUES, fields, at, size)
        theirs = flat(other, VALUES, fields, at, size)
        merged, up, w = merge(choose(second, theirs, mine), choose(second, mine, theirs))
        put_flat(packed, merged, fields, at, size)
        put(up_out, up, at, size)
        put(w_out, w, at, size)


def wall_matrix(fields, span, cells, *refs):
    speed_in, damp_in = refs[0:2]
    packed, damp_out, chunk_up, chunk_down = refs[2:6]
    ups, downs = refs[6:9], refs[9:12]
    elements = refs[12:16]
    size = span * CHUNKS
    for field in range(fields):
        at = field * size

        def speed(i):
            return speed_in[pl.ds(at * cells + i, size, stride=cells), :]

        def damp(i):
            return damp_in[pl.ds(i, size, stride=cells), :]

        for k, step in enumerate(chunk_matrix(speed, damp, cells)):
            if k == (cells - 2) // 2:
                put(elements[0], step, at, size)
                break
            up, down, damps = step
            put(chunk_up, up, at, size, k * UP)
            put(chunk_down, down, at, size, k * CHUNK_DOWN)
            if field == 0:
                put(damp_out, damps, 0, size, k * 2)
    lines = fields * span
    for level, rows in enumerate(levels_of(lines)):
        for at, size in blocks(rows, 8):
            merged, up, down = merge_matrix(*get_both(elements[level], MATRIX, at, size))
            put(elements[level + 1], merged, at, size)
            put(ups[level], up, at, size)
            put(downs[level], down, at, size)
    not_first, not_last = open_ends("normal")
    for v in range(MATRIX):
        value = elements[-1][v]
        if v in (0, 1, 2, 4, 5, 8, 10):
            value = value * not_first
        if v in (5, 7, 10, 11, 13, 14, 15):
            value = value * not_last
        packed[pl.ds(v * lines, lines), :] = value


def wall_round(lines, bit, final, own, other, packed, up_out, down_out, *outer_out):
    second = is_second("normal", bit)
    upper = is_second("normal", bit + 1)
    for at, size in blocks(lines, 8):
        mine = flat(own, MATRIX, lines, at, size)
        theirs = flat(other, MATRIX, lines, at, size)
        merged, up, down = merge_matrix(
            choose(second, theirs, mine), choose(second, mine, theirs)
        )
        put(up_out, up, at, size)
        put(down_out, down, at, size)
        if not final:
            put_flat(packed, merged, lines, at, size)
            continue
        ll, lr, rl, rr = quads(merged)
        outer, into = choose(upper, rr, ll), choose(upper, rl, lr)
        out, middle = choose(upper, lr, rl), choose(upper, ll, rr)
        is_upper = jnp.where(upper, 1.0, 0.0)
        pivot = inverse(
            outer[0] + (1.0 - is_upper), outer[1], outer[2], outer[3] + is_upper
        )
        put_flat(packed, minus(middle, times(out, times(pivot, into))), lines, at, size)
        put(outer_out[0], pivot + into + out, at, size)


def wall_source_round(lines, bit, own, other, down_in, packed, w_out):
    second = is_second("normal", bit)
    for at, size in blocks(lines, 8):
        mine = flat(own, SOURCE, lines, at, size)
        theirs = flat(other, SOURCE, lines, at, size)
        merged, w = merge_source(
            get(down_in, MERGE_DOWN, at, size),
            choose(second, theirs, mine),
            choose(second, mine, theirs),
        )
        put_flat(packed, merged, lines, at, size)
        put(w_out, w, at, size)


def reduce_source(down, factors, second, upper, mine, theirs):
    merged, w = merge_source(
        down, choose(second, theirs, mine), choose(second, mine, theirs)
    )
    outer = apply(factors[0:4], choose(upper, merged[2:4], merged[0:2]))
    centre = choose(upper, merged[0:2], merged[2:4])
    return minus(centre, apply(factors[8:12], outer)), outer, w


def wall_share(lines, bit, own, down_in, outer_in, share):
    second, upper = is_second("normal", bit), is_second("normal", bit + 1)
    for at, size in blocks(lines, 8):
        mine = flat(own, SOURCE, lines, at, size)
        none = tuple(jnp.zeros_like(value) for value in mine)
        down, factors = get(down_in, MERGE_DOWN, at, size), get(outer_in, 12, at, size)
        part, _, _ = reduce_source(down, factors, second, upper, mine, none)
        put_flat(share, part, lines, at, size)


def middle(fields, span, wrap_cells, wall_cells, bits, *refs):
    own, others, refs = refs[0], refs[1:4], refs[4:]
    round_ups, round_ws, refs = refs[:bits], refs[bits : 2 * bits], refs[2 * bits :]
    chunk_up, chunk_w, ups, ws = refs[0], refs[1], refs[2:5], refs[5:8]
    coupling, damps_in, chunk_down, downs = refs[8], refs[9], refs[10], refs[11:14]
    packed, wall_w, wall_ws = refs[14], refs[15], refs[16:19]
    ends, solved_t, solved, mixed = refs[19:23], refs[23], refs[24], refs[25]
    sources = refs[26:30]

    for at, size in blocks(fields, 8):
        odd = is_second("wrap", bits)
        far, opposite, near = (flat(other, VALUES, fields, at, size) for other in others)
        following, before = choose(odd, far, near), choose(odd, near, far)
        rest = merge(merge(following, opposite)[0], before)[0]
        left, right = close_ring(flat(own, VALUES, fields, at, size), rest)
        left, right = round_down(round_ups, round_ws, "wrap", bits, at, size, left, right)
        put(ends[0], left + right, at, size)
    last = split_all(ends[0], ends[1:], ups, ws, levels_of(fields))
    length = wrap_cells * CHUNKS
    for at, size in blocks(fields * CHUNKS, 16):

        def store(i, value):
            solved_t[pl.ds(at * wrap_cells + i, size, stride=wrap_cells), :] = value

        back_substitute(last, chunk_up, chunk_w, wrap_cells, at, size, store)
    lanes = solved.shape[0] // fields
    for field in range(fields):
        solved[pl.ds(field * lanes, lanes), :] = solved_t[pl.ds(field * length, length), :].T

    for at, size in blocks(lanes, 16):
        update = [solved[pl.ds(j * lanes + at, size), :] for j in range(fields)]
        for k in range(fields):
            total = coupling[k, 0, pl.ds(at, size), :].astype(jnp.float32) * update[0]
            for j in range(1, fields):
                total = total + coupling[k, j, pl.ds(at, size), :].astype(jnp.float32) * update[j]
            mixed[pl.ds(k * lanes + at, size), :] = total

    pairs = (wall_cells - 2) // 2
    size = span * CHUNKS
    for field in range(fields):
        at = field * size

        def source(i):
            return mixed[pl.ds(at * wall_cells + i, size, stride=wall_cells), :]

        left, pair = first_pair(source), pair_of(source, 0, wall_cells)
        for k in range(pairs):
            left, pair, w = pair_source(
                get(chunk_down, CHUNK_DOWN, at, size, k * CHUNK_DOWN),
                get(damps_in, 2, 0, size, k * 2),
                left,
                pair,
                pair_of(source, k + 1, wall_cells),
            )
            put(wall_w, w, at, size, k * 2)
        put(sources[0], left + pair, at, size)
    lines = fields * span
    for level, rows in enumerate(levels_of(lines)):
        for at, size in blocks(rows, 8):
            down = get(downs[level], MERGE_DOWN, at, size)
            merged, w = merge_source(down, *get_both(sources[level], SOURCE, at, size))
            put(sources[level + 1], merged, at, size)
            put(wall_ws[level], w, at, size)
    not_first, not_last = open_ends("normal")
    for v, keep in enumerate((not_first, None, None, not_last)):
        value = sources[-1][v]
        packed[pl.ds(v * lines, lines), :] = value if keep is None else value * keep


def wall_up(fields, span, cells, bits, *refs):
    own_matrix, other_matrix, down_in, outer_in, own, other, share_one, share_two = refs[0:8]
    refs = refs[8:]
    round_ups, round_ws, refs = refs[: bits + 1], refs[bits + 1 : 2 * bits + 1], refs[2 * bits + 1 :]
    chunk_up, chunk_w, ups, ws = refs[0], refs[1], refs[2:5], refs[5:8]
    update = refs[8]
    ends, result, sems = refs[9:13], refs[13], refs[14]
    lines = fields * span
    second, upper = is_second("normal", bits), is_second("normal", bits + 1)
    for at, size in blocks(lines, 8):
        down, factors = get(down_in, MERGE_DOWN, at, size), get(outer_in, 12, at, size)
        part, outer, w = reduce_source(
            down,
            factors,
            second,
            upper,
            flat(own, SOURCE, lines, at, size),
            flat(other, SOURCE, lines, at, size),
        )
        shares = plus(flat(share_one, 2, lines, at, size), flat(share_two, 2, lines, at, size))
        matrix = plus(
            flat(own_matrix, 4, lines, at, size), flat(other_matrix, 4, lines, at, size)
        )
        centre = apply(inverse(*matrix), plus(part, shares))
        outer = minus(outer, apply(factors[0:4], apply(factors[4:8], centre)))
        left, right = choose(upper, centre, outer), choose(upper, outer, centre)
        between = inner(get(round_ups[bits], UP, at, size), w, left, right)
        left, right = choose(second, between, left), choose(second, right, between)
        left, right = round_down(round_ups, round_ws, "normal", bits, at, size, left, right)
        put(ends[0], left + right, at, size)
    last = split_all(ends[0], ends[1:], ups, ws, levels_of(lines))
    size = span * CHUNKS
    length = size * cells
    started = []
    for field in range(fields):
        at = field * size

        def store(i, value):
            result[pl.ds(at * cells + i, size, stride=cells), :] = value

        back_substitute(last, chunk_up, chunk_w, cells, at, size, store)
        rows = pl.ds(field * length, length)
        copy = pltpu.make_async_copy(result.at[rows], update.at[rows], sems.at[field])
        copy.start()
        started.append(copy)
    for copy in started:
        copy.wait()


def f32(*shape):
    return jax.ShapeDtypeStruct(shape, jnp.float32)


def vmem(*shape):
    return pltpu.VMEM(shape, jnp.float32)


IN_VMEM = pl.BlockSpec(memory_space=pltpu.VMEM)
IN_HBM = pl.BlockSpec(memory_space=pltpu.HBM)
PARAMS = pltpu.CompilerParams(vmem_limit_bytes=24 * 2**20)


def kernel(name, body, ins, outs, scratch, flops):
    in_bytes = sum(a.size * a.dtype.itemsize for a, _ in ins)
    out_bytes = sum(a.size * 4 for a, _ in outs)
    outputs = pl.pallas_call(
        body,
        out_shape=[a for a, _ in outs],
        in_specs=[spec for _, spec in ins],
        out_specs=[spec for _, spec in outs],
        scratch_shapes=scratch,
        compiler_params=PARAMS,
        cost_estimate=pl.CostEstimate(
            flops=flops, bytes_accessed=in_bytes + out_bytes, transcendentals=0
        ),
        name=name,
    )(*[a for a, _ in ins])
    return list(outputs)


def inside(arrays):
    return [(a, IN_VMEM) for a in arrays]


def outside(arrays):
    return [(pltpu.with_memory_space_constraint(a, pltpu.HBM), IN_HBM) for a in arrays]


def exchange(array, axis, mask):
    count = lax.axis_size(axis)
    return lax.ppermute(array, axis, [(i ^ mask, i) for i in range(count)])


def local(residual, courant_xi, courant_eta, dissip_xi, dissip_eta, coupling):
    fields, span, high, wide = residual.shape
    lanes = span * high
    wrap_cells, wall_cells = wide // CHUNKS, high // CHUNKS
    wrap_pairs, wall_pairs = (wrap_cells - 2) // 2, (wall_cells - 2) // 2
    wrap_count, wall_count = lax.axis_size("wrap"), lax.axis_size("normal")
    lines = fields * span
    wrap_levels, wall_levels = levels_of(fields), levels_of(lines)
    wrap_rows, wall_rows = fields * CHUNKS, lines * CHUNKS

    def rows_of(array):
        return array.reshape(-1, wide)

    wrap_bits = wrap_count.bit_length() - 3
    wall_bits = wall_count.bit_length() - 3
    results = kernel(
        "wrap_down",
        functools.partial(wrap_down, fields, wrap_cells),
        outside(
            [rows_of(a) for a in (residual, courant_xi, dissip_xi, courant_eta, dissip_eta)]
        ),
        inside(
            [
                f32(VALUES * fields, lanes),
                f32(wrap_pairs * UP, wrap_rows, lanes),
                f32(wrap_pairs * 2, wrap_rows, lanes),
            ]
            + [f32(UP, n, lanes) for n in wrap_levels]
            + [f32(2, n, lanes) for n in wrap_levels]
            + [f32(fields * lanes, wide), f32(lanes, wide)]
        ),
        [vmem(fields * lanes, wide)] * 2
        + [vmem(lanes, wide)]
        + [vmem(fields * wide, lanes)] * 2
        + [vmem(wide, lanes)]
        + [vmem(VALUES, n, lanes) for n in [wrap_rows] + wrap_levels]
        + [pltpu.SemaphoreType.DMA((2 * fields + 3,))],
        100 * residual.size,
    )
    element, wrap_factors, wall_inputs = results[0], results[1:9], results[9:11]
    results = kernel(
        "wall_matrix",
        functools.partial(wall_matrix, fields, span, wall_cells),
        inside(wall_inputs),
        inside(
            [
                f32(MATRIX * lines, wide),
                f32(wall_pairs * 2, span * CHUNKS, wide),
                f32(wall_pairs * UP, wall_rows, wide),
                f32(wall_pairs * CHUNK_DOWN, wall_rows, wide),
            ]
            + [f32(UP, n, wide) for n in wall_levels]
            + [f32(MERGE_DOWN, n, wide) for n in wall_levels]
        ),
        [vmem(MATRIX, n, wide) for n in [wall_rows] + wall_levels],
        100 * residual.size,
    )
    matrix, damps, chunk_up, chunk_down = results[0:4]
    wall_ups, wall_downs = results[4:7], results[7:10]
    wrap_ups, wrap_ws = [], []
    for bit in range(wrap_bits):
        element, up, w = kernel(
            f"wrap_round_{bit}",
            functools.partial(wrap_round, fields, bit),
            inside([element, exchange(element, "wrap", 1 << bit), damps]),
            inside([f32(VALUES * fields, lanes), f32(UP, fields, lanes), f32(2, fields, lanes)]),
            [],
            200 * fields * lanes,
        )
        wrap_ups.append(up)
        wrap_ws.append(w)
    wrap_others = [exchange(element, "wrap", mask << wrap_bits) for mask in (3, 2, 1)]
    round_ups, round_downs = [], []
    for bit in range(wall_bits + 1):
        final = bit == wall_bits
        matrix, up, down, *outer = kernel(
            f"wall_round_{bit}",
            functools.partial(wall_round, lines, bit, final),
            inside([matrix, exchange(matrix, "normal", 1 << bit)]),
            inside(
                [
                    f32((4 if final else MATRIX) * lines, wide),
                    f32(UP, lines, wide),
                    f32(MERGE_DOWN, lines, wide),
                ]
                + ([f32(12, lines, wide)] if final else [])
            ),
            [],
            200 * lines * wide,
        )
        round_ups.append(up)
        round_downs.append(down)
    matrix_other = exchange(matrix, "normal", 2 << wall_bits)
    source, *wall_ws = kernel(
        "middle",
        functools.partial(middle, fields, span, wrap_cells, wall_cells, wrap_bits),
        inside(
            [element]
            + wrap_others
            + wrap_ups
            + wrap_ws
            + wrap_factors
            + [coupling.reshape(fields, fields, lanes, wide), damps, chunk_down]
            + wall_downs
        ),
        inside(
            [f32(SOURCE * lines, wide), f32(wall_pairs * 2, wall_rows, wide)]
            + [f32(2, n, wide) for n in wall_levels]
        ),
        [vmem(4, n, lanes) for n in reversed([wrap_rows] + wrap_levels)]
        + [vmem(fields * wide, lanes), vmem(fields * lanes, wide), vmem(fields * lanes, wide)]
        + [vmem(SOURCE, n, wide) for n in [wall_rows] + wall_levels],
        100 * residual.size,
    )
    round_ws = []
    for bit in range(wall_bits):
        source, w = kernel(
            f"wall_source_round_{bit}",
            functools.partial(wall_source_round, lines, bit),
            inside([source, exchange(source, "normal", 1 << bit), round_downs[bit]]),
            inside([f32(SOURCE * lines, wide), f32(2, lines, wide)]),
            [],
            50 * lines * wide,
        )
        round_ws.append(w)
    (share,) = kernel(
        "wall_share",
        functools.partial(wall_share, lines, wall_bits),
        inside([source, round_downs[wall_bits]] + outer),
        inside([f32(2 * lines, wide)]),
        [],
        50 * lines * wide,
    )
    (update,) = kernel(
        "wall_up",
        functools.partial(wall_up, fields, span, wall_cells, wall_bits),
        inside(
            [matrix, matrix_other, round_downs[wall_bits]]
            + outer
            + [source, exchange(source, "normal", 1 << wall_bits)]
            + [exchange(share, "normal", mask << wall_bits) for mask in (3, 2)]
            + round_ups
            + round_ws
            + [chunk_up, wall_ws[0]]
            + wall_ups
            + wall_ws[1:]
        ),
        [(f32(fields * lanes, wide), IN_HBM)],
        [vmem(4, n, wide) for n in reversed([wall_rows] + wall_levels)]
        + [vmem(fields * lanes, wide), pltpu.SemaphoreType.DMA((fields,))],
        30 * residual.size,
    )
    return update.reshape(residual.shape)


def solution(mesh):
    placed = (
        P(None, None, "normal", "wrap"),
        P(None, None, "normal", "wrap"),
        P(None, None, "normal", "wrap"),
        P(None, "normal", "wrap"),
        P(None, "normal", "wrap"),
        P(None, None, None, "normal", "wrap"),
    )
    return jax.shard_map(
        local,
        mesh=mesh,
        in_specs=placed,
        out_specs=P(None, None, "normal", "wrap"),
        check_vma=False,
    )
```

```python
import functools

import jax
import jax.numpy as jnp
from jax import lax
from jax.experimental import pallas as pl
from jax.experimental.pallas import tpu as pltpu
from jax.sharding import PartitionSpec as P

MATRIX = 16
SOURCE = 4
VALUES = MATRIX + SOURCE
UP = 8
CHUNK_DOWN = 9
MERGE_DOWN = 12
CHUNKS = 8


def inverse(a, b, c, d):
    scale = 1.0 / (a * d - b * c)
    return (d * scale, -b * scale, -c * scale, a * scale)


def times(x, y):
    return (
        x[0] * y[0] + x[1] * y[2],
        x[0] * y[1] + x[1] * y[3],
        x[2] * y[0] + x[3] * y[2],
        x[2] * y[1] + x[3] * y[3],
    )


def apply(x, v):
    return (x[0] * v[0] + x[1] * v[1], x[2] * v[0] + x[3] * v[1])


def minus(x, y):
    return tuple(a - b for a, b in zip(x, y))


def plus(x, y):
    return tuple(a + b for a, b in zip(x, y))


def negative(x):
    return tuple(-a for a in x)


def quads(element):
    return (element[0:4], element[4:8], element[8:12], element[12:16])


def merge_matrix(first, second):
    ll, lm, ml, mm = quads(first)
    nn, mr, rm, rr = quads(second)
    pivot = inverse(*plus(mm, nn))
    wl = times(pivot, ml)
    wr = times(pivot, mr)
    merged = (
        minus(ll, times(lm, wl))
        + negative(times(lm, wr))
        + negative(times(rm, wl))
        + minus(rr, times(rm, wr))
    )
    return merged, wl + wr, pivot + lm + rm


def merge_source(down, first, second):
    pivot, lm, rm = down[0:4], down[4:8], down[8:12]
    w = apply(pivot, plus(first[2:4], second[0:2]))
    return minus(first[0:2], apply(lm, w)) + minus(second[2:4], apply(rm, w)), w


def merge(first, second):
    matrix, up, down = merge_matrix(first[:MATRIX], second[:MATRIX])
    source, w = merge_source(down, first[MATRIX:], second[MATRIX:])
    return matrix + source, up, w


def inner(up, w, left, right):
    return minus(minus(w, apply(up[0:4], left)), apply(up[4:8], right))


def chunk_matrix(speed, damp, cells):
    def link(i):
        p = 2.0 * (damp(i) + damp(i + 1))
        q = 0.25 * (speed(i) + speed(i + 1))
        return q - p, -q - p

    def centre(i):
        return 1.0 + damp(i - 1) + 4.0 * damp(i) + damp(i + 1)

    b0, b1 = damp(0), damp(1)
    quarter = 0.25 * speed(0)
    up, low = link(0)
    zero = jnp.zeros_like(b0)
    ll = (b0, quarter - 2.0 * b0, -quarter - 2.0 * b0, 1.0 + 4.0 * b0 + b1)
    lk = (b0, zero, up, b1)
    kl = (b0, low, zero, b1)
    up, low = link(1)
    kk = (centre(1), up, low, centre(2))
    pairs = (cells - 2) // 2
    for k in range(1, pairs + 1):
        i = 2 * k
        pivot = inverse(*kk)
        wl = times(pivot, kl)
        up, low = link(i)
        here, there = damp(i), damp(i + 1)
        wr = (
            pivot[0] * here + pivot[1] * up,
            pivot[1] * there,
            pivot[2] * here + pivot[3] * up,
            pivot[3] * there,
        )
        yield wl + wr, pivot + lk + (low,), (here, there)

        def below(x):
            return (
                here * x[0] + low * x[2],
                here * x[1] + low * x[3],
                there * x[2],
                there * x[3],
            )

        ll = minus(ll, times(lk, wl))
        lk = negative(times(lk, wr))
        kl = negative(below(wl))
        if k < pairs:
            up, low_next = link(i + 1)
            kk = (centre(i + 1), up, low_next, centre(i + 2))
        else:
            quarter = 0.25 * speed(i + 1)
            kk = (
                1.0 + here + 4.0 * there,
                quarter - 2.0 * there,
                -quarter - 2.0 * there,
                there,
            )
        kk = minus(kk, below(wr))
    yield ll + lk + kl + kk


def pair_source(down, damps, left, pair, following):
    pivot, lk, low = down[0:4], down[4:8], down[8]
    w = apply(pivot, pair)
    left = minus(left, apply(lk, w))
    following = minus(following, (damps[0] * w[0] + low * w[1], damps[1] * w[1]))
    return left, following, w


def pair_of(source, k, cells):
    if k == (cells - 2) // 2:
        last = source(cells - 1)
        return (last, jnp.zeros_like(last))
    return (source(2 * k + 1), source(2 * k + 2))


def first_pair(source):
    first = source(0)
    return (jnp.zeros_like(first), first)


def blocks(rows, size):
    return [(at, min(size, rows - at)) for at in range(0, rows, size)]


def get(ref, count, at, size, base=0):
    return tuple(ref[base + v, pl.ds(at, size), :] for v in range(count))


def put(ref, values, at, size, base=0):
    for v, value in enumerate(values):
        ref[base + v, pl.ds(at, size), :] = value


def get_both(ref, count, at, size):
    return tuple(
        tuple(ref[v, pl.ds(2 * at + half, size, stride=2), :] for v in range(count))
        for half in (0, 1)
    )


def levels_of(lines):
    sizes = []
    rows = lines * CHUNKS
    while rows > lines:
        rows //= 2
        sizes.append(rows)
    return sizes


def split_all(top_ref, end_refs, up_refs, w_refs, sizes):
    source = top_ref
    for rows, target, ups, ws in zip(
        reversed(sizes), end_refs, reversed(up_refs), reversed(w_refs)
    ):
        for at, size in blocks(rows, 8):
            ends = get(source, 4, at, size)
            left, right = ends[0:2], ends[2:4]
            middle = inner(get(ups, UP, at, size), get(ws, 2, at, size), left, right)
            for v in range(2):
                target[v, pl.ds(2 * at, size, stride=2), :] = left[v]
                target[v, pl.ds(2 * at + 1, size, stride=2), :] = middle[v]
                target[2 + v, pl.ds(2 * at, size, stride=2), :] = middle[v]
                target[2 + v, pl.ds(2 * at + 1, size, stride=2), :] = right[v]
        source = target
    return source


def back_substitute(ends_ref, up_ref, w_ref, cells, at, size, store):
    ends = get(ends_ref, 4, at, size)
    left, following = ends[0:2], ends[2:4]
    store(0, left[1])
    store(cells - 1, following[0])
    for k in range((cells - 2) // 2 - 1, -1, -1):
        following = inner(
            get(up_ref, UP, at, size, k * UP), get(w_ref, 2, at, size, k * 2), left, following
        )
        store(2 * k + 1, following[0])
        store(2 * k + 2, following[1])


def close_ring(own, rest):
    ll, lr, rl, rr = quads(own)
    nn, nm, mn, mm = quads(rest)
    b = plus(lr, mn)
    c = plus(rl, nm)
    pivot = inverse(*plus(rr, nn))
    f = plus(own[16:18], rest[18:20])
    g = plus(own[18:20], rest[16:18])
    bd = times(b, pivot)
    left = apply(inverse(*minus(plus(ll, mm), times(bd, c))), minus(f, apply(bd, g)))
    right = apply(pivot, minus(g, apply(c, left)))
    return left, right


def open_ends(axis):
    place = lax.axis_index(axis)
    last = lax.axis_size(axis) - 1
    return jnp.where(place > 0, 1.0, 0.0), jnp.where(place < last, 1.0, 0.0)


def is_second(axis, bit):
    return lax.rem(lax.axis_index(axis) // (1 << bit), 2) == 1


def choose(second, one, other):
    return tuple(jnp.where(second, a, b) for a, b in zip(one, other))


def flat(ref, count, rows, at, size):
    return tuple(ref[pl.ds(v * rows + at, size), :] for v in range(count))


def put_flat(ref, values, rows, at, size):
    for v, value in enumerate(values):
        ref[pl.ds(v * rows + at, size), :] = value


def round_down(ups, ws, axis, bits, at, size, left, right, lowest=0):
    for bit in reversed(range(lowest, bits)):
        middle = inner(get(ups[bit], UP, at, size), get(ws[bit], 2, at, size), left, right)
        second = is_second(axis, bit)
        left, right = choose(second, middle, left), choose(second, right, middle)
    return left, right


def copies(pairs, sems, first=0):
    started = []
    for i, (source, target) in enumerate(pairs):
        copy = pltpu.make_async_copy(source, target, sems.at[first + i])
        copy.start()
        started.append(copy)
    return started


def wrap_down(fields, cells, *refs):
    residual, courant, dissip, wall_courant, wall_dissip = refs[0:5]
    packed, chunk_up, chunk_w = refs[5:8]
    ups, ws = refs[8:11], refs[11:14]
    wall_speed, wall_damp = refs[14:16]
    source_in, speed_in, damp_in, source_t, speed_t, damp_t = refs[16:22]
    elements, sems = refs[22:26], refs[26]
    lanes = damp_in.shape[0]
    length = cells * CHUNKS
    started = copies(
        [(dissip, damp_in), (courant, speed_in), (residual, source_in)], sems
    )
    for copy in started:
        copy.wait()
    started = copies([(wall_dissip, wall_damp), (wall_courant, wall_speed)], sems, 3)
    damp_t[...] = damp_in[...].T
    for field in range(fields):
        speed_t[pl.ds(field * length, length), :] = speed_in[pl.ds(field * lanes, lanes), :].T
        source_t[pl.ds(field * length, length), :] = source_in[pl.ds(field * lanes, lanes), :].T
    for at, size in blocks(fields * CHUNKS, 16):
        repeat = size // CHUNKS

        def speed(i):
            return speed_t[pl.ds(at * cells + i, size, stride=cells), :]

        def source(i):
            return source_t[pl.ds(at * cells + i, size, stride=cells), :]

        def damp(i):
            rows = damp_t[pl.ds(i, CHUNKS, stride=cells), :]
            return jnp.concatenate([rows] * repeat, axis=0) if repeat > 1 else rows

        left, pair = first_pair(source), pair_of(source, 0, cells)
        for k, step in enumerate(chunk_matrix(speed, damp, cells)):
            if k == (cells - 2) // 2:
                put(elements[0], step + left + pair, at, size)
                break
            up, down, damps = step
            left, pair, w = pair_source(down, damps, left, pair, pair_of(source, k + 1, cells))
            put(chunk_up, up, at, size, k * UP)
            put(chunk_w, w, at, size, k * 2)
    for level, rows in enumerate(levels_of(fields)):
        for at, size in blocks(rows, 8):
            merged, up, w = merge(*get_both(elements[level], VALUES, at, size))
            put(elements[level + 1], merged, at, size)
            put(ups[level], up, at, size)
            put(ws[level], w, at, size)
    for v in range(VALUES):
        packed[pl.ds(v * fields, fields), :] = elements[-1][v]
    for copy in started:
        copy.wait()


def wrap_round(fields, bit, own, other, after, packed, up_out, w_out):
    second = is_second("wrap", bit)
    for at, size in blocks(fields, 8):
        mine = flat(own, VALUES, fields, at, size)
        theirs = flat(other, VALUES, fields, at, size)
        merged, up, w = merge(choose(second, theirs, mine), choose(second, mine, theirs))
        put_flat(packed, merged, fields, at, size)
        put(up_out, up, at, size)
        put(w_out, w, at, size)


def wall_matrix(fields, span, cells, *refs):
    speed_in, damp_in = refs[0:2]
    packed, damp_out, chunk_up, chunk_down = refs[2:6]
    ups, downs = refs[6:9], refs[9:12]
    elements = refs[12:16]
    size = span * CHUNKS
    for field in range(fields):
        at = field * size

        def speed(i):
            return speed_in[pl.ds(at * cells + i, size, stride=cells), :]

        def damp(i):
            return damp_in[pl.ds(i, size, stride=cells), :]

        for k, step in enumerate(chunk_matrix(speed, damp, cells)):
            if k == (cells - 2) // 2:
                put(elements[0], step, at, size)
                break
            up, down, damps = step
            put(chunk_up, up, at, size, k * UP)
            put(chunk_down, down, at, size, k * CHUNK_DOWN)
            if field == 0:
                put(damp_out, damps, 0, size, k * 2)
    lines = fields * span
    for level, rows in enumerate(levels_of(lines)):
        for at, size in blocks(rows, 8):
            merged, up, down = merge_matrix(*get_both(elements[level], MATRIX, at, size))
            put(elements[level + 1], merged, at, size)
            put(ups[level], up, at, size)
            put(downs[level], down, at, size)
    not_first, not_last = open_ends("normal")
    for v in range(MATRIX):
        value = elements[-1][v]
        if v in (0, 1, 2, 4, 5, 8, 10):
            value = value * not_first
        if v in (5, 7, 10, 11, 13, 14, 15):
            value = value * not_last
        packed[pl.ds(v * lines, lines), :] = value


def wall_round(lines, bit, final, own, other, packed, up_out, down_out, *outer_out):
    second = is_second("normal", bit)
    upper = is_second("normal", bit + 1)
    for at, size in blocks(lines, 8):
        mine = flat(own, MATRIX, lines, at, size)
        theirs = flat(other, MATRIX, lines, at, size)
        merged, up, down = merge_matrix(
            choose(second, theirs, mine), choose(second, mine, theirs)
        )
        put(up_out, up, at, size)
        put(down_out, down, at, size)
        if not final:
            put_flat(packed, merged, lines, at, size)
            continue
        ll, lr, rl, rr = quads(merged)
        outer, into = choose(upper, rr, ll), choose(upper, rl, lr)
        out, middle = choose(upper, lr, rl), choose(upper, ll, rr)
        is_upper = jnp.where(upper, 1.0, 0.0)
        pivot = inverse(
            outer[0] + (1.0 - is_upper), outer[1], outer[2], outer[3] + is_upper
        )
        put_flat(packed, minus(middle, times(out, times(pivot, into))), lines, at, size)
        put(outer_out[0], pivot + into + out, at, size)


def wall_source_round(lines, bit, own, other, down_in, packed, w_out):
    second = is_second("normal", bit)
    for at, size in blocks(lines, 8):
        mine = flat(own, SOURCE, lines, at, size)
        theirs = flat(other, SOURCE, lines, at, size)
        merged, w = merge_source(
            get(down_in, MERGE_DOWN, at, size),
            choose(second, theirs, mine),
            choose(second, mine, theirs),
        )
        put_flat(packed, merged, lines, at, size)
        put(w_out, w, at, size)


def reduce_source(down, factors, second, upper, mine, theirs):
    merged, w = merge_source(
        down, choose(second, theirs, mine), choose(second, mine, theirs)
    )
    outer = apply(factors[0:4], choose(upper, merged[2:4], merged[0:2]))
    centre = choose(upper, merged[0:2], merged[2:4])
    return minus(centre, apply(factors[8:12], outer)), outer, w


def wall_share(lines, bit, own, down_in, outer_in, share, copy):
    copy[...] = own[...]
    second, upper = is_second("normal", bit), is_second("normal", bit + 1)
    for at, size in blocks(lines, 8):
        mine = flat(own, SOURCE, lines, at, size)
        none = tuple(jnp.zeros_like(value) for value in mine)
        down, factors = get(down_in, MERGE_DOWN, at, size), get(outer_in, 12, at, size)
        part, _, _ = reduce_source(down, factors, second, upper, mine, none)
        put_flat(share, part, lines, at, size)


def wrap_close(fields, bits, *refs):
    own, others, refs = refs[0], refs[1:4], refs[4:]
    round_ups, round_ws, own_ends, partner_ends = refs[:bits], refs[bits : 2 * bits], *refs[-2:]
    odd = is_second("wrap", bits)
    for at, size in blocks(fields, 8):
        far, opposite, near = (flat(other, VALUES, fields, at, size) for other in others)
        following, before = choose(odd, far, near), choose(odd, near, far)
        rest = merge(merge(following, opposite)[0], before)[0]
        left, right = close_ring(flat(own, VALUES, fields, at, size), rest)
        left, right = round_down(round_ups, round_ws, "wrap", bits, at, size, left, right, 1)
        between = inner(get(round_ups[0], UP, at, size), get(round_ws[0], 2, at, size), left, right)
        put_flat(partner_ends, left + between, fields, at, size)
        put_flat(own_ends, between + right, fields, at, size)


def middle(fields, span, wrap_cells, wall_cells, *refs):
    own_ends, partner_ends, refs = refs[0], refs[1], refs[2:]
    chunk_up, chunk_w, ups, ws = refs[0], refs[1], refs[2:5], refs[5:8]
    coupling, damps_in, chunk_down, downs = refs[8], refs[9], refs[10], refs[11:14]
    packed, wall_w, wall_ws = refs[14], refs[15], refs[16:19]
    ends, solved_t, solved, mixed = refs[19:23], refs[23], refs[24], refs[25]
    sources = refs[26:30]

    leads = is_second("wrap", 0)
    for at, size in blocks(fields, 8):
        own = flat(own_ends, 4, fields, at, size)
        received = flat(partner_ends, 4, fields, at, size)
        put(ends[0], choose(leads, own, received), at, size)
    last = split_all(ends[0], ends[1:], ups, ws, levels_of(fields))
    length = wrap_cells * CHUNKS
    for at, size in blocks(fields * CHUNKS, 16):

        def store(i, value):
            solved_t[pl.ds(at * wrap_cells + i, size, stride=wrap_cells), :] = value

        back_substitute(last, chunk_up, chunk_w, wrap_cells, at, size, store)
    lanes = solved.shape[0] // fields
    for field in range(fields):
        solved[pl.ds(field * lanes, lanes), :] = solved_t[pl.ds(field * length, length), :].T

    for at, size in blocks(lanes, 16):
        update = [solved[pl.ds(j * lanes + at, size), :] for j in range(fields)]
        for k in range(fields):
            total = coupling[k, 0, pl.ds(at, size), :].astype(jnp.float32) * update[0]
            for j in range(1, fields):
                total = total + coupling[k, j, pl.ds(at, size), :].astype(jnp.float32) * update[j]
            mixed[pl.ds(k * lanes + at, size), :] = total

    pairs = (wall_cells - 2) // 2
    size = span * CHUNKS
    for field in range(fields):
        at = field * size

        def source(i):
            return mixed[pl.ds(at * wall_cells + i, size, stride=wall_cells), :]

        left, pair = first_pair(source), pair_of(source, 0, wall_cells)
        for k in range(pairs):
            left, pair, w = pair_source(
                get(chunk_down, CHUNK_DOWN, at, size, k * CHUNK_DOWN),
                get(damps_in, 2, 0, size, k * 2),
                left,
                pair,
                pair_of(source, k + 1, wall_cells),
            )
            put(wall_w, w, at, size, k * 2)
        put(sources[0], left + pair, at, size)
    lines = fields * span
    for level, rows in enumerate(levels_of(lines)):
        for at, size in blocks(rows, 8):
            down = get(downs[level], MERGE_DOWN, at, size)
            merged, w = merge_source(down, *get_both(sources[level], SOURCE, at, size))
            put(sources[level + 1], merged, at, size)
            put(wall_ws[level], w, at, size)
    not_first, not_last = open_ends("normal")
    for v, keep in enumerate((not_first, None, None, not_last)):
        value = sources[-1][v]
        packed[pl.ds(v * lines, lines), :] = value if keep is None else value * keep


def wall_up(fields, span, cells, bits, *refs):
    own_matrix, other_matrix, down_in, outer_in, own, share_one, share_two, other = refs[0:8]
    refs = refs[8:]
    round_ups, round_ws, refs = refs[: bits + 1], refs[bits + 1 : 2 * bits + 1], refs[2 * bits + 1 :]
    chunk_up, chunk_w, ups, ws = refs[0], refs[1], refs[2:5], refs[5:8]
    update = refs[8]
    ends, result, sems = refs[9:13], refs[13], refs[14]
    lines = fields * span
    second, upper = is_second("normal", bits), is_second("normal", bits + 1)
    for at, size in blocks(lines, 8):
        down, factors = get(down_in, MERGE_DOWN, at, size), get(outer_in, 12, at, size)
        part, outer, w = reduce_source(
            down,
            factors,
            second,
            upper,
            flat(own, SOURCE, lines, at, size),
            flat(other, SOURCE, lines, at, size),
        )
        shares = plus(flat(share_one, 2, lines, at, size), flat(share_two, 2, lines, at, size))
        matrix = plus(
            flat(own_matrix, 4, lines, at, size), flat(other_matrix, 4, lines, at, size)
        )
        centre = apply(inverse(*matrix), plus(part, shares))
        outer = minus(outer, apply(factors[0:4], apply(factors[4:8], centre)))
        left, right = choose(upper, centre, outer), choose(upper, outer, centre)
        between = inner(get(round_ups[bits], UP, at, size), w, left, right)
        left, right = choose(second, between, left), choose(second, right, between)
        left, right = round_down(round_ups, round_ws, "normal", bits, at, size, left, right)
        put(ends[0], left + right, at, size)
    last = split_all(ends[0], ends[1:], ups, ws, levels_of(lines))
    size = span * CHUNKS
    length = size * cells
    started = []
    for field in range(fields):
        at = field * size

        def store(i, value):
            result[pl.ds(at * cells + i, size, stride=cells), :] = value

        back_substitute(last, chunk_up, chunk_w, cells, at, size, store)
        rows = pl.ds(field * length, length)
        copy = pltpu.make_async_copy(result.at[rows], update.at[rows], sems.at[field])
        copy.start()
        started.append(copy)
    for copy in started:
        copy.wait()


def f32(*shape):
    return jax.ShapeDtypeStruct(shape, jnp.float32)


def vmem(*shape):
    return pltpu.VMEM(shape, jnp.float32)


IN_VMEM = pl.BlockSpec(memory_space=pltpu.VMEM)
IN_HBM = pl.BlockSpec(memory_space=pltpu.HBM)
PARAMS = pltpu.CompilerParams(vmem_limit_bytes=24 * 2**20)


def kernel(name, body, ins, outs, scratch, flops):
    in_bytes = sum(a.size * a.dtype.itemsize for a, _ in ins)
    out_bytes = sum(a.size * 4 for a, _ in outs)
    outputs = pl.pallas_call(
        body,
        out_shape=[a for a, _ in outs],
        in_specs=[spec for _, spec in ins],
        out_specs=[spec for _, spec in outs],
        scratch_shapes=scratch,
        compiler_params=PARAMS,
        cost_estimate=pl.CostEstimate(
            flops=flops, bytes_accessed=in_bytes + out_bytes, transcendentals=0
        ),
        name=name,
    )(*[a for a, _ in ins])
    return list(outputs)


def inside(arrays):
    return [(a, IN_VMEM) for a in arrays]


def outside(arrays):
    return [(pltpu.with_memory_space_constraint(a, pltpu.HBM), IN_HBM) for a in arrays]


def exchange(array, axis, mask, senders=lambda i: True):
    count = lax.axis_size(axis)
    return lax.ppermute(array, axis, [(i, i ^ mask) for i in range(count) if senders(i)])


def is_leading(i):
    return i % 2 == 1


def is_led(i):
    return i % 2 == 0


def local(residual, courant_xi, courant_eta, dissip_xi, dissip_eta, coupling):
    fields, span, high, wide = residual.shape
    lanes = span * high
    wrap_cells, wall_cells = wide // CHUNKS, high // CHUNKS
    wrap_pairs, wall_pairs = (wrap_cells - 2) // 2, (wall_cells - 2) // 2
    wrap_count, wall_count = lax.axis_size("wrap"), lax.axis_size("normal")
    lines = fields * span
    wrap_levels, wall_levels = levels_of(fields), levels_of(lines)
    wrap_rows, wall_rows = fields * CHUNKS, lines * CHUNKS

    def rows_of(array):
        return array.reshape(-1, wide)

    wrap_bits = wrap_count.bit_length() - 3
    wall_bits = wall_count.bit_length() - 3
    results = kernel(
        "wrap_down",
        functools.partial(wrap_down, fields, wrap_cells),
        outside(
            [rows_of(a) for a in (residual, courant_xi, dissip_xi, courant_eta, dissip_eta)]
        ),
        inside(
            [
                f32(VALUES * fields, lanes),
                f32(wrap_pairs * UP, wrap_rows, lanes),
                f32(wrap_pairs * 2, wrap_rows, lanes),
            ]
            + [f32(UP, n, lanes) for n in wrap_levels]
            + [f32(2, n, lanes) for n in wrap_levels]
            + [f32(fields * lanes, wide), f32(lanes, wide)]
        ),
        [vmem(fields * lanes, wide)] * 2
        + [vmem(lanes, wide)]
        + [vmem(fields * wide, lanes)] * 2
        + [vmem(wide, lanes)]
        + [vmem(VALUES, n, lanes) for n in [wrap_rows] + wrap_levels]
        + [pltpu.SemaphoreType.DMA((5,))],
        100 * residual.size,
    )
    element, wrap_factors, wall_inputs = results[0], results[1:9], results[9:11]
    results = kernel(
        "wall_matrix",
        functools.partial(wall_matrix, fields, span, wall_cells),
        inside(wall_inputs),
        inside(
            [
                f32(MATRIX * lines, wide),
                f32(wall_pairs * 2, span * CHUNKS, wide),
                f32(wall_pairs * UP, wall_rows, wide),
                f32(wall_pairs * CHUNK_DOWN, wall_rows, wide),
            ]
            + [f32(UP, n, wide) for n in wall_levels]
            + [f32(MERGE_DOWN, n, wide) for n in wall_levels]
        ),
        [vmem(MATRIX, n, wide) for n in [wall_rows] + wall_levels],
        100 * residual.size,
    )
    matrix, damps, chunk_up, chunk_down = results[0:4]
    wall_ups, wall_downs = results[4:7], results[7:10]
    wrap_ups, wrap_ws = [], []
    for bit in range(wrap_bits):
        element, up, w = kernel(
            f"wrap_round_{bit}",
            functools.partial(wrap_round, fields, bit),
            inside(
                [
                    element,
                    exchange(element, "wrap", 1 << bit, is_leading if bit else is_led),
                    damps,
                ]
            ),
            inside([f32(VALUES * fields, lanes), f32(UP, fields, lanes), f32(2, fields, lanes)]),
            [],
            200 * fields * lanes,
        )
        wrap_ups.append(up)
        wrap_ws.append(w)
    wrap_others = [
        exchange(element, "wrap", mask << wrap_bits, is_leading) for mask in (3, 2, 1)
    ]
    own_ends, partner_ends = kernel(
        "wrap_close",
        functools.partial(wrap_close, fields, wrap_bits),
        inside([element] + wrap_others + wrap_ups + wrap_ws),
        inside([f32(4 * fields, lanes)] * 2),
        [],
        500 * fields * lanes,
    )
    partner_ends = exchange(partner_ends, "wrap", 1, is_leading)
    round_ups, round_downs = [], []
    for bit in range(wall_bits + 1):
        final = bit == wall_bits
        matrix, up, down, *outer = kernel(
            f"wall_round_{bit}",
            functools.partial(wall_round, lines, bit, final),
            inside([matrix, exchange(matrix, "normal", 1 << bit)]),
            inside(
                [
                    f32((4 if final else MATRIX) * lines, wide),
                    f32(UP, lines, wide),
                    f32(MERGE_DOWN, lines, wide),
                ]
                + ([f32(12, lines, wide)] if final else [])
            ),
            [],
            200 * lines * wide,
        )
        round_ups.append(up)
        round_downs.append(down)
    matrix_other = exchange(matrix, "normal", 2 << wall_bits)
    source, *wall_ws = kernel(
        "middle",
        functools.partial(middle, fields, span, wrap_cells, wall_cells),
        inside(
            [own_ends, partner_ends]
            + wrap_factors
            + [coupling.reshape(fields, fields, lanes, wide), damps, chunk_down]
            + wall_downs
        ),
        inside(
            [f32(SOURCE * lines, wide), f32(wall_pairs * 2, wall_rows, wide)]
            + [f32(2, n, wide) for n in wall_levels]
        ),
        [vmem(4, n, lanes) for n in reversed([wrap_rows] + wrap_levels)]
        + [vmem(fields * wide, lanes), vmem(fields * lanes, wide), vmem(fields * lanes, wide)]
        + [vmem(SOURCE, n, wide) for n in [wall_rows] + wall_levels],
        100 * residual.size,
    )
    round_ws = []
    for bit in range(wall_bits):
        source, w = kernel(
            f"wall_source_round_{bit}",
            functools.partial(wall_source_round, lines, bit),
            inside([source, exchange(source, "normal", 1 << bit), round_downs[bit]]),
            inside([f32(SOURCE * lines, wide), f32(2, lines, wide)]),
            [],
            50 * lines * wide,
        )
        round_ws.append(w)
    share, source = kernel(
        "wall_share",
        functools.partial(wall_share, lines, wall_bits),
        inside([source, round_downs[wall_bits]] + outer),
        inside([f32(2 * lines, wide), f32(SOURCE * lines, wide)]),
        [],
        50 * lines * wide,
    )
    wall_shares = [exchange(share, "normal", mask << wall_bits) for mask in (2, 3)]
    wall_other = exchange(source, "normal", 1 << wall_bits)
    (update,) = kernel(
        "wall_up",
        functools.partial(wall_up, fields, span, wall_cells, wall_bits),
        inside(
            [matrix, matrix_other, round_downs[wall_bits]]
            + outer
            + [source]
            + wall_shares
            + [wall_other]
            + round_ups
            + round_ws
            + [chunk_up, wall_ws[0]]
            + wall_ups
            + wall_ws[1:]
        ),
        [(f32(fields * lanes, wide), IN_HBM)],
        [vmem(4, n, wide) for n in reversed([wall_rows] + wall_levels)]
        + [vmem(fields * lanes, wide), pltpu.SemaphoreType.DMA((fields,))],
        30 * residual.size,
    )
    return update.reshape(residual.shape)


def solution(mesh):
    placed = (
        P(None, None, "normal", "wrap"),
        P(None, None, "normal", "wrap"),
        P(None, None, "normal", "wrap"),
        P(None, "normal", "wrap"),
        P(None, "normal", "wrap"),
        P(None, None, None, "normal", "wrap"),
    )
    return jax.shard_map(
        local,
        mesh=mesh,
        in_specs=placed,
        out_specs=P(None, None, "normal", "wrap"),
        check_vma=False,
    )
```

```python
import functools

import jax
import jax.numpy as jnp
from jax import lax
from jax.experimental import pallas as pl
from jax.experimental.pallas import tpu as pltpu
from jax.sharding import PartitionSpec as P

MATRIX = 16
SOURCE = 4
VALUES = MATRIX + SOURCE
UP = 8
CHUNK_DOWN = 9
MERGE_DOWN = 12
CHUNKS = 8


def inverse(a, b, c, d):
    scale = 1.0 / (a * d - b * c)
    return (d * scale, -b * scale, -c * scale, a * scale)


def times(x, y):
    return (
        x[0] * y[0] + x[1] * y[2],
        x[0] * y[1] + x[1] * y[3],
        x[2] * y[0] + x[3] * y[2],
        x[2] * y[1] + x[3] * y[3],
    )


def apply(x, v):
    return (x[0] * v[0] + x[1] * v[1], x[2] * v[0] + x[3] * v[1])


def minus(x, y):
    return tuple(a - b for a, b in zip(x, y))


def plus(x, y):
    return tuple(a + b for a, b in zip(x, y))


def negative(x):
    return tuple(-a for a in x)


def quads(element):
    return (element[0:4], element[4:8], element[8:12], element[12:16])


def merge_matrix(first, second):
    ll, lm, ml, mm = quads(first)
    nn, mr, rm, rr = quads(second)
    pivot = inverse(*plus(mm, nn))
    wl = times(pivot, ml)
    wr = times(pivot, mr)
    merged = (
        minus(ll, times(lm, wl))
        + negative(times(lm, wr))
        + negative(times(rm, wl))
        + minus(rr, times(rm, wr))
    )
    return merged, wl + wr, pivot + lm + rm


def merge_source(down, first, second):
    pivot, lm, rm = down[0:4], down[4:8], down[8:12]
    w = apply(pivot, plus(first[2:4], second[0:2]))
    return minus(first[0:2], apply(lm, w)) + minus(second[2:4], apply(rm, w)), w


def merge(first, second):
    matrix, up, down = merge_matrix(first[:MATRIX], second[:MATRIX])
    source, w = merge_source(down, first[MATRIX:], second[MATRIX:])
    return matrix + source, up, w


def inner(up, w, left, right):
    return minus(minus(w, apply(up[0:4], left)), apply(up[4:8], right))


def chunk_matrix(speed, damp, cells):
    def link(i):
        p = 2.0 * (damp(i) + damp(i + 1))
        q = 0.25 * (speed(i) + speed(i + 1))
        return q - p, -q - p

    def centre(i):
        return 1.0 + damp(i - 1) + 4.0 * damp(i) + damp(i + 1)

    b0, b1 = damp(0), damp(1)
    quarter = 0.25 * speed(0)
    up, low = link(0)
    zero = jnp.zeros_like(b0)
    ll = (b0, quarter - 2.0 * b0, -quarter - 2.0 * b0, 1.0 + 4.0 * b0 + b1)
    lk = (b0, zero, up, b1)
    kl = (b0, low, zero, b1)
    up, low = link(1)
    kk = (centre(1), up, low, centre(2))
    pairs = (cells - 2) // 2
    for k in range(1, pairs + 1):
        i = 2 * k
        pivot = inverse(*kk)
        wl = times(pivot, kl)
        up, low = link(i)
        here, there = damp(i), damp(i + 1)
        wr = (
            pivot[0] * here + pivot[1] * up,
            pivot[1] * there,
            pivot[2] * here + pivot[3] * up,
            pivot[3] * there,
        )
        yield wl + wr, pivot + lk + (low,), (here, there)

        def below(x):
            return (
                here * x[0] + low * x[2],
                here * x[1] + low * x[3],
                there * x[2],
                there * x[3],
            )

        ll = minus(ll, times(lk, wl))
        lk = negative(times(lk, wr))
        kl = negative(below(wl))
        if k < pairs:
            up, low_next = link(i + 1)
            kk = (centre(i + 1), up, low_next, centre(i + 2))
        else:
            quarter = 0.25 * speed(i + 1)
            kk = (
                1.0 + here + 4.0 * there,
                quarter - 2.0 * there,
                -quarter - 2.0 * there,
                there,
            )
        kk = minus(kk, below(wr))
    yield ll + lk + kl + kk


def pair_source(down, damps, left, pair, following):
    pivot, lk, low = down[0:4], down[4:8], down[8]
    w = apply(pivot, pair)
    left = minus(left, apply(lk, w))
    following = minus(following, (damps[0] * w[0] + low * w[1], damps[1] * w[1]))
    return left, following, w


def pair_of(source, k, cells):
    if k == (cells - 2) // 2:
        last = source(cells - 1)
        return (last, jnp.zeros_like(last))
    return (source(2 * k + 1), source(2 * k + 2))


def first_pair(source):
    first = source(0)
    return (jnp.zeros_like(first), first)


def blocks(rows, size):
    return [(at, min(size, rows - at)) for at in range(0, rows, size)]


def get(ref, count, at, size, base=0):
    return tuple(ref[base + v, pl.ds(at, size), :] for v in range(count))


def put(ref, values, at, size, base=0):
    for v, value in enumerate(values):
        ref[base + v, pl.ds(at, size), :] = value


def get_both(ref, count, at, size):
    return tuple(
        tuple(ref[v, pl.ds(2 * at + half, size, stride=2), :] for v in range(count))
        for half in (0, 1)
    )


def levels_of(lines):
    sizes = []
    rows = lines * CHUNKS
    while rows > lines:
        rows //= 2
        sizes.append(rows)
    return sizes


def split_all(top_ref, end_refs, up_refs, w_refs, sizes):
    source = top_ref
    for rows, target, ups, ws in zip(
        reversed(sizes), end_refs, reversed(up_refs), reversed(w_refs)
    ):
        for at, size in blocks(rows, 8):
            ends = get(source, 4, at, size)
            left, right = ends[0:2], ends[2:4]
            middle = inner(get(ups, UP, at, size), get(ws, 2, at, size), left, right)
            for v in range(2):
                target[v, pl.ds(2 * at, size, stride=2), :] = left[v]
                target[v, pl.ds(2 * at + 1, size, stride=2), :] = middle[v]
                target[2 + v, pl.ds(2 * at, size, stride=2), :] = middle[v]
                target[2 + v, pl.ds(2 * at + 1, size, stride=2), :] = right[v]
        source = target
    return source


def back_substitute(ends_ref, up_ref, w_ref, cells, at, size, store):
    ends = get(ends_ref, 4, at, size)
    left, following = ends[0:2], ends[2:4]
    store(0, left[1])
    store(cells - 1, following[0])
    for k in range((cells - 2) // 2 - 1, -1, -1):
        following = inner(
            get(up_ref, UP, at, size, k * UP), get(w_ref, 2, at, size, k * 2), left, following
        )
        store(2 * k + 1, following[0])
        store(2 * k + 2, following[1])


def close_ring(own, rest):
    ll, lr, rl, rr = quads(own)
    nn, nm, mn, mm = quads(rest)
    b = plus(lr, mn)
    c = plus(rl, nm)
    pivot = inverse(*plus(rr, nn))
    f = plus(own[16:18], rest[18:20])
    g = plus(own[18:20], rest[16:18])
    bd = times(b, pivot)
    left = apply(inverse(*minus(plus(ll, mm), times(bd, c))), minus(f, apply(bd, g)))
    right = apply(pivot, minus(g, apply(c, left)))
    return left, right


def open_ends(axis):
    place = lax.axis_index(axis)
    last = lax.axis_size(axis) - 1
    return jnp.where(place > 0, 1.0, 0.0), jnp.where(place < last, 1.0, 0.0)


def is_second(axis, bit):
    return lax.rem(lax.axis_index(axis) // (1 << bit), 2) == 1


def choose(second, one, other):
    return tuple(jnp.where(second, a, b) for a, b in zip(one, other))


def flat(ref, count, rows, at, size):
    return tuple(ref[pl.ds(v * rows + at, size), :] for v in range(count))


def put_flat(ref, values, rows, at, size):
    for v, value in enumerate(values):
        ref[pl.ds(v * rows + at, size), :] = value


def round_down(ups, ws, axis, bits, at, size, left, right):
    for bit in reversed(range(bits)):
        middle = inner(get(ups[bit], UP, at, size), get(ws[bit], 2, at, size), left, right)
        second = is_second(axis, bit)
        left, right = choose(second, middle, left), choose(second, right, middle)
    return left, right


def copies(pairs, sems, first=0):
    started = []
    for i, (source, target) in enumerate(pairs):
        copy = pltpu.make_async_copy(source, target, sems.at[first + i])
        copy.start()
        started.append(copy)
    return started


def wrap_down(fields, cells, *refs):
    residual, courant, dissip, wall_courant, wall_dissip = refs[0:5]
    packed, chunk_up, chunk_w = refs[5:8]
    ups, ws = refs[8:11], refs[11:14]
    wall_speed, wall_damp = refs[14:16]
    source_in, speed_in, damp_in, source_t, speed_t, damp_t = refs[16:22]
    elements, sems = refs[22:26], refs[26]
    lanes = damp_in.shape[0]
    length = cells * CHUNKS
    half = lanes // 2

    def halves(source, target, at):
        return [
            (source.at[pl.ds(i, half)], target.at[pl.ds(i, half)]) for i in (at, at + half)
        ]

    moves = halves(dissip, damp_in, 0)
    for field in range(fields):
        moves += halves(courant, speed_in, field * lanes)
        moves += halves(residual, source_in, field * lanes)
    started = copies(moves, sems)

    def arrive(first, count):
        for copy in started[first : first + count]:
            copy.wait()

    arrive(0, 2)
    damp_t[...] = damp_in[...].T

    def turn(field):
        arrive(2 + 4 * field, 2)
        speed_t[pl.ds(field * length, length), :] = speed_in[pl.ds(field * lanes, lanes), :].T
        arrive(4 + 4 * field, 2)
        source_t[pl.ds(field * length, length), :] = source_in[pl.ds(field * lanes, lanes), :].T

    for at, size in blocks(fields * CHUNKS, 16):
        repeat = size // CHUNKS
        for field in range(at // CHUNKS, at // CHUNKS + repeat):
            turn(field)
        if at == 0:
            moves = halves(wall_dissip, wall_damp, 0)
            for field in range(fields):
                moves += halves(wall_courant, wall_speed, field * lanes)
            started += copies(moves, sems, len(started))

        def speed(i):
            return speed_t[pl.ds(at * cells + i, size, stride=cells), :]

        def source(i):
            return source_t[pl.ds(at * cells + i, size, stride=cells), :]

        def damp(i):
            rows = damp_t[pl.ds(i, CHUNKS, stride=cells), :]
            return jnp.concatenate([rows] * repeat, axis=0) if repeat > 1 else rows

        left, pair = first_pair(source), pair_of(source, 0, cells)
        for k, step in enumerate(chunk_matrix(speed, damp, cells)):
            if k == (cells - 2) // 2:
                put(elements[0], step + left + pair, at, size)
                break
            up, down, damps = step
            left, pair, w = pair_source(down, damps, left, pair, pair_of(source, k + 1, cells))
            put(chunk_up, up, at, size, k * UP)
            put(chunk_w, w, at, size, k * 2)
    for level, rows in enumerate(levels_of(fields)):
        for at, size in blocks(rows, 8):
            merged, up, w = merge(*get_both(elements[level], VALUES, at, size))
            put(elements[level + 1], merged, at, size)
            put(ups[level], up, at, size)
            put(ws[level], w, at, size)
    for v in range(VALUES):
        packed[pl.ds(v * fields, fields), :] = elements[-1][v]
    arrive(2 + 4 * fields, 2 + 2 * fields)


def wrap_round(fields, bit, own, other, after, packed, up_out, w_out):
    second = is_second("wrap", bit)
    for at, size in blocks(fields, 8):
        mine = flat(own, VALUES, fields, at, size)
        theirs = flat(other, VALUES, fields, at, size)
        merged, up, w = merge(choose(second, theirs, mine), choose(second, mine, theirs))
        put_flat(packed, merged, fields, at, size)
        put(up_out, up, at, size)
        put(w_out, w, at, size)


def wall_matrix(fields, span, cells, *refs):
    speed_in, damp_in = refs[0:2]
    packed, damp_out, chunk_up, chunk_down = refs[2:6]
    ups, downs = refs[6:9], refs[9:12]
    elements = refs[12:16]
    size = span * CHUNKS
    for field in range(fields):
        at = field * size

        def speed(i):
            return speed_in[pl.ds(at * cells + i, size, stride=cells), :]

        def damp(i):
            return damp_in[pl.ds(i, size, stride=cells), :]

        for k, step in enumerate(chunk_matrix(speed, damp, cells)):
            if k == (cells - 2) // 2:
                put(elements[0], step, at, size)
                break
            up, down, damps = step
            put(chunk_up, up, at, size, k * UP)
            put(chunk_down, down, at, size, k * CHUNK_DOWN)
            if field == 0:
                put(damp_out, damps, 0, size, k * 2)
    lines = fields * span
    for level, rows in enumerate(levels_of(lines)):
        for at, size in blocks(rows, 8):
            merged, up, down = merge_matrix(*get_both(elements[level], MATRIX, at, size))
            put(elements[level + 1], merged, at, size)
            put(ups[level], up, at, size)
            put(downs[level], down, at, size)
    not_first, not_last = open_ends("normal")
    for v in range(MATRIX):
        value = elements[-1][v]
        if v in (0, 1, 2, 4, 5, 8, 10):
            value = value * not_first
        if v in (5, 7, 10, 11, 13, 14, 15):
            value = value * not_last
        packed[pl.ds(v * lines, lines), :] = value


def wall_round(lines, bit, final, own, other, packed, up_out, down_out, *outer_out):
    second = is_second("normal", bit)
    upper = is_second("normal", bit + 1)
    for at, size in blocks(lines, 8):
        mine = flat(own, MATRIX, lines, at, size)
        theirs = flat(other, MATRIX, lines, at, size)
        merged, up, down = merge_matrix(
            choose(second, theirs, mine), choose(second, mine, theirs)
        )
        put(up_out, up, at, size)
        put(down_out, down, at, size)
        if not final:
            put_flat(packed, merged, lines, at, size)
            continue
        ll, lr, rl, rr = quads(merged)
        outer, into = choose(upper, rr, ll), choose(upper, rl, lr)
        out, middle = choose(upper, lr, rl), choose(upper, ll, rr)
        is_upper = jnp.where(upper, 1.0, 0.0)
        pivot = inverse(
            outer[0] + (1.0 - is_upper), outer[1], outer[2], outer[3] + is_upper
        )
        put_flat(packed, minus(middle, times(out, times(pivot, into))), lines, at, size)
        put(outer_out[0], pivot + into + out, at, size)


def wall_source_round(lines, bit, own, other, down_in, packed, w_out):
    second = is_second("normal", bit)
    for at, size in blocks(lines, 8):
        mine = flat(own, SOURCE, lines, at, size)
        theirs = flat(other, SOURCE, lines, at, size)
        merged, w = merge_source(
            get(down_in, MERGE_DOWN, at, size),
            choose(second, theirs, mine),
            choose(second, mine, theirs),
        )
        put_flat(packed, merged, lines, at, size)
        put(w_out, w, at, size)


def reduce_source(down, factors, second, upper, mine, theirs):
    merged, w = merge_source(
        down, choose(second, theirs, mine), choose(second, mine, theirs)
    )
    outer = apply(factors[0:4], choose(upper, merged[2:4], merged[0:2]))
    centre = choose(upper, merged[0:2], merged[2:4])
    return minus(centre, apply(factors[8:12], outer)), outer, w


def wall_share(lines, bit, own, down_in, outer_in, matrix, share, bundle, copy):
    share[pl.ds(2 * lines, 2 * lines), :] = jnp.zeros((2 * lines, share.shape[1]), jnp.float32)
    copy[...] = own[...]
    bundle[pl.ds(2 * lines, 4 * lines), :] = matrix[...]
    second, upper = is_second("normal", bit), is_second("normal", bit + 1)
    for at, size in blocks(lines, 8):
        mine = flat(own, SOURCE, lines, at, size)
        none = tuple(jnp.zeros_like(value) for value in mine)
        down, factors = get(down_in, MERGE_DOWN, at, size), get(outer_in, 12, at, size)
        part, _, _ = reduce_source(down, factors, second, upper, mine, none)
        put_flat(share, part, lines, at, size)
        put_flat(bundle, part, lines, at, size)


def middle(fields, span, wrap_cells, wall_cells, bits, *refs):
    own, others, refs = refs[0], refs[1:4], refs[4:]
    round_ups, round_ws, refs = refs[:bits], refs[bits : 2 * bits], refs[2 * bits :]
    chunk_up, chunk_w, ups, ws = refs[0], refs[1], refs[2:5], refs[5:8]
    coupling, damps_in, chunk_down, downs = refs[8], refs[9], refs[10], refs[11:14]
    packed, wall_w, wall_ws = refs[14], refs[15], refs[16:19]
    ends, solved_t, solved, mixed = refs[19:23], refs[23], refs[24], refs[25]
    sources = refs[26:30]

    for at, size in blocks(fields, 8):
        odd = is_second("wrap", bits)
        near, opposite, far = (flat(other, VALUES, fields, at, size) for other in others)
        following, before = choose(odd, far, near), choose(odd, near, far)
        rest = merge(merge(following, opposite)[0], before)[0]
        left, right = close_ring(flat(own, VALUES, fields, at, size), rest)
        left, right = round_down(round_ups, round_ws, "wrap", bits, at, size, left, right)
        put(ends[0], left + right, at, size)
    last = split_all(ends[0], ends[1:], ups, ws, levels_of(fields))
    length = wrap_cells * CHUNKS
    for at, size in blocks(fields * CHUNKS, 16):

        def store(i, value):
            solved_t[pl.ds(at * wrap_cells + i, size, stride=wrap_cells), :] = value

        back_substitute(last, chunk_up, chunk_w, wrap_cells, at, size, store)
    lanes = solved.shape[0] // fields
    for field in range(fields):
        solved[pl.ds(field * lanes, lanes), :] = solved_t[pl.ds(field * length, length), :].T

    for at, size in blocks(lanes, 16):
        update = [solved[pl.ds(j * lanes + at, size), :] for j in range(fields)]
        for k in range(fields):
            total = coupling[k, 0, pl.ds(at, size), :].astype(jnp.float32) * update[0]
            for j in range(1, fields):
                total = total + coupling[k, j, pl.ds(at, size), :].astype(jnp.float32) * update[j]
            mixed[pl.ds(k * lanes + at, size), :] = total

    pairs = (wall_cells - 2) // 2
    size = span * CHUNKS
    for field in range(fields):
        at = field * size

        def source(i):
            return mixed[pl.ds(at * wall_cells + i, size, stride=wall_cells), :]

        left, pair = first_pair(source), pair_of(source, 0, wall_cells)
        for k in range(pairs):
            left, pair, w = pair_source(
                get(chunk_down, CHUNK_DOWN, at, size, k * CHUNK_DOWN),
                get(damps_in, 2, 0, size, k * 2),
                left,
                pair,
                pair_of(source, k + 1, wall_cells),
            )
            put(wall_w, w, at, size, k * 2)
        put(sources[0], left + pair, at, size)
    lines = fields * span
    for level, rows in enumerate(levels_of(lines)):
        for at, size in blocks(rows, 8):
            down = get(downs[level], MERGE_DOWN, at, size)
            merged, w = merge_source(down, *get_both(sources[level], SOURCE, at, size))
            put(sources[level + 1], merged, at, size)
            put(wall_ws[level], w, at, size)
    not_first, not_last = open_ends("normal")
    for v, keep in enumerate((not_first, None, None, not_last)):
        value = sources[-1][v]
        packed[pl.ds(v * lines, lines), :] = value if keep is None else value * keep


def wall_up(fields, span, cells, bits, *refs):
    own_matrix, down_in, outer_in, own, bundle, other, share = refs[0:7]
    refs = refs[7:]
    round_ups, round_ws, refs = refs[: bits + 1], refs[bits + 1 : 2 * bits + 1], refs[2 * bits + 1 :]
    chunk_up, chunk_w, ups, ws = refs[0], refs[1], refs[2:5], refs[5:8]
    update = refs[8]
    ends, result, sems = refs[9:13], refs[13], refs[14]
    lines = fields * span
    second, upper = is_second("normal", bits), is_second("normal", bits + 1)
    for at, size in blocks(lines, 8):
        down, factors = get(down_in, MERGE_DOWN, at, size), get(outer_in, 12, at, size)
        part, outer, w = reduce_source(
            down,
            factors,
            second,
            upper,
            flat(own, SOURCE, lines, at, size),
            flat(other, SOURCE, lines, at, size),
        )
        opposite = flat(bundle, 6, lines, at, size)
        shares = plus(opposite[0:2], flat(share, 2, lines, at, size))
        matrix = plus(flat(own_matrix, 4, lines, at, size), opposite[2:6])
        centre = apply(inverse(*matrix), plus(part, shares))
        outer = minus(outer, apply(factors[0:4], apply(factors[4:8], centre)))
        left, right = choose(upper, centre, outer), choose(upper, outer, centre)
        between = inner(get(round_ups[bits], UP, at, size), w, left, right)
        left, right = choose(second, between, left), choose(second, right, between)
        left, right = round_down(round_ups, round_ws, "normal", bits, at, size, left, right)
        put(ends[0], left + right, at, size)
    last = split_all(ends[0], ends[1:], ups, ws, levels_of(lines))
    size = span * CHUNKS
    length = size * cells
    started = []
    for field in range(fields):
        at = field * size

        def store(i, value):
            result[pl.ds(at * cells + i, size, stride=cells), :] = value

        back_substitute(last, chunk_up, chunk_w, cells, at, size, store)
        rows = pl.ds(field * length, length)
        copy = pltpu.make_async_copy(result.at[rows], update.at[rows], sems.at[field])
        copy.start()
        started.append(copy)
    for copy in started:
        copy.wait()


def f32(*shape):
    return jax.ShapeDtypeStruct(shape, jnp.float32)


def vmem(*shape):
    return pltpu.VMEM(shape, jnp.float32)


IN_VMEM = pl.BlockSpec(memory_space=pltpu.VMEM)
IN_HBM = pl.BlockSpec(memory_space=pltpu.HBM)
PARAMS = pltpu.CompilerParams(vmem_limit_bytes=24 * 2**20)


def kernel(name, body, ins, outs, scratch, flops):
    in_bytes = sum(a.size * a.dtype.itemsize for a, _ in ins)
    out_bytes = sum(a.size * 4 for a, _ in outs)
    outputs = pl.pallas_call(
        body,
        out_shape=[a for a, _ in outs],
        in_specs=[spec for _, spec in ins],
        out_specs=[spec for _, spec in outs],
        scratch_shapes=scratch,
        compiler_params=PARAMS,
        cost_estimate=pl.CostEstimate(
            flops=flops, bytes_accessed=in_bytes + out_bytes, transcendentals=0
        ),
        name=name,
    )(*[a for a, _ in ins])
    return list(outputs)


def inside(arrays):
    return [(a, IN_VMEM) for a in arrays]


def outside(arrays):
    return [(pltpu.with_memory_space_constraint(a, pltpu.HBM), IN_HBM) for a in arrays]


def exchange(array, axis, mask):
    count = lax.axis_size(axis)
    return lax.ppermute(array, axis, [(i ^ mask, i) for i in range(count)])


def local(residual, courant_xi, courant_eta, dissip_xi, dissip_eta, coupling):
    fields, span, high, wide = residual.shape
    lanes = span * high
    wrap_cells, wall_cells = wide // CHUNKS, high // CHUNKS
    wrap_pairs, wall_pairs = (wrap_cells - 2) // 2, (wall_cells - 2) // 2
    wrap_count, wall_count = lax.axis_size("wrap"), lax.axis_size("normal")
    lines = fields * span
    wrap_levels, wall_levels = levels_of(fields), levels_of(lines)
    wrap_rows, wall_rows = fields * CHUNKS, lines * CHUNKS

    def rows_of(array):
        return array.reshape(-1, wide)

    wrap_bits = wrap_count.bit_length() - 3
    wall_bits = wall_count.bit_length() - 3
    results = kernel(
        "wrap_down",
        functools.partial(wrap_down, fields, wrap_cells),
        outside(
            [rows_of(a) for a in (residual, courant_xi, dissip_xi, courant_eta, dissip_eta)]
        ),
        inside(
            [
                f32(VALUES * fields, lanes),
                f32(wrap_pairs * UP, wrap_rows, lanes),
                f32(wrap_pairs * 2, wrap_rows, lanes),
            ]
            + [f32(UP, n, lanes) for n in wrap_levels]
            + [f32(2, n, lanes) for n in wrap_levels]
            + [f32(fields * lanes, wide), f32(lanes, wide)]
        ),
        [vmem(fields * lanes, wide)] * 2
        + [vmem(lanes, wide)]
        + [vmem(fields * wide, lanes)] * 2
        + [vmem(wide, lanes)]
        + [vmem(VALUES, n, lanes) for n in [wrap_rows] + wrap_levels]
        + [pltpu.SemaphoreType.DMA((6 * fields + 4,))],
        100 * residual.size,
    )
    element, wrap_factors, wall_inputs = results[0], results[1:9], results[9:11]
    results = kernel(
        "wall_matrix",
        functools.partial(wall_matrix, fields, span, wall_cells),
        inside(wall_inputs),
        inside(
            [
                f32(MATRIX * lines, wide),
                f32(wall_pairs * 2, span * CHUNKS, wide),
                f32(wall_pairs * UP, wall_rows, wide),
                f32(wall_pairs * CHUNK_DOWN, wall_rows, wide),
            ]
            + [f32(UP, n, wide) for n in wall_levels]
            + [f32(MERGE_DOWN, n, wide) for n in wall_levels]
        ),
        [vmem(MATRIX, n, wide) for n in [wall_rows] + wall_levels],
        100 * residual.size,
    )
    matrix, damps, chunk_up, chunk_down = results[0:4]
    wall_ups, wall_downs = results[4:7], results[7:10]
    wrap_ups, wrap_ws = [], []
    for bit in range(wrap_bits):
        element, up, w = kernel(
            f"wrap_round_{bit}",
            functools.partial(wrap_round, fields, bit),
            inside([element, exchange(element, "wrap", 1 << bit), damps]),
            inside([f32(VALUES * fields, lanes), f32(UP, fields, lanes), f32(2, fields, lanes)]),
            [],
            200 * fields * lanes,
        )
        wrap_ups.append(up)
        wrap_ws.append(w)
    swap = 1 if wrap_bits > 0 else 0
    wrap_others = [exchange(element, "wrap", mask << wrap_bits | swap) for mask in (1, 2, 3)]
    round_ups, round_downs = [], []
    for bit in range(wall_bits + 1):
        final = bit == wall_bits
        matrix, up, down, *outer = kernel(
            f"wall_round_{bit}",
            functools.partial(wall_round, lines, bit, final),
            inside([matrix, exchange(matrix, "normal", 1 << bit)]),
            inside(
                [
                    f32((4 if final else MATRIX) * lines, wide),
                    f32(UP, lines, wide),
                    f32(MERGE_DOWN, lines, wide),
                ]
                + ([f32(12, lines, wide)] if final else [])
            ),
            [],
            200 * lines * wide,
        )
        round_ups.append(up)
        round_downs.append(down)
    source, *wall_ws = kernel(
        "middle",
        functools.partial(middle, fields, span, wrap_cells, wall_cells, wrap_bits),
        inside(
            [element]
            + wrap_others
            + wrap_ups
            + wrap_ws
            + wrap_factors
            + [coupling.reshape(fields, fields, lanes, wide), damps, chunk_down]
            + wall_downs
        ),
        inside(
            [f32(SOURCE * lines, wide), f32(wall_pairs * 2, wall_rows, wide)]
            + [f32(2, n, wide) for n in wall_levels]
        ),
        [vmem(4, n, lanes) for n in reversed([wrap_rows] + wrap_levels)]
        + [vmem(fields * wide, lanes), vmem(fields * lanes, wide), vmem(fields * lanes, wide)]
        + [vmem(SOURCE, n, wide) for n in [wall_rows] + wall_levels],
        100 * residual.size,
    )
    round_ws = []
    for bit in range(wall_bits):
        source, w = kernel(
            f"wall_source_round_{bit}",
            functools.partial(wall_source_round, lines, bit),
            inside([source, exchange(source, "normal", 1 << bit), round_downs[bit]]),
            inside([f32(SOURCE * lines, wide), f32(2, lines, wide)]),
            [],
            50 * lines * wide,
        )
        round_ws.append(w)
    share, bundle, source = kernel(
        "wall_share",
        functools.partial(wall_share, lines, wall_bits),
        inside([source, round_downs[wall_bits]] + outer + [matrix]),
        inside([f32(SOURCE * lines, wide), f32(6 * lines, wide), f32(SOURCE * lines, wide)]),
        [],
        50 * lines * wide,
    )
    (update,) = kernel(
        "wall_up",
        functools.partial(wall_up, fields, span, wall_cells, wall_bits),
        inside(
            [matrix, round_downs[wall_bits]]
            + outer
            + [
                source,
                exchange(bundle, "normal", 2 << wall_bits),
                exchange(source, "normal", 1 << wall_bits),
                exchange(share, "normal", 3 << wall_bits),
            ]
            + round_ups
            + round_ws
            + [chunk_up, wall_ws[0]]
            + wall_ups
            + wall_ws[1:]
        ),
        [(f32(fields * lanes, wide), IN_HBM)],
        [vmem(4, n, wide) for n in reversed([wall_rows] + wall_levels)]
        + [vmem(fields * lanes, wide), pltpu.SemaphoreType.DMA((fields,))],
        30 * residual.size,
    )
    return update.reshape(residual.shape)


def solution(mesh):
    placed = (
        P(None, None, "normal", "wrap"),
        P(None, None, "normal", "wrap"),
        P(None, None, "normal", "wrap"),
        P(None, "normal", "wrap"),
        P(None, "normal", "wrap"),
        P(None, None, None, "normal", "wrap"),
    )
    return jax.shard_map(
        local,
        mesh=mesh,
        in_specs=placed,
        out_specs=P(None, None, "normal", "wrap"),
        check_vma=False,
    )
```

```python
import functools

import jax
import jax.numpy as jnp
from jax import lax
from jax.experimental import pallas as pl
from jax.experimental.pallas import tpu as pltpu
from jax.sharding import PartitionSpec as P

MATRIX = 16
SOURCE = 4
VALUES = MATRIX + SOURCE
UP = 8
CHUNK_DOWN = 9
MERGE_DOWN = 12
CHUNKS = 8


def inverse(a, b, c, d):
    scale = 1.0 / (a * d - b * c)
    return (d * scale, -b * scale, -c * scale, a * scale)


def times(x, y):
    return (
        x[0] * y[0] + x[1] * y[2],
        x[0] * y[1] + x[1] * y[3],
        x[2] * y[0] + x[3] * y[2],
        x[2] * y[1] + x[3] * y[3],
    )


def apply(x, v):
    return (x[0] * v[0] + x[1] * v[1], x[2] * v[0] + x[3] * v[1])


def minus(x, y):
    return tuple(a - b for a, b in zip(x, y))


def plus(x, y):
    return tuple(a + b for a, b in zip(x, y))


def negative(x):
    return tuple(-a for a in x)


def quads(element):
    return (element[0:4], element[4:8], element[8:12], element[12:16])


def merge_matrix(first, second):
    ll, lm, ml, mm = quads(first)
    nn, mr, rm, rr = quads(second)
    pivot = inverse(*plus(mm, nn))
    wl = times(pivot, ml)
    wr = times(pivot, mr)
    merged = (
        minus(ll, times(lm, wl))
        + negative(times(lm, wr))
        + negative(times(rm, wl))
        + minus(rr, times(rm, wr))
    )
    return merged, wl + wr, pivot + lm + rm


def merge_source(down, first, second):
    pivot, lm, rm = down[0:4], down[4:8], down[8:12]
    w = apply(pivot, plus(first[2:4], second[0:2]))
    return minus(first[0:2], apply(lm, w)) + minus(second[2:4], apply(rm, w)), w


def merge(first, second):
    matrix, up, down = merge_matrix(first[:MATRIX], second[:MATRIX])
    source, w = merge_source(down, first[MATRIX:], second[MATRIX:])
    return matrix + source, up, w


def inner(up, w, left, right):
    return minus(minus(w, apply(up[0:4], left)), apply(up[4:8], right))


def chunk_matrix(speed, damp, cells):
    def link(i):
        p = 2.0 * (damp(i) + damp(i + 1))
        q = 0.25 * (speed(i) + speed(i + 1))
        return q - p, -q - p

    def centre(i):
        return 1.0 + damp(i - 1) + 4.0 * damp(i) + damp(i + 1)

    b0, b1 = damp(0), damp(1)
    quarter = 0.25 * speed(0)
    up, low = link(0)
    zero = jnp.zeros_like(b0)
    ll = (b0, quarter - 2.0 * b0, -quarter - 2.0 * b0, 1.0 + 4.0 * b0 + b1)
    lk = (b0, zero, up, b1)
    kl = (b0, low, zero, b1)
    up, low = link(1)
    kk = (centre(1), up, low, centre(2))
    pairs = (cells - 2) // 2
    for k in range(1, pairs + 1):
        i = 2 * k
        pivot = inverse(*kk)
        wl = times(pivot, kl)
        up, low = link(i)
        here, there = damp(i), damp(i + 1)
        wr = (
            pivot[0] * here + pivot[1] * up,
            pivot[1] * there,
            pivot[2] * here + pivot[3] * up,
            pivot[3] * there,
        )
        yield wl + wr, pivot + lk + (low,), (here, there)

        def below(x):
            return (
                here * x[0] + low * x[2],
                here * x[1] + low * x[3],
                there * x[2],
                there * x[3],
            )

        ll = minus(ll, times(lk, wl))
        lk = negative(times(lk, wr))
        kl = negative(below(wl))
        if k < pairs:
            up, low_next = link(i + 1)
            kk = (centre(i + 1), up, low_next, centre(i + 2))
        else:
            quarter = 0.25 * speed(i + 1)
            kk = (
                1.0 + here + 4.0 * there,
                quarter - 2.0 * there,
                -quarter - 2.0 * there,
                there,
            )
        kk = minus(kk, below(wr))
    yield ll + lk + kl + kk


def pair_source(down, damps, left, pair, following):
    pivot, lk, low = down[0:4], down[4:8], down[8]
    w = apply(pivot, pair)
    left = minus(left, apply(lk, w))
    following = minus(following, (damps[0] * w[0] + low * w[1], damps[1] * w[1]))
    return left, following, w


def pair_of(source, k, cells):
    if k == (cells - 2) // 2:
        last = source(cells - 1)
        return (last, jnp.zeros_like(last))
    return (source(2 * k + 1), source(2 * k + 2))


def first_pair(source):
    first = source(0)
    return (jnp.zeros_like(first), first)


def blocks(rows, size):
    return [(at, min(size, rows - at)) for at in range(0, rows, size)]


def get(ref, count, at, size, base=0):
    return tuple(ref[base + v, pl.ds(at, size), :] for v in range(count))


def put(ref, values, at, size, base=0):
    for v, value in enumerate(values):
        ref[base + v, pl.ds(at, size), :] = value


def get_both(ref, count, at, size):
    return tuple(
        tuple(ref[v, pl.ds(2 * at + half, size, stride=2), :] for v in range(count))
        for half in (0, 1)
    )


def levels_of(lines):
    sizes = []
    rows = lines * CHUNKS
    while rows > lines:
        rows //= 2
        sizes.append(rows)
    return sizes


def split_all(top_ref, end_refs, up_refs, w_refs, sizes):
    source = top_ref
    for rows, target, ups, ws in zip(
        reversed(sizes), end_refs, reversed(up_refs), reversed(w_refs)
    ):
        for at, size in blocks(rows, 8):
            ends = get(source, 4, at, size)
            left, right = ends[0:2], ends[2:4]
            middle = inner(get(ups, UP, at, size), get(ws, 2, at, size), left, right)
            for v in range(2):
                target[v, pl.ds(2 * at, size, stride=2), :] = left[v]
                target[v, pl.ds(2 * at + 1, size, stride=2), :] = middle[v]
                target[2 + v, pl.ds(2 * at, size, stride=2), :] = middle[v]
                target[2 + v, pl.ds(2 * at + 1, size, stride=2), :] = right[v]
        source = target
    return source


def back_substitute(ends_ref, up_ref, w_ref, cells, at, size, store):
    ends = get(ends_ref, 4, at, size)
    left, following = ends[0:2], ends[2:4]
    store(0, left[1])
    store(cells - 1, following[0])
    for k in range((cells - 2) // 2 - 1, -1, -1):
        following = inner(
            get(up_ref, UP, at, size, k * UP), get(w_ref, 2, at, size, k * 2), left, following
        )
        store(2 * k + 1, following[0])
        store(2 * k + 2, following[1])


def close_ring(own, rest):
    ll, lr, rl, rr = quads(own)
    nn, nm, mn, mm = quads(rest)
    b = plus(lr, mn)
    c = plus(rl, nm)
    pivot = inverse(*plus(rr, nn))
    f = plus(own[16:18], rest[18:20])
    g = plus(own[18:20], rest[16:18])
    bd = times(b, pivot)
    left = apply(inverse(*minus(plus(ll, mm), times(bd, c))), minus(f, apply(bd, g)))
    right = apply(pivot, minus(g, apply(c, left)))
    return left, right


def open_ends(axis):
    place = lax.axis_index(axis)
    last = lax.axis_size(axis) - 1
    return jnp.where(place > 0, 1.0, 0.0), jnp.where(place < last, 1.0, 0.0)


def is_second(axis, bit):
    return lax.rem(lax.axis_index(axis) // (1 << bit), 2) == 1


def choose(second, one, other):
    return tuple(jnp.where(second, a, b) for a, b in zip(one, other))


def flat(ref, count, rows, at, size):
    return tuple(ref[pl.ds(v * rows + at, size), :] for v in range(count))


def put_flat(ref, values, rows, at, size):
    for v, value in enumerate(values):
        ref[pl.ds(v * rows + at, size), :] = value


def round_down(ups, ws, axis, bits, at, size, left, right):
    for bit in reversed(range(bits)):
        middle = inner(get(ups[bit], UP, at, size), get(ws[bit], 2, at, size), left, right)
        second = is_second(axis, bit)
        left, right = choose(second, middle, left), choose(second, right, middle)
    return left, right


def copies(pairs, sems, first=0):
    started = []
    for i, (source, target) in enumerate(pairs):
        copy = pltpu.make_async_copy(source, target, sems.at[first + i])
        copy.start()
        started.append(copy)
    return started


def wrap_down(fields, cells, *refs):
    residual, courant, dissip, wall_courant, wall_dissip = refs[0:5]
    packed, chunk_up, chunk_w = refs[5:8]
    ups, ws = refs[8:11], refs[11:14]
    wall_speed, wall_damp = refs[14:16]
    source_in, speed_in, damp_in, source_t, speed_t, damp_t = refs[16:22]
    elements, sems = refs[22:26], refs[26]
    lanes = damp_in.shape[0]
    length = cells * CHUNKS
    rows_of = [pl.ds(field * lanes, lanes) for field in range(fields)]
    moves = [(dissip, damp_in)]
    for rows in rows_of:
        moves.append((courant.at[rows], speed_in.at[rows]))
        moves.append((residual.at[rows], source_in.at[rows]))
    moves.append((wall_dissip, wall_damp))
    moves += [(wall_courant.at[rows], wall_speed.at[rows]) for rows in rows_of]
    started = copies(moves, sems)
    started[0].wait()
    damp_t[...] = damp_in[...].T
    for field in range(fields):
        started[1 + 2 * field].wait()
        speed_t[pl.ds(field * length, length), :] = speed_in[pl.ds(field * lanes, lanes), :].T
        started[2 + 2 * field].wait()
        source_t[pl.ds(field * length, length), :] = source_in[pl.ds(field * lanes, lanes), :].T
    for at, size in blocks(fields * CHUNKS, 16):
        repeat = size // CHUNKS

        def speed(i):
            return speed_t[pl.ds(at * cells + i, size, stride=cells), :]

        def source(i):
            return source_t[pl.ds(at * cells + i, size, stride=cells), :]

        def damp(i):
            rows = damp_t[pl.ds(i, CHUNKS, stride=cells), :]
            return jnp.concatenate([rows] * repeat, axis=0) if repeat > 1 else rows

        left, pair = first_pair(source), pair_of(source, 0, cells)
        for k, step in enumerate(chunk_matrix(speed, damp, cells)):
            if k == (cells - 2) // 2:
                put(elements[0], step + left + pair, at, size)
                break
            up, down, damps = step
            left, pair, w = pair_source(down, damps, left, pair, pair_of(source, k + 1, cells))
            put(chunk_up, up, at, size, k * UP)
            put(chunk_w, w, at, size, k * 2)
    for level, rows in enumerate(levels_of(fields)):
        for at, size in blocks(rows, 8):
            merged, up, w = merge(*get_both(elements[level], VALUES, at, size))
            put(elements[level + 1], merged, at, size)
            put(ups[level], up, at, size)
            put(ws[level], w, at, size)
    for v in range(VALUES):
        packed[pl.ds(v * fields, fields), :] = elements[-1][v]
    for copy in started[1 + 2 * fields :]:
        copy.wait()


def wrap_round(fields, bit, own, other, after, packed, up_out, w_out):
    second = is_second("wrap", bit)
    for at, size in blocks(fields, 8):
        mine = flat(own, VALUES, fields, at, size)
        theirs = flat(other, VALUES, fields, at, size)
        merged, up, w = merge(choose(second, theirs, mine), choose(second, mine, theirs))
        put_flat(packed, merged, fields, at, size)
        put(up_out, up, at, size)
        put(w_out, w, at, size)


def wall_matrix(fields, span, cells, *refs):
    speed_in, damp_in = refs[0:2]
    packed, damp_out, chunk_up, chunk_down = refs[2:6]
    ups, downs = refs[6:9], refs[9:12]
    elements = refs[12:16]
    size = span * CHUNKS
    for field in range(fields):
        at = field * size

        def speed(i):
            return speed_in[pl.ds(at * cells + i, size, stride=cells), :]

        def damp(i):
            return damp_in[pl.ds(i, size, stride=cells), :]

        for k, step in enumerate(chunk_matrix(speed, damp, cells)):
            if k == (cells - 2) // 2:
                put(elements[0], step, at, size)
                break
            up, down, damps = step
            put(chunk_up, up, at, size, k * UP)
            put(chunk_down, down, at, size, k * CHUNK_DOWN)
            if field == 0:
                put(damp_out, damps, 0, size, k * 2)
    lines = fields * span
    for level, rows in enumerate(levels_of(lines)):
        for at, size in blocks(rows, 8):
            merged, up, down = merge_matrix(*get_both(elements[level], MATRIX, at, size))
            put(elements[level + 1], merged, at, size)
            put(ups[level], up, at, size)
            put(downs[level], down, at, size)
    not_first, not_last = open_ends("normal")
    for v in range(MATRIX):
        value = elements[-1][v]
        if v in (0, 1, 2, 4, 5, 8, 10):
            value = value * not_first
        if v in (5, 7, 10, 11, 13, 14, 15):
            value = value * not_last
        packed[pl.ds(v * lines, lines), :] = value


def wall_round(lines, bit, final, own, other, *refs):
    started = []
    if final:
        coupling, packed, up_out, down_out, outer_out, coupling_out, sems = refs
        started = copies(
            [(coupling.at[k], coupling_out.at[k]) for k in range(coupling.shape[0])], sems
        )
    else:
        packed, up_out, down_out = refs
    second = is_second("normal", bit)
    upper = is_second("normal", bit + 1)
    for at, size in blocks(lines, 8):
        mine = flat(own, MATRIX, lines, at, size)
        theirs = flat(other, MATRIX, lines, at, size)
        merged, up, down = merge_matrix(
            choose(second, theirs, mine), choose(second, mine, theirs)
        )
        put(up_out, up, at, size)
        put(down_out, down, at, size)
        if not final:
            put_flat(packed, merged, lines, at, size)
            continue
        ll, lr, rl, rr = quads(merged)
        outer, into = choose(upper, rr, ll), choose(upper, rl, lr)
        out, middle = choose(upper, lr, rl), choose(upper, ll, rr)
        is_upper = jnp.where(upper, 1.0, 0.0)
        pivot = inverse(
            outer[0] + (1.0 - is_upper), outer[1], outer[2], outer[3] + is_upper
        )
        put_flat(packed, minus(middle, times(out, times(pivot, into))), lines, at, size)
        put(outer_out, pivot + into + out, at, size)
    for copy in started:
        copy.wait()


def wall_source_round(lines, bit, own, other, down_in, packed, w_out):
    second = is_second("normal", bit)
    for at, size in blocks(lines, 8):
        mine = flat(own, SOURCE, lines, at, size)
        theirs = flat(other, SOURCE, lines, at, size)
        merged, w = merge_source(
            get(down_in, MERGE_DOWN, at, size),
            choose(second, theirs, mine),
            choose(second, mine, theirs),
        )
        put_flat(packed, merged, lines, at, size)
        put(w_out, w, at, size)


def reduce_source(down, factors, second, upper, mine, theirs):
    merged, w = merge_source(
        down, choose(second, theirs, mine), choose(second, mine, theirs)
    )
    outer = apply(factors[0:4], choose(upper, merged[2:4], merged[0:2]))
    centre = choose(upper, merged[0:2], merged[2:4])
    return minus(centre, apply(factors[8:12], outer)), outer, w


def wall_share(lines, bit, own, down_in, outer_in, matrix, share, bundle, copy):
    share[pl.ds(2 * lines, 2 * lines), :] = jnp.zeros((2 * lines, share.shape[1]), jnp.float32)
    copy[...] = own[...]
    bundle[pl.ds(2 * lines, 4 * lines), :] = matrix[...]
    second, upper = is_second("normal", bit), is_second("normal", bit + 1)
    for at, size in blocks(lines, 8):
        mine = flat(own, SOURCE, lines, at, size)
        none = tuple(jnp.zeros_like(value) for value in mine)
        down, factors = get(down_in, MERGE_DOWN, at, size), get(outer_in, 12, at, size)
        part, _, _ = reduce_source(down, factors, second, upper, mine, none)
        put_flat(share, part, lines, at, size)
        put_flat(bundle, part, lines, at, size)


def middle(fields, span, wrap_cells, wall_cells, bits, *refs):
    own, others, refs = refs[0], refs[1:4], refs[4:]
    round_ups, round_ws, refs = refs[:bits], refs[bits : 2 * bits], refs[2 * bits :]
    chunk_up, chunk_w, ups, ws = refs[0], refs[1], refs[2:5], refs[5:8]
    coupling, damps_in, chunk_down, downs = refs[8], refs[9], refs[10], refs[11:14]
    packed, wall_w, wall_ws = refs[14], refs[15], refs[16:19]
    ends, solved_t, solved, mixed = refs[19:23], refs[23], refs[24], refs[25]
    sources = refs[26:30]

    for at, size in blocks(fields, 8):
        odd = is_second("wrap", bits)
        near, opposite, far = (flat(other, VALUES, fields, at, size) for other in others)
        following, before = choose(odd, far, near), choose(odd, near, far)
        rest = merge(merge(following, opposite)[0], before)[0]
        left, right = close_ring(flat(own, VALUES, fields, at, size), rest)
        left, right = round_down(round_ups, round_ws, "wrap", bits, at, size, left, right)
        put(ends[0], left + right, at, size)
    last = split_all(ends[0], ends[1:], ups, ws, levels_of(fields))
    length = wrap_cells * CHUNKS
    for at, size in blocks(fields * CHUNKS, 16):

        def store(i, value):
            solved_t[pl.ds(at * wrap_cells + i, size, stride=wrap_cells), :] = value

        back_substitute(last, chunk_up, chunk_w, wrap_cells, at, size, store)
    lanes = solved.shape[0] // fields
    for field in range(fields):
        solved[pl.ds(field * lanes, lanes), :] = solved_t[pl.ds(field * length, length), :].T

    for at, size in blocks(lanes, 16):
        update = [solved[pl.ds(j * lanes + at, size), :] for j in range(fields)]
        for k in range(fields):
            total = coupling[k * fields, pl.ds(at, size), :].astype(jnp.float32) * update[0]
            for j in range(1, fields):
                factor = coupling[k * fields + j, pl.ds(at, size), :]
                total = total + factor.astype(jnp.float32) * update[j]
            mixed[pl.ds(k * lanes + at, size), :] = total

    pairs = (wall_cells - 2) // 2
    size = span * CHUNKS
    for field in range(fields):
        at = field * size

        def source(i):
            return mixed[pl.ds(at * wall_cells + i, size, stride=wall_cells), :]

        left, pair = first_pair(source), pair_of(source, 0, wall_cells)
        for k in range(pairs):
            left, pair, w = pair_source(
                get(chunk_down, CHUNK_DOWN, at, size, k * CHUNK_DOWN),
                get(damps_in, 2, 0, size, k * 2),
                left,
                pair,
                pair_of(source, k + 1, wall_cells),
            )
            put(wall_w, w, at, size, k * 2)
        put(sources[0], left + pair, at, size)
    lines = fields * span
    for level, rows in enumerate(levels_of(lines)):
        for at, size in blocks(rows, 8):
            down = get(downs[level], MERGE_DOWN, at, size)
            merged, w = merge_source(down, *get_both(sources[level], SOURCE, at, size))
            put(sources[level + 1], merged, at, size)
            put(wall_ws[level], w, at, size)
    not_first, not_last = open_ends("normal")
    for v, keep in enumerate((not_first, None, None, not_last)):
        value = sources[-1][v]
        packed[pl.ds(v * lines, lines), :] = value if keep is None else value * keep


def wall_up(fields, span, cells, bits, *refs):
    own_matrix, down_in, outer_in, own, bundle, other, share = refs[0:7]
    refs = refs[7:]
    round_ups, round_ws, refs = refs[: bits + 1], refs[bits + 1 : 2 * bits + 1], refs[2 * bits + 1 :]
    chunk_up, chunk_w, ups, ws = refs[0], refs[1], refs[2:5], refs[5:8]
    update = refs[8]
    ends, result, sems = refs[9:13], refs[13], refs[14]
    lines = fields * span
    second, upper = is_second("normal", bits), is_second("normal", bits + 1)
    for at, size in blocks(lines, 8):
        down, factors = get(down_in, MERGE_DOWN, at, size), get(outer_in, 12, at, size)
        part, outer, w = reduce_source(
            down,
            factors,
            second,
            upper,
            flat(own, SOURCE, lines, at, size),
            flat(other, SOURCE, lines, at, size),
        )
        opposite = flat(bundle, 6, lines, at, size)
        shares = plus(opposite[0:2], flat(share, 2, lines, at, size))
        matrix = plus(flat(own_matrix, 4, lines, at, size), opposite[2:6])
        centre = apply(inverse(*matrix), plus(part, shares))
        outer = minus(outer, apply(factors[0:4], apply(factors[4:8], centre)))
        left, right = choose(upper, centre, outer), choose(upper, outer, centre)
        between = inner(get(round_ups[bits], UP, at, size), w, left, right)
        left, right = choose(second, between, left), choose(second, right, between)
        left, right = round_down(round_ups, round_ws, "normal", bits, at, size, left, right)
        put(ends[0], left + right, at, size)
    last = split_all(ends[0], ends[1:], ups, ws, levels_of(lines))
    size = span * CHUNKS
    length = size * cells
    started = []
    for field in range(fields):
        at = field * size

        def store(i, value):
            result[pl.ds(at * cells + i, size, stride=cells), :] = value

        back_substitute(last, chunk_up, chunk_w, cells, at, size, store)
        rows = pl.ds(field * length, length)
        copy = pltpu.make_async_copy(result.at[rows], update.at[rows], sems.at[field])
        copy.start()
        started.append(copy)
    for copy in started:
        copy.wait()


def f32(*shape):
    return jax.ShapeDtypeStruct(shape, jnp.float32)


def vmem(*shape):
    return pltpu.VMEM(shape, jnp.float32)


IN_VMEM = pl.BlockSpec(memory_space=pltpu.VMEM)
IN_HBM = pl.BlockSpec(memory_space=pltpu.HBM)
PARAMS = pltpu.CompilerParams(vmem_limit_bytes=24 * 2**20)


def kernel(name, body, ins, outs, scratch, flops):
    in_bytes = sum(a.size * a.dtype.itemsize for a, _ in ins)
    out_bytes = sum(a.size * 4 for a, _ in outs)
    outputs = pl.pallas_call(
        body,
        out_shape=[a for a, _ in outs],
        in_specs=[spec for _, spec in ins],
        out_specs=[spec for _, spec in outs],
        scratch_shapes=scratch,
        compiler_params=PARAMS,
        cost_estimate=pl.CostEstimate(
            flops=flops, bytes_accessed=in_bytes + out_bytes, transcendentals=0
        ),
        name=name,
    )(*[a for a, _ in ins])
    return list(outputs)


def inside(arrays):
    return [(a, IN_VMEM) for a in arrays]


def outside(arrays):
    return [(pltpu.with_memory_space_constraint(a, pltpu.HBM), IN_HBM) for a in arrays]


def exchange(array, axis, mask):
    count = lax.axis_size(axis)
    return lax.ppermute(array, axis, [(i ^ mask, i) for i in range(count)])


def local(residual, courant_xi, courant_eta, dissip_xi, dissip_eta, coupling):
    fields, span, high, wide = residual.shape
    lanes = span * high
    wrap_cells, wall_cells = wide // CHUNKS, high // CHUNKS
    wrap_pairs, wall_pairs = (wrap_cells - 2) // 2, (wall_cells - 2) // 2
    wrap_count, wall_count = lax.axis_size("wrap"), lax.axis_size("normal")
    lines = fields * span
    wrap_levels, wall_levels = levels_of(fields), levels_of(lines)
    wrap_rows, wall_rows = fields * CHUNKS, lines * CHUNKS

    def rows_of(array):
        return array.reshape(-1, wide)

    wrap_bits = wrap_count.bit_length() - 3
    wall_bits = wall_count.bit_length() - 3
    results = kernel(
        "wrap_down",
        functools.partial(wrap_down, fields, wrap_cells),
        outside(
            [rows_of(a) for a in (residual, courant_xi, dissip_xi, courant_eta, dissip_eta)]
        ),
        inside(
            [
                f32(VALUES * fields, lanes),
                f32(wrap_pairs * UP, wrap_rows, lanes),
                f32(wrap_pairs * 2, wrap_rows, lanes),
            ]
            + [f32(UP, n, lanes) for n in wrap_levels]
            + [f32(2, n, lanes) for n in wrap_levels]
            + [f32(fields * lanes, wide), f32(lanes, wide)]
        ),
        [vmem(fields * lanes, wide)] * 2
        + [vmem(lanes, wide)]
        + [vmem(fields * wide, lanes)] * 2
        + [vmem(wide, lanes)]
        + [vmem(VALUES, n, lanes) for n in [wrap_rows] + wrap_levels]
        + [pltpu.SemaphoreType.DMA((3 * fields + 2,))],
        100 * residual.size,
    )
    element, wrap_factors, wall_inputs = results[0], results[1:9], results[9:11]
    results = kernel(
        "wall_matrix",
        functools.partial(wall_matrix, fields, span, wall_cells),
        inside(wall_inputs),
        inside(
            [
                f32(MATRIX * lines, wide),
                f32(wall_pairs * 2, span * CHUNKS, wide),
                f32(wall_pairs * UP, wall_rows, wide),
                f32(wall_pairs * CHUNK_DOWN, wall_rows, wide),
            ]
            + [f32(UP, n, wide) for n in wall_levels]
            + [f32(MERGE_DOWN, n, wide) for n in wall_levels]
        ),
        [vmem(MATRIX, n, wide) for n in [wall_rows] + wall_levels],
        100 * residual.size,
    )
    matrix, damps, chunk_up, chunk_down = results[0:4]
    wall_ups, wall_downs = results[4:7], results[7:10]
    wrap_ups, wrap_ws = [], []
    for bit in range(wrap_bits):
        element, up, w = kernel(
            f"wrap_round_{bit}",
            functools.partial(wrap_round, fields, bit),
            inside([element, exchange(element, "wrap", 1 << bit), damps]),
            inside([f32(VALUES * fields, lanes), f32(UP, fields, lanes), f32(2, fields, lanes)]),
            [],
            200 * fields * lanes,
        )
        wrap_ups.append(up)
        wrap_ws.append(w)
    swap = 1 if wrap_bits > 0 else 0
    wrap_others = [exchange(element, "wrap", mask << wrap_bits | swap) for mask in (1, 2, 3)]
    round_ups, round_downs = [], []
    for bit in range(wall_bits + 1):
        final = bit == wall_bits
        matrix, up, down, *extra = kernel(
            f"wall_round_{bit}",
            functools.partial(wall_round, lines, bit, final),
            inside([matrix, exchange(matrix, "normal", 1 << bit)])
            + (outside([coupling.reshape(fields * fields, lanes, wide)]) if final else []),
            inside(
                [
                    f32((4 if final else MATRIX) * lines, wide),
                    f32(UP, lines, wide),
                    f32(MERGE_DOWN, lines, wide),
                ]
                + (
                    [
                        f32(12, lines, wide),
                        jax.ShapeDtypeStruct((fields * fields, lanes, wide), coupling.dtype),
                    ]
                    if final
                    else []
                )
            ),
            [pltpu.SemaphoreType.DMA((fields * fields,))] if final else [],
            200 * lines * wide,
        )
        round_ups.append(up)
        round_downs.append(down)
    outer, coupling_in = extra[:1], extra[1]
    source, *wall_ws = kernel(
        "middle",
        functools.partial(middle, fields, span, wrap_cells, wall_cells, wrap_bits),
        inside(
            [element]
            + wrap_others
            + wrap_ups
            + wrap_ws
            + wrap_factors
            + [coupling_in, damps, chunk_down]
            + wall_downs
        ),
        inside(
            [f32(SOURCE * lines, wide), f32(wall_pairs * 2, wall_rows, wide)]
            + [f32(2, n, wide) for n in wall_levels]
        ),
        [vmem(4, n, lanes) for n in reversed([wrap_rows] + wrap_levels)]
        + [vmem(fields * wide, lanes), vmem(fields * lanes, wide), vmem(fields * lanes, wide)]
        + [vmem(SOURCE, n, wide) for n in [wall_rows] + wall_levels],
        100 * residual.size,
    )
    round_ws = []
    for bit in range(wall_bits):
        source, w = kernel(
            f"wall_source_round_{bit}",
            functools.partial(wall_source_round, lines, bit),
            inside([source, exchange(source, "normal", 1 << bit), round_downs[bit]]),
            inside([f32(SOURCE * lines, wide), f32(2, lines, wide)]),
            [],
            50 * lines * wide,
        )
        round_ws.append(w)
    share, bundle, source = kernel(
        "wall_share",
        functools.partial(wall_share, lines, wall_bits),
        inside([source, round_downs[wall_bits]] + outer + [matrix]),
        inside([f32(SOURCE * lines, wide), f32(6 * lines, wide), f32(SOURCE * lines, wide)]),
        [],
        50 * lines * wide,
    )
    (update,) = kernel(
        "wall_up",
        functools.partial(wall_up, fields, span, wall_cells, wall_bits),
        inside(
            [matrix, round_downs[wall_bits]]
            + outer
            + [
                source,
                exchange(bundle, "normal", 2 << wall_bits),
                exchange(source, "normal", 1 << wall_bits),
                exchange(share, "normal", 3 << wall_bits),
            ]
            + round_ups
            + round_ws
            + [chunk_up, wall_ws[0]]
            + wall_ups
            + wall_ws[1:]
        ),
        [(f32(fields * lanes, wide), IN_HBM)],
        [vmem(4, n, wide) for n in reversed([wall_rows] + wall_levels)]
        + [vmem(fields * lanes, wide), pltpu.SemaphoreType.DMA((fields,))],
        30 * residual.size,
    )
    return update.reshape(residual.shape)


def solution(mesh):
    placed = (
        P(None, None, "normal", "wrap"),
        P(None, None, "normal", "wrap"),
        P(None, None, "normal", "wrap"),
        P(None, "normal", "wrap"),
        P(None, "normal", "wrap"),
        P(None, None, None, "normal", "wrap"),
    )
    return jax.shard_map(
        local,
        mesh=mesh,
        in_specs=placed,
        out_specs=P(None, None, "normal", "wrap"),
        check_vma=False,
    )
```

```python
import functools

import jax
import jax.numpy as jnp
from jax import lax
from jax.experimental import pallas as pl
from jax.experimental.pallas import tpu as pltpu
from jax.sharding import PartitionSpec as P

MATRIX = 16
SOURCE = 4
VALUES = MATRIX + SOURCE
UP = 8
CHUNK_DOWN = 9
MERGE_DOWN = 12
CHUNKS = 8


def inverse(a, b, c, d):
    scale = 1.0 / (a * d - b * c)
    return (d * scale, -b * scale, -c * scale, a * scale)


def times(x, y):
    return (
        x[0] * y[0] + x[1] * y[2],
        x[0] * y[1] + x[1] * y[3],
        x[2] * y[0] + x[3] * y[2],
        x[2] * y[1] + x[3] * y[3],
    )


def apply(x, v):
    return (x[0] * v[0] + x[1] * v[1], x[2] * v[0] + x[3] * v[1])


def minus(x, y):
    return tuple(a - b for a, b in zip(x, y))


def plus(x, y):
    return tuple(a + b for a, b in zip(x, y))


def negative(x):
    return tuple(-a for a in x)


def quads(element):
    return (element[0:4], element[4:8], element[8:12], element[12:16])


def merge_matrix(first, second):
    ll, lm, ml, mm = quads(first)
    nn, mr, rm, rr = quads(second)
    pivot = inverse(*plus(mm, nn))
    wl = times(pivot, ml)
    wr = times(pivot, mr)
    merged = (
        minus(ll, times(lm, wl))
        + negative(times(lm, wr))
        + negative(times(rm, wl))
        + minus(rr, times(rm, wr))
    )
    return merged, wl + wr, pivot + lm + rm


def merge_source(down, first, second):
    pivot, lm, rm = down[0:4], down[4:8], down[8:12]
    w = apply(pivot, plus(first[2:4], second[0:2]))
    return minus(first[0:2], apply(lm, w)) + minus(second[2:4], apply(rm, w)), w


def merge(first, second):
    matrix, up, down = merge_matrix(first[:MATRIX], second[:MATRIX])
    source, w = merge_source(down, first[MATRIX:], second[MATRIX:])
    return matrix + source, up, w


def inner(up, w, left, right):
    return minus(minus(w, apply(up[0:4], left)), apply(up[4:8], right))


def chunk_matrix(speed, damp, cells):
    def link(i):
        p = 2.0 * (damp(i) + damp(i + 1))
        q = 0.25 * (speed(i) + speed(i + 1))
        return q - p, -q - p

    def centre(i):
        return 1.0 + damp(i - 1) + 4.0 * damp(i) + damp(i + 1)

    b0, b1 = damp(0), damp(1)
    quarter = 0.25 * speed(0)
    up, low = link(0)
    zero = jnp.zeros_like(b0)
    ll = (b0, quarter - 2.0 * b0, -quarter - 2.0 * b0, 1.0 + 4.0 * b0 + b1)
    lk = (b0, zero, up, b1)
    kl = (b0, low, zero, b1)
    up, low = link(1)
    kk = (centre(1), up, low, centre(2))
    pairs = (cells - 2) // 2
    for k in range(1, pairs + 1):
        i = 2 * k
        pivot = inverse(*kk)
        wl = times(pivot, kl)
        up, low = link(i)
        here, there = damp(i), damp(i + 1)
        wr = (
            pivot[0] * here + pivot[1] * up,
            pivot[1] * there,
            pivot[2] * here + pivot[3] * up,
            pivot[3] * there,
        )
        yield wl + wr, pivot + lk + (low,), (here, there)

        def below(x):
            return (
                here * x[0] + low * x[2],
                here * x[1] + low * x[3],
                there * x[2],
                there * x[3],
            )

        ll = minus(ll, times(lk, wl))
        lk = negative(times(lk, wr))
        kl = negative(below(wl))
        if k < pairs:
            up, low_next = link(i + 1)
            kk = (centre(i + 1), up, low_next, centre(i + 2))
        else:
            quarter = 0.25 * speed(i + 1)
            kk = (
                1.0 + here + 4.0 * there,
                quarter - 2.0 * there,
                -quarter - 2.0 * there,
                there,
            )
        kk = minus(kk, below(wr))
    yield ll + lk + kl + kk


def pair_source(down, damps, left, pair, following):
    pivot, lk, low = down[0:4], down[4:8], down[8]
    w = apply(pivot, pair)
    left = minus(left, apply(lk, w))
    following = minus(following, (damps[0] * w[0] + low * w[1], damps[1] * w[1]))
    return left, following, w


def pair_of(source, k, cells):
    if k == (cells - 2) // 2:
        last = source(cells - 1)
        return (last, jnp.zeros_like(last))
    return (source(2 * k + 1), source(2 * k + 2))


def first_pair(source):
    first = source(0)
    return (jnp.zeros_like(first), first)


def blocks(rows, size):
    return [(at, min(size, rows - at)) for at in range(0, rows, size)]


def get(ref, count, at, size, base=0):
    return tuple(ref[base + v, pl.ds(at, size), :] for v in range(count))


def put(ref, values, at, size, base=0):
    for v, value in enumerate(values):
        ref[base + v, pl.ds(at, size), :] = value


def get_both(ref, count, at, size):
    return tuple(
        tuple(ref[v, pl.ds(2 * at + half, size, stride=2), :] for v in range(count))
        for half in (0, 1)
    )


def levels_of(lines):
    sizes = []
    rows = lines * CHUNKS
    while rows > lines:
        rows //= 2
        sizes.append(rows)
    return sizes


def split_all(top_ref, end_refs, up_refs, w_refs, sizes):
    source = top_ref
    for rows, target, ups, ws in zip(
        reversed(sizes), end_refs, reversed(up_refs), reversed(w_refs)
    ):
        for at, size in blocks(rows, 8):
            ends = get(source, 4, at, size)
            left, right = ends[0:2], ends[2:4]
            middle = inner(get(ups, UP, at, size), get(ws, 2, at, size), left, right)
            for v in range(2):
                target[v, pl.ds(2 * at, size, stride=2), :] = left[v]
                target[v, pl.ds(2 * at + 1, size, stride=2), :] = middle[v]
                target[2 + v, pl.ds(2 * at, size, stride=2), :] = middle[v]
                target[2 + v, pl.ds(2 * at + 1, size, stride=2), :] = right[v]
        source = target
    return source


def back_substitute(ends_ref, up_ref, w_ref, cells, at, size, store):
    ends = get(ends_ref, 4, at, size)
    left, following = ends[0:2], ends[2:4]
    store(0, left[1])
    store(cells - 1, following[0])
    for k in range((cells - 2) // 2 - 1, -1, -1):
        following = inner(
            get(up_ref, UP, at, size, k * UP), get(w_ref, 2, at, size, k * 2), left, following
        )
        store(2 * k + 1, following[0])
        store(2 * k + 2, following[1])


def close_ring(own, rest):
    ll, lr, rl, rr = quads(own)
    nn, nm, mn, mm = quads(rest)
    b = plus(lr, mn)
    c = plus(rl, nm)
    pivot = inverse(*plus(rr, nn))
    f = plus(own[16:18], rest[18:20])
    g = plus(own[18:20], rest[16:18])
    bd = times(b, pivot)
    left = apply(inverse(*minus(plus(ll, mm), times(bd, c))), minus(f, apply(bd, g)))
    right = apply(pivot, minus(g, apply(c, left)))
    return left, right


def open_ends(axis):
    place = lax.axis_index(axis)
    last = lax.axis_size(axis) - 1
    return jnp.where(place > 0, 1.0, 0.0), jnp.where(place < last, 1.0, 0.0)


def is_second(axis, bit):
    return lax.rem(lax.axis_index(axis) // (1 << bit), 2) == 1


def choose(second, one, other):
    return tuple(jnp.where(second, a, b) for a, b in zip(one, other))


def flat(ref, count, rows, at, size):
    return tuple(ref[pl.ds(v * rows + at, size), :] for v in range(count))


def put_flat(ref, values, rows, at, size):
    for v, value in enumerate(values):
        ref[pl.ds(v * rows + at, size), :] = value


def round_down(ups, ws, axis, bits, at, size, left, right):
    for bit in reversed(range(bits)):
        middle = inner(get(ups[bit], UP, at, size), get(ws[bit], 2, at, size), left, right)
        second = is_second(axis, bit)
        left, right = choose(second, middle, left), choose(second, right, middle)
    return left, right


def copies(pairs, sems, first=0):
    started = []
    for i, (source, target) in enumerate(pairs):
        copy = pltpu.make_async_copy(source, target, sems.at[first + i])
        copy.start()
        started.append(copy)
    return started


def wrap_down(fields, cells, *refs):
    residual, courant, dissip, wall_courant, wall_dissip = refs[0:5]
    packed, chunk_up, chunk_w = refs[5:8]
    ups, ws = refs[8:11], refs[11:14]
    wall_speed, wall_damp = refs[14:16]
    source_in, speed_in, damp_in, source_t, speed_t, damp_t = refs[16:22]
    elements, sems = refs[22:26], refs[26]
    lanes = damp_in.shape[0]
    length = cells * CHUNKS
    parts = [(0, 2), (2, fields)] if fields > 2 else [(0, fields)]
    moves = [(dissip, damp_in)]
    for first, last in parts:
        rows = pl.ds(first * lanes, (last - first) * lanes)
        moves.append((courant.at[rows], speed_in.at[rows]))
        moves.append((residual.at[rows], source_in.at[rows]))
    moves += [(wall_dissip, wall_damp), (wall_courant, wall_speed)]
    started = copies(moves, sems)
    started[0].wait()
    damp_t[...] = damp_in[...].T
    for part, (first, last) in enumerate(parts):
        at, size, repeat = first * CHUNKS, (last - first) * CHUNKS, last - first
        for inner_copy, taken, turned in (
            (started[1 + 2 * part], speed_in, speed_t),
            (started[2 + 2 * part], source_in, source_t),
        ):
            inner_copy.wait()
            for field in range(first, last):
                turned[pl.ds(field * length, length), :] = taken[pl.ds(field * lanes, lanes), :].T

        def speed(i):
            return speed_t[pl.ds(at * cells + i, size, stride=cells), :]

        def source(i):
            return source_t[pl.ds(at * cells + i, size, stride=cells), :]

        def damp(i):
            rows = damp_t[pl.ds(i, CHUNKS, stride=cells), :]
            return jnp.concatenate([rows] * repeat, axis=0) if repeat > 1 else rows

        left, pair = first_pair(source), pair_of(source, 0, cells)
        for k, step in enumerate(chunk_matrix(speed, damp, cells)):
            if k == (cells - 2) // 2:
                put(elements[0], step + left + pair, at, size)
                break
            up, down, damps = step
            left, pair, w = pair_source(down, damps, left, pair, pair_of(source, k + 1, cells))
            put(chunk_up, up, at, size, k * UP)
            put(chunk_w, w, at, size, k * 2)
    for level, rows in enumerate(levels_of(fields)):
        for at, size in blocks(rows, 8):
            merged, up, w = merge(*get_both(elements[level], VALUES, at, size))
            put(elements[level + 1], merged, at, size)
            put(ups[level], up, at, size)
            put(ws[level], w, at, size)
    for v in range(VALUES):
        packed[pl.ds(v * fields, fields), :] = elements[-1][v]
    for copy in started[-2:]:
        copy.wait()


def wrap_round(fields, bit, own, other, after, packed, up_out, w_out):
    second = is_second("wrap", bit)
    for at, size in blocks(fields, 8):
        mine = flat(own, VALUES, fields, at, size)
        theirs = flat(other, VALUES, fields, at, size)
        merged, up, w = merge(choose(second, theirs, mine), choose(second, mine, theirs))
        put_flat(packed, merged, fields, at, size)
        put(up_out, up, at, size)
        put(w_out, w, at, size)


def wall_matrix(fields, span, cells, *refs):
    speed_in, damp_in = refs[0:2]
    packed, damp_out, chunk_up, chunk_down = refs[2:6]
    ups, downs = refs[6:9], refs[9:12]
    elements = refs[12:16]
    size = span * CHUNKS
    for field in range(fields):
        at = field * size

        def speed(i):
            return speed_in[pl.ds(at * cells + i, size, stride=cells), :]

        def damp(i):
            return damp_in[pl.ds(i, size, stride=cells), :]

        for k, step in enumerate(chunk_matrix(speed, damp, cells)):
            if k == (cells - 2) // 2:
                put(elements[0], step, at, size)
                break
            up, down, damps = step
            put(chunk_up, up, at, size, k * UP)
            put(chunk_down, down, at, size, k * CHUNK_DOWN)
            if field == 0:
                put(damp_out, damps, 0, size, k * 2)
    lines = fields * span
    for level, rows in enumerate(levels_of(lines)):
        for at, size in blocks(rows, 8):
            merged, up, down = merge_matrix(*get_both(elements[level], MATRIX, at, size))
            put(elements[level + 1], merged, at, size)
            put(ups[level], up, at, size)
            put(downs[level], down, at, size)
    not_first, not_last = open_ends("normal")
    for v in range(MATRIX):
        value = elements[-1][v]
        if v in (0, 1, 2, 4, 5, 8, 10):
            value = value * not_first
        if v in (5, 7, 10, 11, 13, 14, 15):
            value = value * not_last
        packed[pl.ds(v * lines, lines), :] = value


def wall_round(lines, bit, final, own, other, *refs):
    started = []
    if final:
        coupling, packed, up_out, down_out, outer_out, coupling_out, sems = refs
        started = copies(
            [(coupling.at[k], coupling_out.at[k]) for k in range(coupling.shape[0])], sems
        )
    else:
        packed, up_out, down_out = refs
    second = is_second("normal", bit)
    upper = is_second("normal", bit + 1)
    for at, size in blocks(lines, 8):
        mine = flat(own, MATRIX, lines, at, size)
        theirs = flat(other, MATRIX, lines, at, size)
        merged, up, down = merge_matrix(
            choose(second, theirs, mine), choose(second, mine, theirs)
        )
        put(up_out, up, at, size)
        put(down_out, down, at, size)
        if not final:
            put_flat(packed, merged, lines, at, size)
            continue
        ll, lr, rl, rr = quads(merged)
        outer, into = choose(upper, rr, ll), choose(upper, rl, lr)
        out, middle = choose(upper, lr, rl), choose(upper, ll, rr)
        is_upper = jnp.where(upper, 1.0, 0.0)
        pivot = inverse(
            outer[0] + (1.0 - is_upper), outer[1], outer[2], outer[3] + is_upper
        )
        put_flat(packed, minus(middle, times(out, times(pivot, into))), lines, at, size)
        put(outer_out, pivot + into + out, at, size)
    for copy in started:
        copy.wait()


def wall_source_round(lines, bit, own, other, down_in, packed, w_out):
    second = is_second("normal", bit)
    for at, size in blocks(lines, 8):
        mine = flat(own, SOURCE, lines, at, size)
        theirs = flat(other, SOURCE, lines, at, size)
        merged, w = merge_source(
            get(down_in, MERGE_DOWN, at, size),
            choose(second, theirs, mine),
            choose(second, mine, theirs),
        )
        put_flat(packed, merged, lines, at, size)
        put(w_out, w, at, size)


def reduce_source(down, factors, second, upper, mine, theirs):
    merged, w = merge_source(
        down, choose(second, theirs, mine), choose(second, mine, theirs)
    )
    outer = apply(factors[0:4], choose(upper, merged[2:4], merged[0:2]))
    centre = choose(upper, merged[0:2], merged[2:4])
    return minus(centre, apply(factors[8:12], outer)), outer, w


def wall_share(lines, bit, own, down_in, outer_in, matrix, share, bundle, copy):
    share[pl.ds(2 * lines, 2 * lines), :] = jnp.zeros((2 * lines, share.shape[1]), jnp.float32)
    copy[...] = own[...]
    bundle[pl.ds(2 * lines, 4 * lines), :] = matrix[...]
    second, upper = is_second("normal", bit), is_second("normal", bit + 1)
    for at, size in blocks(lines, 8):
        mine = flat(own, SOURCE, lines, at, size)
        none = tuple(jnp.zeros_like(value) for value in mine)
        down, factors = get(down_in, MERGE_DOWN, at, size), get(outer_in, 12, at, size)
        part, _, _ = reduce_source(down, factors, second, upper, mine, none)
        put_flat(share, part, lines, at, size)
        put_flat(bundle, part, lines, at, size)


def middle(fields, span, wrap_cells, wall_cells, bits, *refs):
    own, others, refs = refs[0], refs[1:4], refs[4:]
    round_ups, round_ws, refs = refs[:bits], refs[bits : 2 * bits], refs[2 * bits :]
    chunk_up, chunk_w, ups, ws = refs[0], refs[1], refs[2:5], refs[5:8]
    coupling, damps_in, chunk_down, downs = refs[8], refs[9], refs[10], refs[11:14]
    packed, wall_w, wall_ws = refs[14], refs[15], refs[16:19]
    ends, solved_t, solved, mixed = refs[19:23], refs[23], refs[24], refs[25]
    sources = refs[26:30]

    for at, size in blocks(fields, 8):
        odd = is_second("wrap", bits)
        near, opposite, far = (flat(other, VALUES, fields, at, size) for other in others)
        following, before = choose(odd, far, near), choose(odd, near, far)
        rest = merge(merge(following, opposite)[0], before)[0]
        left, right = close_ring(flat(own, VALUES, fields, at, size), rest)
        left, right = round_down(round_ups, round_ws, "wrap", bits, at, size, left, right)
        put(ends[0], left + right, at, size)
    last = split_all(ends[0], ends[1:], ups, ws, levels_of(fields))
    length = wrap_cells * CHUNKS
    for at, size in blocks(fields * CHUNKS, 16):

        def store(i, value):
            solved_t[pl.ds(at * wrap_cells + i, size, stride=wrap_cells), :] = value

        back_substitute(last, chunk_up, chunk_w, wrap_cells, at, size, store)
    lanes = solved.shape[0] // fields
    for field in range(fields):
        solved[pl.ds(field * lanes, lanes), :] = solved_t[pl.ds(field * length, length), :].T

    for at, size in blocks(lanes, 16):
        update = [solved[pl.ds(j * lanes + at, size), :] for j in range(fields)]
        for k in range(fields):
            total = coupling[k * fields, pl.ds(at, size), :].astype(jnp.float32) * update[0]
            for j in range(1, fields):
                factor = coupling[k * fields + j, pl.ds(at, size), :]
                total = total + factor.astype(jnp.float32) * update[j]
            mixed[pl.ds(k * lanes + at, size), :] = total

    pairs = (wall_cells - 2) // 2
    size = span * CHUNKS
    for field in range(fields):
        at = field * size

        def source(i):
            return mixed[pl.ds(at * wall_cells + i, size, stride=wall_cells), :]

        left, pair = first_pair(source), pair_of(source, 0, wall_cells)
        for k in range(pairs):
            left, pair, w = pair_source(
                get(chunk_down, CHUNK_DOWN, at, size, k * CHUNK_DOWN),
                get(damps_in, 2, 0, size, k * 2),
                left,
                pair,
                pair_of(source, k + 1, wall_cells),
            )
            put(wall_w, w, at, size, k * 2)
        put(sources[0], left + pair, at, size)
    lines = fields * span
    for level, rows in enumerate(levels_of(lines)):
        for at, size in blocks(rows, 8):
            down = get(downs[level], MERGE_DOWN, at, size)
            merged, w = merge_source(down, *get_both(sources[level], SOURCE, at, size))
            put(sources[level + 1], merged, at, size)
            put(wall_ws[level], w, at, size)
    not_first, not_last = open_ends("normal")
    for v, keep in enumerate((not_first, None, None, not_last)):
        value = sources[-1][v]
        packed[pl.ds(v * lines, lines), :] = value if keep is None else value * keep


def wall_up(fields, span, cells, bits, *refs):
    own_matrix, down_in, outer_in, own, bundle, other, share = refs[0:7]
    refs = refs[7:]
    round_ups, round_ws, refs = refs[: bits + 1], refs[bits + 1 : 2 * bits + 1], refs[2 * bits + 1 :]
    chunk_up, chunk_w, ups, ws = refs[0], refs[1], refs[2:5], refs[5:8]
    update = refs[8]
    ends, result, sems = refs[9:13], refs[13], refs[14]
    lines = fields * span
    second, upper = is_second("normal", bits), is_second("normal", bits + 1)
    for at, size in blocks(lines, 8):
        down, factors = get(down_in, MERGE_DOWN, at, size), get(outer_in, 12, at, size)
        part, outer, w = reduce_source(
            down,
            factors,
            second,
            upper,
            flat(own, SOURCE, lines, at, size),
            flat(other, SOURCE, lines, at, size),
        )
        opposite = flat(bundle, 6, lines, at, size)
        shares = plus(opposite[0:2], flat(share, 2, lines, at, size))
        matrix = plus(flat(own_matrix, 4, lines, at, size), opposite[2:6])
        centre = apply(inverse(*matrix), plus(part, shares))
        outer = minus(outer, apply(factors[0:4], apply(factors[4:8], centre)))
        left, right = choose(upper, centre, outer), choose(upper, outer, centre)
        between = inner(get(round_ups[bits], UP, at, size), w, left, right)
        left, right = choose(second, between, left), choose(second, right, between)
        left, right = round_down(round_ups, round_ws, "normal", bits, at, size, left, right)
        put(ends[0], left + right, at, size)
    last = split_all(ends[0], ends[1:], ups, ws, levels_of(lines))
    size = span * CHUNKS
    length = size * cells
    started = []
    for field in range(fields):
        at = field * size

        def store(i, value):
            result[pl.ds(at * cells + i, size, stride=cells), :] = value

        back_substitute(last, chunk_up, chunk_w, cells, at, size, store)
        rows = pl.ds(field * length, length)
        copy = pltpu.make_async_copy(result.at[rows], update.at[rows], sems.at[field])
        copy.start()
        started.append(copy)
    for copy in started:
        copy.wait()


def f32(*shape):
    return jax.ShapeDtypeStruct(shape, jnp.float32)


def vmem(*shape):
    return pltpu.VMEM(shape, jnp.float32)


IN_VMEM = pl.BlockSpec(memory_space=pltpu.VMEM)
IN_HBM = pl.BlockSpec(memory_space=pltpu.HBM)
PARAMS = pltpu.CompilerParams(vmem_limit_bytes=24 * 2**20)


def kernel(name, body, ins, outs, scratch, flops):
    in_bytes = sum(a.size * a.dtype.itemsize for a, _ in ins)
    out_bytes = sum(a.size * 4 for a, _ in outs)
    outputs = pl.pallas_call(
        body,
        out_shape=[a for a, _ in outs],
        in_specs=[spec for _, spec in ins],
        out_specs=[spec for _, spec in outs],
        scratch_shapes=scratch,
        compiler_params=PARAMS,
        cost_estimate=pl.CostEstimate(
            flops=flops, bytes_accessed=in_bytes + out_bytes, transcendentals=0
        ),
        name=name,
    )(*[a for a, _ in ins])
    return list(outputs)


def inside(arrays):
    return [(a, IN_VMEM) for a in arrays]


def outside(arrays):
    return [(pltpu.with_memory_space_constraint(a, pltpu.HBM), IN_HBM) for a in arrays]


def exchange(array, axis, mask):
    count = lax.axis_size(axis)
    return lax.ppermute(array, axis, [(i, i ^ mask) for i in range(count)])


def pass_on(array, axis, bit, targets):
    count = lax.axis_size(axis)

    def target(i):
        place = i // (1 << bit) % 4
        return i + (targets[place] - place) * (1 << bit)

    return lax.ppermute(array, axis, [(i, target(i)) for i in range(count)])


def local(residual, courant_xi, courant_eta, dissip_xi, dissip_eta, coupling):
    fields, span, high, wide = residual.shape
    lanes = span * high
    wrap_cells, wall_cells = wide // CHUNKS, high // CHUNKS
    wrap_pairs, wall_pairs = (wrap_cells - 2) // 2, (wall_cells - 2) // 2
    wrap_count, wall_count = lax.axis_size("wrap"), lax.axis_size("normal")
    lines = fields * span
    wrap_levels, wall_levels = levels_of(fields), levels_of(lines)
    wrap_rows, wall_rows = fields * CHUNKS, lines * CHUNKS

    def rows_of(array):
        return array.reshape(-1, wide)

    wrap_bits = wrap_count.bit_length() - 3
    wall_bits = wall_count.bit_length() - 3
    results = kernel(
        "wrap_down",
        functools.partial(wrap_down, fields, wrap_cells),
        outside(
            [rows_of(a) for a in (residual, courant_xi, dissip_xi, courant_eta, dissip_eta)]
        ),
        inside(
            [
                f32(VALUES * fields, lanes),
                f32(wrap_pairs * UP, wrap_rows, lanes),
                f32(wrap_pairs * 2, wrap_rows, lanes),
            ]
            + [f32(UP, n, lanes) for n in wrap_levels]
            + [f32(2, n, lanes) for n in wrap_levels]
            + [f32(fields * lanes, wide), f32(lanes, wide)]
        ),
        [vmem(fields * lanes, wide)] * 2
        + [vmem(lanes, wide)]
        + [vmem(fields * wide, lanes)] * 2
        + [vmem(wide, lanes)]
        + [vmem(VALUES, n, lanes) for n in [wrap_rows] + wrap_levels]
        + [pltpu.SemaphoreType.DMA((7,))],
        100 * residual.size,
    )
    element, wrap_factors, wall_inputs = results[0], results[1:9], results[9:11]
    results = kernel(
        "wall_matrix",
        functools.partial(wall_matrix, fields, span, wall_cells),
        inside(wall_inputs),
        inside(
            [
                f32(MATRIX * lines, wide),
                f32(wall_pairs * 2, span * CHUNKS, wide),
                f32(wall_pairs * UP, wall_rows, wide),
                f32(wall_pairs * CHUNK_DOWN, wall_rows, wide),
            ]
            + [f32(UP, n, wide) for n in wall_levels]
            + [f32(MERGE_DOWN, n, wide) for n in wall_levels]
        ),
        [vmem(MATRIX, n, wide) for n in [wall_rows] + wall_levels],
        100 * residual.size,
    )
    matrix, damps, chunk_up, chunk_down = results[0:4]
    wall_ups, wall_downs = results[4:7], results[7:10]
    wrap_ups, wrap_ws = [], []
    for bit in range(wrap_bits):
        element, up, w = kernel(
            f"wrap_round_{bit}",
            functools.partial(wrap_round, fields, bit),
            inside([element, exchange(element, "wrap", 1 << bit), damps]),
            inside([f32(VALUES * fields, lanes), f32(UP, fields, lanes), f32(2, fields, lanes)]),
            [],
            200 * fields * lanes,
        )
        wrap_ups.append(up)
        wrap_ws.append(w)
    swap = 1 if wrap_bits > 0 else 0
    wrap_others = [exchange(element, "wrap", mask << wrap_bits | swap) for mask in (1, 2, 3)]
    round_ups, round_downs = [], []
    for bit in range(wall_bits + 1):
        final = bit == wall_bits
        matrix, up, down, *extra = kernel(
            f"wall_round_{bit}",
            functools.partial(wall_round, lines, bit, final),
            inside([matrix, exchange(matrix, "normal", 1 << bit)])
            + (outside([coupling.reshape(fields * fields, lanes, wide)]) if final else []),
            inside(
                [
                    f32((4 if final else MATRIX) * lines, wide),
                    f32(UP, lines, wide),
                    f32(MERGE_DOWN, lines, wide),
                ]
                + (
                    [
                        f32(12, lines, wide),
                        jax.ShapeDtypeStruct((fields * fields, lanes, wide), coupling.dtype),
                    ]
                    if final
                    else []
                )
            ),
            [pltpu.SemaphoreType.DMA((fields * fields,))] if final else [],
            200 * lines * wide,
        )
        round_ups.append(up)
        round_downs.append(down)
    outer, coupling_in = extra[:1], extra[1]
    source, *wall_ws = kernel(
        "middle",
        functools.partial(middle, fields, span, wrap_cells, wall_cells, wrap_bits),
        inside(
            [element]
            + wrap_others
            + wrap_ups
            + wrap_ws
            + wrap_factors
            + [coupling_in, damps, chunk_down]
            + wall_downs
        ),
        inside(
            [f32(SOURCE * lines, wide), f32(wall_pairs * 2, wall_rows, wide)]
            + [f32(2, n, wide) for n in wall_levels]
        ),
        [vmem(4, n, lanes) for n in reversed([wrap_rows] + wrap_levels)]
        + [vmem(fields * wide, lanes), vmem(fields * lanes, wide), vmem(fields * lanes, wide)]
        + [vmem(SOURCE, n, wide) for n in [wall_rows] + wall_levels],
        100 * residual.size,
    )
    round_ws = []
    for bit in range(wall_bits):
        source, w = kernel(
            f"wall_source_round_{bit}",
            functools.partial(wall_source_round, lines, bit),
            inside([source, exchange(source, "normal", 1 << bit), round_downs[bit]]),
            inside([f32(SOURCE * lines, wide), f32(2, lines, wide)]),
            [],
            50 * lines * wide,
        )
        round_ws.append(w)
    share, bundle, source = kernel(
        "wall_share",
        functools.partial(wall_share, lines, wall_bits),
        inside([source, round_downs[wall_bits]] + outer + [matrix]),
        inside([f32(SOURCE * lines, wide), f32(6 * lines, wide), f32(SOURCE * lines, wide)]),
        [],
        50 * lines * wide,
    )
    (update,) = kernel(
        "wall_up",
        functools.partial(wall_up, fields, span, wall_cells, wall_bits),
        inside(
            [matrix, round_downs[wall_bits]]
            + outer
            + [
                source,
                pass_on(bundle, "normal", wall_bits, (2, 3, 1, 0)),
                exchange(source, "normal", 1 << wall_bits),
                pass_on(share, "normal", wall_bits, (3, 2, 0, 1)),
            ]
            + round_ups
            + round_ws
            + [chunk_up, wall_ws[0]]
            + wall_ups
            + wall_ws[1:]
        ),
        [(f32(fields * lanes, wide), IN_HBM)],
        [vmem(4, n, wide) for n in reversed([wall_rows] + wall_levels)]
        + [vmem(fields * lanes, wide), pltpu.SemaphoreType.DMA((fields,))],
        30 * residual.size,
    )
    return update.reshape(residual.shape)


def solution(mesh):
    placed = (
        P(None, None, "normal", "wrap"),
        P(None, None, "normal", "wrap"),
        P(None, None, "normal", "wrap"),
        P(None, "normal", "wrap"),
        P(None, "normal", "wrap"),
        P(None, None, None, "normal", "wrap"),
    )
    return jax.shard_map(
        local,
        mesh=mesh,
        in_specs=placed,
        out_specs=P(None, None, "normal", "wrap"),
        check_vma=False,
    )
```

```python
import functools

import jax
import jax.numpy as jnp
from jax import lax
from jax.experimental import pallas as pl
from jax.experimental.pallas import tpu as pltpu
from jax.sharding import PartitionSpec as P

MATRIX = 16
SOURCE = 4
VALUES = MATRIX + SOURCE
UP = 8
CHUNK_DOWN = 9
MERGE_DOWN = 12
CHUNKS = 8
WIDE = 24


def inverse(a, b, c, d):
    scale = 1.0 / (a * d - b * c)
    return (d * scale, -b * scale, -c * scale, a * scale)


def times(x, y):
    return (
        x[0] * y[0] + x[1] * y[2],
        x[0] * y[1] + x[1] * y[3],
        x[2] * y[0] + x[3] * y[2],
        x[2] * y[1] + x[3] * y[3],
    )


def apply(x, v):
    return (x[0] * v[0] + x[1] * v[1], x[2] * v[0] + x[3] * v[1])


def minus(x, y):
    return tuple(a - b for a, b in zip(x, y))


def plus(x, y):
    return tuple(a + b for a, b in zip(x, y))


def negative(x):
    return tuple(-a for a in x)


def quads(element):
    return (element[0:4], element[4:8], element[8:12], element[12:16])


def merge_matrix(first, second):
    ll, lm, ml, mm = quads(first)
    nn, mr, rm, rr = quads(second)
    pivot = inverse(*plus(mm, nn))
    wl = times(pivot, ml)
    wr = times(pivot, mr)
    merged = (
        minus(ll, times(lm, wl))
        + negative(times(lm, wr))
        + negative(times(rm, wl))
        + minus(rr, times(rm, wr))
    )
    return merged, wl + wr, pivot + lm + rm


def merge_source(down, first, second):
    pivot, lm, rm = down[0:4], down[4:8], down[8:12]
    w = apply(pivot, plus(first[2:4], second[0:2]))
    return minus(first[0:2], apply(lm, w)) + minus(second[2:4], apply(rm, w)), w


def merge(first, second):
    matrix, up, down = merge_matrix(first[:MATRIX], second[:MATRIX])
    source, w = merge_source(down, first[MATRIX:], second[MATRIX:])
    return matrix + source, up, w


def inner(up, w, left, right):
    return minus(minus(w, apply(up[0:4], left)), apply(up[4:8], right))


def chunk_matrix(speed, damp, cells):
    def link(i):
        p = 2.0 * (damp(i) + damp(i + 1))
        q = 0.25 * (speed(i) + speed(i + 1))
        return q - p, -q - p

    def centre(i):
        return 1.0 + damp(i - 1) + 4.0 * damp(i) + damp(i + 1)

    b0, b1 = damp(0), damp(1)
    quarter = 0.25 * speed(0)
    up, low = link(0)
    zero = jnp.zeros_like(b0)
    ll = (b0, quarter - 2.0 * b0, -quarter - 2.0 * b0, 1.0 + 4.0 * b0 + b1)
    lk = (b0, zero, up, b1)
    kl = (b0, low, zero, b1)
    up, low = link(1)
    kk = (centre(1), up, low, centre(2))
    pairs = (cells - 2) // 2
    for k in range(1, pairs + 1):
        i = 2 * k
        pivot = inverse(*kk)
        wl = times(pivot, kl)
        up, low = link(i)
        here, there = damp(i), damp(i + 1)
        wr = (
            pivot[0] * here + pivot[1] * up,
            pivot[1] * there,
            pivot[2] * here + pivot[3] * up,
            pivot[3] * there,
        )
        yield wl + wr, pivot + lk + (low,), (here, there)

        def below(x):
            return (
                here * x[0] + low * x[2],
                here * x[1] + low * x[3],
                there * x[2],
                there * x[3],
            )

        ll = minus(ll, times(lk, wl))
        lk = negative(times(lk, wr))
        kl = negative(below(wl))
        if k < pairs:
            up, low_next = link(i + 1)
            kk = (centre(i + 1), up, low_next, centre(i + 2))
        else:
            quarter = 0.25 * speed(i + 1)
            kk = (
                1.0 + here + 4.0 * there,
                quarter - 2.0 * there,
                -quarter - 2.0 * there,
                there,
            )
        kk = minus(kk, below(wr))
    yield ll + lk + kl + kk


def pair_source(down, damps, left, pair, following):
    pivot, lk, low = down[0:4], down[4:8], down[8]
    w = apply(pivot, pair)
    left = minus(left, apply(lk, w))
    following = minus(following, (damps[0] * w[0] + low * w[1], damps[1] * w[1]))
    return left, following, w


def pair_of(source, k, cells):
    if k == (cells - 2) // 2:
        last = source(cells - 1)
        return (last, jnp.zeros_like(last))
    return (source(2 * k + 1), source(2 * k + 2))


def first_pair(source):
    first = source(0)
    return (jnp.zeros_like(first), first)


def field_parts(fields):
    half = (fields + 1) // 2
    return [(0, half), (half, fields)]


def repeated(rows, count):
    return jnp.concatenate([rows] * count, axis=0) if count > 1 else rows


def blocks(rows, size):
    return [(at, min(size, rows - at)) for at in range(0, rows, size)]


def get(ref, count, at, size, base=0):
    return tuple(ref[base + v, pl.ds(at, size), :] for v in range(count))


def put(ref, values, at, size, base=0):
    for v, value in enumerate(values):
        ref[base + v, pl.ds(at, size), :] = value


def get_both(ref, count, at, size):
    return tuple(
        tuple(ref[v, pl.ds(2 * at + half, size, stride=2), :] for v in range(count))
        for half in (0, 1)
    )


def levels_of(lines):
    sizes = []
    rows = lines * CHUNKS
    while rows > lines:
        rows //= 2
        sizes.append(rows)
    return sizes


def split_all(top_ref, end_refs, up_refs, w_refs, sizes):
    source = top_ref
    for rows, target, ups, ws in zip(
        reversed(sizes), end_refs, reversed(up_refs), reversed(w_refs)
    ):
        for at, size in blocks(rows, WIDE):
            ends = get(source, 4, at, size)
            left, right = ends[0:2], ends[2:4]
            middle = inner(get(ups, UP, at, size), get(ws, 2, at, size), left, right)
            for v in range(2):
                target[v, pl.ds(2 * at, size, stride=2), :] = left[v]
                target[v, pl.ds(2 * at + 1, size, stride=2), :] = middle[v]
                target[2 + v, pl.ds(2 * at, size, stride=2), :] = middle[v]
                target[2 + v, pl.ds(2 * at + 1, size, stride=2), :] = right[v]
        source = target
    return source


def back_substitute(ends_ref, up_ref, w_ref, cells, at, size, store):
    ends = get(ends_ref, 4, at, size)
    left, following = ends[0:2], ends[2:4]
    store(0, left[1])
    store(cells - 1, following[0])
    for k in range((cells - 2) // 2 - 1, -1, -1):
        following = inner(
            get(up_ref, UP, at, size, k * UP), get(w_ref, 2, at, size, k * 2), left, following
        )
        store(2 * k + 1, following[0])
        store(2 * k + 2, following[1])


def close_ring(own, rest):
    ll, lr, rl, rr = quads(own)
    nn, nm, mn, mm = quads(rest)
    b = plus(lr, mn)
    c = plus(rl, nm)
    pivot = inverse(*plus(rr, nn))
    f = plus(own[16:18], rest[18:20])
    g = plus(own[18:20], rest[16:18])
    bd = times(b, pivot)
    left = apply(inverse(*minus(plus(ll, mm), times(bd, c))), minus(f, apply(bd, g)))
    right = apply(pivot, minus(g, apply(c, left)))
    return left, right


def open_ends(axis):
    place = lax.axis_index(axis)
    last = lax.axis_size(axis) - 1
    return jnp.where(place > 0, 1.0, 0.0), jnp.where(place < last, 1.0, 0.0)


def is_second(axis, bit):
    return lax.rem(lax.axis_index(axis) // (1 << bit), 2) == 1


def choose(second, one, other):
    return tuple(jnp.where(second, a, b) for a, b in zip(one, other))


def flat(ref, count, rows, at, size):
    return tuple(ref[pl.ds(v * rows + at, size), :] for v in range(count))


def put_flat(ref, values, rows, at, size):
    for v, value in enumerate(values):
        ref[pl.ds(v * rows + at, size), :] = value


def round_down(ups, ws, axis, bits, at, size, left, right):
    for bit in reversed(range(bits)):
        middle = inner(get(ups[bit], UP, at, size), get(ws[bit], 2, at, size), left, right)
        second = is_second(axis, bit)
        left, right = choose(second, middle, left), choose(second, right, middle)
    return left, right


def copies(pairs, sems, first=0):
    started = []
    for i, (source, target) in enumerate(pairs):
        copy = pltpu.make_async_copy(source, target, sems.at[first + i])
        copy.start()
        started.append(copy)
    return started


def wrap_down(fields, cells, *refs):
    residual, courant, dissip, wall_courant, wall_dissip = refs[0:5]
    packed, chunk_up, chunk_w = refs[5:8]
    ups, ws = refs[8:11], refs[11:14]
    wall_speed, wall_damp = refs[14:16]
    source_in, speed_in, damp_in, source_t, speed_t, damp_t = refs[16:22]
    elements, sems = refs[22:26], refs[26]
    lanes = damp_in.shape[0]
    length = cells * CHUNKS
    parts = [(0, 2), (2, fields)] if fields > 2 else [(0, fields)]
    moves = [(dissip, damp_in)]
    for first, last in parts:
        rows = pl.ds(first * lanes, (last - first) * lanes)
        moves.append((courant.at[rows], speed_in.at[rows]))
        moves.append((residual.at[rows], source_in.at[rows]))
    moves += [(wall_dissip, wall_damp), (wall_courant, wall_speed)]
    started = copies(moves, sems)
    started[0].wait()
    damp_t[...] = damp_in[...].T
    for part, (first, last) in enumerate(parts):
        for copy, taken, turned in (
            (started[1 + 2 * part], speed_in, speed_t),
            (started[2 + 2 * part], source_in, source_t),
        ):
            copy.wait()
            for field in range(first, last):
                turned[pl.ds(field * length, length), :] = taken[pl.ds(field * lanes, lanes), :].T
    for at, size in blocks(fields * CHUNKS, 40):
        repeat = size // CHUNKS

        def speed(i):
            return speed_t[pl.ds(at * cells + i, size, stride=cells), :]

        def source(i):
            return source_t[pl.ds(at * cells + i, size, stride=cells), :]

        def damp(i):
            return repeated(damp_t[pl.ds(i, CHUNKS, stride=cells), :], repeat)

        left, pair = first_pair(source), pair_of(source, 0, cells)
        for k, step in enumerate(chunk_matrix(speed, damp, cells)):
            if k == (cells - 2) // 2:
                put(elements[0], step + left + pair, at, size)
                break
            up, down, damps = step
            left, pair, w = pair_source(down, damps, left, pair, pair_of(source, k + 1, cells))
            put(chunk_up, up, at, size, k * UP)
            put(chunk_w, w, at, size, k * 2)
    for level, rows in enumerate(levels_of(fields)):
        for at, size in blocks(rows, WIDE):
            merged, up, w = merge(*get_both(elements[level], VALUES, at, size))
            put(elements[level + 1], merged, at, size)
            put(ups[level], up, at, size)
            put(ws[level], w, at, size)
    for v in range(VALUES):
        packed[pl.ds(v * fields, fields), :] = elements[-1][v]
    for copy in started[-2:]:
        copy.wait()


def wrap_round(fields, bit, own, other, after, packed, up_out, w_out):
    second = is_second("wrap", bit)
    for at, size in blocks(fields, 8):
        mine = flat(own, VALUES, fields, at, size)
        theirs = flat(other, VALUES, fields, at, size)
        merged, up, w = merge(choose(second, theirs, mine), choose(second, mine, theirs))
        put_flat(packed, merged, fields, at, size)
        put(up_out, up, at, size)
        put(w_out, w, at, size)


def wall_matrix(fields, span, cells, *refs):
    speed_in, damp_in = refs[0:2]
    packed, damp_out, chunk_up, chunk_down = refs[2:6]
    ups, downs = refs[6:9], refs[9:12]
    elements = refs[12:16]
    rows = span * CHUNKS
    for first, last in field_parts(fields):
        at, size = first * rows, (last - first) * rows

        def speed(i):
            return speed_in[pl.ds(at * cells + i, size, stride=cells), :]

        def damp(i):
            return repeated(damp_in[pl.ds(i, rows, stride=cells), :], last - first)

        for k, step in enumerate(chunk_matrix(speed, damp, cells)):
            if k == (cells - 2) // 2:
                put(elements[0], step, at, size)
                break
            up, down, damps = step
            put(chunk_up, up, at, size, k * UP)
            put(chunk_down, down, at, size, k * CHUNK_DOWN)
            if first == 0:
                put(damp_out, tuple(value[:rows] for value in damps), 0, rows, k * 2)
    lines = fields * span
    for level, rows in enumerate(levels_of(lines)):
        for at, size in blocks(rows, WIDE):
            merged, up, down = merge_matrix(*get_both(elements[level], MATRIX, at, size))
            put(elements[level + 1], merged, at, size)
            put(ups[level], up, at, size)
            put(downs[level], down, at, size)
    not_first, not_last = open_ends("normal")
    for v in range(MATRIX):
        value = elements[-1][v]
        if v in (0, 1, 2, 4, 5, 8, 10):
            value = value * not_first
        if v in (5, 7, 10, 11, 13, 14, 15):
            value = value * not_last
        packed[pl.ds(v * lines, lines), :] = value


def wall_round(lines, bit, final, own, other, *refs):
    started = []
    if final:
        coupling, packed, up_out, down_out, outer_out, coupling_out, sems = refs
        count = sems.shape[0]
        parts = [pl.ds(k * count, count) for k in range(count)]
        started = copies([(coupling.at[k], coupling_out.at[k]) for k in parts], sems)
    else:
        packed, up_out, down_out = refs
    second = is_second("normal", bit)
    upper = is_second("normal", bit + 1)
    for at, size in blocks(lines, WIDE):
        mine = flat(own, MATRIX, lines, at, size)
        theirs = flat(other, MATRIX, lines, at, size)
        merged, up, down = merge_matrix(
            choose(second, theirs, mine), choose(second, mine, theirs)
        )
        put(up_out, up, at, size)
        put(down_out, down, at, size)
        if not final:
            put_flat(packed, merged, lines, at, size)
            continue
        ll, lr, rl, rr = quads(merged)
        outer, into = choose(upper, rr, ll), choose(upper, rl, lr)
        out, middle = choose(upper, lr, rl), choose(upper, ll, rr)
        is_upper = jnp.where(upper, 1.0, 0.0)
        pivot = inverse(
            outer[0] + (1.0 - is_upper), outer[1], outer[2], outer[3] + is_upper
        )
        put_flat(packed, minus(middle, times(out, times(pivot, into))), lines, at, size)
        put(outer_out, pivot + into + out, at, size)
    for copy in started:
        copy.wait()


def wall_source_round(lines, bit, own, other, down_in, packed, w_out):
    second = is_second("normal", bit)
    for at, size in blocks(lines, WIDE):
        mine = flat(own, SOURCE, lines, at, size)
        theirs = flat(other, SOURCE, lines, at, size)
        merged, w = merge_source(
            get(down_in, MERGE_DOWN, at, size),
            choose(second, theirs, mine),
            choose(second, mine, theirs),
        )
        put_flat(packed, merged, lines, at, size)
        put(w_out, w, at, size)


def reduce_source(down, factors, second, upper, mine, theirs):
    merged, w = merge_source(
        down, choose(second, theirs, mine), choose(second, mine, theirs)
    )
    outer = apply(factors[0:4], choose(upper, merged[2:4], merged[0:2]))
    centre = choose(upper, merged[0:2], merged[2:4])
    return minus(centre, apply(factors[8:12], outer)), outer, w


def wall_share(lines, bit, own, down_in, outer_in, matrix, share, bundle, copy):
    share[pl.ds(2 * lines, 2 * lines), :] = jnp.zeros((2 * lines, share.shape[1]), jnp.float32)
    copy[...] = own[...]
    bundle[pl.ds(2 * lines, 4 * lines), :] = matrix[...]
    second, upper = is_second("normal", bit), is_second("normal", bit + 1)
    for at, size in blocks(lines, WIDE):
        mine = flat(own, SOURCE, lines, at, size)
        none = tuple(jnp.zeros_like(value) for value in mine)
        down, factors = get(down_in, MERGE_DOWN, at, size), get(outer_in, 12, at, size)
        part, _, _ = reduce_source(down, factors, second, upper, mine, none)
        put_flat(share, part, lines, at, size)
        put_flat(bundle, part, lines, at, size)


def middle(fields, span, wrap_cells, wall_cells, bits, *refs):
    own, others, refs = refs[0], refs[1:4], refs[4:]
    round_ups, round_ws, refs = refs[:bits], refs[bits : 2 * bits], refs[2 * bits :]
    chunk_up, chunk_w, ups, ws = refs[0], refs[1], refs[2:5], refs[5:8]
    coupling, damps_in, chunk_down, downs = refs[8], refs[9], refs[10], refs[11:14]
    packed, wall_w, wall_ws = refs[14], refs[15], refs[16:19]
    ends, solved_t, solved, mixed = refs[19:23], refs[23], refs[24], refs[25]
    sources = refs[26:30]

    for at, size in blocks(fields, 8):
        odd = is_second("wrap", bits)
        near, opposite, far = (flat(other, VALUES, fields, at, size) for other in others)
        following, before = choose(odd, far, near), choose(odd, near, far)
        rest = merge(merge(following, opposite)[0], before)[0]
        left, right = close_ring(flat(own, VALUES, fields, at, size), rest)
        left, right = round_down(round_ups, round_ws, "wrap", bits, at, size, left, right)
        put(ends[0], left + right, at, size)
    last = split_all(ends[0], ends[1:], ups, ws, levels_of(fields))
    length = wrap_cells * CHUNKS
    for at, size in blocks(fields * CHUNKS, 40):

        def store(i, value):
            solved_t[pl.ds(at * wrap_cells + i, size, stride=wrap_cells), :] = value

        back_substitute(last, chunk_up, chunk_w, wrap_cells, at, size, store)
    lanes = solved.shape[0] // fields
    for field in range(fields):
        solved[pl.ds(field * lanes, lanes), :] = solved_t[pl.ds(field * length, length), :].T

    for at, size in blocks(lanes, 16):
        update = [solved[pl.ds(j * lanes + at, size), :] for j in range(fields)]
        for k in range(fields):
            total = coupling[k * fields, pl.ds(at, size), :].astype(jnp.float32) * update[0]
            for j in range(1, fields):
                factor = coupling[k * fields + j, pl.ds(at, size), :]
                total = total + factor.astype(jnp.float32) * update[j]
            mixed[pl.ds(k * lanes + at, size), :] = total

    pairs = (wall_cells - 2) // 2
    rows = span * CHUNKS
    for first, last in field_parts(fields):
        at, size = first * rows, (last - first) * rows

        def source(i):
            return mixed[pl.ds(at * wall_cells + i, size, stride=wall_cells), :]

        left, pair = first_pair(source), pair_of(source, 0, wall_cells)
        for k in range(pairs):
            left, pair, w = pair_source(
                get(chunk_down, CHUNK_DOWN, at, size, k * CHUNK_DOWN),
                tuple(repeated(d, last - first) for d in get(damps_in, 2, 0, rows, k * 2)),
                left,
                pair,
                pair_of(source, k + 1, wall_cells),
            )
            put(wall_w, w, at, size, k * 2)
        put(sources[0], left + pair, at, size)
    lines = fields * span
    for level, rows in enumerate(levels_of(lines)):
        for at, size in blocks(rows, WIDE):
            down = get(downs[level], MERGE_DOWN, at, size)
            merged, w = merge_source(down, *get_both(sources[level], SOURCE, at, size))
            put(sources[level + 1], merged, at, size)
            put(wall_ws[level], w, at, size)
    not_first, not_last = open_ends("normal")
    for v, keep in enumerate((not_first, None, None, not_last)):
        value = sources[-1][v]
        packed[pl.ds(v * lines, lines), :] = value if keep is None else value * keep


def wall_up(fields, span, cells, bits, *refs):
    own_matrix, down_in, outer_in, own, bundle, other, share = refs[0:7]
    refs = refs[7:]
    round_ups, round_ws, refs = refs[: bits + 1], refs[bits + 1 : 2 * bits + 1], refs[2 * bits + 1 :]
    chunk_up, chunk_w, ups, ws = refs[0], refs[1], refs[2:5], refs[5:8]
    update = refs[8]
    ends, result, sems = refs[9:13], refs[13], refs[14]
    lines = fields * span
    second, upper = is_second("normal", bits), is_second("normal", bits + 1)
    for at, size in blocks(lines, WIDE):
        down, factors = get(down_in, MERGE_DOWN, at, size), get(outer_in, 12, at, size)
        part, outer, w = reduce_source(
            down,
            factors,
            second,
            upper,
            flat(own, SOURCE, lines, at, size),
            flat(other, SOURCE, lines, at, size),
        )
        opposite = flat(bundle, 6, lines, at, size)
        shares = plus(opposite[0:2], flat(share, 2, lines, at, size))
        matrix = plus(flat(own_matrix, 4, lines, at, size), opposite[2:6])
        centre = apply(inverse(*matrix), plus(part, shares))
        outer = minus(outer, apply(factors[0:4], apply(factors[4:8], centre)))
        left, right = choose(upper, centre, outer), choose(upper, outer, centre)
        between = inner(get(round_ups[bits], UP, at, size), w, left, right)
        left, right = choose(second, between, left), choose(second, right, between)
        left, right = round_down(round_ups, round_ws, "normal", bits, at, size, left, right)
        put(ends[0], left + right, at, size)
    own_ends = split_all(ends[0], ends[1:], ups, ws, levels_of(lines))
    rows = span * CHUNKS
    started = []
    for first, last in field_parts(fields):
        at, size = first * rows, (last - first) * rows

        def store(i, value):
            result[pl.ds(at * cells + i, size, stride=cells), :] = value

        back_substitute(own_ends, chunk_up, chunk_w, cells, at, size, store)
        part = pl.ds(at * cells, size * cells)
        started += copies([(result.at[part], update.at[part])], sems, len(started))
    for copy in started:
        copy.wait()


def f32(*shape):
    return jax.ShapeDtypeStruct(shape, jnp.float32)


def vmem(*shape):
    return pltpu.VMEM(shape, jnp.float32)


IN_VMEM = pl.BlockSpec(memory_space=pltpu.VMEM)
IN_HBM = pl.BlockSpec(memory_space=pltpu.HBM)
PARAMS = pltpu.CompilerParams(vmem_limit_bytes=24 * 2**20)


def kernel(name, body, ins, outs, scratch, flops):
    in_bytes = sum(a.size * a.dtype.itemsize for a, _ in ins)
    out_bytes = sum(a.size * 4 for a, _ in outs)
    outputs = pl.pallas_call(
        body,
        out_shape=[a for a, _ in outs],
        in_specs=[spec for _, spec in ins],
        out_specs=[spec for _, spec in outs],
        scratch_shapes=scratch,
        compiler_params=PARAMS,
        cost_estimate=pl.CostEstimate(
            flops=flops, bytes_accessed=in_bytes + out_bytes, transcendentals=0
        ),
        name=name,
    )(*[a for a, _ in ins])
    return list(outputs)


def inside(arrays):
    return [(a, IN_VMEM) for a in arrays]


def outside(arrays):
    return [(pltpu.with_memory_space_constraint(a, pltpu.HBM), IN_HBM) for a in arrays]


def exchange(array, axis, mask):
    count = lax.axis_size(axis)
    return lax.ppermute(array, axis, [(i, i ^ mask) for i in range(count)])


def pass_on(array, axis, bit, targets):
    count = lax.axis_size(axis)

    def target(i):
        place = i // (1 << bit) % 4
        return i + (targets[place] - place) * (1 << bit)

    return lax.ppermute(array, axis, [(i, target(i)) for i in range(count)])


def local(residual, courant_xi, courant_eta, dissip_xi, dissip_eta, coupling):
    fields, span, high, wide = residual.shape
    lanes = span * high
    wrap_cells, wall_cells = wide // CHUNKS, high // CHUNKS
    wrap_pairs, wall_pairs = (wrap_cells - 2) // 2, (wall_cells - 2) // 2
    wrap_count, wall_count = lax.axis_size("wrap"), lax.axis_size("normal")
    lines = fields * span
    wrap_levels, wall_levels = levels_of(fields), levels_of(lines)
    wrap_rows, wall_rows = fields * CHUNKS, lines * CHUNKS

    def rows_of(array):
        return array.reshape(-1, wide)

    wrap_bits = wrap_count.bit_length() - 3
    wall_bits = wall_count.bit_length() - 3
    results = kernel(
        "wrap_down",
        functools.partial(wrap_down, fields, wrap_cells),
        outside(
            [rows_of(a) for a in (residual, courant_xi, dissip_xi, courant_eta, dissip_eta)]
        ),
        inside(
            [
                f32(VALUES * fields, lanes),
                f32(wrap_pairs * UP, wrap_rows, lanes),
                f32(wrap_pairs * 2, wrap_rows, lanes),
            ]
            + [f32(UP, n, lanes) for n in wrap_levels]
            + [f32(2, n, lanes) for n in wrap_levels]
            + [f32(fields * lanes, wide), f32(lanes, wide)]
        ),
        [vmem(fields * lanes, wide)] * 2
        + [vmem(lanes, wide)]
        + [vmem(fields * wide, lanes)] * 2
        + [vmem(wide, lanes)]
        + [vmem(VALUES, n, lanes) for n in [wrap_rows] + wrap_levels]
        + [pltpu.SemaphoreType.DMA((7,))],
        100 * residual.size,
    )
    element, wrap_factors, wall_inputs = results[0], results[1:9], results[9:11]
    results = kernel(
        "wall_matrix",
        functools.partial(wall_matrix, fields, span, wall_cells),
        inside(wall_inputs),
        inside(
            [
                f32(MATRIX * lines, wide),
                f32(wall_pairs * 2, span * CHUNKS, wide),
                f32(wall_pairs * UP, wall_rows, wide),
                f32(wall_pairs * CHUNK_DOWN, wall_rows, wide),
            ]
            + [f32(UP, n, wide) for n in wall_levels]
            + [f32(MERGE_DOWN, n, wide) for n in wall_levels]
        ),
        [vmem(MATRIX, n, wide) for n in [wall_rows] + wall_levels],
        100 * residual.size,
    )
    matrix, damps, chunk_up, chunk_down = results[0:4]
    wall_ups, wall_downs = results[4:7], results[7:10]
    wrap_ups, wrap_ws = [], []
    for bit in range(wrap_bits):
        element, up, w = kernel(
            f"wrap_round_{bit}",
            functools.partial(wrap_round, fields, bit),
            inside([element, exchange(element, "wrap", 1 << bit), damps]),
            inside([f32(VALUES * fields, lanes), f32(UP, fields, lanes), f32(2, fields, lanes)]),
            [],
            200 * fields * lanes,
        )
        wrap_ups.append(up)
        wrap_ws.append(w)
    swap = 1 if wrap_bits > 0 else 0
    wrap_others = [exchange(element, "wrap", mask << wrap_bits | swap) for mask in (1, 2, 3)]
    round_ups, round_downs = [], []
    for bit in range(wall_bits + 1):
        final = bit == wall_bits
        matrix, up, down, *extra = kernel(
            f"wall_round_{bit}",
            functools.partial(wall_round, lines, bit, final),
            inside([matrix, exchange(matrix, "normal", 1 << bit)])
            + (outside([coupling.reshape(fields * fields, lanes, wide)]) if final else []),
            inside(
                [
                    f32((4 if final else MATRIX) * lines, wide),
                    f32(UP, lines, wide),
                    f32(MERGE_DOWN, lines, wide),
                ]
                + (
                    [
                        f32(12, lines, wide),
                        jax.ShapeDtypeStruct((fields * fields, lanes, wide), coupling.dtype),
                    ]
                    if final
                    else []
                )
            ),
            [pltpu.SemaphoreType.DMA((fields,))] if final else [],
            200 * lines * wide,
        )
        round_ups.append(up)
        round_downs.append(down)
    outer, coupling_in = extra[:1], extra[1]
    source, *wall_ws = kernel(
        "middle",
        functools.partial(middle, fields, span, wrap_cells, wall_cells, wrap_bits),
        inside(
            [element]
            + wrap_others
            + wrap_ups
            + wrap_ws
            + wrap_factors
            + [coupling_in, damps, chunk_down]
            + wall_downs
        ),
        inside(
            [f32(SOURCE * lines, wide), f32(wall_pairs * 2, wall_rows, wide)]
            + [f32(2, n, wide) for n in wall_levels]
        ),
        [vmem(4, n, lanes) for n in reversed([wrap_rows] + wrap_levels)]
        + [vmem(fields * wide, lanes), vmem(fields * lanes, wide), vmem(fields * lanes, wide)]
        + [vmem(SOURCE, n, wide) for n in [wall_rows] + wall_levels],
        100 * residual.size,
    )
    round_ws = []
    for bit in range(wall_bits):
        source, w = kernel(
            f"wall_source_round_{bit}",
            functools.partial(wall_source_round, lines, bit),
            inside([source, exchange(source, "normal", 1 << bit), round_downs[bit]]),
            inside([f32(SOURCE * lines, wide), f32(2, lines, wide)]),
            [],
            50 * lines * wide,
        )
        round_ws.append(w)
    share, bundle, source = kernel(
        "wall_share",
        functools.partial(wall_share, lines, wall_bits),
        inside([source, round_downs[wall_bits]] + outer + [matrix]),
        inside([f32(SOURCE * lines, wide), f32(6 * lines, wide), f32(SOURCE * lines, wide)]),
        [],
        50 * lines * wide,
    )
    (update,) = kernel(
        "wall_up",
        functools.partial(wall_up, fields, span, wall_cells, wall_bits),
        inside(
            [matrix, round_downs[wall_bits]]
            + outer
            + [
                source,
                pass_on(bundle, "normal", wall_bits, (2, 3, 1, 0)),
                exchange(source, "normal", 1 << wall_bits),
                pass_on(share, "normal", wall_bits, (3, 2, 0, 1)),
            ]
            + round_ups
            + round_ws
            + [chunk_up, wall_ws[0]]
            + wall_ups
            + wall_ws[1:]
        ),
        [(f32(fields * lanes, wide), IN_HBM)],
        [vmem(4, n, wide) for n in reversed([wall_rows] + wall_levels)]
        + [vmem(fields * lanes, wide), pltpu.SemaphoreType.DMA((2,))],
        30 * residual.size,
    )
    return update.reshape(residual.shape)


def solution(mesh):
    placed = (
        P(None, None, "normal", "wrap"),
        P(None, None, "normal", "wrap"),
        P(None, None, "normal", "wrap"),
        P(None, "normal", "wrap"),
        P(None, "normal", "wrap"),
        P(None, None, None, "normal", "wrap"),
    )
    return jax.shard_map(
        local,
        mesh=mesh,
        in_specs=placed,
        out_specs=P(None, None, "normal", "wrap"),
        check_vma=False,
    )
```

```python
import functools

import jax
import jax.numpy as jnp
from jax import lax
from jax.experimental import pallas as pl
from jax.experimental.pallas import tpu as pltpu
from jax.sharding import PartitionSpec as P

MATRIX = 16
SOURCE = 4
VALUES = MATRIX + SOURCE
UP = 8
CHUNK_DOWN = 9
MERGE_DOWN = 12
CHUNKS = 8


def inverse(a, b, c, d):
    scale = 1.0 / (a * d - b * c)
    return (d * scale, -b * scale, -c * scale, a * scale)


def times(x, y):
    return (
        x[0] * y[0] + x[1] * y[2],
        x[0] * y[1] + x[1] * y[3],
        x[2] * y[0] + x[3] * y[2],
        x[2] * y[1] + x[3] * y[3],
    )


def apply(x, v):
    return (x[0] * v[0] + x[1] * v[1], x[2] * v[0] + x[3] * v[1])


def minus(x, y):
    return tuple(a - b for a, b in zip(x, y))


def plus(x, y):
    return tuple(a + b for a, b in zip(x, y))


def negative(x):
    return tuple(-a for a in x)


def quads(element):
    return (element[0:4], element[4:8], element[8:12], element[12:16])


def merge_matrix(first, second):
    ll, lm, ml, mm = quads(first)
    nn, mr, rm, rr = quads(second)
    pivot = inverse(*plus(mm, nn))
    wl = times(pivot, ml)
    wr = times(pivot, mr)
    merged = (
        minus(ll, times(lm, wl))
        + negative(times(lm, wr))
        + negative(times(rm, wl))
        + minus(rr, times(rm, wr))
    )
    return merged, wl + wr, pivot + lm + rm


def merge_source(down, first, second):
    pivot, lm, rm = down[0:4], down[4:8], down[8:12]
    w = apply(pivot, plus(first[2:4], second[0:2]))
    return minus(first[0:2], apply(lm, w)) + minus(second[2:4], apply(rm, w)), w


def merge(first, second):
    matrix, up, down = merge_matrix(first[:MATRIX], second[:MATRIX])
    source, w = merge_source(down, first[MATRIX:], second[MATRIX:])
    return matrix + source, up, w


def inner(up, w, left, right):
    return minus(minus(w, apply(up[0:4], left)), apply(up[4:8], right))


def chunk_matrix(speed, damp, cells):
    def link(i):
        p = 2.0 * (damp(i) + damp(i + 1))
        q = 0.25 * (speed(i) + speed(i + 1))
        return q - p, -q - p

    def centre(i):
        return 1.0 + damp(i - 1) + 4.0 * damp(i) + damp(i + 1)

    b0, b1 = damp(0), damp(1)
    quarter = 0.25 * speed(0)
    up, low = link(0)
    zero = jnp.zeros_like(b0)
    ll = (b0, quarter - 2.0 * b0, -quarter - 2.0 * b0, 1.0 + 4.0 * b0 + b1)
    lk = (b0, zero, up, b1)
    kl = (b0, low, zero, b1)
    up, low = link(1)
    kk = (centre(1), up, low, centre(2))
    pairs = (cells - 2) // 2
    for k in range(1, pairs + 1):
        i = 2 * k
        pivot = inverse(*kk)
        wl = times(pivot, kl)
        up, low = link(i)
        here, there = damp(i), damp(i + 1)
        wr = (
            pivot[0] * here + pivot[1] * up,
            pivot[1] * there,
            pivot[2] * here + pivot[3] * up,
            pivot[3] * there,
        )
        yield wl + wr, pivot + lk + (low,), (here, there)

        def below(x):
            return (
                here * x[0] + low * x[2],
                here * x[1] + low * x[3],
                there * x[2],
                there * x[3],
            )

        ll = minus(ll, times(lk, wl))
        lk = negative(times(lk, wr))
        kl = negative(below(wl))
        if k < pairs:
            up, low_next = link(i + 1)
            kk = (centre(i + 1), up, low_next, centre(i + 2))
        else:
            quarter = 0.25 * speed(i + 1)
            kk = (
                1.0 + here + 4.0 * there,
                quarter - 2.0 * there,
                -quarter - 2.0 * there,
                there,
            )
        kk = minus(kk, below(wr))
    yield ll + lk + kl + kk


def pair_source(down, damps, left, pair, following):
    pivot, lk, low = down[0:4], down[4:8], down[8]
    w = apply(pivot, pair)
    left = minus(left, apply(lk, w))
    following = minus(following, (damps[0] * w[0] + low * w[1], damps[1] * w[1]))
    return left, following, w


def pair_of(source, k, cells):
    if k == (cells - 2) // 2:
        last = source(cells - 1)
        return (last, jnp.zeros_like(last))
    return (source(2 * k + 1), source(2 * k + 2))


def first_pair(source):
    first = source(0)
    return (jnp.zeros_like(first), first)


def blocks(rows, size):
    return [(at, min(size, rows - at)) for at in range(0, rows, size)]


def get(ref, count, at, size, base=0):
    return tuple(ref[base + v, pl.ds(at, size), :] for v in range(count))


def put(ref, values, at, size, base=0):
    for v, value in enumerate(values):
        ref[base + v, pl.ds(at, size), :] = value


def get_both(ref, count, at, size):
    return tuple(
        tuple(ref[v, pl.ds(2 * at + half, size, stride=2), :] for v in range(count))
        for half in (0, 1)
    )


def levels_of(lines):
    sizes = []
    rows = lines * CHUNKS
    while rows > lines:
        rows //= 2
        sizes.append(rows)
    return sizes


def split_all(top_ref, end_refs, up_refs, w_refs, sizes):
    source = top_ref
    for rows, target, ups, ws in zip(
        reversed(sizes), end_refs, reversed(up_refs), reversed(w_refs)
    ):
        for at, size in blocks(rows, 8):
            ends = get(source, 4, at, size)
            left, right = ends[0:2], ends[2:4]
            middle = inner(get(ups, UP, at, size), get(ws, 2, at, size), left, right)
            for v in range(2):
                target[v, pl.ds(2 * at, size, stride=2), :] = left[v]
                target[v, pl.ds(2 * at + 1, size, stride=2), :] = middle[v]
                target[2 + v, pl.ds(2 * at, size, stride=2), :] = middle[v]
                target[2 + v, pl.ds(2 * at + 1, size, stride=2), :] = right[v]
        source = target
    return source


def back_substitute(ends_ref, up_ref, w_ref, cells, at, size, store):
    ends = get(ends_ref, 4, at, size)
    left, following = ends[0:2], ends[2:4]
    store(0, left[1])
    store(cells - 1, following[0])
    for k in range((cells - 2) // 2 - 1, -1, -1):
        following = inner(
            get(up_ref, UP, at, size, k * UP), get(w_ref, 2, at, size, k * 2), left, following
        )
        store(2 * k + 1, following[0])
        store(2 * k + 2, following[1])


def close_ring(own, rest):
    ll, lr, rl, rr = quads(own)
    nn, nm, mn, mm = quads(rest)
    b = plus(lr, mn)
    c = plus(rl, nm)
    pivot = inverse(*plus(rr, nn))
    f = plus(own[16:18], rest[18:20])
    g = plus(own[18:20], rest[16:18])
    bd = times(b, pivot)
    left = apply(inverse(*minus(plus(ll, mm), times(bd, c))), minus(f, apply(bd, g)))
    right = apply(pivot, minus(g, apply(c, left)))
    return left, right


def open_ends(axis):
    place = lax.axis_index(axis)
    last = lax.axis_size(axis) - 1
    return jnp.where(place > 0, 1.0, 0.0), jnp.where(place < last, 1.0, 0.0)


def is_second(axis, bit):
    return lax.rem(lax.axis_index(axis) // (1 << bit), 2) == 1


def choose(second, one, other):
    return tuple(jnp.where(second, a, b) for a, b in zip(one, other))


def flat(ref, count, rows, at, size):
    return tuple(ref[pl.ds(v * rows + at, size), :] for v in range(count))


def put_flat(ref, values, rows, at, size):
    for v, value in enumerate(values):
        ref[pl.ds(v * rows + at, size), :] = value


def round_down(ups, ws, axis, bits, at, size, left, right):
    for bit in reversed(range(bits)):
        middle = inner(get(ups[bit], UP, at, size), get(ws[bit], 2, at, size), left, right)
        second = is_second(axis, bit)
        left, right = choose(second, middle, left), choose(second, right, middle)
    return left, right


def copies(pairs, sems, first=0):
    started = []
    for i, (source, target) in enumerate(pairs):
        copy = pltpu.make_async_copy(source, target, sems.at[first + i])
        copy.start()
        started.append(copy)
    return started


def wrap_down(fields, cells, *refs):
    residual, courant, dissip, wall_courant, wall_dissip = refs[0:5]
    packed, chunk_up, chunk_w = refs[5:8]
    ups, ws = refs[8:11], refs[11:14]
    wall_speed, wall_damp = refs[14:16]
    source_in, speed_in, damp_in, source_t, speed_t, damp_t = refs[16:22]
    elements, sems = refs[22:26], refs[26]
    lanes = damp_in.shape[0]
    length = cells * CHUNKS
    parts = [(0, 2), (2, fields)] if fields > 2 else [(0, fields)]
    moves = [(dissip, damp_in)]
    for first, last in parts:
        rows = pl.ds(first * lanes, (last - first) * lanes)
        moves.append((courant.at[rows], speed_in.at[rows]))
        moves.append((residual.at[rows], source_in.at[rows]))
    started = copies(moves, sems)
    started[0].wait()
    damp_t[...] = damp_in[...].T
    for part, (first, last) in enumerate(parts):
        at, size, repeat = first * CHUNKS, (last - first) * CHUNKS, last - first
        for inner_copy, taken, turned in (
            (started[1 + 2 * part], speed_in, speed_t),
            (started[2 + 2 * part], source_in, source_t),
        ):
            inner_copy.wait()
            for field in range(first, last):
                turned[pl.ds(field * length, length), :] = taken[pl.ds(field * lanes, lanes), :].T

        if part == 0:
            moves = [(wall_dissip, wall_damp), (wall_courant, wall_speed)]
            wall_started = copies(moves, sems, len(started))

        def speed(i):
            return speed_t[pl.ds(at * cells + i, size, stride=cells), :]

        def source(i):
            return source_t[pl.ds(at * cells + i, size, stride=cells), :]

        def damp(i):
            rows = damp_t[pl.ds(i, CHUNKS, stride=cells), :]
            return jnp.concatenate([rows] * repeat, axis=0) if repeat > 1 else rows

        left, pair = first_pair(source), pair_of(source, 0, cells)
        for k, step in enumerate(chunk_matrix(speed, damp, cells)):
            if k == (cells - 2) // 2:
                put(elements[0], step + left + pair, at, size)
                break
            up, down, damps = step
            left, pair, w = pair_source(down, damps, left, pair, pair_of(source, k + 1, cells))
            put(chunk_up, up, at, size, k * UP)
            put(chunk_w, w, at, size, k * 2)
    for level, rows in enumerate(levels_of(fields)):
        for at, size in blocks(rows, 8):
            merged, up, w = merge(*get_both(elements[level], VALUES, at, size))
            put(elements[level + 1], merged, at, size)
            put(ups[level], up, at, size)
            put(ws[level], w, at, size)
    for v in range(VALUES):
        packed[pl.ds(v * fields, fields), :] = elements[-1][v]
    for copy in wall_started:
        copy.wait()


def wrap_round(fields, bit, own, other, after, packed, up_out, w_out):
    second = is_second("wrap", bit)
    for at, size in blocks(fields, 8):
        mine = flat(own, VALUES, fields, at, size)
        theirs = flat(other, VALUES, fields, at, size)
        merged, up, w = merge(choose(second, theirs, mine), choose(second, mine, theirs))
        put_flat(packed, merged, fields, at, size)
        put(up_out, up, at, size)
        put(w_out, w, at, size)


def wall_matrix(fields, span, cells, *refs):
    speed_in, damp_in = refs[0:2]
    packed, damp_out, chunk_up, chunk_down = refs[2:6]
    ups, downs = refs[6:9], refs[9:12]
    elements = refs[12:16]
    size = span * CHUNKS
    for field in range(fields):
        at = field * size

        def speed(i):
            return speed_in[pl.ds(at * cells + i, size, stride=cells), :]

        def damp(i):
            return damp_in[pl.ds(i, size, stride=cells), :]

        for k, step in enumerate(chunk_matrix(speed, damp, cells)):
            if k == (cells - 2) // 2:
                put(elements[0], step, at, size)
                break
            up, down, damps = step
            put(chunk_up, up, at, size, k * UP)
            put(chunk_down, down, at, size, k * CHUNK_DOWN)
            if field == 0:
                put(damp_out, damps, 0, size, k * 2)
    lines = fields * span
    for level, rows in enumerate(levels_of(lines)):
        for at, size in blocks(rows, 8):
            merged, up, down = merge_matrix(*get_both(elements[level], MATRIX, at, size))
            put(elements[level + 1], merged, at, size)
            put(ups[level], up, at, size)
            put(downs[level], down, at, size)
    not_first, not_last = open_ends("normal")
    for v in range(MATRIX):
        value = elements[-1][v]
        if v in (0, 1, 2, 4, 5, 8, 10):
            value = value * not_first
        if v in (5, 7, 10, 11, 13, 14, 15):
            value = value * not_last
        packed[pl.ds(v * lines, lines), :] = value


def wall_round(lines, bit, final, own, other, *refs):
    started = []
    if final:
        coupling, packed, up_out, down_out, outer_out, coupling_out, sems = refs
        count = sems.shape[0]
        parts = [pl.ds(k * count, count) for k in range(count)]
        started = copies([(coupling.at[k], coupling_out.at[k]) for k in parts], sems)
    else:
        packed, up_out, down_out = refs
    second = is_second("normal", bit)
    upper = is_second("normal", bit + 1)
    for at, size in blocks(lines, 8):
        mine = flat(own, MATRIX, lines, at, size)
        theirs = flat(other, MATRIX, lines, at, size)
        merged, up, down = merge_matrix(
            choose(second, theirs, mine), choose(second, mine, theirs)
        )
        put(up_out, up, at, size)
        put(down_out, down, at, size)
        if not final:
            put_flat(packed, merged, lines, at, size)
            continue
        ll, lr, rl, rr = quads(merged)
        outer, into = choose(upper, rr, ll), choose(upper, rl, lr)
        out, middle = choose(upper, lr, rl), choose(upper, ll, rr)
        is_upper = jnp.where(upper, 1.0, 0.0)
        pivot = inverse(
            outer[0] + (1.0 - is_upper), outer[1], outer[2], outer[3] + is_upper
        )
        put_flat(packed, minus(middle, times(out, times(pivot, into))), lines, at, size)
        put(outer_out, pivot + into + out, at, size)
    for copy in started:
        copy.wait()


def wall_source_round(lines, bit, own, other, down_in, packed, w_out):
    second = is_second("normal", bit)
    for at, size in blocks(lines, 8):
        mine = flat(own, SOURCE, lines, at, size)
        theirs = flat(other, SOURCE, lines, at, size)
        merged, w = merge_source(
            get(down_in, MERGE_DOWN, at, size),
            choose(second, theirs, mine),
            choose(second, mine, theirs),
        )
        put_flat(packed, merged, lines, at, size)
        put(w_out, w, at, size)


def reduce_source(down, factors, second, upper, mine, theirs):
    merged, w = merge_source(
        down, choose(second, theirs, mine), choose(second, mine, theirs)
    )
    outer = apply(factors[0:4], choose(upper, merged[2:4], merged[0:2]))
    centre = choose(upper, merged[0:2], merged[2:4])
    return minus(centre, apply(factors[8:12], outer)), outer, w


def wall_share(lines, bit, own, down_in, outer_in, matrix, share, bundle, copy):
    share[pl.ds(2 * lines, 2 * lines), :] = jnp.zeros((2 * lines, share.shape[1]), jnp.float32)
    copy[...] = own[...]
    bundle[pl.ds(2 * lines, 4 * lines), :] = matrix[...]
    second, upper = is_second("normal", bit), is_second("normal", bit + 1)
    for at, size in blocks(lines, 8):
        mine = flat(own, SOURCE, lines, at, size)
        none = tuple(jnp.zeros_like(value) for value in mine)
        down, factors = get(down_in, MERGE_DOWN, at, size), get(outer_in, 12, at, size)
        part, _, _ = reduce_source(down, factors, second, upper, mine, none)
        put_flat(share, part, lines, at, size)
        put_flat(bundle, part, lines, at, size)


def wrap_three(fields, own, following, before, packed, back_up, back_w, next_up, next_w):
    for at, size in blocks(fields, 8):
        run, up, w = merge(
            flat(before, VALUES, fields, at, size), flat(own, VALUES, fields, at, size)
        )
        put(back_up, up, at, size)
        put(back_w, w, at, size)
        run, up, w = merge(run, flat(following, VALUES, fields, at, size))
        put(next_up, up, at, size)
        put(next_w, w, at, size)
        put_flat(packed, run, fields, at, size)


def middle(fields, span, wrap_cells, wall_cells, bits, *refs):
    three, opposite, back_up, back_w, next_up, next_w = refs[0:6]
    refs = refs[6:]
    round_ups, round_ws, refs = refs[:bits], refs[bits : 2 * bits], refs[2 * bits :]
    chunk_up, chunk_w, ups, ws = refs[0], refs[1], refs[2:5], refs[5:8]
    coupling, damps_in, chunk_down, downs = refs[8], refs[9], refs[10], refs[11:14]
    packed, wall_w, wall_ws = refs[14], refs[15], refs[16:19]
    ends, solved_t, solved, mixed = refs[19:23], refs[23], refs[24], refs[25]
    sources = refs[26:30]

    for at, size in blocks(fields, 8):
        outer_left, outer_right = close_ring(
            flat(three, VALUES, fields, at, size), flat(opposite, VALUES, fields, at, size)
        )
        right = inner(get(next_up, UP, at, size), get(next_w, 2, at, size), outer_left, outer_right)
        left = inner(get(back_up, UP, at, size), get(back_w, 2, at, size), outer_left, right)
        left, right = round_down(round_ups, round_ws, "wrap", bits, at, size, left, right)
        put(ends[0], left + right, at, size)
    last = split_all(ends[0], ends[1:], ups, ws, levels_of(fields))
    length = wrap_cells * CHUNKS
    for at, size in blocks(fields * CHUNKS, 16):

        def store(i, value):
            solved_t[pl.ds(at * wrap_cells + i, size, stride=wrap_cells), :] = value

        back_substitute(last, chunk_up, chunk_w, wrap_cells, at, size, store)
    lanes = solved.shape[0] // fields
    for field in range(fields):
        solved[pl.ds(field * lanes, lanes), :] = solved_t[pl.ds(field * length, length), :].T

    for at, size in blocks(lanes, 16):
        update = [solved[pl.ds(j * lanes + at, size), :] for j in range(fields)]
        for k in range(fields):
            total = coupling[k * fields, pl.ds(at, size), :].astype(jnp.float32) * update[0]
            for j in range(1, fields):
                factor = coupling[k * fields + j, pl.ds(at, size), :]
                total = total + factor.astype(jnp.float32) * update[j]
            mixed[pl.ds(k * lanes + at, size), :] = total

    pairs = (wall_cells - 2) // 2
    size = span * CHUNKS
    for field in range(fields):
        at = field * size

        def source(i):
            return mixed[pl.ds(at * wall_cells + i, size, stride=wall_cells), :]

        left, pair = first_pair(source), pair_of(source, 0, wall_cells)
        for k in range(pairs):
            left, pair, w = pair_source(
                get(chunk_down, CHUNK_DOWN, at, size, k * CHUNK_DOWN),
                get(damps_in, 2, 0, size, k * 2),
                left,
                pair,
                pair_of(source, k + 1, wall_cells),
            )
            put(wall_w, w, at, size, k * 2)
        put(sources[0], left + pair, at, size)
    lines = fields * span
    for level, rows in enumerate(levels_of(lines)):
        for at, size in blocks(rows, 8):
            down = get(downs[level], MERGE_DOWN, at, size)
            merged, w = merge_source(down, *get_both(sources[level], SOURCE, at, size))
            put(sources[level + 1], merged, at, size)
            put(wall_ws[level], w, at, size)
    not_first, not_last = open_ends("normal")
    for v, keep in enumerate((not_first, None, None, not_last)):
        value = sources[-1][v]
        packed[pl.ds(v * lines, lines), :] = value if keep is None else value * keep


def wall_up(fields, span, cells, bits, *refs):
    own_matrix, down_in, outer_in, own, bundle, other, share = refs[0:7]
    refs = refs[7:]
    round_ups, round_ws, refs = refs[: bits + 1], refs[bits + 1 : 2 * bits + 1], refs[2 * bits + 1 :]
    chunk_up, chunk_w, ups, ws = refs[0], refs[1], refs[2:5], refs[5:8]
    update = refs[8]
    ends, result, sems = refs[9:13], refs[13], refs[14]
    lines = fields * span
    second, upper = is_second("normal", bits), is_second("normal", bits + 1)
    for at, size in blocks(lines, 8):
        down, factors = get(down_in, MERGE_DOWN, at, size), get(outer_in, 12, at, size)
        part, outer, w = reduce_source(
            down,
            factors,
            second,
            upper,
            flat(own, SOURCE, lines, at, size),
            flat(other, SOURCE, lines, at, size),
        )
        opposite = flat(bundle, 6, lines, at, size)
        shares = plus(opposite[0:2], flat(share, 2, lines, at, size))
        matrix = plus(flat(own_matrix, 4, lines, at, size), opposite[2:6])
        centre = apply(inverse(*matrix), plus(part, shares))
        outer = minus(outer, apply(factors[0:4], apply(factors[4:8], centre)))
        left, right = choose(upper, centre, outer), choose(upper, outer, centre)
        between = inner(get(round_ups[bits], UP, at, size), w, left, right)
        left, right = choose(second, between, left), choose(second, right, between)
        left, right = round_down(round_ups, round_ws, "normal", bits, at, size, left, right)
        put(ends[0], left + right, at, size)
    last = split_all(ends[0], ends[1:], ups, ws, levels_of(lines))
    size = span * CHUNKS
    length = size * cells
    started = []
    for field in range(fields):
        at = field * size

        def store(i, value):
            result[pl.ds(at * cells + i, size, stride=cells), :] = value

        back_substitute(last, chunk_up, chunk_w, cells, at, size, store)
        rows = pl.ds(field * length, length)
        copy = pltpu.make_async_copy(result.at[rows], update.at[rows], sems.at[field])
        copy.start()
        started.append(copy)
    for copy in started:
        copy.wait()


def f32(*shape):
    return jax.ShapeDtypeStruct(shape, jnp.float32)


def vmem(*shape):
    return pltpu.VMEM(shape, jnp.float32)


IN_VMEM = pl.BlockSpec(memory_space=pltpu.VMEM)
IN_HBM = pl.BlockSpec(memory_space=pltpu.HBM)
PARAMS = pltpu.CompilerParams(vmem_limit_bytes=24 * 2**20)


def kernel(name, body, ins, outs, scratch, flops):
    in_bytes = sum(a.size * a.dtype.itemsize for a, _ in ins)
    out_bytes = sum(a.size * 4 for a, _ in outs)
    outputs = pl.pallas_call(
        body,
        out_shape=[a for a, _ in outs],
        in_specs=[spec for _, spec in ins],
        out_specs=[spec for _, spec in outs],
        scratch_shapes=scratch,
        compiler_params=PARAMS,
        cost_estimate=pl.CostEstimate(
            flops=flops, bytes_accessed=in_bytes + out_bytes, transcendentals=0
        ),
        name=name,
    )(*[a for a, _ in ins])
    return list(outputs)


def inside(arrays):
    return [(a, IN_VMEM) for a in arrays]


def outside(arrays):
    return [(pltpu.with_memory_space_constraint(a, pltpu.HBM), IN_HBM) for a in arrays]


def exchange(array, axis, mask):
    count = lax.axis_size(axis)
    return lax.ppermute(array, axis, [(i, i ^ mask) for i in range(count)])


def pass_on(array, axis, bit, targets, swap=0):
    count = lax.axis_size(axis)

    def target(i):
        place = i // (1 << bit) % 4
        return (i + (targets[place] - place) * (1 << bit)) ^ swap

    return lax.ppermute(array, axis, [(i, target(i)) for i in range(count)])


def local(residual, courant_xi, courant_eta, dissip_xi, dissip_eta, coupling):
    fields, span, high, wide = residual.shape
    lanes = span * high
    wrap_cells, wall_cells = wide // CHUNKS, high // CHUNKS
    wrap_pairs, wall_pairs = (wrap_cells - 2) // 2, (wall_cells - 2) // 2
    wrap_count, wall_count = lax.axis_size("wrap"), lax.axis_size("normal")
    lines = fields * span
    wrap_levels, wall_levels = levels_of(fields), levels_of(lines)
    wrap_rows, wall_rows = fields * CHUNKS, lines * CHUNKS

    def rows_of(array):
        return array.reshape(-1, wide)

    wrap_bits = wrap_count.bit_length() - 3
    wall_bits = wall_count.bit_length() - 3
    results = kernel(
        "wrap_down",
        functools.partial(wrap_down, fields, wrap_cells),
        outside(
            [rows_of(a) for a in (residual, courant_xi, dissip_xi, courant_eta, dissip_eta)]
        ),
        inside(
            [
                f32(VALUES * fields, lanes),
                f32(wrap_pairs * UP, wrap_rows, lanes),
                f32(wrap_pairs * 2, wrap_rows, lanes),
            ]
            + [f32(UP, n, lanes) for n in wrap_levels]
            + [f32(2, n, lanes) for n in wrap_levels]
            + [f32(fields * lanes, wide), f32(lanes, wide)]
        ),
        [vmem(fields * lanes, wide)] * 2
        + [vmem(lanes, wide)]
        + [vmem(fields * wide, lanes)] * 2
        + [vmem(wide, lanes)]
        + [vmem(VALUES, n, lanes) for n in [wrap_rows] + wrap_levels]
        + [pltpu.SemaphoreType.DMA((7,))],
        100 * residual.size,
    )
    element, wrap_factors, wall_inputs = results[0], results[1:9], results[9:11]
    results = kernel(
        "wall_matrix",
        functools.partial(wall_matrix, fields, span, wall_cells),
        inside(wall_inputs),
        inside(
            [
                f32(MATRIX * lines, wide),
                f32(wall_pairs * 2, span * CHUNKS, wide),
                f32(wall_pairs * UP, wall_rows, wide),
                f32(wall_pairs * CHUNK_DOWN, wall_rows, wide),
            ]
            + [f32(UP, n, wide) for n in wall_levels]
            + [f32(MERGE_DOWN, n, wide) for n in wall_levels]
        ),
        [vmem(MATRIX, n, wide) for n in [wall_rows] + wall_levels],
        100 * residual.size,
    )
    matrix, damps, chunk_up, chunk_down = results[0:4]
    wall_ups, wall_downs = results[4:7], results[7:10]
    wrap_ups, wrap_ws = [], []
    for bit in range(wrap_bits):
        element, up, w = kernel(
            f"wrap_round_{bit}",
            functools.partial(wrap_round, fields, bit),
            inside([element, exchange(element, "wrap", 1 << bit), damps]),
            inside([f32(VALUES * fields, lanes), f32(UP, fields, lanes), f32(2, fields, lanes)]),
            [],
            200 * fields * lanes,
        )
        wrap_ups.append(up)
        wrap_ws.append(w)
    swap = 1 if wrap_bits > 0 else 0
    before, following, opposite = (
        pass_on(element, "wrap", wrap_bits, targets, swap)
        for targets in ((1, 2, 3, 0), (3, 0, 1, 2), (2, 3, 0, 1))
    )
    three = kernel(
        "wrap_three",
        functools.partial(wrap_three, fields),
        inside([element, following, before]),
        inside(
            [f32(VALUES * fields, lanes)]
            + [f32(UP, fields, lanes), f32(2, fields, lanes)] * 2
        ),
        [],
        400 * fields * lanes,
    )
    round_ups, round_downs = [], []
    for bit in range(wall_bits + 1):
        final = bit == wall_bits
        matrix, up, down, *extra = kernel(
            f"wall_round_{bit}",
            functools.partial(wall_round, lines, bit, final),
            inside([matrix, exchange(matrix, "normal", 1 << bit)])
            + (outside([coupling.reshape(fields * fields, lanes, wide)]) if final else []),
            inside(
                [
                    f32((4 if final else MATRIX) * lines, wide),
                    f32(UP, lines, wide),
                    f32(MERGE_DOWN, lines, wide),
                ]
                + (
                    [
                        f32(12, lines, wide),
                        jax.ShapeDtypeStruct((fields * fields, lanes, wide), coupling.dtype),
                    ]
                    if final
                    else []
                )
            ),
            [pltpu.SemaphoreType.DMA((fields,))] if final else [],
            200 * lines * wide,
        )
        round_ups.append(up)
        round_downs.append(down)
    outer, coupling_in = extra[:1], extra[1]
    source, *wall_ws = kernel(
        "middle",
        functools.partial(middle, fields, span, wrap_cells, wall_cells, wrap_bits),
        inside(
            [three[0], opposite]
            + three[1:]
            + wrap_ups
            + wrap_ws
            + wrap_factors
            + [coupling_in, damps, chunk_down]
            + wall_downs
        ),
        inside(
            [f32(SOURCE * lines, wide), f32(wall_pairs * 2, wall_rows, wide)]
            + [f32(2, n, wide) for n in wall_levels]
        ),
        [vmem(4, n, lanes) for n in reversed([wrap_rows] + wrap_levels)]
        + [vmem(fields * wide, lanes), vmem(fields * lanes, wide), vmem(fields * lanes, wide)]
        + [vmem(SOURCE, n, wide) for n in [wall_rows] + wall_levels],
        100 * residual.size,
    )
    round_ws = []
    for bit in range(wall_bits):
        source, w = kernel(
            f"wall_source_round_{bit}",
            functools.partial(wall_source_round, lines, bit),
            inside([source, exchange(source, "normal", 1 << bit), round_downs[bit]]),
            inside([f32(SOURCE * lines, wide), f32(2, lines, wide)]),
            [],
            50 * lines * wide,
        )
        round_ws.append(w)
    share, bundle, source = kernel(
        "wall_share",
        functools.partial(wall_share, lines, wall_bits),
        inside([source, round_downs[wall_bits]] + outer + [matrix]),
        inside([f32(SOURCE * lines, wide), f32(6 * lines, wide), f32(SOURCE * lines, wide)]),
        [],
        50 * lines * wide,
    )
    (update,) = kernel(
        "wall_up",
        functools.partial(wall_up, fields, span, wall_cells, wall_bits),
        inside(
            [matrix, round_downs[wall_bits]]
            + outer
            + [
                source,
                pass_on(bundle, "normal", wall_bits, (2, 3, 1, 0)),
                exchange(source, "normal", 1 << wall_bits),
                pass_on(share, "normal", wall_bits, (3, 2, 0, 1)),
            ]
            + round_ups
            + round_ws
            + [chunk_up, wall_ws[0]]
            + wall_ups
            + wall_ws[1:]
        ),
        [(f32(fields * lanes, wide), IN_HBM)],
        [vmem(4, n, wide) for n in reversed([wall_rows] + wall_levels)]
        + [vmem(fields * lanes, wide), pltpu.SemaphoreType.DMA((fields,))],
        30 * residual.size,
    )
    return update.reshape(residual.shape)


def solution(mesh):
    placed = (
        P(None, None, "normal", "wrap"),
        P(None, None, "normal", "wrap"),
        P(None, None, "normal", "wrap"),
        P(None, "normal", "wrap"),
        P(None, "normal", "wrap"),
        P(None, None, None, "normal", "wrap"),
    )
    return jax.shard_map(
        local,
        mesh=mesh,
        in_specs=placed,
        out_specs=P(None, None, "normal", "wrap"),
        check_vma=False,
    )
```

```python
import functools

import jax
import jax.numpy as jnp
from jax import lax
from jax.experimental import pallas as pl
from jax.experimental.pallas import tpu as pltpu
from jax.sharding import PartitionSpec as P

MATRIX = 16
SOURCE = 4
VALUES = MATRIX + SOURCE
UP = 8
CHUNK_DOWN = 9
MERGE_DOWN = 12
CHUNKS = 8


def inverse(a, b, c, d):
    scale = 1.0 / (a * d - b * c)
    return (d * scale, -b * scale, -c * scale, a * scale)


def times(x, y):
    return (
        x[0] * y[0] + x[1] * y[2],
        x[0] * y[1] + x[1] * y[3],
        x[2] * y[0] + x[3] * y[2],
        x[2] * y[1] + x[3] * y[3],
    )


def apply(x, v):
    return (x[0] * v[0] + x[1] * v[1], x[2] * v[0] + x[3] * v[1])


def minus(x, y):
    return tuple(a - b for a, b in zip(x, y))


def plus(x, y):
    return tuple(a + b for a, b in zip(x, y))


def negative(x):
    return tuple(-a for a in x)


def quads(element):
    return (element[0:4], element[4:8], element[8:12], element[12:16])


def merge_matrix(first, second):
    ll, lm, ml, mm = quads(first)
    nn, mr, rm, rr = quads(second)
    pivot = inverse(*plus(mm, nn))
    wl = times(pivot, ml)
    wr = times(pivot, mr)
    merged = (
        minus(ll, times(lm, wl))
        + negative(times(lm, wr))
        + negative(times(rm, wl))
        + minus(rr, times(rm, wr))
    )
    return merged, wl + wr, pivot + lm + rm


def merge_source(down, first, second):
    pivot, lm, rm = down[0:4], down[4:8], down[8:12]
    w = apply(pivot, plus(first[2:4], second[0:2]))
    return minus(first[0:2], apply(lm, w)) + minus(second[2:4], apply(rm, w)), w


def merge(first, second):
    matrix, up, down = merge_matrix(first[:MATRIX], second[:MATRIX])
    source, w = merge_source(down, first[MATRIX:], second[MATRIX:])
    return matrix + source, up, w


def inner(up, w, left, right):
    return minus(minus(w, apply(up[0:4], left)), apply(up[4:8], right))


def chunk_matrix(speed, damp, cells):
    def link(i):
        p = 2.0 * (damp(i) + damp(i + 1))
        q = 0.25 * (speed(i) + speed(i + 1))
        return q - p, -q - p

    def centre(i):
        return 1.0 + damp(i - 1) + 4.0 * damp(i) + damp(i + 1)

    b0, b1 = damp(0), damp(1)
    quarter = 0.25 * speed(0)
    up, low = link(0)
    zero = jnp.zeros_like(b0)
    ll = (b0, quarter - 2.0 * b0, -quarter - 2.0 * b0, 1.0 + 4.0 * b0 + b1)
    lk = (b0, zero, up, b1)
    kl = (b0, low, zero, b1)
    up, low = link(1)
    kk = (centre(1), up, low, centre(2))
    pairs = (cells - 2) // 2
    for k in range(1, pairs + 1):
        i = 2 * k
        pivot = inverse(*kk)
        wl = times(pivot, kl)
        up, low = link(i)
        here, there = damp(i), damp(i + 1)
        wr = (
            pivot[0] * here + pivot[1] * up,
            pivot[1] * there,
            pivot[2] * here + pivot[3] * up,
            pivot[3] * there,
        )
        yield wl + wr, pivot + lk + (low,), (here, there)

        def below(x):
            return (
                here * x[0] + low * x[2],
                here * x[1] + low * x[3],
                there * x[2],
                there * x[3],
            )

        ll = minus(ll, times(lk, wl))
        lk = negative(times(lk, wr))
        kl = negative(below(wl))
        if k < pairs:
            up, low_next = link(i + 1)
            kk = (centre(i + 1), up, low_next, centre(i + 2))
        else:
            quarter = 0.25 * speed(i + 1)
            kk = (
                1.0 + here + 4.0 * there,
                quarter - 2.0 * there,
                -quarter - 2.0 * there,
                there,
            )
        kk = minus(kk, below(wr))
    yield ll + lk + kl + kk


def pair_source(down, damps, left, pair, following):
    pivot, lk, low = down[0:4], down[4:8], down[8]
    w = apply(pivot, pair)
    left = minus(left, apply(lk, w))
    following = minus(following, (damps[0] * w[0] + low * w[1], damps[1] * w[1]))
    return left, following, w


def pair_of(source, k, cells):
    if k == (cells - 2) // 2:
        last = source(cells - 1)
        return (last, jnp.zeros_like(last))
    return (source(2 * k + 1), source(2 * k + 2))


def first_pair(source):
    first = source(0)
    return (jnp.zeros_like(first), first)


def blocks(rows, size):
    return [(at, min(size, rows - at)) for at in range(0, rows, size)]


def get(ref, count, at, size, base=0):
    return tuple(ref[base + v, pl.ds(at, size), :] for v in range(count))


def put(ref, values, at, size, base=0):
    for v, value in enumerate(values):
        ref[base + v, pl.ds(at, size), :] = value


def get_both(ref, count, at, size):
    return tuple(
        tuple(ref[v, pl.ds(2 * at + half, size, stride=2), :] for v in range(count))
        for half in (0, 1)
    )


def levels_of(lines):
    sizes = []
    rows = lines * CHUNKS
    while rows > lines:
        rows //= 2
        sizes.append(rows)
    return sizes


def split_all(top_ref, end_refs, up_refs, w_refs, sizes):
    source = top_ref
    for rows, target, ups, ws in zip(
        reversed(sizes), end_refs, reversed(up_refs), reversed(w_refs)
    ):
        for at, size in blocks(rows, 8):
            ends = get(source, 4, at, size)
            left, right = ends[0:2], ends[2:4]
            middle = inner(get(ups, UP, at, size), get(ws, 2, at, size), left, right)
            for v in range(2):
                target[v, pl.ds(2 * at, size, stride=2), :] = left[v]
                target[v, pl.ds(2 * at + 1, size, stride=2), :] = middle[v]
                target[2 + v, pl.ds(2 * at, size, stride=2), :] = middle[v]
                target[2 + v, pl.ds(2 * at + 1, size, stride=2), :] = right[v]
        source = target
    return source


def back_substitute(ends_ref, up_ref, w_ref, cells, at, size, store):
    ends = get(ends_ref, 4, at, size)
    left, following = ends[0:2], ends[2:4]
    store(0, left[1])
    store(cells - 1, following[0])
    for k in range((cells - 2) // 2 - 1, -1, -1):
        following = inner(
            get(up_ref, UP, at, size, k * UP), get(w_ref, 2, at, size, k * 2), left, following
        )
        store(2 * k + 1, following[0])
        store(2 * k + 2, following[1])


def close_ring(own, rest):
    ll, lr, rl, rr = quads(own)
    nn, nm, mn, mm = quads(rest)
    b = plus(lr, mn)
    c = plus(rl, nm)
    pivot = inverse(*plus(rr, nn))
    f = plus(own[16:18], rest[18:20])
    g = plus(own[18:20], rest[16:18])
    bd = times(b, pivot)
    left = apply(inverse(*minus(plus(ll, mm), times(bd, c))), minus(f, apply(bd, g)))
    right = apply(pivot, minus(g, apply(c, left)))
    return left, right


def open_ends(axis):
    place = lax.axis_index(axis)
    last = lax.axis_size(axis) - 1
    return jnp.where(place > 0, 1.0, 0.0), jnp.where(place < last, 1.0, 0.0)


def is_second(axis, bit):
    return lax.rem(lax.axis_index(axis) // (1 << bit), 2) == 1


def choose(second, one, other):
    return tuple(jnp.where(second, a, b) for a, b in zip(one, other))


def flat(ref, count, rows, at, size):
    return tuple(ref[pl.ds(v * rows + at, size), :] for v in range(count))


def put_flat(ref, values, rows, at, size):
    for v, value in enumerate(values):
        ref[pl.ds(v * rows + at, size), :] = value


def round_down(ups, ws, axis, bits, at, size, left, right):
    for bit in reversed(range(bits)):
        middle = inner(get(ups[bit], UP, at, size), get(ws[bit], 2, at, size), left, right)
        second = is_second(axis, bit)
        left, right = choose(second, middle, left), choose(second, right, middle)
    return left, right


def copies(pairs, sems, first=0):
    started = []
    for i, (source, target) in enumerate(pairs):
        copy = pltpu.make_async_copy(source, target, sems.at[first + i])
        copy.start()
        started.append(copy)
    return started


def wrap_down(fields, cells, *refs):
    residual, courant, dissip, wall_courant, wall_dissip = refs[0:5]
    packed, chunk_up, chunk_w = refs[5:8]
    ups, ws = refs[8:11], refs[11:14]
    wall_speed, wall_damp = refs[14:16]
    source_in, speed_in, damp_in, source_t, speed_t, damp_t = refs[16:22]
    elements, sems = refs[22:26], refs[26]
    lanes = damp_in.shape[0]
    length = cells * CHUNKS
    parts = [(0, 2), (2, fields)] if fields > 2 else [(0, fields)]
    moves = [(dissip, damp_in)]
    for first, last in parts:
        rows = pl.ds(first * lanes, (last - first) * lanes)
        moves.append((courant.at[rows], speed_in.at[rows]))
        moves.append((residual.at[rows], source_in.at[rows]))
    started = copies(moves, sems)
    started[0].wait()
    damp_t[...] = damp_in[...].T
    for part, (first, last) in enumerate(parts):
        at, size, repeat = first * CHUNKS, (last - first) * CHUNKS, last - first
        for inner_copy, taken, turned in (
            (started[1 + 2 * part], speed_in, speed_t),
            (started[2 + 2 * part], source_in, source_t),
        ):
            inner_copy.wait()
            for field in range(first, last):
                turned[pl.ds(field * length, length), :] = taken[pl.ds(field * lanes, lanes), :].T

        if part == 0:
            moves = [(wall_dissip, wall_damp), (wall_courant, wall_speed)]
            wall_started = copies(moves, sems, len(started))

        def speed(i):
            return speed_t[pl.ds(at * cells + i, size, stride=cells), :]

        def source(i):
            return source_t[pl.ds(at * cells + i, size, stride=cells), :]

        def damp(i):
            rows = damp_t[pl.ds(i, CHUNKS, stride=cells), :]
            return jnp.concatenate([rows] * repeat, axis=0) if repeat > 1 else rows

        left, pair = first_pair(source), pair_of(source, 0, cells)
        for k, step in enumerate(chunk_matrix(speed, damp, cells)):
            if k == (cells - 2) // 2:
                put(elements[0], step + left + pair, at, size)
                break
            up, down, damps = step
            left, pair, w = pair_source(down, damps, left, pair, pair_of(source, k + 1, cells))
            put(chunk_up, up, at, size, k * UP)
            put(chunk_w, w, at, size, k * 2)
    for level, rows in enumerate(levels_of(fields)):
        for at, size in blocks(rows, 8):
            merged, up, w = merge(*get_both(elements[level], VALUES, at, size))
            put(elements[level + 1], merged, at, size)
            put(ups[level], up, at, size)
            put(ws[level], w, at, size)
    for v in range(VALUES):
        packed[pl.ds(v * fields, fields), :] = elements[-1][v]
    for copy in wall_started:
        copy.wait()


def wrap_round(fields, bit, own, other, after, packed, up_out, w_out):
    second = is_second("wrap", bit)
    for at, size in blocks(fields, 8):
        mine = flat(own, VALUES, fields, at, size)
        theirs = flat(other, VALUES, fields, at, size)
        merged, up, w = merge(choose(second, theirs, mine), choose(second, mine, theirs))
        put_flat(packed, merged, fields, at, size)
        put(up_out, up, at, size)
        put(w_out, w, at, size)


def wall_matrix(fields, span, cells, *refs):
    speed_in, damp_in = refs[0:2]
    packed, damp_out, chunk_up, chunk_down = refs[2:6]
    ups, downs = refs[6:9], refs[9:12]
    elements = refs[12:16]
    size = span * CHUNKS
    for field in range(fields):
        at = field * size

        def speed(i):
            return speed_in[pl.ds(at * cells + i, size, stride=cells), :]

        def damp(i):
            return damp_in[pl.ds(i, size, stride=cells), :]

        for k, step in enumerate(chunk_matrix(speed, damp, cells)):
            if k == (cells - 2) // 2:
                put(elements[0], step, at, size)
                break
            up, down, damps = step
            put(chunk_up, up, at, size, k * UP)
            put(chunk_down, down, at, size, k * CHUNK_DOWN)
            if field == 0:
                put(damp_out, damps, 0, size, k * 2)
    lines = fields * span
    for level, rows in enumerate(levels_of(lines)):
        for at, size in blocks(rows, 8):
            merged, up, down = merge_matrix(*get_both(elements[level], MATRIX, at, size))
            put(elements[level + 1], merged, at, size)
            put(ups[level], up, at, size)
            put(downs[level], down, at, size)
    not_first, not_last = open_ends("normal")
    for v in range(MATRIX):
        value = elements[-1][v]
        if v in (0, 1, 2, 4, 5, 8, 10):
            value = value * not_first
        if v in (5, 7, 10, 11, 13, 14, 15):
            value = value * not_last
        packed[pl.ds(v * lines, lines), :] = value


def wall_round(lines, bit, final, own, other, *refs):
    started = []
    if final:
        coupling, packed, up_out, down_out, outer_out, coupling_out, sems = refs
        count = sems.shape[0]
        parts = [pl.ds(k * count, count) for k in range(count)]
        started = copies([(coupling.at[k], coupling_out.at[k]) for k in parts], sems)
    else:
        packed, up_out, down_out = refs
    second = is_second("normal", bit)
    upper = is_second("normal", bit + 1)
    for at, size in blocks(lines, 8):
        mine = flat(own, MATRIX, lines, at, size)
        theirs = flat(other, MATRIX, lines, at, size)
        merged, up, down = merge_matrix(
            choose(second, theirs, mine), choose(second, mine, theirs)
        )
        put(up_out, up, at, size)
        put(down_out, down, at, size)
        if not final:
            put_flat(packed, merged, lines, at, size)
            continue
        ll, lr, rl, rr = quads(merged)
        outer, into = choose(upper, rr, ll), choose(upper, rl, lr)
        out, middle = choose(upper, lr, rl), choose(upper, ll, rr)
        is_upper = jnp.where(upper, 1.0, 0.0)
        pivot = inverse(
            outer[0] + (1.0 - is_upper), outer[1], outer[2], outer[3] + is_upper
        )
        put_flat(packed, minus(middle, times(out, times(pivot, into))), lines, at, size)
        put(outer_out, pivot + into + out, at, size)
    for copy in started:
        copy.wait()


def wall_source_round(lines, bit, own, other, down_in, packed, w_out):
    second = is_second("normal", bit)
    for at, size in blocks(lines, 8):
        mine = flat(own, SOURCE, lines, at, size)
        theirs = flat(other, SOURCE, lines, at, size)
        merged, w = merge_source(
            get(down_in, MERGE_DOWN, at, size),
            choose(second, theirs, mine),
            choose(second, mine, theirs),
        )
        put_flat(packed, merged, lines, at, size)
        put(w_out, w, at, size)


def reduce_source(down, factors, second, upper, mine, theirs):
    merged, w = merge_source(
        down, choose(second, theirs, mine), choose(second, mine, theirs)
    )
    outer = apply(factors[0:4], choose(upper, merged[2:4], merged[0:2]))
    centre = choose(upper, merged[0:2], merged[2:4])
    return minus(centre, apply(factors[8:12], outer)), outer, w


def wall_share(lines, bit, own, down_in, outer_in, matrix, share_one, share_two, copy):
    copy[...] = own[...]
    half = pl.ds(2 * lines, 2 * lines)
    share_one[half, :] = matrix[pl.ds(0, 2 * lines), :]
    share_two[half, :] = matrix[half, :]
    second, upper = is_second("normal", bit), is_second("normal", bit + 1)
    for at, size in blocks(lines, 8):
        mine = flat(own, SOURCE, lines, at, size)
        none = tuple(jnp.zeros_like(value) for value in mine)
        down, factors = get(down_in, MERGE_DOWN, at, size), get(outer_in, 12, at, size)
        part, _, _ = reduce_source(down, factors, second, upper, mine, none)
        put_flat(share_one, part, lines, at, size)
        put_flat(share_two, part, lines, at, size)


def wrap_three(fields, own, following, before, packed, back_up, back_w, next_up, next_w):
    for at, size in blocks(fields, 8):
        run, up, w = merge(
            flat(before, VALUES, fields, at, size), flat(own, VALUES, fields, at, size)
        )
        put(back_up, up, at, size)
        put(back_w, w, at, size)
        run, up, w = merge(run, flat(following, VALUES, fields, at, size))
        put(next_up, up, at, size)
        put(next_w, w, at, size)
        put_flat(packed, run, fields, at, size)


def middle(fields, span, wrap_cells, wall_cells, bits, *refs):
    three, opposite, back_up, back_w, next_up, next_w = refs[0:6]
    refs = refs[6:]
    round_ups, round_ws, refs = refs[:bits], refs[bits : 2 * bits], refs[2 * bits :]
    chunk_up, chunk_w, ups, ws = refs[0], refs[1], refs[2:5], refs[5:8]
    coupling, damps_in, chunk_down, downs = refs[8], refs[9], refs[10], refs[11:14]
    packed, wall_w, wall_ws = refs[14], refs[15], refs[16:19]
    ends, solved_t, solved, mixed = refs[19:23], refs[23], refs[24], refs[25]
    sources = refs[26:30]

    for at, size in blocks(fields, 8):
        outer_left, outer_right = close_ring(
            flat(three, VALUES, fields, at, size), flat(opposite, VALUES, fields, at, size)
        )
        right = inner(get(next_up, UP, at, size), get(next_w, 2, at, size), outer_left, outer_right)
        left = inner(get(back_up, UP, at, size), get(back_w, 2, at, size), outer_left, right)
        left, right = round_down(round_ups, round_ws, "wrap", bits, at, size, left, right)
        put(ends[0], left + right, at, size)
    last = split_all(ends[0], ends[1:], ups, ws, levels_of(fields))
    length = wrap_cells * CHUNKS
    for at, size in blocks(fields * CHUNKS, 16):

        def store(i, value):
            solved_t[pl.ds(at * wrap_cells + i, size, stride=wrap_cells), :] = value

        back_substitute(last, chunk_up, chunk_w, wrap_cells, at, size, store)
    lanes = solved.shape[0] // fields
    for field in range(fields):
        solved[pl.ds(field * lanes, lanes), :] = solved_t[pl.ds(field * length, length), :].T

    for at, size in blocks(lanes, 16):
        update = [solved[pl.ds(j * lanes + at, size), :] for j in range(fields)]
        for k in range(fields):
            total = coupling[k * fields, pl.ds(at, size), :].astype(jnp.float32) * update[0]
            for j in range(1, fields):
                factor = coupling[k * fields + j, pl.ds(at, size), :]
                total = total + factor.astype(jnp.float32) * update[j]
            mixed[pl.ds(k * lanes + at, size), :] = total

    pairs = (wall_cells - 2) // 2
    size = span * CHUNKS
    for field in range(fields):
        at = field * size

        def source(i):
            return mixed[pl.ds(at * wall_cells + i, size, stride=wall_cells), :]

        left, pair = first_pair(source), pair_of(source, 0, wall_cells)
        for k in range(pairs):
            left, pair, w = pair_source(
                get(chunk_down, CHUNK_DOWN, at, size, k * CHUNK_DOWN),
                get(damps_in, 2, 0, size, k * 2),
                left,
                pair,
                pair_of(source, k + 1, wall_cells),
            )
            put(wall_w, w, at, size, k * 2)
        put(sources[0], left + pair, at, size)
    lines = fields * span
    for level, rows in enumerate(levels_of(lines)):
        for at, size in blocks(rows, 8):
            down = get(downs[level], MERGE_DOWN, at, size)
            merged, w = merge_source(down, *get_both(sources[level], SOURCE, at, size))
            put(sources[level + 1], merged, at, size)
            put(wall_ws[level], w, at, size)
    not_first, not_last = open_ends("normal")
    for v, keep in enumerate((not_first, None, None, not_last)):
        value = sources[-1][v]
        packed[pl.ds(v * lines, lines), :] = value if keep is None else value * keep


def wall_up(fields, span, cells, bits, *refs):
    own_matrix, down_in, outer_in, own, other, share_two, share_one = refs[0:7]
    refs = refs[7:]
    round_ups, round_ws, refs = refs[: bits + 1], refs[bits + 1 : 2 * bits + 1], refs[2 * bits + 1 :]
    chunk_up, chunk_w, ups, ws = refs[0], refs[1], refs[2:5], refs[5:8]
    update = refs[8]
    ends, result, sems = refs[9:13], refs[13], refs[14]
    lines = fields * span
    second, upper = is_second("normal", bits), is_second("normal", bits + 1)
    for at, size in blocks(lines, 8):
        down, factors = get(down_in, MERGE_DOWN, at, size), get(outer_in, 12, at, size)
        part, outer, w = reduce_source(
            down,
            factors,
            second,
            upper,
            flat(own, SOURCE, lines, at, size),
            flat(other, SOURCE, lines, at, size),
        )
        one, two = (flat(share, 4, lines, at, size) for share in (share_one, share_two))
        shares = plus(one[0:2], two[0:2])
        matrix = plus(flat(own_matrix, 4, lines, at, size), one[2:4] + two[2:4])
        centre = apply(inverse(*matrix), plus(part, shares))
        outer = minus(outer, apply(factors[0:4], apply(factors[4:8], centre)))
        left, right = choose(upper, centre, outer), choose(upper, outer, centre)
        between = inner(get(round_ups[bits], UP, at, size), w, left, right)
        left, right = choose(second, between, left), choose(second, right, between)
        left, right = round_down(round_ups, round_ws, "normal", bits, at, size, left, right)
        put(ends[0], left + right, at, size)
    last = split_all(ends[0], ends[1:], ups, ws, levels_of(lines))
    size = span * CHUNKS
    length = size * cells
    started = []
    for field in range(fields):
        at = field * size

        def store(i, value):
            result[pl.ds(at * cells + i, size, stride=cells), :] = value

        back_substitute(last, chunk_up, chunk_w, cells, at, size, store)
        rows = pl.ds(field * length, length)
        copy = pltpu.make_async_copy(result.at[rows], update.at[rows], sems.at[field])
        copy.start()
        started.append(copy)
    for copy in started:
        copy.wait()


def f32(*shape):
    return jax.ShapeDtypeStruct(shape, jnp.float32)


def vmem(*shape):
    return pltpu.VMEM(shape, jnp.float32)


IN_VMEM = pl.BlockSpec(memory_space=pltpu.VMEM)
IN_HBM = pl.BlockSpec(memory_space=pltpu.HBM)
PARAMS = pltpu.CompilerParams(vmem_limit_bytes=24 * 2**20)


def kernel(name, body, ins, outs, scratch, flops):
    in_bytes = sum(a.size * a.dtype.itemsize for a, _ in ins)
    out_bytes = sum(a.size * 4 for a, _ in outs)
    outputs = pl.pallas_call(
        body,
        out_shape=[a for a, _ in outs],
        in_specs=[spec for _, spec in ins],
        out_specs=[spec for _, spec in outs],
        scratch_shapes=scratch,
        compiler_params=PARAMS,
        cost_estimate=pl.CostEstimate(
            flops=flops, bytes_accessed=in_bytes + out_bytes, transcendentals=0
        ),
        name=name,
    )(*[a for a, _ in ins])
    return list(outputs)


def inside(arrays):
    return [(a, IN_VMEM) for a in arrays]


def outside(arrays):
    return [(pltpu.with_memory_space_constraint(a, pltpu.HBM), IN_HBM) for a in arrays]


def exchange(array, axis, mask):
    count = lax.axis_size(axis)
    return lax.ppermute(array, axis, [(i, i ^ mask) for i in range(count)])


def pass_on(array, axis, bit, targets, swap=0):
    count = lax.axis_size(axis)

    def target(i):
        place = i // (1 << bit) % 4
        return (i + (targets[place] - place) * (1 << bit)) ^ swap

    return lax.ppermute(array, axis, [(i, target(i)) for i in range(count)])


def local(residual, courant_xi, courant_eta, dissip_xi, dissip_eta, coupling):
    fields, span, high, wide = residual.shape
    lanes = span * high
    wrap_cells, wall_cells = wide // CHUNKS, high // CHUNKS
    wrap_pairs, wall_pairs = (wrap_cells - 2) // 2, (wall_cells - 2) // 2
    wrap_count, wall_count = lax.axis_size("wrap"), lax.axis_size("normal")
    lines = fields * span
    wrap_levels, wall_levels = levels_of(fields), levels_of(lines)
    wrap_rows, wall_rows = fields * CHUNKS, lines * CHUNKS

    def rows_of(array):
        return array.reshape(-1, wide)

    wrap_bits = wrap_count.bit_length() - 3
    wall_bits = wall_count.bit_length() - 3
    results = kernel(
        "wrap_down",
        functools.partial(wrap_down, fields, wrap_cells),
        outside(
            [rows_of(a) for a in (residual, courant_xi, dissip_xi, courant_eta, dissip_eta)]
        ),
        inside(
            [
                f32(VALUES * fields, lanes),
                f32(wrap_pairs * UP, wrap_rows, lanes),
                f32(wrap_pairs * 2, wrap_rows, lanes),
            ]
            + [f32(UP, n, lanes) for n in wrap_levels]
            + [f32(2, n, lanes) for n in wrap_levels]
            + [f32(fields * lanes, wide), f32(lanes, wide)]
        ),
        [vmem(fields * lanes, wide)] * 2
        + [vmem(lanes, wide)]
        + [vmem(fields * wide, lanes)] * 2
        + [vmem(wide, lanes)]
        + [vmem(VALUES, n, lanes) for n in [wrap_rows] + wrap_levels]
        + [pltpu.SemaphoreType.DMA((7,))],
        100 * residual.size,
    )
    element, wrap_factors, wall_inputs = results[0], results[1:9], results[9:11]
    results = kernel(
        "wall_matrix",
        functools.partial(wall_matrix, fields, span, wall_cells),
        inside(wall_inputs),
        inside(
            [
                f32(MATRIX * lines, wide),
                f32(wall_pairs * 2, span * CHUNKS, wide),
                f32(wall_pairs * UP, wall_rows, wide),
                f32(wall_pairs * CHUNK_DOWN, wall_rows, wide),
            ]
            + [f32(UP, n, wide) for n in wall_levels]
            + [f32(MERGE_DOWN, n, wide) for n in wall_levels]
        ),
        [vmem(MATRIX, n, wide) for n in [wall_rows] + wall_levels],
        100 * residual.size,
    )
    matrix, damps, chunk_up, chunk_down = results[0:4]
    wall_ups, wall_downs = results[4:7], results[7:10]
    wrap_ups, wrap_ws = [], []
    for bit in range(wrap_bits):
        element, up, w = kernel(
            f"wrap_round_{bit}",
            functools.partial(wrap_round, fields, bit),
            inside([element, exchange(element, "wrap", 1 << bit), damps]),
            inside([f32(VALUES * fields, lanes), f32(UP, fields, lanes), f32(2, fields, lanes)]),
            [],
            200 * fields * lanes,
        )
        wrap_ups.append(up)
        wrap_ws.append(w)
    swap = 1 if wrap_bits > 0 else 0
    before, following, opposite = (
        pass_on(element, "wrap", wrap_bits, targets, swap)
        for targets in ((1, 2, 3, 0), (3, 0, 1, 2), (2, 3, 0, 1))
    )
    three = kernel(
        "wrap_three",
        functools.partial(wrap_three, fields),
        inside([element, following, before]),
        inside(
            [f32(VALUES * fields, lanes)]
            + [f32(UP, fields, lanes), f32(2, fields, lanes)] * 2
        ),
        [],
        400 * fields * lanes,
    )
    round_ups, round_downs = [], []
    for bit in range(wall_bits + 1):
        final = bit == wall_bits
        matrix, up, down, *extra = kernel(
            f"wall_round_{bit}",
            functools.partial(wall_round, lines, bit, final),
            inside([matrix, exchange(matrix, "normal", 1 << bit)])
            + (outside([coupling.reshape(fields * fields, lanes, wide)]) if final else []),
            inside(
                [
                    f32((4 if final else MATRIX) * lines, wide),
                    f32(UP, lines, wide),
                    f32(MERGE_DOWN, lines, wide),
                ]
                + (
                    [
                        f32(12, lines, wide),
                        jax.ShapeDtypeStruct((fields * fields, lanes, wide), coupling.dtype),
                    ]
                    if final
                    else []
                )
            ),
            [pltpu.SemaphoreType.DMA((fields,))] if final else [],
            200 * lines * wide,
        )
        round_ups.append(up)
        round_downs.append(down)
    outer, coupling_in = extra[:1], extra[1]
    source, *wall_ws = kernel(
        "middle",
        functools.partial(middle, fields, span, wrap_cells, wall_cells, wrap_bits),
        inside(
            [three[0], opposite]
            + three[1:]
            + wrap_ups
            + wrap_ws
            + wrap_factors
            + [coupling_in, damps, chunk_down]
            + wall_downs
        ),
        inside(
            [f32(SOURCE * lines, wide), f32(wall_pairs * 2, wall_rows, wide)]
            + [f32(2, n, wide) for n in wall_levels]
        ),
        [vmem(4, n, lanes) for n in reversed([wrap_rows] + wrap_levels)]
        + [vmem(fields * wide, lanes), vmem(fields * lanes, wide), vmem(fields * lanes, wide)]
        + [vmem(SOURCE, n, wide) for n in [wall_rows] + wall_levels],
        100 * residual.size,
    )
    round_ws = []
    for bit in range(wall_bits):
        source, w = kernel(
            f"wall_source_round_{bit}",
            functools.partial(wall_source_round, lines, bit),
            inside([source, exchange(source, "normal", 1 << bit), round_downs[bit]]),
            inside([f32(SOURCE * lines, wide), f32(2, lines, wide)]),
            [],
            50 * lines * wide,
        )
        round_ws.append(w)
    share_one, share_two, source = kernel(
        "wall_share",
        functools.partial(wall_share, lines, wall_bits),
        inside([source, round_downs[wall_bits]] + outer + [matrix]),
        inside([f32(SOURCE * lines, wide)] * 3),
        [],
        50 * lines * wide,
    )
    (update,) = kernel(
        "wall_up",
        functools.partial(wall_up, fields, span, wall_cells, wall_bits),
        inside(
            [matrix, round_downs[wall_bits]]
            + outer
            + [
                source,
                exchange(source, "normal", 1 << wall_bits),
                pass_on(share_two, "normal", wall_bits, (3, 2, 0, 1)),
                pass_on(share_one, "normal", wall_bits, (2, 3, 1, 0)),
            ]
            + round_ups
            + round_ws
            + [chunk_up, wall_ws[0]]
            + wall_ups
            + wall_ws[1:]
        ),
        [(f32(fields * lanes, wide), IN_HBM)],
        [vmem(4, n, wide) for n in reversed([wall_rows] + wall_levels)]
        + [vmem(fields * lanes, wide), pltpu.SemaphoreType.DMA((fields,))],
        30 * residual.size,
    )
    return update.reshape(residual.shape)


def solution(mesh):
    placed = (
        P(None, None, "normal", "wrap"),
        P(None, None, "normal", "wrap"),
        P(None, None, "normal", "wrap"),
        P(None, "normal", "wrap"),
        P(None, "normal", "wrap"),
        P(None, None, None, "normal", "wrap"),
    )
    return jax.shard_map(
        local,
        mesh=mesh,
        in_specs=placed,
        out_specs=P(None, None, "normal", "wrap"),
        check_vma=False,
    )
```

```python
import functools

import jax
import jax.numpy as jnp
from jax import lax
from jax.experimental import pallas as pl
from jax.experimental.pallas import tpu as pltpu
from jax.sharding import PartitionSpec as P

MATRIX = 16
SOURCE = 4
VALUES = MATRIX + SOURCE
UP = 8
CHUNK_DOWN = 9
MERGE_DOWN = 12
CHUNKS = 8


def inverse(a, b, c, d):
    scale = 1.0 / (a * d - b * c)
    return (d * scale, -b * scale, -c * scale, a * scale)


def times(x, y):
    return (
        x[0] * y[0] + x[1] * y[2],
        x[0] * y[1] + x[1] * y[3],
        x[2] * y[0] + x[3] * y[2],
        x[2] * y[1] + x[3] * y[3],
    )


def apply(x, v):
    return (x[0] * v[0] + x[1] * v[1], x[2] * v[0] + x[3] * v[1])


def minus(x, y):
    return tuple(a - b for a, b in zip(x, y))


def plus(x, y):
    return tuple(a + b for a, b in zip(x, y))


def negative(x):
    return tuple(-a for a in x)


def quads(element):
    return (element[0:4], element[4:8], element[8:12], element[12:16])


def merge_matrix(first, second):
    ll, lm, ml, mm = quads(first)
    nn, mr, rm, rr = quads(second)
    pivot = inverse(*plus(mm, nn))
    wl = times(pivot, ml)
    wr = times(pivot, mr)
    merged = (
        minus(ll, times(lm, wl))
        + negative(times(lm, wr))
        + negative(times(rm, wl))
        + minus(rr, times(rm, wr))
    )
    return merged, wl + wr, pivot + lm + rm


def merge_source(down, first, second):
    pivot, lm, rm = down[0:4], down[4:8], down[8:12]
    w = apply(pivot, plus(first[2:4], second[0:2]))
    return minus(first[0:2], apply(lm, w)) + minus(second[2:4], apply(rm, w)), w


def merge(first, second):
    matrix, up, down = merge_matrix(first[:MATRIX], second[:MATRIX])
    source, w = merge_source(down, first[MATRIX:], second[MATRIX:])
    return matrix + source, up, w


def inner(up, w, left, right):
    return minus(minus(w, apply(up[0:4], left)), apply(up[4:8], right))


def chunk_matrix(speed, damp, cells):
    def link(i):
        p = 2.0 * (damp(i) + damp(i + 1))
        q = 0.25 * (speed(i) + speed(i + 1))
        return q - p, -q - p

    def centre(i):
        return 1.0 + damp(i - 1) + 4.0 * damp(i) + damp(i + 1)

    b0, b1 = damp(0), damp(1)
    quarter = 0.25 * speed(0)
    up, low = link(0)
    zero = jnp.zeros_like(b0)
    ll = (b0, quarter - 2.0 * b0, -quarter - 2.0 * b0, 1.0 + 4.0 * b0 + b1)
    lk = (b0, zero, up, b1)
    kl = (b0, low, zero, b1)
    up, low = link(1)
    kk = (centre(1), up, low, centre(2))
    pairs = (cells - 2) // 2
    for k in range(1, pairs + 1):
        i = 2 * k
        pivot = inverse(*kk)
        wl = times(pivot, kl)
        up, low = link(i)
        here, there = damp(i), damp(i + 1)
        wr = (
            pivot[0] * here + pivot[1] * up,
            pivot[1] * there,
            pivot[2] * here + pivot[3] * up,
            pivot[3] * there,
        )
        yield wl + wr, pivot + lk + (low,), (here, there)

        def below(x):
            return (
                here * x[0] + low * x[2],
                here * x[1] + low * x[3],
                there * x[2],
                there * x[3],
            )

        ll = minus(ll, times(lk, wl))
        lk = negative(times(lk, wr))
        kl = negative(below(wl))
        if k < pairs:
            up, low_next = link(i + 1)
            kk = (centre(i + 1), up, low_next, centre(i + 2))
        else:
            quarter = 0.25 * speed(i + 1)
            kk = (
                1.0 + here + 4.0 * there,
                quarter - 2.0 * there,
                -quarter - 2.0 * there,
                there,
            )
        kk = minus(kk, below(wr))
    yield ll + lk + kl + kk


def pair_source(down, damps, left, pair, following):
    pivot, lk, low = down[0:4], down[4:8], down[8]
    w = apply(pivot, pair)
    left = minus(left, apply(lk, w))
    following = minus(following, (damps[0] * w[0] + low * w[1], damps[1] * w[1]))
    return left, following, w


def pair_of(source, k, cells):
    if k == (cells - 2) // 2:
        last = source(cells - 1)
        return (last, jnp.zeros_like(last))
    return (source(2 * k + 1), source(2 * k + 2))


def first_pair(source):
    first = source(0)
    return (jnp.zeros_like(first), first)


def blocks(rows, size):
    return [(at, min(size, rows - at)) for at in range(0, rows, size)]


def get(ref, count, at, size, base=0):
    return tuple(ref[base + v, pl.ds(at, size), :] for v in range(count))


def put(ref, values, at, size, base=0):
    for v, value in enumerate(values):
        ref[base + v, pl.ds(at, size), :] = value


def get_both(ref, count, at, size):
    return tuple(
        tuple(ref[v, pl.ds(2 * at + half, size, stride=2), :] for v in range(count))
        for half in (0, 1)
    )


def levels_of(lines):
    sizes = []
    rows = lines * CHUNKS
    while rows > lines:
        rows //= 2
        sizes.append(rows)
    return sizes


def split_all(top_ref, end_refs, up_refs, w_refs, sizes):
    source = top_ref
    for rows, target, ups, ws in zip(
        reversed(sizes), end_refs, reversed(up_refs), reversed(w_refs)
    ):
        for at, size in blocks(rows, 8):
            ends = get(source, 4, at, size)
            left, right = ends[0:2], ends[2:4]
            middle = inner(get(ups, UP, at, size), get(ws, 2, at, size), left, right)
            for v in range(2):
                target[v, pl.ds(2 * at, size, stride=2), :] = left[v]
                target[v, pl.ds(2 * at + 1, size, stride=2), :] = middle[v]
                target[2 + v, pl.ds(2 * at, size, stride=2), :] = middle[v]
                target[2 + v, pl.ds(2 * at + 1, size, stride=2), :] = right[v]
        source = target
    return source


def back_substitute(ends_ref, up_ref, w_ref, cells, at, size, store):
    ends = get(ends_ref, 4, at, size)
    left, following = ends[0:2], ends[2:4]
    store(0, left[1])
    store(cells - 1, following[0])
    for k in range((cells - 2) // 2 - 1, -1, -1):
        following = inner(
            get(up_ref, UP, at, size, k * UP), get(w_ref, 2, at, size, k * 2), left, following
        )
        store(2 * k + 1, following[0])
        store(2 * k + 2, following[1])


def close_ring(own, rest):
    ll, lr, rl, rr = quads(own)
    nn, nm, mn, mm = quads(rest)
    b = plus(lr, mn)
    c = plus(rl, nm)
    pivot = inverse(*plus(rr, nn))
    f = plus(own[16:18], rest[18:20])
    g = plus(own[18:20], rest[16:18])
    bd = times(b, pivot)
    left = apply(inverse(*minus(plus(ll, mm), times(bd, c))), minus(f, apply(bd, g)))
    right = apply(pivot, minus(g, apply(c, left)))
    return left, right


def open_ends(axis):
    place = lax.axis_index(axis)
    last = lax.axis_size(axis) - 1
    return jnp.where(place > 0, 1.0, 0.0), jnp.where(place < last, 1.0, 0.0)


def is_second(axis, bit):
    return lax.rem(lax.axis_index(axis) // (1 << bit), 2) == 1


def choose(second, one, other):
    return tuple(jnp.where(second, a, b) for a, b in zip(one, other))


def flat(ref, count, rows, at, size):
    return tuple(ref[pl.ds(v * rows + at, size), :] for v in range(count))


def put_flat(ref, values, rows, at, size):
    for v, value in enumerate(values):
        ref[pl.ds(v * rows + at, size), :] = value


def round_down(ups, ws, axis, bits, at, size, left, right):
    for bit in reversed(range(bits)):
        middle = inner(get(ups[bit], UP, at, size), get(ws[bit], 2, at, size), left, right)
        second = is_second(axis, bit)
        left, right = choose(second, middle, left), choose(second, right, middle)
    return left, right


def copies(pairs, sems, first=0):
    started = []
    for i, (source, target) in enumerate(pairs):
        copy = pltpu.make_async_copy(source, target, sems.at[first + i])
        copy.start()
        started.append(copy)
    return started


def wrap_down(fields, cells, *refs):
    residual, courant, dissip, wall_courant, wall_dissip = refs[0:5]
    packed, chunk_up, chunk_w = refs[5:8]
    ups, ws = refs[8:11], refs[11:14]
    wall_speed, wall_damp = refs[14:16]
    source_in, speed_in, damp_in, source_t, speed_t, damp_t = refs[16:22]
    elements, sems = refs[22:26], refs[26]
    lanes = damp_in.shape[0]
    length = cells * CHUNKS
    parts = [(0, 2), (2, fields)] if fields > 2 else [(0, fields)]
    moves = [(dissip, damp_in)]
    for first, last in parts:
        rows = pl.ds(first * lanes, (last - first) * lanes)
        moves.append((courant.at[rows], speed_in.at[rows]))
        moves.append((residual.at[rows], source_in.at[rows]))
    started = copies(moves, sems)
    started[0].wait()
    damp_t[...] = damp_in[...].T
    for part, (first, last) in enumerate(parts):
        at, size, repeat = first * CHUNKS, (last - first) * CHUNKS, last - first
        for inner_copy, taken, turned in (
            (started[1 + 2 * part], speed_in, speed_t),
            (started[2 + 2 * part], source_in, source_t),
        ):
            inner_copy.wait()
            for field in range(first, last):
                turned[pl.ds(field * length, length), :] = taken[pl.ds(field * lanes, lanes), :].T

        if part == 0:
            moves = [(wall_dissip, wall_damp), (wall_courant, wall_speed)]
            wall_started = copies(moves, sems, len(started))

        def speed(i):
            return speed_t[pl.ds(at * cells + i, size, stride=cells), :]

        def source(i):
            return source_t[pl.ds(at * cells + i, size, stride=cells), :]

        def damp(i):
            rows = damp_t[pl.ds(i, CHUNKS, stride=cells), :]
            return jnp.concatenate([rows] * repeat, axis=0) if repeat > 1 else rows

        left, pair = first_pair(source), pair_of(source, 0, cells)
        for k, step in enumerate(chunk_matrix(speed, damp, cells)):
            if k == (cells - 2) // 2:
                put(elements[0], step + left + pair, at, size)
                break
            up, down, damps = step
            left, pair, w = pair_source(down, damps, left, pair, pair_of(source, k + 1, cells))
            put(chunk_up, up, at, size, k * UP)
            put(chunk_w, w, at, size, k * 2)
    for level, rows in enumerate(levels_of(fields)):
        for at, size in blocks(rows, 8):
            merged, up, w = merge(*get_both(elements[level], VALUES, at, size))
            put(elements[level + 1], merged, at, size)
            put(ups[level], up, at, size)
            put(ws[level], w, at, size)
    for v in range(VALUES):
        packed[pl.ds(v * fields, fields), :] = elements[-1][v]
    for copy in wall_started:
        copy.wait()


def wrap_round(fields, bit, own, other, after, packed, up_out, w_out):
    second = is_second("wrap", bit)
    for at, size in blocks(fields, 8):
        mine = flat(own, VALUES, fields, at, size)
        theirs = flat(other, VALUES, fields, at, size)
        merged, up, w = merge(choose(second, theirs, mine), choose(second, mine, theirs))
        put_flat(packed, merged, fields, at, size)
        put(up_out, up, at, size)
        put(w_out, w, at, size)


def wall_matrix(fields, span, cells, *refs):
    speed_in, damp_in = refs[0:2]
    packed, damp_out, chunk_up, chunk_down = refs[2:6]
    ups, downs = refs[6:9], refs[9:12]
    elements = refs[12:16]
    size = span * CHUNKS
    for field in range(fields):
        at = field * size

        def speed(i):
            return speed_in[pl.ds(at * cells + i, size, stride=cells), :]

        def damp(i):
            return damp_in[pl.ds(i, size, stride=cells), :]

        for k, step in enumerate(chunk_matrix(speed, damp, cells)):
            if k == (cells - 2) // 2:
                put(elements[0], step, at, size)
                break
            up, down, damps = step
            put(chunk_up, up, at, size, k * UP)
            put(chunk_down, down, at, size, k * CHUNK_DOWN)
            if field == 0:
                put(damp_out, damps, 0, size, k * 2)
    lines = fields * span
    for level, rows in enumerate(levels_of(lines)):
        for at, size in blocks(rows, 8):
            merged, up, down = merge_matrix(*get_both(elements[level], MATRIX, at, size))
            put(elements[level + 1], merged, at, size)
            put(ups[level], up, at, size)
            put(downs[level], down, at, size)
    not_first, not_last = open_ends("normal")
    for v in range(MATRIX):
        value = elements[-1][v]
        if v in (0, 1, 2, 4, 5, 8, 10):
            value = value * not_first
        if v in (5, 7, 10, 11, 13, 14, 15):
            value = value * not_last
        packed[pl.ds(v * lines, lines), :] = value


def wall_round(lines, bit, final, own, other, *refs):
    started = []
    if final:
        coupling, packed, up_out, down_out, outer_out, coupling_out, sems = refs
        count = sems.shape[0]
        parts = [pl.ds(k * count, count) for k in range(count)]
        started = copies([(coupling.at[k], coupling_out.at[k]) for k in parts], sems)
    else:
        packed, up_out, down_out = refs
    second = is_second("normal", bit)
    upper = is_second("normal", bit + 1)
    for at, size in blocks(lines, 8):
        mine = flat(own, MATRIX, lines, at, size)
        theirs = flat(other, MATRIX, lines, at, size)
        merged, up, down = merge_matrix(
            choose(second, theirs, mine), choose(second, mine, theirs)
        )
        put(up_out, up, at, size)
        put(down_out, down, at, size)
        if not final:
            put_flat(packed, merged, lines, at, size)
            continue
        ll, lr, rl, rr = quads(merged)
        outer, into = choose(upper, rr, ll), choose(upper, rl, lr)
        out, middle = choose(upper, lr, rl), choose(upper, ll, rr)
        is_upper = jnp.where(upper, 1.0, 0.0)
        pivot = inverse(
            outer[0] + (1.0 - is_upper), outer[1], outer[2], outer[3] + is_upper
        )
        put_flat(packed, minus(middle, times(out, times(pivot, into))), lines, at, size)
        put(outer_out, pivot + into + out, at, size)
    for copy in started:
        copy.wait()


def wall_source_round(lines, bit, own, other, down_in, packed, w_out):
    second = is_second("normal", bit)
    for at, size in blocks(lines, 8):
        mine = flat(own, SOURCE, lines, at, size)
        theirs = flat(other, SOURCE, lines, at, size)
        merged, w = merge_source(
            get(down_in, MERGE_DOWN, at, size),
            choose(second, theirs, mine),
            choose(second, mine, theirs),
        )
        put_flat(packed, merged, lines, at, size)
        put(w_out, w, at, size)


def reduce_source(down, factors, second, upper, mine, theirs):
    merged, w = merge_source(
        down, choose(second, theirs, mine), choose(second, mine, theirs)
    )
    outer = apply(factors[0:4], choose(upper, merged[2:4], merged[0:2]))
    centre = choose(upper, merged[0:2], merged[2:4])
    return minus(centre, apply(factors[8:12], outer)), outer, w


def wall_share(lines, bit, own, down_in, outer_in, matrix, share_one, share_two, copy):
    copy[...] = own[...]
    half = pl.ds(2 * lines, 2 * lines)
    share_one[half, :] = matrix[pl.ds(0, 2 * lines), :]
    share_two[half, :] = matrix[half, :]
    second, upper = is_second("normal", bit), is_second("normal", bit + 1)
    for at, size in blocks(lines, 8):
        mine = flat(own, SOURCE, lines, at, size)
        none = tuple(jnp.zeros_like(value) for value in mine)
        down, factors = get(down_in, MERGE_DOWN, at, size), get(outer_in, 12, at, size)
        part, _, _ = reduce_source(down, factors, second, upper, mine, none)
        put_flat(share_one, part, lines, at, size)
        put_flat(share_two, part, lines, at, size)


def wrap_three(fields, own, following, before, packed, back_up, back_w, next_up, next_w):
    for at, size in blocks(fields, 8):
        run, up, w = merge(
            flat(before, VALUES, fields, at, size), flat(own, VALUES, fields, at, size)
        )
        put(back_up, up, at, size)
        put(back_w, w, at, size)
        run, up, w = merge(run, flat(following, VALUES, fields, at, size))
        put(next_up, up, at, size)
        put(next_w, w, at, size)
        put_flat(packed, run, fields, at, size)


def middle(fields, span, wrap_cells, wall_cells, bits, *refs):
    three, opposite, back_up, back_w, next_up, next_w = refs[0:6]
    refs = refs[6:]
    round_ups, round_ws, refs = refs[:bits], refs[bits : 2 * bits], refs[2 * bits :]
    chunk_up, chunk_w, ups, ws = refs[0], refs[1], refs[2:5], refs[5:8]
    coupling, damps_in, chunk_down, downs = refs[8], refs[9], refs[10], refs[11:14]
    packed, wall_w, wall_ws = refs[14], refs[15], refs[16:19]
    ends, solved_t, solved, mixed = refs[19:23], refs[23], refs[24], refs[25]
    sources = refs[26:30]

    for at, size in blocks(fields, 8):
        outer_left, outer_right = close_ring(
            flat(three, VALUES, fields, at, size), flat(opposite, VALUES, fields, at, size)
        )
        right = inner(get(next_up, UP, at, size), get(next_w, 2, at, size), outer_left, outer_right)
        left = inner(get(back_up, UP, at, size), get(back_w, 2, at, size), outer_left, right)
        left, right = round_down(round_ups, round_ws, "wrap", bits, at, size, left, right)
        put(ends[0], left + right, at, size)
    last = split_all(ends[0], ends[1:], ups, ws, levels_of(fields))
    length = wrap_cells * CHUNKS
    for at, size in blocks(fields * CHUNKS, 16):

        def store(i, value):
            solved_t[pl.ds(at * wrap_cells + i, size, stride=wrap_cells), :] = value

        back_substitute(last, chunk_up, chunk_w, wrap_cells, at, size, store)
    lanes = solved.shape[0] // fields
    for field in range(fields):
        solved[pl.ds(field * lanes, lanes), :] = solved_t[pl.ds(field * length, length), :].T

    for at, size in blocks(lanes, 16):
        update = [solved[pl.ds(j * lanes + at, size), :] for j in range(fields)]
        for k in range(fields):
            total = coupling[k * fields, pl.ds(at, size), :].astype(jnp.float32) * update[0]
            for j in range(1, fields):
                factor = coupling[k * fields + j, pl.ds(at, size), :]
                total = total + factor.astype(jnp.float32) * update[j]
            mixed[pl.ds(k * lanes + at, size), :] = total

    pairs = (wall_cells - 2) // 2
    size = span * CHUNKS
    for field in range(fields):
        at = field * size

        def source(i):
            return mixed[pl.ds(at * wall_cells + i, size, stride=wall_cells), :]

        left, pair = first_pair(source), pair_of(source, 0, wall_cells)
        for k in range(pairs):
            left, pair, w = pair_source(
                get(chunk_down, CHUNK_DOWN, at, size, k * CHUNK_DOWN),
                get(damps_in, 2, 0, size, k * 2),
                left,
                pair,
                pair_of(source, k + 1, wall_cells),
            )
            put(wall_w, w, at, size, k * 2)
        put(sources[0], left + pair, at, size)
    lines = fields * span
    for level, rows in enumerate(levels_of(lines)):
        for at, size in blocks(rows, 8):
            down = get(downs[level], MERGE_DOWN, at, size)
            merged, w = merge_source(down, *get_both(sources[level], SOURCE, at, size))
            put(sources[level + 1], merged, at, size)
            put(wall_ws[level], w, at, size)
    not_first, not_last = open_ends("normal")
    for v, keep in enumerate((not_first, None, None, not_last)):
        value = sources[-1][v]
        packed[pl.ds(v * lines, lines), :] = value if keep is None else value * keep


def wall_up(fields, span, cells, bits, *refs):
    own_matrix, down_in, outer_in, own, other, share_two, share_one = refs[0:7]
    refs = refs[7:]
    round_ups, round_ws, refs = refs[: bits + 1], refs[bits + 1 : 2 * bits + 1], refs[2 * bits + 1 :]
    chunk_up, chunk_w, ups, ws = refs[0], refs[1], refs[2:5], refs[5:8]
    update = refs[8]
    ends, result, sems = refs[9:13], refs[13], refs[14]
    lines = fields * span
    second, upper = is_second("normal", bits), is_second("normal", bits + 1)
    for at, size in blocks(lines, 8):
        down, factors = get(down_in, MERGE_DOWN, at, size), get(outer_in, 12, at, size)
        part, outer, w = reduce_source(
            down,
            factors,
            second,
            upper,
            flat(own, SOURCE, lines, at, size),
            flat(other, SOURCE, lines, at, size),
        )
        one, two = (flat(share, 4, lines, at, size) for share in (share_one, share_two))
        shares = plus(one[0:2], two[0:2])
        matrix = plus(flat(own_matrix, 4, lines, at, size), one[2:4] + two[2:4])
        centre = apply(inverse(*matrix), plus(part, shares))
        outer = minus(outer, apply(factors[0:4], apply(factors[4:8], centre)))
        left, right = choose(upper, centre, outer), choose(upper, outer, centre)
        between = inner(get(round_ups[bits], UP, at, size), w, left, right)
        left, right = choose(second, between, left), choose(second, right, between)
        left, right = round_down(round_ups, round_ws, "normal", bits, at, size, left, right)
        put(ends[0], left + right, at, size)
    last = split_all(ends[0], ends[1:], ups, ws, levels_of(lines))
    size = span * CHUNKS
    length = size * cells
    started = []
    for field in range(fields):
        at = field * size

        def store(i, value):
            result[pl.ds(at * cells + i, size, stride=cells), :] = value

        back_substitute(last, chunk_up, chunk_w, cells, at, size, store)
        rows = pl.ds(field * length, length)
        copy = pltpu.make_async_copy(result.at[rows], update.at[rows], sems.at[field])
        copy.start()
        started.append(copy)
    for copy in started:
        copy.wait()


def f32(*shape):
    return jax.ShapeDtypeStruct(shape, jnp.float32)


def vmem(*shape):
    return pltpu.VMEM(shape, jnp.float32)


IN_VMEM = pl.BlockSpec(memory_space=pltpu.VMEM)
IN_HBM = pl.BlockSpec(memory_space=pltpu.HBM)
PARAMS = pltpu.CompilerParams(vmem_limit_bytes=24 * 2**20)


def kernel(name, body, ins, outs, scratch, flops):
    in_bytes = sum(a.size * a.dtype.itemsize for a, _ in ins)
    out_bytes = sum(a.size * 4 for a, _ in outs)
    outputs = pl.pallas_call(
        body,
        out_shape=[a for a, _ in outs],
        in_specs=[spec for _, spec in ins],
        out_specs=[spec for _, spec in outs],
        scratch_shapes=scratch,
        compiler_params=PARAMS,
        cost_estimate=pl.CostEstimate(
            flops=flops, bytes_accessed=in_bytes + out_bytes, transcendentals=0
        ),
        name=name,
    )(*[a for a, _ in ins])
    return list(outputs)


def inside(arrays):
    return [(a, IN_VMEM) for a in arrays]


def outside(arrays):
    return [(pltpu.with_memory_space_constraint(a, pltpu.HBM), IN_HBM) for a in arrays]


def exchange(array, axis, mask):
    count = lax.axis_size(axis)
    return lax.ppermute(array, axis, [(i, i ^ mask) for i in range(count)])


def pass_on(array, axis, bit, targets, swap=0):
    count = lax.axis_size(axis)

    def target(i):
        place = i // (1 << bit) % 4
        return (i + (targets[place] - place) * (1 << bit)) ^ swap

    return lax.ppermute(array, axis, [(i, target(i)) for i in range(count)])


def local(residual, courant_xi, courant_eta, dissip_xi, dissip_eta, coupling):
    fields, span, high, wide = residual.shape
    lanes = span * high
    wrap_cells, wall_cells = wide // CHUNKS, high // CHUNKS
    wrap_pairs, wall_pairs = (wrap_cells - 2) // 2, (wall_cells - 2) // 2
    wrap_count, wall_count = lax.axis_size("wrap"), lax.axis_size("normal")
    lines = fields * span
    wrap_levels, wall_levels = levels_of(fields), levels_of(lines)
    wrap_rows, wall_rows = fields * CHUNKS, lines * CHUNKS

    def rows_of(array):
        return array.reshape(-1, wide)

    wrap_bits = wrap_count.bit_length() - 3
    wall_bits = wall_count.bit_length() - 3
    results = kernel(
        "wrap_down",
        functools.partial(wrap_down, fields, wrap_cells),
        outside(
            [rows_of(a) for a in (residual, courant_xi, dissip_xi, courant_eta, dissip_eta)]
        ),
        inside(
            [
                f32(VALUES * fields, lanes),
                f32(wrap_pairs * UP, wrap_rows, lanes),
                f32(wrap_pairs * 2, wrap_rows, lanes),
            ]
            + [f32(UP, n, lanes) for n in wrap_levels]
            + [f32(2, n, lanes) for n in wrap_levels]
            + [f32(fields * lanes, wide), f32(lanes, wide)]
        ),
        [vmem(fields * lanes, wide)] * 2
        + [vmem(lanes, wide)]
        + [vmem(fields * wide, lanes)] * 2
        + [vmem(wide, lanes)]
        + [vmem(VALUES, n, lanes) for n in [wrap_rows] + wrap_levels]
        + [pltpu.SemaphoreType.DMA((7,))],
        100 * residual.size,
    )
    element, wrap_factors, wall_inputs = results[0], results[1:9], results[9:11]
    results = kernel(
        "wall_matrix",
        functools.partial(wall_matrix, fields, span, wall_cells),
        inside(wall_inputs),
        inside(
            [
                f32(MATRIX * lines, wide),
                f32(wall_pairs * 2, span * CHUNKS, wide),
                f32(wall_pairs * UP, wall_rows, wide),
                f32(wall_pairs * CHUNK_DOWN, wall_rows, wide),
            ]
            + [f32(UP, n, wide) for n in wall_levels]
            + [f32(MERGE_DOWN, n, wide) for n in wall_levels]
        ),
        [vmem(MATRIX, n, wide) for n in [wall_rows] + wall_levels],
        100 * residual.size,
    )
    matrix, damps, chunk_up, chunk_down = results[0:4]
    wall_ups, wall_downs = results[4:7], results[7:10]
    wrap_ups, wrap_ws = [], []
    for bit in range(wrap_bits):
        element, up, w = kernel(
            f"wrap_round_{bit}",
            functools.partial(wrap_round, fields, bit),
            inside([element, exchange(element, "wrap", 1 << bit), damps]),
            inside([f32(VALUES * fields, lanes), f32(UP, fields, lanes), f32(2, fields, lanes)]),
            [],
            200 * fields * lanes,
        )
        wrap_ups.append(up)
        wrap_ws.append(w)
    swap = 1 if wrap_bits > 0 else 0
    before, following, opposite = (
        pass_on(element, "wrap", wrap_bits, targets, swap)
        for targets in ((1, 2, 3, 0), (3, 0, 1, 2), (2, 3, 0, 1))
    )
    three = kernel(
        "wrap_three",
        functools.partial(wrap_three, fields),
        inside([element, following, before]),
        inside(
            [f32(VALUES * fields, lanes)]
            + [f32(UP, fields, lanes), f32(2, fields, lanes)] * 2
        ),
        [],
        400 * fields * lanes,
    )
    round_ups, round_downs = [], []
    for bit in range(wall_bits + 1):
        final = bit == wall_bits
        matrix, up, down, *extra = kernel(
            f"wall_round_{bit}",
            functools.partial(wall_round, lines, bit, final),
            inside([matrix, exchange(matrix, "normal", 1 << bit)])
            + (outside([coupling.reshape(fields * fields, lanes, wide)]) if final else []),
            inside(
                [
                    f32((4 if final else MATRIX) * lines, wide),
                    f32(UP, lines, wide),
                    f32(MERGE_DOWN, lines, wide),
                ]
                + (
                    [
                        f32(12, lines, wide),
                        jax.ShapeDtypeStruct((fields * fields, lanes, wide), coupling.dtype),
                    ]
                    if final
                    else []
                )
            ),
            [pltpu.SemaphoreType.DMA((fields,))] if final else [],
            200 * lines * wide,
        )
        round_ups.append(up)
        round_downs.append(down)
    outer, coupling_in = extra[:1], extra[1]
    source, *wall_ws = kernel(
        "middle",
        functools.partial(middle, fields, span, wrap_cells, wall_cells, wrap_bits),
        inside(
            [three[0], opposite]
            + three[1:]
            + wrap_ups
            + wrap_ws
            + wrap_factors
            + [coupling_in, damps, chunk_down]
            + wall_downs
        ),
        inside(
            [f32(SOURCE * lines, wide), f32(wall_pairs * 2, wall_rows, wide)]
            + [f32(2, n, wide) for n in wall_levels]
        ),
        [vmem(4, n, lanes) for n in reversed([wrap_rows] + wrap_levels)]
        + [vmem(fields * wide, lanes), vmem(fields * lanes, wide), vmem(fields * lanes, wide)]
        + [vmem(SOURCE, n, wide) for n in [wall_rows] + wall_levels],
        100 * residual.size,
    )
    round_ws = []
    for bit in range(wall_bits):
        source, w = kernel(
            f"wall_source_round_{bit}",
            functools.partial(wall_source_round, lines, bit),
            inside([source, exchange(source, "normal", 1 << bit), round_downs[bit]]),
            inside([f32(SOURCE * lines, wide), f32(2, lines, wide)]),
            [],
            50 * lines * wide,
        )
        round_ws.append(w)
    share_one, share_two, source = kernel(
        "wall_share",
        functools.partial(wall_share, lines, wall_bits),
        inside([source, round_downs[wall_bits]] + outer + [matrix]),
        inside([f32(SOURCE * lines, wide)] * 3),
        [],
        50 * lines * wide,
    )
    (update,) = kernel(
        "wall_up",
        functools.partial(wall_up, fields, span, wall_cells, wall_bits),
        inside(
            [matrix, round_downs[wall_bits]]
            + outer
            + [
                source,
                exchange(source, "normal", 1 << wall_bits),
                pass_on(share_two, "normal", wall_bits, (2, 3, 1, 0)),
                pass_on(share_one, "normal", wall_bits, (3, 2, 0, 1)),
            ]
            + round_ups
            + round_ws
            + [chunk_up, wall_ws[0]]
            + wall_ups
            + wall_ws[1:]
        ),
        [(f32(fields * lanes, wide), IN_HBM)],
        [vmem(4, n, wide) for n in reversed([wall_rows] + wall_levels)]
        + [vmem(fields * lanes, wide), pltpu.SemaphoreType.DMA((fields,))],
        30 * residual.size,
    )
    return update.reshape(residual.shape)


def solution(mesh):
    placed = (
        P(None, None, "normal", "wrap"),
        P(None, None, "normal", "wrap"),
        P(None, None, "normal", "wrap"),
        P(None, "normal", "wrap"),
        P(None, "normal", "wrap"),
        P(None, None, None, "normal", "wrap"),
    )
    return jax.shard_map(
        local,
        mesh=mesh,
        in_specs=placed,
        out_specs=P(None, None, "normal", "wrap"),
        check_vma=False,
    )
```

```python
import functools

import jax
import jax.numpy as jnp
from jax import lax
from jax.experimental import pallas as pl
from jax.experimental.pallas import tpu as pltpu
from jax.sharding import PartitionSpec as P

MATRIX = 16
SOURCE = 4
VALUES = MATRIX + SOURCE
UP = 8
CHUNK_DOWN = 9
MERGE_DOWN = 12
CHUNKS = 8


def inverse(a, b, c, d):
    scale = 1.0 / (a * d - b * c)
    return (d * scale, -b * scale, -c * scale, a * scale)


def times(x, y):
    return (
        x[0] * y[0] + x[1] * y[2],
        x[0] * y[1] + x[1] * y[3],
        x[2] * y[0] + x[3] * y[2],
        x[2] * y[1] + x[3] * y[3],
    )


def apply(x, v):
    return (x[0] * v[0] + x[1] * v[1], x[2] * v[0] + x[3] * v[1])


def minus(x, y):
    return tuple(a - b for a, b in zip(x, y))


def plus(x, y):
    return tuple(a + b for a, b in zip(x, y))


def negative(x):
    return tuple(-a for a in x)


def quads(element):
    return (element[0:4], element[4:8], element[8:12], element[12:16])


def merge_matrix(first, second):
    ll, lm, ml, mm = quads(first)
    nn, mr, rm, rr = quads(second)
    pivot = inverse(*plus(mm, nn))
    wl = times(pivot, ml)
    wr = times(pivot, mr)
    merged = (
        minus(ll, times(lm, wl))
        + negative(times(lm, wr))
        + negative(times(rm, wl))
        + minus(rr, times(rm, wr))
    )
    return merged, wl + wr, pivot + lm + rm


def merge_source(down, first, second):
    pivot, lm, rm = down[0:4], down[4:8], down[8:12]
    w = apply(pivot, plus(first[2:4], second[0:2]))
    return minus(first[0:2], apply(lm, w)) + minus(second[2:4], apply(rm, w)), w


def merge(first, second):
    matrix, up, down = merge_matrix(first[:MATRIX], second[:MATRIX])
    source, w = merge_source(down, first[MATRIX:], second[MATRIX:])
    return matrix + source, up, w


def inner(up, w, left, right):
    return minus(minus(w, apply(up[0:4], left)), apply(up[4:8], right))


def chunk_matrix(speed, damp, cells):
    def link(i):
        p = 2.0 * (damp(i) + damp(i + 1))
        q = 0.25 * (speed(i) + speed(i + 1))
        return q - p, -q - p

    def centre(i):
        return 1.0 + damp(i - 1) + 4.0 * damp(i) + damp(i + 1)

    b0, b1 = damp(0), damp(1)
    quarter = 0.25 * speed(0)
    up, low = link(0)
    zero = jnp.zeros_like(b0)
    ll = (b0, quarter - 2.0 * b0, -quarter - 2.0 * b0, 1.0 + 4.0 * b0 + b1)
    lk = (b0, zero, up, b1)
    kl = (b0, low, zero, b1)
    up, low = link(1)
    kk = (centre(1), up, low, centre(2))
    pairs = (cells - 2) // 2
    for k in range(1, pairs + 1):
        i = 2 * k
        pivot = inverse(*kk)
        wl = times(pivot, kl)
        up, low = link(i)
        here, there = damp(i), damp(i + 1)
        wr = (
            pivot[0] * here + pivot[1] * up,
            pivot[1] * there,
            pivot[2] * here + pivot[3] * up,
            pivot[3] * there,
        )
        yield wl + wr, pivot + lk + (low,), (here, there)

        def below(x):
            return (
                here * x[0] + low * x[2],
                here * x[1] + low * x[3],
                there * x[2],
                there * x[3],
            )

        ll = minus(ll, times(lk, wl))
        lk = negative(times(lk, wr))
        kl = negative(below(wl))
        if k < pairs:
            up, low_next = link(i + 1)
            kk = (centre(i + 1), up, low_next, centre(i + 2))
        else:
            quarter = 0.25 * speed(i + 1)
            kk = (
                1.0 + here + 4.0 * there,
                quarter - 2.0 * there,
                -quarter - 2.0 * there,
                there,
            )
        kk = minus(kk, below(wr))
    yield ll + lk + kl + kk


def pair_source(down, damps, left, pair, following):
    pivot, lk, low = down[0:4], down[4:8], down[8]
    w = apply(pivot, pair)
    left = minus(left, apply(lk, w))
    following = minus(following, (damps[0] * w[0] + low * w[1], damps[1] * w[1]))
    return left, following, w


def pair_of(source, k, cells):
    if k == (cells - 2) // 2:
        last = source(cells - 1)
        return (last, jnp.zeros_like(last))
    return (source(2 * k + 1), source(2 * k + 2))


def first_pair(source):
    first = source(0)
    return (jnp.zeros_like(first), first)


def blocks(rows, size):
    return [(at, min(size, rows - at)) for at in range(0, rows, size)]


def get(ref, count, at, size, base=0):
    return tuple(ref[base + v, pl.ds(at, size), :] for v in range(count))


def put(ref, values, at, size, base=0):
    for v, value in enumerate(values):
        ref[base + v, pl.ds(at, size), :] = value


def get_both(ref, count, at, size):
    return tuple(
        tuple(ref[v, pl.ds(2 * at + half, size, stride=2), :] for v in range(count))
        for half in (0, 1)
    )


def levels_of(lines):
    sizes = []
    rows = lines * CHUNKS
    while rows > lines:
        rows //= 2
        sizes.append(rows)
    return sizes


def split_all(top_ref, end_refs, up_refs, w_refs, sizes):
    source = top_ref
    for rows, target, ups, ws in zip(
        reversed(sizes), end_refs, reversed(up_refs), reversed(w_refs)
    ):
        for at, size in blocks(rows, 8):
            ends = get(source, 4, at, size)
            left, right = ends[0:2], ends[2:4]
            middle = inner(get(ups, UP, at, size), get(ws, 2, at, size), left, right)
            for v in range(2):
                target[v, pl.ds(2 * at, size, stride=2), :] = left[v]
                target[v, pl.ds(2 * at + 1, size, stride=2), :] = middle[v]
                target[2 + v, pl.ds(2 * at, size, stride=2), :] = middle[v]
                target[2 + v, pl.ds(2 * at + 1, size, stride=2), :] = right[v]
        source = target
    return source


def back_substitute(ends_ref, up_ref, w_ref, cells, at, size, store):
    ends = get(ends_ref, 4, at, size)
    left, following = ends[0:2], ends[2:4]
    store(0, left[1])
    store(cells - 1, following[0])
    for k in range((cells - 2) // 2 - 1, -1, -1):
        following = inner(
            get(up_ref, UP, at, size, k * UP), get(w_ref, 2, at, size, k * 2), left, following
        )
        store(2 * k + 1, following[0])
        store(2 * k + 2, following[1])


def close_ring(own, rest):
    ll, lr, rl, rr = quads(own)
    nn, nm, mn, mm = quads(rest)
    b = plus(lr, mn)
    c = plus(rl, nm)
    pivot = inverse(*plus(rr, nn))
    f = plus(own[16:18], rest[18:20])
    g = plus(own[18:20], rest[16:18])
    bd = times(b, pivot)
    left = apply(inverse(*minus(plus(ll, mm), times(bd, c))), minus(f, apply(bd, g)))
    right = apply(pivot, minus(g, apply(c, left)))
    return left, right


def open_ends(axis):
    place = lax.axis_index(axis)
    last = lax.axis_size(axis) - 1
    return jnp.where(place > 0, 1.0, 0.0), jnp.where(place < last, 1.0, 0.0)


def is_second(axis, bit):
    return lax.rem(lax.axis_index(axis) // (1 << bit), 2) == 1


def choose(second, one, other):
    return tuple(jnp.where(second, a, b) for a, b in zip(one, other))


def flat(ref, count, rows, at, size):
    return tuple(ref[pl.ds(v * rows + at, size), :] for v in range(count))


def put_flat(ref, values, rows, at, size):
    for v, value in enumerate(values):
        ref[pl.ds(v * rows + at, size), :] = value


def round_down(ups, ws, axis, bits, at, size, left, right):
    for bit in reversed(range(bits)):
        middle = inner(get(ups[bit], UP, at, size), get(ws[bit], 2, at, size), left, right)
        second = is_second(axis, bit)
        left, right = choose(second, middle, left), choose(second, right, middle)
    return left, right


def copies(pairs, sems, first=0):
    started = []
    for i, (source, target) in enumerate(pairs):
        copy = pltpu.make_async_copy(source, target, sems.at[first + i])
        copy.start()
        started.append(copy)
    return started


def wrap_down(fields, cells, *refs):
    residual, courant, dissip, wall_courant, wall_dissip = refs[0:5]
    packed, chunk_up, chunk_w = refs[5:8]
    ups, ws = refs[8:11], refs[11:14]
    wall_speed, wall_damp = refs[14:16]
    source_in, speed_in, damp_in, source_t, speed_t, damp_t = refs[16:22]
    elements, sems = refs[22:26], refs[26]
    lanes = damp_in.shape[0]
    length = cells * CHUNKS
    parts = [(0, 2), (2, fields)] if fields > 2 else [(0, fields)]
    moves = [(dissip, damp_in)]
    for first, last in parts:
        rows = pl.ds(first * lanes, (last - first) * lanes)
        moves.append((courant.at[rows], speed_in.at[rows]))
        moves.append((residual.at[rows], source_in.at[rows]))
    started = copies(moves, sems)
    started[0].wait()
    damp_t[...] = damp_in[...].T
    for part, (first, last) in enumerate(parts):
        at, size, repeat = first * CHUNKS, (last - first) * CHUNKS, last - first
        for inner_copy, taken, turned in (
            (started[1 + 2 * part], speed_in, speed_t),
            (started[2 + 2 * part], source_in, source_t),
        ):
            inner_copy.wait()
            for field in range(first, last):
                turned[pl.ds(field * length, length), :] = taken[pl.ds(field * lanes, lanes), :].T

        if part == 0:
            moves = [(wall_dissip, wall_damp), (wall_courant, wall_speed)]
            wall_started = copies(moves, sems, len(started))

        def speed(i):
            return speed_t[pl.ds(at * cells + i, size, stride=cells), :]

        def source(i):
            return source_t[pl.ds(at * cells + i, size, stride=cells), :]

        def damp(i):
            rows = damp_t[pl.ds(i, CHUNKS, stride=cells), :]
            return jnp.concatenate([rows] * repeat, axis=0) if repeat > 1 else rows

        left, pair = first_pair(source), pair_of(source, 0, cells)
        for k, step in enumerate(chunk_matrix(speed, damp, cells)):
            if k == (cells - 2) // 2:
                put(elements[0], step + left + pair, at, size)
                break
            up, down, damps = step
            left, pair, w = pair_source(down, damps, left, pair, pair_of(source, k + 1, cells))
            put(chunk_up, up, at, size, k * UP)
            put(chunk_w, w, at, size, k * 2)
    for level, rows in enumerate(levels_of(fields)):
        for at, size in blocks(rows, 8):
            merged, up, w = merge(*get_both(elements[level], VALUES, at, size))
            put(elements[level + 1], merged, at, size)
            put(ups[level], up, at, size)
            put(ws[level], w, at, size)
    for v in range(VALUES):
        packed[pl.ds(v * fields, fields), :] = elements[-1][v]
    for copy in wall_started:
        copy.wait()


def wrap_round(fields, bit, own, other, after, packed, up_out, w_out):
    second = is_second("wrap", bit)
    for at, size in blocks(fields, 8):
        mine = flat(own, VALUES, fields, at, size)
        theirs = flat(other, VALUES, fields, at, size)
        merged, up, w = merge(choose(second, theirs, mine), choose(second, mine, theirs))
        put_flat(packed, merged, fields, at, size)
        put(up_out, up, at, size)
        put(w_out, w, at, size)


def wall_matrix(fields, span, cells, *refs):
    speed_in, damp_in = refs[0:2]
    packed, damp_out, chunk_up, chunk_down = refs[2:6]
    ups, downs = refs[6:9], refs[9:12]
    elements = refs[12:16]
    size = span * CHUNKS
    for field in range(fields):
        at = field * size

        def speed(i):
            return speed_in[pl.ds(at * cells + i, size, stride=cells), :]

        def damp(i):
            return damp_in[pl.ds(i, size, stride=cells), :]

        for k, step in enumerate(chunk_matrix(speed, damp, cells)):
            if k == (cells - 2) // 2:
                put(elements[0], step, at, size)
                break
            up, down, damps = step
            put(chunk_up, up, at, size, k * UP)
            put(chunk_down, down, at, size, k * CHUNK_DOWN)
            if field == 0:
                put(damp_out, damps, 0, size, k * 2)
    lines = fields * span
    for level, rows in enumerate(levels_of(lines)):
        for at, size in blocks(rows, 8):
            merged, up, down = merge_matrix(*get_both(elements[level], MATRIX, at, size))
            put(elements[level + 1], merged, at, size)
            put(ups[level], up, at, size)
            put(downs[level], down, at, size)
    not_first, not_last = open_ends("normal")
    for v in range(MATRIX):
        value = elements[-1][v]
        if v in (0, 1, 2, 4, 5, 8, 10):
            value = value * not_first
        if v in (5, 7, 10, 11, 13, 14, 15):
            value = value * not_last
        packed[pl.ds(v * lines, lines), :] = value


def wall_round(lines, bit, final, own, other, *refs):
    started = []
    if final:
        coupling, packed, up_out, down_out, outer_out, coupling_out, sems = refs
        count = sems.shape[0]
        parts = [pl.ds(k * count, count) for k in range(count)]
        started = copies([(coupling.at[k], coupling_out.at[k]) for k in parts], sems)
    else:
        packed, up_out, down_out = refs
    second = is_second("normal", bit)
    upper = is_second("normal", bit + 1)
    for at, size in blocks(lines, 8):
        mine = flat(own, MATRIX, lines, at, size)
        theirs = flat(other, MATRIX, lines, at, size)
        merged, up, down = merge_matrix(
            choose(second, theirs, mine), choose(second, mine, theirs)
        )
        put(up_out, up, at, size)
        put(down_out, down, at, size)
        if not final:
            put_flat(packed, merged, lines, at, size)
            continue
        ll, lr, rl, rr = quads(merged)
        outer, into = choose(upper, rr, ll), choose(upper, rl, lr)
        out, middle = choose(upper, lr, rl), choose(upper, ll, rr)
        is_upper = jnp.where(upper, 1.0, 0.0)
        pivot = inverse(
            outer[0] + (1.0 - is_upper), outer[1], outer[2], outer[3] + is_upper
        )
        put_flat(packed, minus(middle, times(out, times(pivot, into))), lines, at, size)
        put(outer_out, pivot + into + out, at, size)
    for copy in started:
        copy.wait()


def wall_source_round(lines, bit, own, other, down_in, packed, w_out):
    second = is_second("normal", bit)
    for at, size in blocks(lines, 8):
        mine = flat(own, SOURCE, lines, at, size)
        theirs = flat(other, SOURCE, lines, at, size)
        merged, w = merge_source(
            get(down_in, MERGE_DOWN, at, size),
            choose(second, theirs, mine),
            choose(second, mine, theirs),
        )
        put_flat(packed, merged, lines, at, size)
        put(w_out, w, at, size)


def reduce_source(down, factors, second, upper, mine, theirs):
    merged, w = merge_source(
        down, choose(second, theirs, mine), choose(second, mine, theirs)
    )
    outer = apply(factors[0:4], choose(upper, merged[2:4], merged[0:2]))
    centre = choose(upper, merged[0:2], merged[2:4])
    return minus(centre, apply(factors[8:12], outer)), outer, w


def wall_share(lines, bit, own, down_in, outer_in, matrix, share_one, share_two, copy):
    copy[...] = own[...]
    half = pl.ds(2 * lines, 2 * lines)
    share_one[half, :] = matrix[pl.ds(0, 2 * lines), :]
    share_two[half, :] = matrix[half, :]
    second, upper = is_second("normal", bit), is_second("normal", bit + 1)
    for at, size in blocks(lines, 8):
        mine = flat(own, SOURCE, lines, at, size)
        none = tuple(jnp.zeros_like(value) for value in mine)
        down, factors = get(down_in, MERGE_DOWN, at, size), get(outer_in, 12, at, size)
        part, _, _ = reduce_source(down, factors, second, upper, mine, none)
        put_flat(share_one, part, lines, at, size)
        put_flat(share_two, part, lines, at, size)


def wrap_three(fields, own, following, before, packed, back_up, back_w, next_up, next_w):
    for at, size in blocks(fields, 8):
        run, up, w = merge(
            flat(before, VALUES, fields, at, size), flat(own, VALUES, fields, at, size)
        )
        put(back_up, up, at, size)
        put(back_w, w, at, size)
        run, up, w = merge(run, flat(following, VALUES, fields, at, size))
        put(next_up, up, at, size)
        put(next_w, w, at, size)
        put_flat(packed, run, fields, at, size)


def middle(fields, span, wrap_cells, wall_cells, bits, *refs):
    three, opposite, back_up, back_w, next_up, next_w = refs[0:6]
    refs = refs[6:]
    round_ups, round_ws, refs = refs[:bits], refs[bits : 2 * bits], refs[2 * bits :]
    chunk_up, chunk_w, ups, ws = refs[0], refs[1], refs[2:5], refs[5:8]
    coupling, damps_in, chunk_down, downs = refs[8], refs[9], refs[10], refs[11:14]
    packed, wall_w, wall_ws = refs[14], refs[15], refs[16:19]
    ends, solved_t, solved, mixed = refs[19:23], refs[23], refs[24], refs[25]
    sources = refs[26:30]

    for at, size in blocks(fields, 8):
        outer_left, outer_right = close_ring(
            flat(three, VALUES, fields, at, size), flat(opposite, VALUES, fields, at, size)
        )
        right = inner(get(next_up, UP, at, size), get(next_w, 2, at, size), outer_left, outer_right)
        left = inner(get(back_up, UP, at, size), get(back_w, 2, at, size), outer_left, right)
        left, right = round_down(round_ups, round_ws, "wrap", bits, at, size, left, right)
        put(ends[0], left + right, at, size)
    last = split_all(ends[0], ends[1:], ups, ws, levels_of(fields))
    length = wrap_cells * CHUNKS
    for at, size in blocks(fields * CHUNKS, 16):

        def store(i, value):
            solved_t[pl.ds(at * wrap_cells + i, size, stride=wrap_cells), :] = value

        back_substitute(last, chunk_up, chunk_w, wrap_cells, at, size, store)
    lanes = solved.shape[0] // fields
    for field in range(fields):
        solved[pl.ds(field * lanes, lanes), :] = solved_t[pl.ds(field * length, length), :].T

    for at, size in blocks(lanes, 16):
        update = [solved[pl.ds(j * lanes + at, size), :] for j in range(fields)]
        for k in range(fields):
            total = coupling[k * fields, pl.ds(at, size), :].astype(jnp.float32) * update[0]
            for j in range(1, fields):
                factor = coupling[k * fields + j, pl.ds(at, size), :]
                total = total + factor.astype(jnp.float32) * update[j]
            mixed[pl.ds(k * lanes + at, size), :] = total

    pairs = (wall_cells - 2) // 2
    size = span * CHUNKS
    for field in range(fields):
        at = field * size

        def source(i):
            return mixed[pl.ds(at * wall_cells + i, size, stride=wall_cells), :]

        left, pair = first_pair(source), pair_of(source, 0, wall_cells)
        for k in range(pairs):
            left, pair, w = pair_source(
                get(chunk_down, CHUNK_DOWN, at, size, k * CHUNK_DOWN),
                get(damps_in, 2, 0, size, k * 2),
                left,
                pair,
                pair_of(source, k + 1, wall_cells),
            )
            put(wall_w, w, at, size, k * 2)
        put(sources[0], left + pair, at, size)
    lines = fields * span
    for level, rows in enumerate(levels_of(lines)):
        for at, size in blocks(rows, 8):
            down = get(downs[level], MERGE_DOWN, at, size)
            merged, w = merge_source(down, *get_both(sources[level], SOURCE, at, size))
            put(sources[level + 1], merged, at, size)
            put(wall_ws[level], w, at, size)
    not_first, not_last = open_ends("normal")
    for v, keep in enumerate((not_first, None, None, not_last)):
        value = sources[-1][v]
        packed[pl.ds(v * lines, lines), :] = value if keep is None else value * keep


def wall_up(fields, span, cells, bits, *refs):
    own_matrix, down_in, outer_in, own, other, share_two, share_one = refs[0:7]
    refs = refs[7:]
    round_ups, round_ws, refs = refs[: bits + 1], refs[bits + 1 : 2 * bits + 1], refs[2 * bits + 1 :]
    chunk_up, chunk_w, ups, ws = refs[0], refs[1], refs[2:5], refs[5:8]
    update = refs[8]
    ends, result, sems = refs[9:13], refs[13], refs[14]
    lines = fields * span
    second, upper = is_second("normal", bits), is_second("normal", bits + 1)
    for at, size in blocks(lines, 8):
        down, factors = get(down_in, MERGE_DOWN, at, size), get(outer_in, 12, at, size)
        part, outer, w = reduce_source(
            down,
            factors,
            second,
            upper,
            flat(own, SOURCE, lines, at, size),
            flat(other, SOURCE, lines, at, size),
        )
        one, two = (flat(share, 4, lines, at, size) for share in (share_one, share_two))
        shares = plus(one[0:2], two[0:2])
        matrix = plus(flat(own_matrix, 4, lines, at, size), one[2:4] + two[2:4])
        centre = apply(inverse(*matrix), plus(part, shares))
        outer = minus(outer, apply(factors[0:4], apply(factors[4:8], centre)))
        left, right = choose(upper, centre, outer), choose(upper, outer, centre)
        between = inner(get(round_ups[bits], UP, at, size), w, left, right)
        left, right = choose(second, between, left), choose(second, right, between)
        left, right = round_down(round_ups, round_ws, "normal", bits, at, size, left, right)
        put(ends[0], left + right, at, size)
    last = split_all(ends[0], ends[1:], ups, ws, levels_of(lines))
    size = span * CHUNKS
    length = size * cells
    started = []
    for field in range(fields):
        at = field * size

        def store(i, value):
            result[pl.ds(at * cells + i, size, stride=cells), :] = value

        back_substitute(last, chunk_up, chunk_w, cells, at, size, store)
        rows = pl.ds(field * length, length)
        copy = pltpu.make_async_copy(result.at[rows], update.at[rows], sems.at[field])
        copy.start()
        started.append(copy)
    for copy in started:
        copy.wait()


def f32(*shape):
    return jax.ShapeDtypeStruct(shape, jnp.float32)


def vmem(*shape):
    return pltpu.VMEM(shape, jnp.float32)


IN_VMEM = pl.BlockSpec(memory_space=pltpu.VMEM)
IN_HBM = pl.BlockSpec(memory_space=pltpu.HBM)
PARAMS = pltpu.CompilerParams(vmem_limit_bytes=24 * 2**20)


def kernel(name, body, ins, outs, scratch, flops):
    in_bytes = sum(a.size * a.dtype.itemsize for a, _ in ins)
    out_bytes = sum(a.size * 4 for a, _ in outs)
    outputs = pl.pallas_call(
        body,
        out_shape=[a for a, _ in outs],
        in_specs=[spec for _, spec in ins],
        out_specs=[spec for _, spec in outs],
        scratch_shapes=scratch,
        compiler_params=PARAMS,
        cost_estimate=pl.CostEstimate(
            flops=flops, bytes_accessed=in_bytes + out_bytes, transcendentals=0
        ),
        name=name,
    )(*[a for a, _ in ins])
    return list(outputs)


def inside(arrays):
    return [(a, IN_VMEM) for a in arrays]


def outside(arrays):
    return [(pltpu.with_memory_space_constraint(a, pltpu.HBM), IN_HBM) for a in arrays]


def exchange(array, axis, mask):
    count = lax.axis_size(axis)
    return lax.ppermute(array, axis, [(i, i ^ mask) for i in range(count)])


def pass_on(array, axis, bit, targets, swap=0):
    count = lax.axis_size(axis)

    def target(i):
        place = i // (1 << bit) % 4
        return (i + (targets[place] - place) * (1 << bit)) ^ swap

    return lax.ppermute(array, axis, [(i, target(i)) for i in range(count)])


def local(residual, courant_xi, courant_eta, dissip_xi, dissip_eta, coupling):
    fields, span, high, wide = residual.shape
    lanes = span * high
    wrap_cells, wall_cells = wide // CHUNKS, high // CHUNKS
    wrap_pairs, wall_pairs = (wrap_cells - 2) // 2, (wall_cells - 2) // 2
    wrap_count, wall_count = lax.axis_size("wrap"), lax.axis_size("normal")
    lines = fields * span
    wrap_levels, wall_levels = levels_of(fields), levels_of(lines)
    wrap_rows, wall_rows = fields * CHUNKS, lines * CHUNKS

    def rows_of(array):
        return array.reshape(-1, wide)

    wrap_bits = wrap_count.bit_length() - 3
    wall_bits = wall_count.bit_length() - 3
    results = kernel(
        "wrap_down",
        functools.partial(wrap_down, fields, wrap_cells),
        outside(
            [rows_of(a) for a in (residual, courant_xi, dissip_xi, courant_eta, dissip_eta)]
        ),
        inside(
            [
                f32(VALUES * fields, lanes),
                f32(wrap_pairs * UP, wrap_rows, lanes),
                f32(wrap_pairs * 2, wrap_rows, lanes),
            ]
            + [f32(UP, n, lanes) for n in wrap_levels]
            + [f32(2, n, lanes) for n in wrap_levels]
            + [f32(fields * lanes, wide), f32(lanes, wide)]
        ),
        [vmem(fields * lanes, wide)] * 2
        + [vmem(lanes, wide)]
        + [vmem(fields * wide, lanes)] * 2
        + [vmem(wide, lanes)]
        + [vmem(VALUES, n, lanes) for n in [wrap_rows] + wrap_levels]
        + [pltpu.SemaphoreType.DMA((7,))],
        100 * residual.size,
    )
    element, wrap_factors, wall_inputs = results[0], results[1:9], results[9:11]
    results = kernel(
        "wall_matrix",
        functools.partial(wall_matrix, fields, span, wall_cells),
        inside(wall_inputs),
        inside(
            [
                f32(MATRIX * lines, wide),
                f32(wall_pairs * 2, span * CHUNKS, wide),
                f32(wall_pairs * UP, wall_rows, wide),
                f32(wall_pairs * CHUNK_DOWN, wall_rows, wide),
            ]
            + [f32(UP, n, wide) for n in wall_levels]
            + [f32(MERGE_DOWN, n, wide) for n in wall_levels]
        ),
        [vmem(MATRIX, n, wide) for n in [wall_rows] + wall_levels],
        100 * residual.size,
    )
    matrix, damps, chunk_up, chunk_down = results[0:4]
    wall_ups, wall_downs = results[4:7], results[7:10]
    wrap_ups, wrap_ws = [], []
    for bit in range(wrap_bits):
        element, up, w = kernel(
            f"wrap_round_{bit}",
            functools.partial(wrap_round, fields, bit),
            inside([element, exchange(element, "wrap", 1 << bit), damps]),
            inside([f32(VALUES * fields, lanes), f32(UP, fields, lanes), f32(2, fields, lanes)]),
            [],
            200 * fields * lanes,
        )
        wrap_ups.append(up)
        wrap_ws.append(w)
    swap = 1 if wrap_bits > 0 else 0
    before, following, opposite = (
        pass_on(element, "wrap", wrap_bits, targets, swap)
        for targets in ((1, 2, 3, 0), (3, 0, 1, 2), (2, 3, 0, 1))
    )
    three = kernel(
        "wrap_three",
        functools.partial(wrap_three, fields),
        inside([element, following, before]),
        inside(
            [f32(VALUES * fields, lanes)]
            + [f32(UP, fields, lanes), f32(2, fields, lanes)] * 2
        ),
        [],
        400 * fields * lanes,
    )
    round_ups, round_downs = [], []
    for bit in range(wall_bits + 1):
        final = bit == wall_bits
        matrix, up, down, *extra = kernel(
            f"wall_round_{bit}",
            functools.partial(wall_round, lines, bit, final),
            inside([matrix, exchange(matrix, "normal", 1 << bit)])
            + (outside([coupling.reshape(fields * fields, lanes, wide)]) if final else []),
            inside(
                [
                    f32((4 if final else MATRIX) * lines, wide),
                    f32(UP, lines, wide),
                    f32(MERGE_DOWN, lines, wide),
                ]
                + (
                    [
                        f32(12, lines, wide),
                        jax.ShapeDtypeStruct((fields * fields, lanes, wide), coupling.dtype),
                    ]
                    if final
                    else []
                )
            ),
            [pltpu.SemaphoreType.DMA((fields,))] if final else [],
            200 * lines * wide,
        )
        round_ups.append(up)
        round_downs.append(down)
    outer, coupling_in = extra[:1], extra[1]
    source, *wall_ws = kernel(
        "middle",
        functools.partial(middle, fields, span, wrap_cells, wall_cells, wrap_bits),
        inside(
            [three[0], opposite]
            + three[1:]
            + wrap_ups
            + wrap_ws
            + wrap_factors
            + [coupling_in, damps, chunk_down]
            + wall_downs
        ),
        inside(
            [f32(SOURCE * lines, wide), f32(wall_pairs * 2, wall_rows, wide)]
            + [f32(2, n, wide) for n in wall_levels]
        ),
        [vmem(4, n, lanes) for n in reversed([wrap_rows] + wrap_levels)]
        + [vmem(fields * wide, lanes), vmem(fields * lanes, wide), vmem(fields * lanes, wide)]
        + [vmem(SOURCE, n, wide) for n in [wall_rows] + wall_levels],
        100 * residual.size,
    )
    round_ws = []
    for bit in range(wall_bits):
        source, w = kernel(
            f"wall_source_round_{bit}",
            functools.partial(wall_source_round, lines, bit),
            inside([source, exchange(source, "normal", 1 << bit), round_downs[bit]]),
            inside([f32(SOURCE * lines, wide), f32(2, lines, wide)]),
            [],
            50 * lines * wide,
        )
        round_ws.append(w)
    share_one, share_two, source = kernel(
        "wall_share",
        functools.partial(wall_share, lines, wall_bits),
        inside([source, round_downs[wall_bits]] + outer + [matrix]),
        inside([f32(SOURCE * lines, wide)] * 3),
        [],
        50 * lines * wide,
    )
    (update,) = kernel(
        "wall_up",
        functools.partial(wall_up, fields, span, wall_cells, wall_bits),
        inside(
            [matrix, round_downs[wall_bits]]
            + outer
            + [
                source,
                exchange(source, "normal", 1 << wall_bits),
                pass_on(share_two, "normal", wall_bits, (3, 2, 1, 0)),
                pass_on(share_one, "normal", wall_bits, (2, 3, 0, 1)),
            ]
            + round_ups
            + round_ws
            + [chunk_up, wall_ws[0]]
            + wall_ups
            + wall_ws[1:]
        ),
        [(f32(fields * lanes, wide), IN_HBM)],
        [vmem(4, n, wide) for n in reversed([wall_rows] + wall_levels)]
        + [vmem(fields * lanes, wide), pltpu.SemaphoreType.DMA((fields,))],
        30 * residual.size,
    )
    return update.reshape(residual.shape)


def solution(mesh):
    placed = (
        P(None, None, "normal", "wrap"),
        P(None, None, "normal", "wrap"),
        P(None, None, "normal", "wrap"),
        P(None, "normal", "wrap"),
        P(None, "normal", "wrap"),
        P(None, None, None, "normal", "wrap"),
    )
    return jax.shard_map(
        local,
        mesh=mesh,
        in_specs=placed,
        out_specs=P(None, None, "normal", "wrap"),
        check_vma=False,
    )
```

```python
import functools

import jax
import jax.numpy as jnp
from jax import lax
from jax.experimental import pallas as pl
from jax.experimental.pallas import tpu as pltpu
from jax.sharding import PartitionSpec as P

MATRIX = 16
SOURCE = 4
VALUES = MATRIX + SOURCE
UP = 8
CHUNK_DOWN = 9
MERGE_DOWN = 12
CHUNKS = 8


def inverse(a, b, c, d):
    scale = 1.0 / (a * d - b * c)
    return (d * scale, -b * scale, -c * scale, a * scale)


def times(x, y):
    return (
        x[0] * y[0] + x[1] * y[2],
        x[0] * y[1] + x[1] * y[3],
        x[2] * y[0] + x[3] * y[2],
        x[2] * y[1] + x[3] * y[3],
    )


def apply(x, v):
    return (x[0] * v[0] + x[1] * v[1], x[2] * v[0] + x[3] * v[1])


def minus(x, y):
    return tuple(a - b for a, b in zip(x, y))


def plus(x, y):
    return tuple(a + b for a, b in zip(x, y))


def negative(x):
    return tuple(-a for a in x)


def quads(element):
    return (element[0:4], element[4:8], element[8:12], element[12:16])


def merge_matrix(first, second):
    ll, lm, ml, mm = quads(first)
    nn, mr, rm, rr = quads(second)
    pivot = inverse(*plus(mm, nn))
    wl = times(pivot, ml)
    wr = times(pivot, mr)
    merged = (
        minus(ll, times(lm, wl))
        + negative(times(lm, wr))
        + negative(times(rm, wl))
        + minus(rr, times(rm, wr))
    )
    return merged, wl + wr, pivot + lm + rm


def merge_source(down, first, second):
    pivot, lm, rm = down[0:4], down[4:8], down[8:12]
    w = apply(pivot, plus(first[2:4], second[0:2]))
    return minus(first[0:2], apply(lm, w)) + minus(second[2:4], apply(rm, w)), w


def merge(first, second):
    matrix, up, down = merge_matrix(first[:MATRIX], second[:MATRIX])
    source, w = merge_source(down, first[MATRIX:], second[MATRIX:])
    return matrix + source, up, w


def inner(up, w, left, right):
    return minus(minus(w, apply(up[0:4], left)), apply(up[4:8], right))


def chunk_matrix(speed, damp, cells):
    def link(i):
        p = 2.0 * (damp(i) + damp(i + 1))
        q = 0.25 * (speed(i) + speed(i + 1))
        return q - p, -q - p

    def centre(i):
        return 1.0 + damp(i - 1) + 4.0 * damp(i) + damp(i + 1)

    b0, b1 = damp(0), damp(1)
    quarter = 0.25 * speed(0)
    up, low = link(0)
    zero = jnp.zeros_like(b0)
    ll = (b0, quarter - 2.0 * b0, -quarter - 2.0 * b0, 1.0 + 4.0 * b0 + b1)
    lk = (b0, zero, up, b1)
    kl = (b0, low, zero, b1)
    up, low = link(1)
    kk = (centre(1), up, low, centre(2))
    pairs = (cells - 2) // 2
    for k in range(1, pairs + 1):
        i = 2 * k
        pivot = inverse(*kk)
        wl = times(pivot, kl)
        up, low = link(i)
        here, there = damp(i), damp(i + 1)
        wr = (
            pivot[0] * here + pivot[1] * up,
            pivot[1] * there,
            pivot[2] * here + pivot[3] * up,
            pivot[3] * there,
        )
        yield wl + wr, pivot + lk + (low,), (here, there)

        def below(x):
            return (
                here * x[0] + low * x[2],
                here * x[1] + low * x[3],
                there * x[2],
                there * x[3],
            )

        ll = minus(ll, times(lk, wl))
        lk = negative(times(lk, wr))
        kl = negative(below(wl))
        if k < pairs:
            up, low_next = link(i + 1)
            kk = (centre(i + 1), up, low_next, centre(i + 2))
        else:
            quarter = 0.25 * speed(i + 1)
            kk = (
                1.0 + here + 4.0 * there,
                quarter - 2.0 * there,
                -quarter - 2.0 * there,
                there,
            )
        kk = minus(kk, below(wr))
    yield ll + lk + kl + kk


def pair_source(down, damps, left, pair, following):
    pivot, lk, low = down[0:4], down[4:8], down[8]
    w = apply(pivot, pair)
    left = minus(left, apply(lk, w))
    following = minus(following, (damps[0] * w[0] + low * w[1], damps[1] * w[1]))
    return left, following, w


def pair_of(source, k, cells):
    if k == (cells - 2) // 2:
        last = source(cells - 1)
        return (last, jnp.zeros_like(last))
    return (source(2 * k + 1), source(2 * k + 2))


def first_pair(source):
    first = source(0)
    return (jnp.zeros_like(first), first)


def blocks(rows, size):
    return [(at, min(size, rows - at)) for at in range(0, rows, size)]


def get(ref, count, at, size, base=0):
    return tuple(ref[base + v, pl.ds(at, size), :] for v in range(count))


def put(ref, values, at, size, base=0):
    for v, value in enumerate(values):
        ref[base + v, pl.ds(at, size), :] = value


def get_both(ref, count, at, size):
    return tuple(
        tuple(ref[v, pl.ds(2 * at + half, size, stride=2), :] for v in range(count))
        for half in (0, 1)
    )


def levels_of(lines):
    sizes = []
    rows = lines * CHUNKS
    while rows > lines:
        rows //= 2
        sizes.append(rows)
    return sizes


def split_all(top_ref, end_refs, up_refs, w_refs, sizes):
    source = top_ref
    for rows, target, ups, ws in zip(
        reversed(sizes), end_refs, reversed(up_refs), reversed(w_refs)
    ):
        for at, size in blocks(rows, 8):
            ends = get(source, 4, at, size)
            left, right = ends[0:2], ends[2:4]
            middle = inner(get(ups, UP, at, size), get(ws, 2, at, size), left, right)
            for v in range(2):
                target[v, pl.ds(2 * at, size, stride=2), :] = left[v]
                target[v, pl.ds(2 * at + 1, size, stride=2), :] = middle[v]
                target[2 + v, pl.ds(2 * at, size, stride=2), :] = middle[v]
                target[2 + v, pl.ds(2 * at + 1, size, stride=2), :] = right[v]
        source = target
    return source


def back_substitute(ends_ref, up_ref, w_ref, cells, at, size, store):
    ends = get(ends_ref, 4, at, size)
    left, following = ends[0:2], ends[2:4]
    store(0, left[1])
    store(cells - 1, following[0])
    for k in range((cells - 2) // 2 - 1, -1, -1):
        following = inner(
            get(up_ref, UP, at, size, k * UP), get(w_ref, 2, at, size, k * 2), left, following
        )
        store(2 * k + 1, following[0])
        store(2 * k + 2, following[1])


def close_ring(own, rest):
    ll, lr, rl, rr = quads(own)
    nn, nm, mn, mm = quads(rest)
    b = plus(lr, mn)
    c = plus(rl, nm)
    pivot = inverse(*plus(rr, nn))
    f = plus(own[16:18], rest[18:20])
    g = plus(own[18:20], rest[16:18])
    bd = times(b, pivot)
    left = apply(inverse(*minus(plus(ll, mm), times(bd, c))), minus(f, apply(bd, g)))
    right = apply(pivot, minus(g, apply(c, left)))
    return left, right


def open_ends(axis):
    place = lax.axis_index(axis)
    last = lax.axis_size(axis) - 1
    return jnp.where(place > 0, 1.0, 0.0), jnp.where(place < last, 1.0, 0.0)


def is_second(axis, bit):
    return lax.rem(lax.axis_index(axis) // (1 << bit), 2) == 1


def choose(second, one, other):
    return tuple(jnp.where(second, a, b) for a, b in zip(one, other))


def flat(ref, count, rows, at, size):
    return tuple(ref[pl.ds(v * rows + at, size), :] for v in range(count))


def put_flat(ref, values, rows, at, size):
    for v, value in enumerate(values):
        ref[pl.ds(v * rows + at, size), :] = value


def round_down(ups, ws, axis, bits, at, size, left, right):
    for bit in reversed(range(bits)):
        middle = inner(get(ups[bit], UP, at, size), get(ws[bit], 2, at, size), left, right)
        second = is_second(axis, bit)
        left, right = choose(second, middle, left), choose(second, right, middle)
    return left, right


def copies(pairs, sems, first=0):
    started = []
    for i, (source, target) in enumerate(pairs):
        copy = pltpu.make_async_copy(source, target, sems.at[first + i])
        copy.start()
        started.append(copy)
    return started


def wrap_down(fields, cells, *refs):
    residual, courant, dissip, wall_courant, wall_dissip = refs[0:5]
    packed, chunk_up, chunk_w = refs[5:8]
    ups, ws = refs[8:11], refs[11:14]
    wall_speed, wall_damp = refs[14:16]
    source_in, speed_in, damp_in, source_t, speed_t, damp_t = refs[16:22]
    elements, sems = refs[22:26], refs[26]
    lanes = damp_in.shape[0]
    length = cells * CHUNKS
    parts = [(0, 2), (2, fields)] if fields > 2 else [(0, fields)]
    moves = [(dissip, damp_in)]
    for first, last in parts:
        rows = pl.ds(first * lanes, (last - first) * lanes)
        moves.append((courant.at[rows], speed_in.at[rows]))
        moves.append((residual.at[rows], source_in.at[rows]))
    started = copies(moves, sems)
    started[0].wait()
    damp_t[...] = damp_in[...].T
    for part, (first, last) in enumerate(parts):
        at, size, repeat = first * CHUNKS, (last - first) * CHUNKS, last - first
        for inner_copy, taken, turned in (
            (started[1 + 2 * part], speed_in, speed_t),
            (started[2 + 2 * part], source_in, source_t),
        ):
            inner_copy.wait()
            for field in range(first, last):
                turned[pl.ds(field * length, length), :] = taken[pl.ds(field * lanes, lanes), :].T

        if part == 0:
            moves = [(wall_dissip, wall_damp), (wall_courant, wall_speed)]
            wall_started = copies(moves, sems, len(started))

        def speed(i):
            return speed_t[pl.ds(at * cells + i, size, stride=cells), :]

        def source(i):
            return source_t[pl.ds(at * cells + i, size, stride=cells), :]

        def damp(i):
            rows = damp_t[pl.ds(i, CHUNKS, stride=cells), :]
            return jnp.concatenate([rows] * repeat, axis=0) if repeat > 1 else rows

        left, pair = first_pair(source), pair_of(source, 0, cells)
        for k, step in enumerate(chunk_matrix(speed, damp, cells)):
            if k == (cells - 2) // 2:
                put(elements[0], step + left + pair, at, size)
                break
            up, down, damps = step
            left, pair, w = pair_source(down, damps, left, pair, pair_of(source, k + 1, cells))
            put(chunk_up, up, at, size, k * UP)
            put(chunk_w, w, at, size, k * 2)
    for level, rows in enumerate(levels_of(fields)):
        for at, size in blocks(rows, 8):
            merged, up, w = merge(*get_both(elements[level], VALUES, at, size))
            put(elements[level + 1], merged, at, size)
            put(ups[level], up, at, size)
            put(ws[level], w, at, size)
    for v in range(VALUES):
        packed[pl.ds(v * fields, fields), :] = elements[-1][v]
    for copy in wall_started:
        copy.wait()


def wrap_round(fields, bit, own, other, after, packed, up_out, w_out):
    second = is_second("wrap", bit)
    for at, size in blocks(fields, 8):
        mine = flat(own, VALUES, fields, at, size)
        theirs = flat(other, VALUES, fields, at, size)
        merged, up, w = merge(choose(second, theirs, mine), choose(second, mine, theirs))
        put_flat(packed, merged, fields, at, size)
        put(up_out, up, at, size)
        put(w_out, w, at, size)


def wall_matrix(fields, span, cells, *refs):
    speed_in, damp_in = refs[0:2]
    packed, damp_out, chunk_up, chunk_down = refs[2:6]
    ups, downs = refs[6:9], refs[9:12]
    elements = refs[12:16]
    size = span * CHUNKS
    for field in range(fields):
        at = field * size

        def speed(i):
            return speed_in[pl.ds(at * cells + i, size, stride=cells), :]

        def damp(i):
            return damp_in[pl.ds(i, size, stride=cells), :]

        for k, step in enumerate(chunk_matrix(speed, damp, cells)):
            if k == (cells - 2) // 2:
                put(elements[0], step, at, size)
                break
            up, down, damps = step
            put(chunk_up, up, at, size, k * UP)
            put(chunk_down, down, at, size, k * CHUNK_DOWN)
            if field == 0:
                put(damp_out, damps, 0, size, k * 2)
    lines = fields * span
    for level, rows in enumerate(levels_of(lines)):
        for at, size in blocks(rows, 8):
            merged, up, down = merge_matrix(*get_both(elements[level], MATRIX, at, size))
            put(elements[level + 1], merged, at, size)
            put(ups[level], up, at, size)
            put(downs[level], down, at, size)
    not_first, not_last = open_ends("normal")
    for v in range(MATRIX):
        value = elements[-1][v]
        if v in (0, 1, 2, 4, 5, 8, 10):
            value = value * not_first
        if v in (5, 7, 10, 11, 13, 14, 15):
            value = value * not_last
        packed[pl.ds(v * lines, lines), :] = value


def wall_round(lines, bit, final, own, other, *refs):
    started = []
    if final:
        coupling, packed, up_out, down_out, outer_out, coupling_out, sems = refs
        count = sems.shape[0]
        parts = [pl.ds(k * count, count) for k in range(count)]
        started = copies([(coupling.at[k], coupling_out.at[k]) for k in parts], sems)
    else:
        packed, up_out, down_out = refs
    second = is_second("normal", bit)
    upper = is_second("normal", bit + 1)
    for at, size in blocks(lines, 8):
        mine = flat(own, MATRIX, lines, at, size)
        theirs = flat(other, MATRIX, lines, at, size)
        merged, up, down = merge_matrix(
            choose(second, theirs, mine), choose(second, mine, theirs)
        )
        put(up_out, up, at, size)
        put(down_out, down, at, size)
        if not final:
            put_flat(packed, merged, lines, at, size)
            continue
        ll, lr, rl, rr = quads(merged)
        outer, into = choose(upper, rr, ll), choose(upper, rl, lr)
        out, middle = choose(upper, lr, rl), choose(upper, ll, rr)
        is_upper = jnp.where(upper, 1.0, 0.0)
        pivot = inverse(
            outer[0] + (1.0 - is_upper), outer[1], outer[2], outer[3] + is_upper
        )
        put_flat(packed, minus(middle, times(out, times(pivot, into))), lines, at, size)
        put(outer_out, pivot + into + out, at, size)
    for copy in started:
        copy.wait()


def wall_source_round(lines, bit, own, other, down_in, packed, w_out):
    second = is_second("normal", bit)
    for at, size in blocks(lines, 8):
        mine = flat(own, SOURCE, lines, at, size)
        theirs = flat(other, SOURCE, lines, at, size)
        merged, w = merge_source(
            get(down_in, MERGE_DOWN, at, size),
            choose(second, theirs, mine),
            choose(second, mine, theirs),
        )
        put_flat(packed, merged, lines, at, size)
        put(w_out, w, at, size)


def reduce_source(down, factors, second, upper, mine, theirs):
    merged, w = merge_source(
        down, choose(second, theirs, mine), choose(second, mine, theirs)
    )
    outer = apply(factors[0:4], choose(upper, merged[2:4], merged[0:2]))
    centre = choose(upper, merged[0:2], merged[2:4])
    return minus(centre, apply(factors[8:12], outer)), outer, w


def wall_share(lines, bit, own, down_in, outer_in, matrix, forth, over, back):
    second, upper = is_second("normal", bit), is_second("normal", bit + 1)
    for at, size in blocks(lines, 8):
        mine = flat(own, SOURCE, lines, at, size)
        none = tuple(jnp.zeros_like(value) for value in mine)
        down, factors = get(down_in, MERGE_DOWN, at, size), get(outer_in, 12, at, size)
        part, _, _ = reduce_source(down, factors, second, upper, mine, none)
        halves = flat(matrix, 4, lines, at, size)
        share = part + halves[0:2]
        put_flat(forth, choose(second, share, mine), lines, at, size)
        put_flat(over, part + halves[2:4], lines, at, size)
        put_flat(back, choose(second, mine, share), lines, at, size)


def wrap_three(fields, own, following, before, packed, back_up, back_w, next_up, next_w):
    for at, size in blocks(fields, 8):
        run, up, w = merge(
            flat(before, VALUES, fields, at, size), flat(own, VALUES, fields, at, size)
        )
        put(back_up, up, at, size)
        put(back_w, w, at, size)
        run, up, w = merge(run, flat(following, VALUES, fields, at, size))
        put(next_up, up, at, size)
        put(next_w, w, at, size)
        put_flat(packed, run, fields, at, size)


def middle(fields, span, wrap_cells, wall_cells, bits, *refs):
    three, opposite, back_up, back_w, next_up, next_w = refs[0:6]
    refs = refs[6:]
    round_ups, round_ws, refs = refs[:bits], refs[bits : 2 * bits], refs[2 * bits :]
    chunk_up, chunk_w, ups, ws = refs[0], refs[1], refs[2:5], refs[5:8]
    coupling, damps_in, chunk_down, downs = refs[8], refs[9], refs[10], refs[11:14]
    packed, wall_w, wall_ws = refs[14], refs[15], refs[16:19]
    ends, solved_t, solved, mixed = refs[19:23], refs[23], refs[24], refs[25]
    sources = refs[26:30]

    for at, size in blocks(fields, 8):
        outer_left, outer_right = close_ring(
            flat(three, VALUES, fields, at, size), flat(opposite, VALUES, fields, at, size)
        )
        right = inner(get(next_up, UP, at, size), get(next_w, 2, at, size), outer_left, outer_right)
        left = inner(get(back_up, UP, at, size), get(back_w, 2, at, size), outer_left, right)
        left, right = round_down(round_ups, round_ws, "wrap", bits, at, size, left, right)
        put(ends[0], left + right, at, size)
    last = split_all(ends[0], ends[1:], ups, ws, levels_of(fields))
    length = wrap_cells * CHUNKS
    for at, size in blocks(fields * CHUNKS, 16):

        def store(i, value):
            solved_t[pl.ds(at * wrap_cells + i, size, stride=wrap_cells), :] = value

        back_substitute(last, chunk_up, chunk_w, wrap_cells, at, size, store)
    lanes = solved.shape[0] // fields
    for field in range(fields):
        solved[pl.ds(field * lanes, lanes), :] = solved_t[pl.ds(field * length, length), :].T

    for at, size in blocks(lanes, 16):
        update = [solved[pl.ds(j * lanes + at, size), :] for j in range(fields)]
        for k in range(fields):
            total = coupling[k * fields, pl.ds(at, size), :].astype(jnp.float32) * update[0]
            for j in range(1, fields):
                factor = coupling[k * fields + j, pl.ds(at, size), :]
                total = total + factor.astype(jnp.float32) * update[j]
            mixed[pl.ds(k * lanes + at, size), :] = total

    pairs = (wall_cells - 2) // 2
    size = span * CHUNKS
    for field in range(fields):
        at = field * size

        def source(i):
            return mixed[pl.ds(at * wall_cells + i, size, stride=wall_cells), :]

        left, pair = first_pair(source), pair_of(source, 0, wall_cells)
        for k in range(pairs):
            left, pair, w = pair_source(
                get(chunk_down, CHUNK_DOWN, at, size, k * CHUNK_DOWN),
                get(damps_in, 2, 0, size, k * 2),
                left,
                pair,
                pair_of(source, k + 1, wall_cells),
            )
            put(wall_w, w, at, size, k * 2)
        put(sources[0], left + pair, at, size)
    lines = fields * span
    for level, rows in enumerate(levels_of(lines)):
        for at, size in blocks(rows, 8):
            down = get(downs[level], MERGE_DOWN, at, size)
            merged, w = merge_source(down, *get_both(sources[level], SOURCE, at, size))
            put(sources[level + 1], merged, at, size)
            put(wall_ws[level], w, at, size)
    not_first, not_last = open_ends("normal")
    for v, keep in enumerate((not_first, None, None, not_last)):
        value = sources[-1][v]
        packed[pl.ds(v * lines, lines), :] = value if keep is None else value * keep


def wall_up(fields, span, cells, bits, *refs):
    own_matrix, down_in, outer_in, own, from_next, from_previous, from_opposite = refs[0:7]
    refs = refs[7:]
    round_ups, round_ws, refs = refs[: bits + 1], refs[bits + 1 : 2 * bits + 1], refs[2 * bits + 1 :]
    chunk_up, chunk_w, ups, ws = refs[0], refs[1], refs[2:5], refs[5:8]
    update = refs[8]
    ends, result, sems = refs[9:13], refs[13], refs[14]
    lines = fields * span
    second, upper = is_second("normal", bits), is_second("normal", bits + 1)
    for at, size in blocks(lines, 8):
        previous = flat(from_previous, 4, lines, at, size)
        following = flat(from_next, 4, lines, at, size)
        down, factors = get(down_in, MERGE_DOWN, at, size), get(outer_in, 12, at, size)
        part, outer, w = reduce_source(
            down,
            factors,
            second,
            upper,
            flat(own, SOURCE, lines, at, size),
            choose(second, previous, following),
        )
        one = choose(second, following, previous)
        two = flat(from_opposite, 4, lines, at, size)
        shares = plus(one[0:2], two[0:2])
        matrix = plus(flat(own_matrix, 4, lines, at, size), one[2:4] + two[2:4])
        centre = apply(inverse(*matrix), plus(part, shares))
        outer = minus(outer, apply(factors[0:4], apply(factors[4:8], centre)))
        left, right = choose(upper, centre, outer), choose(upper, outer, centre)
        between = inner(get(round_ups[bits], UP, at, size), w, left, right)
        left, right = choose(second, between, left), choose(second, right, between)
        left, right = round_down(round_ups, round_ws, "normal", bits, at, size, left, right)
        put(ends[0], left + right, at, size)
    last = split_all(ends[0], ends[1:], ups, ws, levels_of(lines))
    size = span * CHUNKS
    length = size * cells
    started = []
    for field in range(fields):
        at = field * size

        def store(i, value):
            result[pl.ds(at * cells + i, size, stride=cells), :] = value

        back_substitute(last, chunk_up, chunk_w, cells, at, size, store)
        rows = pl.ds(field * length, length)
        copy = pltpu.make_async_copy(result.at[rows], update.at[rows], sems.at[field])
        copy.start()
        started.append(copy)
    for copy in started:
        copy.wait()


def f32(*shape):
    return jax.ShapeDtypeStruct(shape, jnp.float32)


def vmem(*shape):
    return pltpu.VMEM(shape, jnp.float32)


IN_VMEM = pl.BlockSpec(memory_space=pltpu.VMEM)
IN_HBM = pl.BlockSpec(memory_space=pltpu.HBM)
PARAMS = pltpu.CompilerParams(vmem_limit_bytes=24 * 2**20)


def kernel(name, body, ins, outs, scratch, flops):
    in_bytes = sum(a.size * a.dtype.itemsize for a, _ in ins)
    out_bytes = sum(a.size * 4 for a, _ in outs)
    outputs = pl.pallas_call(
        body,
        out_shape=[a for a, _ in outs],
        in_specs=[spec for _, spec in ins],
        out_specs=[spec for _, spec in outs],
        scratch_shapes=scratch,
        compiler_params=PARAMS,
        cost_estimate=pl.CostEstimate(
            flops=flops, bytes_accessed=in_bytes + out_bytes, transcendentals=0
        ),
        name=name,
    )(*[a for a, _ in ins])
    return list(outputs)


def inside(arrays):
    return [(a, IN_VMEM) for a in arrays]


def outside(arrays):
    return [(pltpu.with_memory_space_constraint(a, pltpu.HBM), IN_HBM) for a in arrays]


def exchange(array, axis, mask):
    count = lax.axis_size(axis)
    return lax.ppermute(array, axis, [(i, i ^ mask) for i in range(count)])


def pass_on(array, axis, bit, targets, swap=0):
    count = lax.axis_size(axis)

    def target(i):
        place = i // (1 << bit) % 4
        return (i + (targets[place] - place) * (1 << bit)) ^ swap

    return lax.ppermute(array, axis, [(i, target(i)) for i in range(count)])


def local(residual, courant_xi, courant_eta, dissip_xi, dissip_eta, coupling):
    fields, span, high, wide = residual.shape
    lanes = span * high
    wrap_cells, wall_cells = wide // CHUNKS, high // CHUNKS
    wrap_pairs, wall_pairs = (wrap_cells - 2) // 2, (wall_cells - 2) // 2
    wrap_count, wall_count = lax.axis_size("wrap"), lax.axis_size("normal")
    lines = fields * span
    wrap_levels, wall_levels = levels_of(fields), levels_of(lines)
    wrap_rows, wall_rows = fields * CHUNKS, lines * CHUNKS

    def rows_of(array):
        return array.reshape(-1, wide)

    wrap_bits = wrap_count.bit_length() - 3
    wall_bits = wall_count.bit_length() - 3
    results = kernel(
        "wrap_down",
        functools.partial(wrap_down, fields, wrap_cells),
        outside(
            [rows_of(a) for a in (residual, courant_xi, dissip_xi, courant_eta, dissip_eta)]
        ),
        inside(
            [
                f32(VALUES * fields, lanes),
                f32(wrap_pairs * UP, wrap_rows, lanes),
                f32(wrap_pairs * 2, wrap_rows, lanes),
            ]
            + [f32(UP, n, lanes) for n in wrap_levels]
            + [f32(2, n, lanes) for n in wrap_levels]
            + [f32(fields * lanes, wide), f32(lanes, wide)]
        ),
        [vmem(fields * lanes, wide)] * 2
        + [vmem(lanes, wide)]
        + [vmem(fields * wide, lanes)] * 2
        + [vmem(wide, lanes)]
        + [vmem(VALUES, n, lanes) for n in [wrap_rows] + wrap_levels]
        + [pltpu.SemaphoreType.DMA((7,))],
        100 * residual.size,
    )
    element, wrap_factors, wall_inputs = results[0], results[1:9], results[9:11]
    results = kernel(
        "wall_matrix",
        functools.partial(wall_matrix, fields, span, wall_cells),
        inside(wall_inputs),
        inside(
            [
                f32(MATRIX * lines, wide),
                f32(wall_pairs * 2, span * CHUNKS, wide),
                f32(wall_pairs * UP, wall_rows, wide),
                f32(wall_pairs * CHUNK_DOWN, wall_rows, wide),
            ]
            + [f32(UP, n, wide) for n in wall_levels]
            + [f32(MERGE_DOWN, n, wide) for n in wall_levels]
        ),
        [vmem(MATRIX, n, wide) for n in [wall_rows] + wall_levels],
        100 * residual.size,
    )
    matrix, damps, chunk_up, chunk_down = results[0:4]
    wall_ups, wall_downs = results[4:7], results[7:10]
    wrap_ups, wrap_ws = [], []
    for bit in range(wrap_bits):
        element, up, w = kernel(
            f"wrap_round_{bit}",
            functools.partial(wrap_round, fields, bit),
            inside([element, exchange(element, "wrap", 1 << bit), damps]),
            inside([f32(VALUES * fields, lanes), f32(UP, fields, lanes), f32(2, fields, lanes)]),
            [],
            200 * fields * lanes,
        )
        wrap_ups.append(up)
        wrap_ws.append(w)
    swap = 1 if wrap_bits > 0 else 0
    before, following, opposite = (
        pass_on(element, "wrap", wrap_bits, targets, swap)
        for targets in ((1, 2, 3, 0), (3, 0, 1, 2), (2, 3, 0, 1))
    )
    three = kernel(
        "wrap_three",
        functools.partial(wrap_three, fields),
        inside([element, following, before]),
        inside(
            [f32(VALUES * fields, lanes)]
            + [f32(UP, fields, lanes), f32(2, fields, lanes)] * 2
        ),
        [],
        400 * fields * lanes,
    )
    round_ups, round_downs = [], []
    for bit in range(wall_bits + 1):
        final = bit == wall_bits
        matrix, up, down, *extra = kernel(
            f"wall_round_{bit}",
            functools.partial(wall_round, lines, bit, final),
            inside([matrix, exchange(matrix, "normal", 1 << bit)])
            + (outside([coupling.reshape(fields * fields, lanes, wide)]) if final else []),
            inside(
                [
                    f32((4 if final else MATRIX) * lines, wide),
                    f32(UP, lines, wide),
                    f32(MERGE_DOWN, lines, wide),
                ]
                + (
                    [
                        f32(12, lines, wide),
                        jax.ShapeDtypeStruct((fields * fields, lanes, wide), coupling.dtype),
                    ]
                    if final
                    else []
                )
            ),
            [pltpu.SemaphoreType.DMA((fields,))] if final else [],
            200 * lines * wide,
        )
        round_ups.append(up)
        round_downs.append(down)
    outer, coupling_in = extra[:1], extra[1]
    source, *wall_ws = kernel(
        "middle",
        functools.partial(middle, fields, span, wrap_cells, wall_cells, wrap_bits),
        inside(
            [three[0], opposite]
            + three[1:]
            + wrap_ups
            + wrap_ws
            + wrap_factors
            + [coupling_in, damps, chunk_down]
            + wall_downs
        ),
        inside(
            [f32(SOURCE * lines, wide), f32(wall_pairs * 2, wall_rows, wide)]
            + [f32(2, n, wide) for n in wall_levels]
        ),
        [vmem(4, n, lanes) for n in reversed([wrap_rows] + wrap_levels)]
        + [vmem(fields * wide, lanes), vmem(fields * lanes, wide), vmem(fields * lanes, wide)]
        + [vmem(SOURCE, n, wide) for n in [wall_rows] + wall_levels],
        100 * residual.size,
    )
    round_ws = []
    for bit in range(wall_bits):
        source, w = kernel(
            f"wall_source_round_{bit}",
            functools.partial(wall_source_round, lines, bit),
            inside([source, exchange(source, "normal", 1 << bit), round_downs[bit]]),
            inside([f32(SOURCE * lines, wide), f32(2, lines, wide)]),
            [],
            50 * lines * wide,
        )
        round_ws.append(w)
    forth, over, back = kernel(
        "wall_share",
        functools.partial(wall_share, lines, wall_bits),
        inside([source, round_downs[wall_bits]] + outer + [matrix]),
        inside([f32(SOURCE * lines, wide)] * 3),
        [],
        50 * lines * wide,
    )
    (update,) = kernel(
        "wall_up",
        functools.partial(wall_up, fields, span, wall_cells, wall_bits),
        inside(
            [matrix, round_downs[wall_bits]]
            + outer
            + [
                source,
                pass_on(back, "normal", wall_bits, (3, 0, 1, 2)),
                pass_on(forth, "normal", wall_bits, (1, 2, 3, 0)),
                pass_on(over, "normal", wall_bits, (2, 3, 0, 1)),
            ]
            + round_ups
            + round_ws
            + [chunk_up, wall_ws[0]]
            + wall_ups
            + wall_ws[1:]
        ),
        [(f32(fields * lanes, wide), IN_HBM)],
        [vmem(4, n, wide) for n in reversed([wall_rows] + wall_levels)]
        + [vmem(fields * lanes, wide), pltpu.SemaphoreType.DMA((fields,))],
        30 * residual.size,
    )
    return update.reshape(residual.shape)


def solution(mesh):
    placed = (
        P(None, None, "normal", "wrap"),
        P(None, None, "normal", "wrap"),
        P(None, None, "normal", "wrap"),
        P(None, "normal", "wrap"),
        P(None, "normal", "wrap"),
        P(None, None, None, "normal", "wrap"),
    )
    return jax.shard_map(
        local,
        mesh=mesh,
        in_specs=placed,
        out_specs=P(None, None, "normal", "wrap"),
        check_vma=False,
    )
```

```python
import functools

import jax
import jax.numpy as jnp
from jax import lax
from jax.experimental import pallas as pl
from jax.experimental.pallas import tpu as pltpu
from jax.sharding import PartitionSpec as P

MATRIX = 16
SOURCE = 4
VALUES = MATRIX + SOURCE
UP = 8
CHUNK_DOWN = 9
MERGE_DOWN = 12
CHUNKS = 8


def inverse(a, b, c, d):
    scale = 1.0 / (a * d - b * c)
    return (d * scale, -b * scale, -c * scale, a * scale)


def times(x, y):
    return (
        x[0] * y[0] + x[1] * y[2],
        x[0] * y[1] + x[1] * y[3],
        x[2] * y[0] + x[3] * y[2],
        x[2] * y[1] + x[3] * y[3],
    )


def apply(x, v):
    return (x[0] * v[0] + x[1] * v[1], x[2] * v[0] + x[3] * v[1])


def minus(x, y):
    return tuple(a - b for a, b in zip(x, y))


def plus(x, y):
    return tuple(a + b for a, b in zip(x, y))


def negative(x):
    return tuple(-a for a in x)


def quads(element):
    return (element[0:4], element[4:8], element[8:12], element[12:16])


def merge_matrix(first, second):
    ll, lm, ml, mm = quads(first)
    nn, mr, rm, rr = quads(second)
    pivot = inverse(*plus(mm, nn))
    wl = times(pivot, ml)
    wr = times(pivot, mr)
    merged = (
        minus(ll, times(lm, wl))
        + negative(times(lm, wr))
        + negative(times(rm, wl))
        + minus(rr, times(rm, wr))
    )
    return merged, wl + wr, pivot + lm + rm


def merge_source(down, first, second):
    pivot, lm, rm = down[0:4], down[4:8], down[8:12]
    w = apply(pivot, plus(first[2:4], second[0:2]))
    return minus(first[0:2], apply(lm, w)) + minus(second[2:4], apply(rm, w)), w


def merge(first, second):
    matrix, up, down = merge_matrix(first[:MATRIX], second[:MATRIX])
    source, w = merge_source(down, first[MATRIX:], second[MATRIX:])
    return matrix + source, up, w


def inner(up, w, left, right):
    return minus(minus(w, apply(up[0:4], left)), apply(up[4:8], right))


def chunk_matrix(speed, damp, cells):
    def link(i):
        p = 2.0 * (damp(i) + damp(i + 1))
        q = 0.25 * (speed(i) + speed(i + 1))
        return q - p, -q - p

    def centre(i):
        return 1.0 + damp(i - 1) + 4.0 * damp(i) + damp(i + 1)

    b0, b1 = damp(0), damp(1)
    quarter = 0.25 * speed(0)
    up, low = link(0)
    zero = jnp.zeros_like(b0)
    ll = (b0, quarter - 2.0 * b0, -quarter - 2.0 * b0, 1.0 + 4.0 * b0 + b1)
    lk = (b0, zero, up, b1)
    kl = (b0, low, zero, b1)
    up, low = link(1)
    kk = (centre(1), up, low, centre(2))
    pairs = (cells - 2) // 2
    for k in range(1, pairs + 1):
        i = 2 * k
        pivot = inverse(*kk)
        wl = times(pivot, kl)
        up, low = link(i)
        here, there = damp(i), damp(i + 1)
        wr = (
            pivot[0] * here + pivot[1] * up,
            pivot[1] * there,
            pivot[2] * here + pivot[3] * up,
            pivot[3] * there,
        )
        yield wl + wr, pivot + lk + (low,), (here, there)

        def below(x):
            return (
                here * x[0] + low * x[2],
                here * x[1] + low * x[3],
                there * x[2],
                there * x[3],
            )

        ll = minus(ll, times(lk, wl))
        lk = negative(times(lk, wr))
        kl = negative(below(wl))
        if k < pairs:
            up, low_next = link(i + 1)
            kk = (centre(i + 1), up, low_next, centre(i + 2))
        else:
            quarter = 0.25 * speed(i + 1)
            kk = (
                1.0 + here + 4.0 * there,
                quarter - 2.0 * there,
                -quarter - 2.0 * there,
                there,
            )
        kk = minus(kk, below(wr))
    yield ll + lk + kl + kk


def pair_source(down, damps, left, pair, following):
    pivot, lk, low = down[0:4], down[4:8], down[8]
    w = apply(pivot, pair)
    left = minus(left, apply(lk, w))
    following = minus(following, (damps[0] * w[0] + low * w[1], damps[1] * w[1]))
    return left, following, w


def pair_of(source, k, cells):
    if k == (cells - 2) // 2:
        last = source(cells - 1)
        return (last, jnp.zeros_like(last))
    return (source(2 * k + 1), source(2 * k + 2))


def first_pair(source):
    first = source(0)
    return (jnp.zeros_like(first), first)


def blocks(rows, size):
    return [(at, min(size, rows - at)) for at in range(0, rows, size)]


def get(ref, count, at, size, base=0):
    return tuple(ref[base + v, pl.ds(at, size), :] for v in range(count))


def put(ref, values, at, size, base=0):
    for v, value in enumerate(values):
        ref[base + v, pl.ds(at, size), :] = value


def get_both(ref, count, at, size):
    return tuple(
        tuple(ref[v, pl.ds(2 * at + half, size, stride=2), :] for v in range(count))
        for half in (0, 1)
    )


def levels_of(lines):
    sizes = []
    rows = lines * CHUNKS
    while rows > lines:
        rows //= 2
        sizes.append(rows)
    return sizes


def split_all(top_ref, end_refs, up_refs, w_refs, sizes):
    source = top_ref
    for rows, target, ups, ws in zip(
        reversed(sizes), end_refs, reversed(up_refs), reversed(w_refs)
    ):
        for at, size in blocks(rows, 8):
            ends = get(source, 4, at, size)
            left, right = ends[0:2], ends[2:4]
            middle = inner(get(ups, UP, at, size), get(ws, 2, at, size), left, right)
            for v in range(2):
                target[v, pl.ds(2 * at, size, stride=2), :] = left[v]
                target[v, pl.ds(2 * at + 1, size, stride=2), :] = middle[v]
                target[2 + v, pl.ds(2 * at, size, stride=2), :] = middle[v]
                target[2 + v, pl.ds(2 * at + 1, size, stride=2), :] = right[v]
        source = target
    return source


def back_substitute(ends_ref, up_ref, w_ref, cells, at, size, store):
    ends = get(ends_ref, 4, at, size)
    left, following = ends[0:2], ends[2:4]
    store(0, left[1])
    store(cells - 1, following[0])
    for k in range((cells - 2) // 2 - 1, -1, -1):
        following = inner(
            get(up_ref, UP, at, size, k * UP), get(w_ref, 2, at, size, k * 2), left, following
        )
        store(2 * k + 1, following[0])
        store(2 * k + 2, following[1])


def close_ring(own, rest):
    ll, lr, rl, rr = quads(own)
    nn, nm, mn, mm = quads(rest)
    b = plus(lr, mn)
    c = plus(rl, nm)
    pivot = inverse(*plus(rr, nn))
    f = plus(own[16:18], rest[18:20])
    g = plus(own[18:20], rest[16:18])
    bd = times(b, pivot)
    left = apply(inverse(*minus(plus(ll, mm), times(bd, c))), minus(f, apply(bd, g)))
    right = apply(pivot, minus(g, apply(c, left)))
    return left, right


def open_ends(axis):
    place = lax.axis_index(axis)
    last = lax.axis_size(axis) - 1
    return jnp.where(place > 0, 1.0, 0.0), jnp.where(place < last, 1.0, 0.0)


def is_second(axis, bit):
    return lax.rem(lax.axis_index(axis) // (1 << bit), 2) == 1


def choose(second, one, other):
    return tuple(jnp.where(second, a, b) for a, b in zip(one, other))


def flat(ref, count, rows, at, size):
    return tuple(ref[pl.ds(v * rows + at, size), :] for v in range(count))


def put_flat(ref, values, rows, at, size):
    for v, value in enumerate(values):
        ref[pl.ds(v * rows + at, size), :] = value


def round_down(ups, ws, axis, bits, at, size, left, right):
    for bit in reversed(range(bits)):
        middle = inner(get(ups[bit], UP, at, size), get(ws[bit], 2, at, size), left, right)
        second = is_second(axis, bit)
        left, right = choose(second, middle, left), choose(second, right, middle)
    return left, right


def copies(pairs, sems, first=0):
    started = []
    for i, (source, target) in enumerate(pairs):
        copy = pltpu.make_async_copy(source, target, sems.at[first + i])
        copy.start()
        started.append(copy)
    return started


def wrap_down(fields, cells, *refs):
    residual, courant, dissip, wall_courant, wall_dissip = refs[0:5]
    packed, chunk_up, chunk_w = refs[5:8]
    ups, ws = refs[8:11], refs[11:14]
    wall_speed, wall_damp = refs[14:16]
    source_in, speed_in, damp_in, source_t, speed_t, damp_t = refs[16:22]
    elements, sems = refs[22:26], refs[26]
    lanes = damp_in.shape[0]
    length = cells * CHUNKS
    parts = [(0, 2), (2, fields)] if fields > 2 else [(0, fields)]
    moves = [(dissip, damp_in)]
    for first, last in parts:
        rows = pl.ds(first * lanes, (last - first) * lanes)
        moves.append((courant.at[rows], speed_in.at[rows]))
        moves.append((residual.at[rows], source_in.at[rows]))
    started = copies(moves, sems)
    started[0].wait()
    damp_t[...] = damp_in[...].T
    for part, (first, last) in enumerate(parts):
        at, size, repeat = first * CHUNKS, (last - first) * CHUNKS, last - first
        for inner_copy, taken, turned in (
            (started[1 + 2 * part], speed_in, speed_t),
            (started[2 + 2 * part], source_in, source_t),
        ):
            inner_copy.wait()
            for field in range(first, last):
                turned[pl.ds(field * length, length), :] = taken[pl.ds(field * lanes, lanes), :].T

        if part == 0:
            moves = [(wall_dissip, wall_damp), (wall_courant, wall_speed)]
            wall_started = copies(moves, sems, len(started))

        def speed(i):
            return speed_t[pl.ds(at * cells + i, size, stride=cells), :]

        def source(i):
            return source_t[pl.ds(at * cells + i, size, stride=cells), :]

        def damp(i):
            rows = damp_t[pl.ds(i, CHUNKS, stride=cells), :]
            return jnp.concatenate([rows] * repeat, axis=0) if repeat > 1 else rows

        left, pair = first_pair(source), pair_of(source, 0, cells)
        for k, step in enumerate(chunk_matrix(speed, damp, cells)):
            if k == (cells - 2) // 2:
                put(elements[0], step + left + pair, at, size)
                break
            up, down, damps = step
            left, pair, w = pair_source(down, damps, left, pair, pair_of(source, k + 1, cells))
            put(chunk_up, up, at, size, k * UP)
            put(chunk_w, w, at, size, k * 2)
    for level, rows in enumerate(levels_of(fields)):
        for at, size in blocks(rows, 8):
            merged, up, w = merge(*get_both(elements[level], VALUES, at, size))
            put(elements[level + 1], merged, at, size)
            put(ups[level], up, at, size)
            put(ws[level], w, at, size)
    for v in range(VALUES):
        packed[pl.ds(v * fields, fields), :] = elements[-1][v]
    for copy in wall_started:
        copy.wait()


def wrap_round(fields, bit, own, other, after, packed, up_out, w_out):
    second = is_second("wrap", bit)
    for at, size in blocks(fields, 8):
        mine = flat(own, VALUES, fields, at, size)
        theirs = flat(other, VALUES, fields, at, size)
        merged, up, w = merge(choose(second, theirs, mine), choose(second, mine, theirs))
        put_flat(packed, merged, fields, at, size)
        put(up_out, up, at, size)
        put(w_out, w, at, size)


def wall_matrix(fields, span, cells, *refs):
    speed_in, damp_in = refs[0:2]
    packed, damp_out, chunk_up, chunk_down = refs[2:6]
    ups, downs = refs[6:9], refs[9:12]
    elements = refs[12:16]
    size = span * CHUNKS
    for field in range(fields):
        at = field * size

        def speed(i):
            return speed_in[pl.ds(at * cells + i, size, stride=cells), :]

        def damp(i):
            return damp_in[pl.ds(i, size, stride=cells), :]

        for k, step in enumerate(chunk_matrix(speed, damp, cells)):
            if k == (cells - 2) // 2:
                put(elements[0], step, at, size)
                break
            up, down, damps = step
            put(chunk_up, up, at, size, k * UP)
            put(chunk_down, down, at, size, k * CHUNK_DOWN)
            if field == 0:
                put(damp_out, damps, 0, size, k * 2)
    lines = fields * span
    for level, rows in enumerate(levels_of(lines)):
        for at, size in blocks(rows, 8):
            merged, up, down = merge_matrix(*get_both(elements[level], MATRIX, at, size))
            put(elements[level + 1], merged, at, size)
            put(ups[level], up, at, size)
            put(downs[level], down, at, size)
    not_first, not_last = open_ends("normal")
    for v in range(MATRIX):
        value = elements[-1][v]
        if v in (0, 1, 2, 4, 5, 8, 10):
            value = value * not_first
        if v in (5, 7, 10, 11, 13, 14, 15):
            value = value * not_last
        packed[pl.ds(v * lines, lines), :] = value


def wall_round(lines, bit, final, own, other, *refs):
    started = []
    if final:
        coupling, packed, up_out, down_out, outer_out, coupling_out, sems = refs
        count = sems.shape[0]
        parts = [pl.ds(k * count, count) for k in range(count)]
        started = copies([(coupling.at[k], coupling_out.at[k]) for k in parts], sems)
    else:
        packed, up_out, down_out = refs
    second = is_second("normal", bit)
    upper = is_second("normal", bit + 1)
    for at, size in blocks(lines, 8):
        mine = flat(own, MATRIX, lines, at, size)
        theirs = flat(other, MATRIX, lines, at, size)
        merged, up, down = merge_matrix(
            choose(second, theirs, mine), choose(second, mine, theirs)
        )
        put(up_out, up, at, size)
        put(down_out, down, at, size)
        if not final:
            put_flat(packed, merged, lines, at, size)
            continue
        ll, lr, rl, rr = quads(merged)
        outer, into = choose(upper, rr, ll), choose(upper, rl, lr)
        out, middle = choose(upper, lr, rl), choose(upper, ll, rr)
        is_upper = jnp.where(upper, 1.0, 0.0)
        pivot = inverse(
            outer[0] + (1.0 - is_upper), outer[1], outer[2], outer[3] + is_upper
        )
        put_flat(packed, minus(middle, times(out, times(pivot, into))), lines, at, size)
        put(outer_out, pivot + into + out, at, size)
    for copy in started:
        copy.wait()


def wall_source_round(lines, bit, own, other, down_in, packed, w_out):
    second = is_second("normal", bit)
    for at, size in blocks(lines, 8):
        mine = flat(own, SOURCE, lines, at, size)
        theirs = flat(other, SOURCE, lines, at, size)
        merged, w = merge_source(
            get(down_in, MERGE_DOWN, at, size),
            choose(second, theirs, mine),
            choose(second, mine, theirs),
        )
        put_flat(packed, merged, lines, at, size)
        put(w_out, w, at, size)


def reduce_source(down, factors, second, upper, mine, theirs):
    merged, w = merge_source(
        down, choose(second, theirs, mine), choose(second, mine, theirs)
    )
    outer = apply(factors[0:4], choose(upper, merged[2:4], merged[0:2]))
    centre = choose(upper, merged[0:2], merged[2:4])
    return minus(centre, apply(factors[8:12], outer)), outer, w


def wall_share(lines, bit, own, down_in, outer_in, matrix, forth, over, back):
    second, upper = is_second("normal", bit), is_second("normal", bit + 1)
    for at, size in blocks(lines, 8):
        mine = flat(own, SOURCE, lines, at, size)
        none = tuple(jnp.zeros_like(value) for value in mine)
        down, factors = get(down_in, MERGE_DOWN, at, size), get(outer_in, 12, at, size)
        part, _, _ = reduce_source(down, factors, second, upper, mine, none)
        halves = flat(matrix, 4, lines, at, size)
        share = part + halves[0:2]
        put_flat(forth, choose(second, share, mine), lines, at, size)
        put_flat(over, part + halves[2:4], lines, at, size)
        put_flat(back, choose(second, mine, share), lines, at, size)


def wrap_three(fields, own, following, before, packed, back_up, back_w, next_up, next_w):
    for at, size in blocks(fields, 8):
        run, up, w = merge(
            flat(before, VALUES, fields, at, size), flat(own, VALUES, fields, at, size)
        )
        put(back_up, up, at, size)
        put(back_w, w, at, size)
        run, up, w = merge(run, flat(following, VALUES, fields, at, size))
        put(next_up, up, at, size)
        put(next_w, w, at, size)
        put_flat(packed, run, fields, at, size)


def middle(fields, span, wrap_cells, wall_cells, bits, *refs):
    three, opposite, back_up, back_w, next_up, next_w = refs[0:6]
    refs = refs[6:]
    round_ups, round_ws, refs = refs[:bits], refs[bits : 2 * bits], refs[2 * bits :]
    chunk_up, chunk_w, ups, ws = refs[0], refs[1], refs[2:5], refs[5:8]
    coupling, damps_in, chunk_down, downs = refs[8], refs[9], refs[10], refs[11:14]
    packed, wall_w, wall_ws = refs[14], refs[15], refs[16:19]
    ends, solved_t, solved, mixed = refs[19:23], refs[23], refs[24], refs[25]
    sources = refs[26:30]

    for at, size in blocks(fields, 8):
        outer_left, outer_right = close_ring(
            flat(three, VALUES, fields, at, size), flat(opposite, VALUES, fields, at, size)
        )
        right = inner(get(next_up, UP, at, size), get(next_w, 2, at, size), outer_left, outer_right)
        left = inner(get(back_up, UP, at, size), get(back_w, 2, at, size), outer_left, right)
        left, right = round_down(round_ups, round_ws, "wrap", bits, at, size, left, right)
        put(ends[0], left + right, at, size)
    last = split_all(ends[0], ends[1:], ups, ws, levels_of(fields))
    length = wrap_cells * CHUNKS
    for at, size in blocks(fields * CHUNKS, 16):

        def store(i, value):
            solved_t[pl.ds(at * wrap_cells + i, size, stride=wrap_cells), :] = value

        back_substitute(last, chunk_up, chunk_w, wrap_cells, at, size, store)
    lanes = solved.shape[0] // fields
    for field in range(fields):
        solved[pl.ds(field * lanes, lanes), :] = solved_t[pl.ds(field * length, length), :].T

    for at, size in blocks(lanes, 16):
        update = [solved[pl.ds(j * lanes + at, size), :] for j in range(fields)]
        for k in range(fields):
            total = coupling[k * fields, pl.ds(at, size), :].astype(jnp.float32) * update[0]
            for j in range(1, fields):
                factor = coupling[k * fields + j, pl.ds(at, size), :]
                total = total + factor.astype(jnp.float32) * update[j]
            mixed[pl.ds(k * lanes + at, size), :] = total

    pairs = (wall_cells - 2) // 2
    size = span * CHUNKS
    for field in range(fields):
        at = field * size

        def source(i):
            return mixed[pl.ds(at * wall_cells + i, size, stride=wall_cells), :]

        left, pair = first_pair(source), pair_of(source, 0, wall_cells)
        for k in range(pairs):
            left, pair, w = pair_source(
                get(chunk_down, CHUNK_DOWN, at, size, k * CHUNK_DOWN),
                get(damps_in, 2, 0, size, k * 2),
                left,
                pair,
                pair_of(source, k + 1, wall_cells),
            )
            put(wall_w, w, at, size, k * 2)
        put(sources[0], left + pair, at, size)
    lines = fields * span
    for level, rows in enumerate(levels_of(lines)):
        for at, size in blocks(rows, 8):
            down = get(downs[level], MERGE_DOWN, at, size)
            merged, w = merge_source(down, *get_both(sources[level], SOURCE, at, size))
            put(sources[level + 1], merged, at, size)
            put(wall_ws[level], w, at, size)
    not_first, not_last = open_ends("normal")
    for v, keep in enumerate((not_first, None, None, not_last)):
        value = sources[-1][v]
        packed[pl.ds(v * lines, lines), :] = value if keep is None else value * keep


def wall_up(fields, span, cells, bits, *refs):
    own_matrix, down_in, outer_in, own, from_previous, from_opposite, from_next = refs[0:7]
    refs = refs[7:]
    round_ups, round_ws, refs = refs[: bits + 1], refs[bits + 1 : 2 * bits + 1], refs[2 * bits + 1 :]
    chunk_up, chunk_w, ups, ws = refs[0], refs[1], refs[2:5], refs[5:8]
    update = refs[8]
    ends, result, sems = refs[9:13], refs[13], refs[14]
    lines = fields * span
    second, upper = is_second("normal", bits), is_second("normal", bits + 1)
    for at, size in blocks(lines, 8):
        previous = flat(from_previous, 4, lines, at, size)
        following = flat(from_next, 4, lines, at, size)
        down, factors = get(down_in, MERGE_DOWN, at, size), get(outer_in, 12, at, size)
        part, outer, w = reduce_source(
            down,
            factors,
            second,
            upper,
            flat(own, SOURCE, lines, at, size),
            choose(second, previous, following),
        )
        one = choose(second, following, previous)
        two = flat(from_opposite, 4, lines, at, size)
        shares = plus(one[0:2], two[0:2])
        matrix = plus(flat(own_matrix, 4, lines, at, size), one[2:4] + two[2:4])
        centre = apply(inverse(*matrix), plus(part, shares))
        outer = minus(outer, apply(factors[0:4], apply(factors[4:8], centre)))
        left, right = choose(upper, centre, outer), choose(upper, outer, centre)
        between = inner(get(round_ups[bits], UP, at, size), w, left, right)
        left, right = choose(second, between, left), choose(second, right, between)
        left, right = round_down(round_ups, round_ws, "normal", bits, at, size, left, right)
        put(ends[0], left + right, at, size)
    last = split_all(ends[0], ends[1:], ups, ws, levels_of(lines))
    size = span * CHUNKS
    length = size * cells
    started = []
    for field in range(fields):
        at = field * size

        def store(i, value):
            result[pl.ds(at * cells + i, size, stride=cells), :] = value

        back_substitute(last, chunk_up, chunk_w, cells, at, size, store)
        rows = pl.ds(field * length, length)
        copy = pltpu.make_async_copy(result.at[rows], update.at[rows], sems.at[field])
        copy.start()
        started.append(copy)
    for copy in started:
        copy.wait()


def f32(*shape):
    return jax.ShapeDtypeStruct(shape, jnp.float32)


def vmem(*shape):
    return pltpu.VMEM(shape, jnp.float32)


IN_VMEM = pl.BlockSpec(memory_space=pltpu.VMEM)
IN_HBM = pl.BlockSpec(memory_space=pltpu.HBM)
PARAMS = pltpu.CompilerParams(vmem_limit_bytes=24 * 2**20)


def kernel(name, body, ins, outs, scratch, flops):
    in_bytes = sum(a.size * a.dtype.itemsize for a, _ in ins)
    out_bytes = sum(a.size * 4 for a, _ in outs)
    outputs = pl.pallas_call(
        body,
        out_shape=[a for a, _ in outs],
        in_specs=[spec for _, spec in ins],
        out_specs=[spec for _, spec in outs],
        scratch_shapes=scratch,
        compiler_params=PARAMS,
        cost_estimate=pl.CostEstimate(
            flops=flops, bytes_accessed=in_bytes + out_bytes, transcendentals=0
        ),
        name=name,
    )(*[a for a, _ in ins])
    return list(outputs)


def inside(arrays):
    return [(a, IN_VMEM) for a in arrays]


def outside(arrays):
    return [(pltpu.with_memory_space_constraint(a, pltpu.HBM), IN_HBM) for a in arrays]


def exchange(array, axis, mask):
    count = lax.axis_size(axis)
    return lax.ppermute(array, axis, [(i, i ^ mask) for i in range(count)])


def pass_on(array, axis, bit, targets, swap=0):
    count = lax.axis_size(axis)

    def target(i):
        place = i // (1 << bit) % 4
        return (i + (targets[place] - place) * (1 << bit)) ^ swap

    return lax.ppermute(array, axis, [(i, target(i)) for i in range(count)])


def local(residual, courant_xi, courant_eta, dissip_xi, dissip_eta, coupling):
    fields, span, high, wide = residual.shape
    lanes = span * high
    wrap_cells, wall_cells = wide // CHUNKS, high // CHUNKS
    wrap_pairs, wall_pairs = (wrap_cells - 2) // 2, (wall_cells - 2) // 2
    wrap_count, wall_count = lax.axis_size("wrap"), lax.axis_size("normal")
    lines = fields * span
    wrap_levels, wall_levels = levels_of(fields), levels_of(lines)
    wrap_rows, wall_rows = fields * CHUNKS, lines * CHUNKS

    def rows_of(array):
        return array.reshape(-1, wide)

    wrap_bits = wrap_count.bit_length() - 3
    wall_bits = wall_count.bit_length() - 3
    results = kernel(
        "wrap_down",
        functools.partial(wrap_down, fields, wrap_cells),
        outside(
            [rows_of(a) for a in (residual, courant_xi, dissip_xi, courant_eta, dissip_eta)]
        ),
        inside(
            [
                f32(VALUES * fields, lanes),
                f32(wrap_pairs * UP, wrap_rows, lanes),
                f32(wrap_pairs * 2, wrap_rows, lanes),
            ]
            + [f32(UP, n, lanes) for n in wrap_levels]
            + [f32(2, n, lanes) for n in wrap_levels]
            + [f32(fields * lanes, wide), f32(lanes, wide)]
        ),
        [vmem(fields * lanes, wide)] * 2
        + [vmem(lanes, wide)]
        + [vmem(fields * wide, lanes)] * 2
        + [vmem(wide, lanes)]
        + [vmem(VALUES, n, lanes) for n in [wrap_rows] + wrap_levels]
        + [pltpu.SemaphoreType.DMA((7,))],
        100 * residual.size,
    )
    element, wrap_factors, wall_inputs = results[0], results[1:9], results[9:11]
    results = kernel(
        "wall_matrix",
        functools.partial(wall_matrix, fields, span, wall_cells),
        inside(wall_inputs),
        inside(
            [
                f32(MATRIX * lines, wide),
                f32(wall_pairs * 2, span * CHUNKS, wide),
                f32(wall_pairs * UP, wall_rows, wide),
                f32(wall_pairs * CHUNK_DOWN, wall_rows, wide),
            ]
            + [f32(UP, n, wide) for n in wall_levels]
            + [f32(MERGE_DOWN, n, wide) for n in wall_levels]
        ),
        [vmem(MATRIX, n, wide) for n in [wall_rows] + wall_levels],
        100 * residual.size,
    )
    matrix, damps, chunk_up, chunk_down = results[0:4]
    wall_ups, wall_downs = results[4:7], results[7:10]
    wrap_ups, wrap_ws = [], []
    for bit in range(wrap_bits):
        element, up, w = kernel(
            f"wrap_round_{bit}",
            functools.partial(wrap_round, fields, bit),
            inside([element, exchange(element, "wrap", 1 << bit), damps]),
            inside([f32(VALUES * fields, lanes), f32(UP, fields, lanes), f32(2, fields, lanes)]),
            [],
            200 * fields * lanes,
        )
        wrap_ups.append(up)
        wrap_ws.append(w)
    swap = 1 if wrap_bits > 0 else 0
    before, following, opposite = (
        pass_on(element, "wrap", wrap_bits, targets, swap)
        for targets in ((1, 2, 3, 0), (3, 0, 1, 2), (2, 3, 0, 1))
    )
    three = kernel(
        "wrap_three",
        functools.partial(wrap_three, fields),
        inside([element, following, before]),
        inside(
            [f32(VALUES * fields, lanes)]
            + [f32(UP, fields, lanes), f32(2, fields, lanes)] * 2
        ),
        [],
        400 * fields * lanes,
    )
    round_ups, round_downs = [], []
    for bit in range(wall_bits + 1):
        final = bit == wall_bits
        matrix, up, down, *extra = kernel(
            f"wall_round_{bit}",
            functools.partial(wall_round, lines, bit, final),
            inside([matrix, exchange(matrix, "normal", 1 << bit)])
            + (outside([coupling.reshape(fields * fields, lanes, wide)]) if final else []),
            inside(
                [
                    f32((4 if final else MATRIX) * lines, wide),
                    f32(UP, lines, wide),
                    f32(MERGE_DOWN, lines, wide),
                ]
                + (
                    [
                        f32(12, lines, wide),
                        jax.ShapeDtypeStruct((fields * fields, lanes, wide), coupling.dtype),
                    ]
                    if final
                    else []
                )
            ),
            [pltpu.SemaphoreType.DMA((fields,))] if final else [],
            200 * lines * wide,
        )
        round_ups.append(up)
        round_downs.append(down)
    outer, coupling_in = extra[:1], extra[1]
    source, *wall_ws = kernel(
        "middle",
        functools.partial(middle, fields, span, wrap_cells, wall_cells, wrap_bits),
        inside(
            [three[0], opposite]
            + three[1:]
            + wrap_ups
            + wrap_ws
            + wrap_factors
            + [coupling_in, damps, chunk_down]
            + wall_downs
        ),
        inside(
            [f32(SOURCE * lines, wide), f32(wall_pairs * 2, wall_rows, wide)]
            + [f32(2, n, wide) for n in wall_levels]
        ),
        [vmem(4, n, lanes) for n in reversed([wrap_rows] + wrap_levels)]
        + [vmem(fields * wide, lanes), vmem(fields * lanes, wide), vmem(fields * lanes, wide)]
        + [vmem(SOURCE, n, wide) for n in [wall_rows] + wall_levels],
        100 * residual.size,
    )
    round_ws = []
    for bit in range(wall_bits):
        source, w = kernel(
            f"wall_source_round_{bit}",
            functools.partial(wall_source_round, lines, bit),
            inside([source, exchange(source, "normal", 1 << bit), round_downs[bit]]),
            inside([f32(SOURCE * lines, wide), f32(2, lines, wide)]),
            [],
            50 * lines * wide,
        )
        round_ws.append(w)
    forth, over, back = kernel(
        "wall_share",
        functools.partial(wall_share, lines, wall_bits),
        inside([source, round_downs[wall_bits]] + outer + [matrix]),
        inside([f32(SOURCE * lines, wide)] * 3),
        [],
        50 * lines * wide,
    )
    (update,) = kernel(
        "wall_up",
        functools.partial(wall_up, fields, span, wall_cells, wall_bits),
        inside(
            [matrix, round_downs[wall_bits]]
            + outer
            + [
                source,
                pass_on(forth, "normal", wall_bits, (1, 2, 3, 0)),
                pass_on(over, "normal", wall_bits, (2, 3, 0, 1)),
                pass_on(back, "normal", wall_bits, (3, 0, 1, 2)),
            ]
            + round_ups
            + round_ws
            + [chunk_up, wall_ws[0]]
            + wall_ups
            + wall_ws[1:]
        ),
        [(f32(fields * lanes, wide), IN_HBM)],
        [vmem(4, n, wide) for n in reversed([wall_rows] + wall_levels)]
        + [vmem(fields * lanes, wide), pltpu.SemaphoreType.DMA((fields,))],
        30 * residual.size,
    )
    return update.reshape(residual.shape)


def solution(mesh):
    placed = (
        P(None, None, "normal", "wrap"),
        P(None, None, "normal", "wrap"),
        P(None, None, "normal", "wrap"),
        P(None, "normal", "wrap"),
        P(None, "normal", "wrap"),
        P(None, None, None, "normal", "wrap"),
    )
    return jax.shard_map(
        local,
        mesh=mesh,
        in_specs=placed,
        out_specs=P(None, None, "normal", "wrap"),
        check_vma=False,
    )
```
